32 devices in a mesh: fsdp: 16 (over z, x, core), tp: 2 (over y).
Axes of the slice: x: 2, y: 2, z: 4, core: 2. Of those that a mesh axis runs over, the one named last changes fastest.
Arguments:
- tokens: bfloat16 [8192, 1024], P('fsdp'), may hold values from -6 to 6
- cotangent: bfloat16 [8192, 1024], P('fsdp'), may hold values from -6 to 6
- segments: int32 [8192], P('fsdp'), may hold values from 0 to 7, never falling along the last dimension, each value on 1 to 2000 neighbouring positions
- doc_batch: int32 [8], replicated, may hold values from 0 to 2
- ln1_gain: float32 [2, 1024], replicated, may hold values from 0.5 to 1.5
- ln1_bias: float32 [2, 1024], replicated, may hold values from -4 to 4
- w_qkv: bfloat16 [2, 1024, 3, 1024], P(None, 'fsdp', None, 'tp'), may hold values from -0.1875 to 0.1875
- b_qv: float32 [2, 2, 1024], P(None, None, 'tp'), may hold values from -6 to 6
- w_out: bfloat16 [2, 1024, 1024], P(None, 'tp', 'fsdp'), may hold values from -3 to 3
- b_out: float32 [2, 1024], replicated, may hold values from -4 to 4
- ln2_gain: float32 [2, 1024], replicated, may hold values from 0.5 to 1.5
- ln2_bias: float32 [2, 1024], replicated, may hold values from -4 to 4
- w_fc: bfloat16 [2, 1024, 4096], P(None, 'fsdp', 'tp'), may hold values from -0.1875 to 0.1875
- b_fc: float32 [2, 4096], P(None, 'tp'), may hold values from -4 to 4
- w_proj: bfloat16 [2, 4096, 1024], P(None, 'tp', 'fsdp'), may hold values from -0.09375 to 0.09375
- b_proj: float32 [2, 1024], replicated, may hold values from -4 to 4
Outputs:
- outputs: bfloat16 [8192, 1024], P('fsdp')
- grad_tokens: float32 [8192, 1024], P('fsdp')
- grad_ln1_gain: float32 [2, 1024], replicated
- grad_ln1_bias: float32 [2, 1024], replicated
- grad_w_qkv: float32 [2, 1024, 3, 1024], P(None, 'fsdp', None, 'tp')
- grad_b_qv: float32 [2, 2, 1024], P(None, None, 'tp')
- grad_w_out: float32 [2, 1024, 1024], P(None, 'tp', 'fsdp')
- grad_b_out: float32 [2, 1024], replicated
- grad_ln2_gain: float32 [2, 1024], replicated
- grad_ln2_bias: float32 [2, 1024], replicated
- grad_w_fc: float32 [2, 1024, 4096], P(None, 'fsdp', 'tp')
- grad_b_fc: float32 [2, 4096], P(None, 'tp')
- grad_w_proj: float32 [2, 4096, 1024], P(None, 'tp', 'fsdp')
- grad_b_proj: float32 [2, 1024], replicated
The draws below stay inside these ranges and needn't reach their ends.
Inputs may be any that keep to these rules, and one draw needn't show every extreme that they name: `segments`: documents are contiguous and numbered in order, each of 1 to 2000 tokens, one of exactly 2000.
All inputs are finite; a program needn't handle non-finite values.
Results may differ from the reference program's by a relative error of at most 0.013.
Values may be sent and summed in bfloat16 or wider, within the bound.
A program may use at most 192 MiB of HBM per device.

```python
import math
import jax
import jax.numpy as jnp
import numpy as np
from jax import lax

D = 1024
HEADS = 16
HEAD_DIM = 64
FF = 4096
LAYERS = 2
MB = 3
DOC_MAX = 2000
TOK_DEV = 512
TOKENS = 8192
DOCS = 8
REACH = 4


def place_ends(values, stream_key, least, largest):
    place = [jax.random.randint(jax.random.fold_in(stream_key, axis), (), 0, length) for axis, length in enumerate(values.shape)]
    longest = values.shape.index(max(values.shape))
    next_to = place[:longest] + [(place[longest] + 1) % values.shape[longest]] + place[longest + 1:]
    return values.at[tuple(place)].set(least).at[tuple(next_to)].set(largest)


def steps_of(stream_key, extent, shards, smallest, top_value):
    gain, own = 1.0, jax.random.fold_in(stream_key, 6)
    for dim, parts in shards:
        steps = jnp.exp(jax.random.uniform(jax.random.fold_in(own, dim), (parts,), jnp.float32, smallest / len(shards), top_value / len(shards)))
        gain = gain * jnp.repeat(steps, extent[dim] // parts).reshape([-1 if axis == dim else 1 for axis in range(len(extent))])
    return gain


def profile(amount, total, reach, skew):
    portions = [(1 << 20) // math.isqrt(standing ** skew) + 1 for standing in range(2, amount + 1)]
    spare, given = total - reach - (amount - 1), [1] * (amount - 1)
    while spare > 0:
        free = [i for i in range(amount - 1) if given[i] < reach]
        whole, left = sum([portions[i] for i in free]), spare
        for i in free:
            addition = min(reach - given[i], max(1, left * portions[i] // whole), spare)
            given[i] = given[i] + addition
            spare = spare - addition
    return np.array([reach] + given)


def ragged(own_key, amount, total, limit, skew):
    if amount == 2:
        one = jax.random.randint(own_key, (), max(1, total - limit), min(limit, total - 1) + 1)
        return jnp.stack([one, total - one])
    sizes = jnp.asarray(profile(amount, total, limit, skew), jnp.int32)
    couples = (amount - 1) // 2
    donor, sink = sizes[1:1 + 2 * couples:2], sizes[2:2 + 2 * couples:2]
    margin = jnp.minimum(donor - 1, limit - sink)
    shifted = jax.random.randint(jax.random.fold_in(own_key, 1), (couples,), 0, 1 << 20) % (margin + 1)
    sizes = sizes.at[1:1 + 2 * couples:2].set(donor - shifted).at[2:2 + 2 * couples:2].set(sink + shifted)
    return sizes[jax.random.permutation(jax.random.fold_in(own_key, 2), amount)]


def bell_draw(key, extent, scale, limit, split=(), kind=jnp.bfloat16):
    loudness = steps_of(key, extent, split, -0.22, 0.18) if split else 1.0
    entries = jax.random.normal(key, extent, jnp.float32) * scale * loudness
    return jnp.minimum(jnp.maximum(entries, -limit), limit).astype(kind)


def setup_inputs(seed: int = 0) -> dict:
    streams_of = jax.random.split(jax.random.key(seed), 17)
    tokens = bell_draw(streams_of[0], (TOKENS, D), 1.0, 6.0, ((0, 16),))
    cotangent = bell_draw(streams_of[1], (TOKENS, D), 1.0, 6.0, ((0, 16),))
    segments = jnp.searchsorted(jnp.cumsum(ragged(streams_of[2], DOCS, TOKENS, DOC_MAX, 0)), jnp.arange(TOKENS), side="right").astype(jnp.int32)
    doc_batch = place_ends(jax.random.randint(streams_of[3], (DOCS,), 0, MB), jax.random.fold_in(streams_of[3], 1), 0, MB - 1).astype(jnp.int32)
    ln1_gain = jnp.clip(1.0 + 0.1 * jax.random.normal(streams_of[4], (LAYERS, D), jnp.float32), 0.5, 1.5)
    ln1_bias = bell_draw(streams_of[5], (LAYERS, D), 0.3, 4.0, (), jnp.float32)
    w_qkv = bell_draw(streams_of[6], (LAYERS, D, 3, D), D ** -0.5, 0.1875, ((1, 16), (3, 2)))
    b_qv = bell_draw(streams_of[7], (LAYERS, 2, D), 0.5, 6.0, ((2, 2),), jnp.float32)
    w_out = bell_draw(streams_of[8], (LAYERS, D, D), (HEAD_DIM // 16) ** -0.5, 3.0, ((1, 2), (2, 16)))
    b_out = bell_draw(streams_of[9], (LAYERS, D), 0.3, 4.0, (), jnp.float32)
    ln2_gain = jnp.clip(1.0 + 0.1 * jax.random.normal(streams_of[10], (LAYERS, D), jnp.float32), 0.5, 1.5)
    ln2_bias = bell_draw(streams_of[11], (LAYERS, D), 0.3, 4.0, (), jnp.float32)
    w_fc = bell_draw(streams_of[12], (LAYERS, D, FF), D ** -0.5, 0.1875, ((1, 16), (2, 2)))
    b_fc = bell_draw(streams_of[13], (LAYERS, FF), 0.3, 4.0, ((1, 2),), jnp.float32)
    w_proj = bell_draw(streams_of[14], (LAYERS, FF, D), FF ** -0.5, 0.09375, ((1, 2), (2, 16)))
    b_proj = bell_draw(streams_of[15], (LAYERS, D), 0.3, 4.0, (), jnp.float32)
    return {"tokens": tokens, "cotangent": cotangent, "segments": segments, "doc_batch": doc_batch, "ln1_gain": ln1_gain, "ln1_bias": ln1_bias, "w_qkv": w_qkv, "b_qv": b_qv, "w_out": w_out, "b_out": b_out, "ln2_gain": ln2_gain, "ln2_bias": ln2_bias, "w_fc": w_fc, "b_fc": b_fc, "w_proj": w_proj, "b_proj": b_proj}


EPS = 1e-05
HIGH = lax.Precision.HIGHEST

@jax.custom_vjp
def low(v):
    return lax.optimization_barrier(v.astype(jnp.bfloat16)).astype(jnp.float32)

@jax.custom_vjp
def low_back(v):
    return v

def low_keep(v):
    return (low(v), None)

def low_pass(kept, grad):
    return (grad,)

def back_keep(v):
    return (v, None)

def back_low(kept, grad):
    return (low(grad),)
low.defvjp(low_keep, low_pass)
low_back.defvjp(back_keep, back_low)

def matmul_high(left, right):
    return jnp.dot(left, right, precision=HIGH, preferred_element_type=jnp.float32)

def layer_norm(inputs, gain_vec, bias_vec):
    row_mean = lax.optimization_barrier(jnp.mean(inputs, -1, keepdims=True))
    centred = inputs - row_mean
    row_var = lax.optimization_barrier(jnp.mean(centred * centred, -1, keepdims=True))
    return centred * lax.rsqrt(row_var + EPS) * gain_vec + bias_vec

def gelu_tanh(inputs):
    return 0.5 * inputs * (1.0 + jnp.tanh(0.7978845608028654 * (inputs + 0.044715 * inputs * inputs * inputs)))

def attention(queries, keys_all, values_all, segments):
    back_rows = REACH * TOK_DEV
    keys_pad = jnp.pad(keys_all, ((back_rows, 0), (0, 0), (0, 0)))
    values_pad = jnp.pad(values_all, ((back_rows, 0), (0, 0), (0, 0)))
    seg_pad = jnp.pad(segments, (back_rows, 0), constant_values=-1)
    query_pos = jnp.arange(TOK_DEV, dtype=jnp.int32) + back_rows
    key_pos = jnp.arange(back_rows + TOK_DEV, dtype=jnp.int32)

    @jax.checkpoint
    def one_block(block_id):
        first_row = (block_id * TOK_DEV).astype(jnp.int32)
        query_blk = lax.dynamic_slice_in_dim(queries, first_row, TOK_DEV, 0)
        key_blk = lax.dynamic_slice_in_dim(keys_pad, first_row, back_rows + TOK_DEV, 0)
        value_blk = lax.dynamic_slice_in_dim(values_pad, first_row, back_rows + TOK_DEV, 0)
        seg_query = lax.dynamic_slice_in_dim(segments, first_row, TOK_DEV, 0)
        seg_key = lax.dynamic_slice_in_dim(seg_pad, first_row, back_rows + TOK_DEV, 0)
        allowed = (seg_query[:, None] == seg_key[None, :]) & (key_pos[None, :] <= query_pos[:, None])
        scores = low_back(jnp.einsum('qhd,khd->hqk', query_blk, key_blk, precision=HIGH) * HEAD_DIM ** (-0.5))
        scores = jnp.where(allowed[None], scores, -jnp.inf)
        attn_probs = low(jax.nn.softmax(scores, axis=-1))
        return jnp.einsum('hqk,khd->qhd', attn_probs, value_blk, precision=HIGH)
    blocks = lax.map(one_block, jnp.arange(TOKENS // TOK_DEV, dtype=jnp.int32))
    return blocks.reshape(TOKENS, HEADS * HEAD_DIM)

def reference(tokens, cotangent, segments, doc_batch, ln1_gain, ln1_bias, w_qkv, b_qv, w_out, b_out, ln2_gain, ln2_bias, w_fc, b_fc, w_proj, b_proj):
    batch_ids = doc_batch[segments]
    onehot = (batch_ids[:, None] == jnp.arange(MB, dtype=jnp.int32)[None, :]).astype(jnp.float32)
    counts = lax.optimization_barrier(jnp.sum(onehot, 0))
    row_weight = TOKENS / (MB * lax.optimization_barrier(jnp.sum(onehot * counts[None, :], 1)))
    params = (ln1_gain.astype(jnp.float32), ln1_bias.astype(jnp.float32), w_qkv.astype(jnp.float32), b_qv.astype(jnp.float32), w_out.astype(jnp.float32), b_out.astype(jnp.float32), ln2_gain.astype(jnp.float32), ln2_bias.astype(jnp.float32), w_fc.astype(jnp.float32), b_fc.astype(jnp.float32), w_proj.astype(jnp.float32), b_proj.astype(jnp.float32))

    def forward(stream, weights):
        gain_one, bias_one, mat_qkv, bias_qv, mat_out, bias_out, gain_two, bias_two, mat_fc, bias_fc, mat_proj, bias_proj = weights
        for layer_at in range(LAYERS):
            normed = low(layer_norm(stream, gain_one[layer_at], bias_one[layer_at]))
            bias_three = jnp.stack([bias_qv[layer_at, 0], jnp.zeros_like(bias_qv[layer_at, 0]), bias_qv[layer_at, 1]])
            qkv = jnp.einsum('td,dcf->tcf', normed, mat_qkv[layer_at], precision=HIGH) + bias_three[None]
            qkv = low_back(low(qkv))
            queries = qkv[:, 0].reshape(TOKENS, HEADS, HEAD_DIM)
            keys_all = qkv[:, 1].reshape(TOKENS, HEADS, HEAD_DIM)
            values_all = qkv[:, 2].reshape(TOKENS, HEADS, HEAD_DIM)
            mixed = low_back(low(attention(queries, keys_all, values_all, segments)))
            middle = stream + low_back(matmul_high(mixed, mat_out[layer_at]) + bias_out[layer_at])
            normed_two = low(layer_norm(middle, gain_two[layer_at], bias_two[layer_at]))
            hidden = low_back(matmul_high(normed_two, mat_fc[layer_at]) + bias_fc[layer_at])
            act_low = low(gelu_tanh(hidden))
            stream = middle + low_back(matmul_high(act_low, mat_proj[layer_at]) + bias_proj[layer_at])
        return stream
    result, pull_back = jax.vjp(forward, tokens.astype(jnp.float32), params)
    grad_in, grads = pull_back(cotangent.astype(jnp.float32) * row_weight[:, None])
    return (result.astype(jnp.bfloat16), grad_in, grads[0], grads[1], grads[2], grads[3], grads[4], grads[5], grads[6], grads[7], grads[8], grads[9], grads[10], grads[11])
```

```python
import functools

import jax
import jax.numpy as jnp
from jax import lax
from jax.experimental import pallas as pl
from jax.experimental.pallas import tpu as pltpu
from jax.sharding import PartitionSpec as P

HEAD_DIM = 64
LAYERS = 2
MB = 3
REACH = 4

EPS = 1e-05
GROUP = REACH
QB = 256
KB = 256
NEG = -1e30
F32 = jnp.float32
BF16 = jnp.bfloat16
VMEM_BYTES = 56 * 1024 * 1024
LAST = (((1,), (1,)), ((), ()))
FIRST = (((0,), (0,)), ((), ()))


def dot(left, right):
    return jnp.dot(left, right, preferred_element_type=F32)


def dot_last(left, right):
    return lax.dot_general(left, right, LAST, preferred_element_type=F32)


def shape(dims, dtype):
    return jax.ShapeDtypeStruct(dims, dtype)


def whole(dims):
    return pl.BlockSpec(dims, lambda *_: (0,) * len(dims))


def run_kernel(body, grid, scalars, ins, outs, scratch=(), flops=0, moved=0):
    return pl.pallas_call(
        body,
        grid_spec=pltpu.PrefetchScalarGridSpec(
            num_scalar_prefetch=1,
            grid=grid,
            in_specs=[spec for spec, _ in ins],
            out_specs=[spec for spec, _ in outs],
            scratch_shapes=list(scratch),
        ),
        out_shape=[out for _, out in outs],
        compiler_params=pltpu.CompilerParams(
            vmem_limit_bytes=VMEM_BYTES, dimension_semantics=("arbitrary",) * len(grid)
        ),
        cost_estimate=pl.CostEstimate(flops=flops, bytes_accessed=moved, transcendentals=0),
    )(scalars, *[array for _, array in ins])


def each_rows(count, chunk, body):
    def step(at, carry):
        body(pl.ds(pl.multiple_of(at * chunk, chunk), chunk))
        return carry

    lax.fori_loop(0, count // chunk, step, 0)


def norm_parts(rows):
    centred = rows - jnp.mean(rows, -1, keepdims=True)
    inv_scale = lax.rsqrt(jnp.mean(centred * centred, -1, keepdims=True) + EPS)
    return centred * inv_scale, inv_scale


def norm_pull(grad_rows, unit_rows, inv_scale, gain):
    scaled = grad_rows * gain
    return inv_scale * (
        scaled
        - jnp.mean(scaled, -1, keepdims=True)
        - unit_rows * jnp.mean(scaled * unit_rows, -1, keepdims=True)
    )


def eight_rows(rows):
    return jnp.sum(rows.reshape(rows.shape[0] // 8, 8, rows.shape[1]), 0)


def norm_qkv_body(summed, sc, *refs):
    if summed:
        base, own, got, badd, gain, bias, w, bq, stream, low, piece = refs
    else:
        base, gain, bias, w, bq, stream, low, piece = refs

    @pl.when(pl.program_id(0) == 0)
    def _():
        def rows(at):
            value = base[at, :].astype(F32)
            if summed:
                value = value + (own[at, :].astype(F32) + got[at, :].astype(F32)) + badd[...]
            stream[at, :] = value
            unit, _ = norm_parts(value)
            low[at, :] = (unit * gain[...] + bias[...]).astype(BF16)

        each_rows(base.shape[0], 32, rows)

    piece[0] = (dot(low[...], w[...]) + bq[...]).astype(BF16)


def norm_qkv(sc, base, sums, gain, bias, weights, first_block, bq):
    rows, width = base.shape
    cols = bq.shape[1] // GROUP
    ins = [(whole(base.shape), base)]
    if sums is not None:
        own, got, badd = sums
        ins += [(whole(own.shape), own), (whole(got.shape), got), (whole(badd.shape), badd)]
    ins += [
        (whole(gain.shape), gain),
        (whole(bias.shape), bias),
        (pl.BlockSpec((width, cols), lambda s, sc: (0, first_block + (sc[0] ^ s))), weights),
        (pl.BlockSpec((1, cols), lambda s, sc: (0, sc[0] ^ s)), bq),
    ]
    outs = [
        (whole((rows, width)), shape((rows, width), F32)),
        (whole((rows, width)), shape((rows, width), BF16)),
        (pl.BlockSpec((1, rows, cols), lambda s, sc: (s, 0, 0)), shape((GROUP, rows, cols), BF16)),
    ]
    return run_kernel(
        functools.partial(norm_qkv_body, sums is not None),
        (GROUP,),
        sc,
        ins,
        outs,
        flops=2 * rows * width * cols * GROUP,
        moved=rows * width * 12 + width * cols * GROUP * 2,
    )


def out_proj_body(sc, p0, p1, p2, p3, w, full, partial):
    cols = p1.shape[1]
    for s, piece in enumerate((p0, p1, p2, p3)):
        value = piece[0] if s == 0 else piece[...]
        full[:, pl.ds(pl.multiple_of((sc[0] ^ s) * cols, cols), cols)] = value
    tile = 256
    for at in range(0, partial.shape[1], tile):
        partial[:, at : at + tile] = dot_last(full[...], w[at : at + tile, :]).astype(BF16)


def out_proj(sc, mixed_all, got, weights):
    rows, cols = got[0].shape
    width = weights.shape[0]
    ins = [(whole((1, rows, cols)), mixed_all)]
    ins += [(whole((rows, cols)), piece) for piece in got]
    ins += [(whole((width, GROUP * cols)), weights)]
    outs = [
        (whole((rows, GROUP * cols)), shape((rows, GROUP * cols), BF16)),
        (whole((rows, width)), shape((rows, width), BF16)),
    ]
    return run_kernel(
        out_proj_body,
        (1,),
        sc,
        ins,
        outs,
        flops=2 * rows * width * GROUP * cols,
        moved=rows * width * 4 + width * GROUP * cols * 2,
    )


def gelu_rows(value):
    return 0.5 * value * (1.0 + jnp.tanh(0.7978845608028654 * (value + 0.044715 * value * value * value)))


def gelu_slope(value):
    square = value * value
    top = jnp.tanh(0.7978845608028654 * (value + 0.044715 * square * value))
    inner = 0.7978845608028654 * (1.0 + 3.0 * 0.044715 * square)
    return 0.5 * (1.0 + top) + 0.5 * value * (1.0 - top * top) * inner


def feed_body(
    sc, base, own, got, badd, gain, bias, fc, bfc, proj, middle, low, hidden, act, partial, total
):
    at_chunk = pl.program_id(0)

    @pl.when(at_chunk == 0)
    def _():
        def rows(at):
            value = base[at, :] + (own[at, :].astype(F32) + got[at, :].astype(F32)) + badd[...]
            middle[at, :] = value
            unit, _ = norm_parts(value)
            low[at, :] = (unit * gain[...] + bias[...]).astype(BF16)

        each_rows(base.shape[0], 32, rows)

    hidden[...] = dot(low[...], fc[...]) + bfc[...]

    def rows_act(at):
        act[at, :] = gelu_rows(hidden[at, :]).astype(BF16)

    each_rows(hidden.shape[0], 32, rows_act)
    part = dot_last(act[...], proj[...])

    @pl.when(at_chunk == 0)
    def _():
        total[...] = part

    @pl.when(at_chunk > 0)
    def _():
        total[...] += part

    @pl.when(at_chunk == pl.num_programs(0) - 1)
    def _():
        partial[...] = total[...].astype(BF16)


def feed(sc, base, own, got, badd, gain, bias, weights, fc_at, proj_at, bfc):
    rows, width = base.shape
    units, chunk = bfc.shape[1], 512
    ins = [
        (whole(base.shape), base),
        (whole(own.shape), own),
        (whole(got.shape), got),
        (whole(badd.shape), badd),
        (whole(gain.shape), gain),
        (whole(bias.shape), bias),
        (pl.BlockSpec((width, chunk), lambda j, sc: (0, fc_at // chunk + j)), weights),
        (pl.BlockSpec((1, chunk), lambda j, sc: (0, j)), bfc),
        (pl.BlockSpec((width, chunk), lambda j, sc: (0, proj_at // chunk + j)), weights),
    ]
    outs = [
        (whole((rows, width)), shape((rows, width), F32)),
        (whole((rows, width)), shape((rows, width), BF16)),
        (pl.BlockSpec((rows, chunk), lambda j, sc: (0, j)), shape((rows, units), F32)),
        (pl.BlockSpec((rows, chunk), lambda j, sc: (0, j)), shape((rows, units), BF16)),
        (whole((rows, width)), shape((rows, width), BF16)),
    ]
    return run_kernel(
        feed_body,
        (units // chunk,),
        sc,
        ins,
        outs,
        scratch=[pltpu.VMEM((rows, width), F32)],
        flops=4 * rows * width * units,
        moved=rows * width * 16 + width * units * 4 + rows * units * 6,
    )


def feed_pull_body(sc, grad, hidden, proj, fc, low, sum_low, slope_grad, sum_hidden, partial, total, grad_act):
    at_chunk = pl.program_id(0)

    @pl.when(at_chunk == 0)
    def _():
        sum_low[...] = jnp.zeros_like(sum_low)

        def rows(at):
            value = grad[at, :].astype(BF16)
            low[at, :] = value
            sum_low[...] += eight_rows(value.astype(F32))

        each_rows(grad.shape[0], 32, rows)

    grad_act[...] = dot(low[...], proj[...])
    sum_hidden[...] = jnp.zeros_like(sum_hidden)

    def rows_slope(at):
        value = (grad_act[at, :] * gelu_slope(hidden[at, :])).astype(BF16)
        slope_grad[at, :] = value
        sum_hidden[...] += eight_rows(value.astype(F32))

    each_rows(grad.shape[0], 32, rows_slope)
    part = dot_last(slope_grad[...], fc[...])

    @pl.when(at_chunk == 0)
    def _():
        total[...] = part

    @pl.when(at_chunk > 0)
    def _():
        total[...] += part

    @pl.when(at_chunk == pl.num_programs(0) - 1)
    def _():
        partial[...] = total[...].astype(BF16)


def feed_pull(sc, grad, hidden, weights, fc_at, proj_at):
    rows, width = grad.shape
    units, chunk = hidden.shape[1], 512
    ins = [
        (whole(grad.shape), grad),
        (pl.BlockSpec((rows, chunk), lambda j, sc: (0, j)), hidden),
        (pl.BlockSpec((width, chunk), lambda j, sc: (0, proj_at // chunk + j)), weights),
        (pl.BlockSpec((width, chunk), lambda j, sc: (0, fc_at // chunk + j)), weights),
    ]
    outs = [
        (whole((rows, width)), shape((rows, width), BF16)),
        (whole((8, width)), shape((8, width), F32)),
        (pl.BlockSpec((rows, chunk), lambda j, sc: (0, j)), shape((rows, units), BF16)),
        (pl.BlockSpec((8, chunk), lambda j, sc: (0, j)), shape((8, units), F32)),
        (whole((rows, width)), shape((rows, width), BF16)),
    ]
    return run_kernel(
        feed_pull_body,
        (units // chunk,),
        sc,
        ins,
        outs,
        scratch=[pltpu.VMEM((rows, width), F32), pltpu.VMEM((rows, chunk), F32)],
        flops=4 * rows * width * units,
        moved=rows * width * 8 + width * units * 4 + rows * units * 6,
    )


def norm_pull_rows(at, grad, own, got, inputs, gain, grad_new, sum_gain, sum_bias):
    grad_rows = own[at, :].astype(F32) + got[at, :].astype(F32)
    unit, inv_scale = norm_parts(inputs[at, :])
    value = grad[at, :] + norm_pull(grad_rows, unit, inv_scale, gain[...])
    grad_new[at, :] = value
    sum_gain[...] += eight_rows(grad_rows * unit)
    sum_bias[...] += eight_rows(grad_rows)
    return value


def mid_pull_body(sc, grad, own, got, inputs, gain, w, grad_new, low, pieces, sum_gain, sum_bias, sum_low, mixed):
    for total in (sum_gain, sum_bias, sum_low):
        total[...] = jnp.zeros_like(total)

    def rows(at):
        value = norm_pull_rows(at, grad, own, got, inputs, gain, grad_new, sum_gain, sum_bias)
        value = value.astype(BF16)
        low[at, :] = value
        sum_low[...] += eight_rows(value.astype(F32))

    each_rows(grad.shape[0], 32, rows)
    mixed[...] = dot(low[...], w[...]).astype(BF16)
    cols = pieces.shape[2]
    for s in range(GROUP):
        pieces[s] = mixed[:, pl.ds(pl.multiple_of((sc[0] ^ s) * cols, cols), cols)]


def mid_pull(sc, grad, own, got, inputs, gain, weights, out_cols):
    rows, width = grad.shape
    cols = out_cols // GROUP
    ins = [
        (whole(grad.shape), grad),
        (whole(own.shape), own),
        (whole(got.shape), got),
        (whole(inputs.shape), inputs),
        (whole(gain.shape), gain),
        (whole((width, out_cols)), weights),
    ]
    sums = (whole((8, width)), shape((8, width), F32))
    outs = [
        (whole((rows, width)), shape((rows, width), F32)),
        (whole((rows, width)), shape((rows, width), BF16)),
        (whole((GROUP, rows, cols)), shape((GROUP, rows, cols), BF16)),
        sums,
        sums,
        sums,
    ]
    return run_kernel(
        mid_pull_body,
        (1,),
        sc,
        ins,
        outs,
        scratch=[pltpu.VMEM((rows, out_cols), BF16)],
        flops=2 * rows * width * out_cols,
        moved=rows * width * 18 + width * out_cols * 2,
    )


def qkv_pull_body(sc, p0, p1, p2, p3, w, full, partial, sums):
    cols = p1.shape[1]
    for s, piece in enumerate((p0, p1, p2, p3)):
        value = piece[0] if s == 0 else piece[...]
        full[:, pl.ds(pl.multiple_of((sc[0] ^ s) * cols, cols), cols)] = value
    sums[...] = jnp.zeros_like(sums)

    def rows(at):
        sums[...] += eight_rows(full[at, :].astype(F32))

    each_rows(full.shape[0], 32, rows)
    tile = 256
    for at in range(0, partial.shape[1], tile):
        partial[:, at : at + tile] = dot_last(full[...], w[at : at + tile, :]).astype(BF16)


def qkv_pull(sc, own, got, weights, block_at):
    rows, cols = got[0].shape
    width, total = weights.shape[0], GROUP * cols
    ins = [(whole((1, rows, cols)), own)]
    ins += [(whole((rows, cols)), piece) for piece in got]
    ins += [(pl.BlockSpec((width, total), lambda j, sc: (0, block_at)), weights)]
    outs = [
        (whole((rows, total)), shape((rows, total), BF16)),
        (whole((rows, width)), shape((rows, width), BF16)),
        (whole((8, total)), shape((8, total), F32)),
    ]
    return run_kernel(
        qkv_pull_body,
        (1,),
        sc,
        ins,
        outs,
        flops=2 * rows * width * total,
        moved=rows * width * 6 + width * total * 2,
    )


def first_pull_body(sc, grad, own, got, inputs, gain, grad_new, sum_gain, sum_bias):
    for total in (sum_gain, sum_bias):
        total[...] = jnp.zeros_like(total)

    def rows(at):
        norm_pull_rows(at, grad, own, got, inputs, gain, grad_new, sum_gain, sum_bias)

    each_rows(grad.shape[0], 32, rows)


def first_pull(sc, grad, own, got, inputs, gain):
    rows, width = grad.shape
    arrays = (grad, own, got, inputs, gain)
    sums = (whole((8, width)), shape((8, width), F32))
    return run_kernel(
        first_pull_body,
        (1,),
        sc,
        [(whole(array.shape), array) for array in arrays],
        [(whole((rows, width)), shape((rows, width), F32)), sums, sums],
        moved=rows * width * 16,
    )


def weight_pull_body(first_steps, sc, x0, g0, x1, g1, out, flipped):
    at = pl.program_id(0)

    @pl.when(at == 0)
    def _():
        flipped[...] = x0[...].T

    @pl.when(at == first_steps)
    def _():
        flipped[...] = x1[...].T

    @pl.when(at < first_steps)
    def _():
        out[...] = dot(flipped[...], g0[...]).astype(BF16)

    @pl.when(at >= first_steps)
    def _():
        out[...] = dot(flipped[...], g1[...]).astype(BF16)


def weight_pull(sc, x0, g0, x1, g1):
    rows, width = x0.shape
    chunk = 512
    n0, n1 = g0.shape[1] // chunk, g1.shape[1] // chunk
    ins = [
        (whole(x0.shape), x0),
        (pl.BlockSpec((rows, chunk), lambda j, sc: (0, jnp.minimum(j, n0 - 1))), g0),
        (whole(x1.shape), x1),
        (pl.BlockSpec((rows, chunk), lambda j, sc: (0, jnp.maximum(j - n0, 0))), g1),
    ]
    outs = [
        (
            pl.BlockSpec((width, chunk), lambda j, sc: (0, j)),
            shape((width, (n0 + n1) * chunk), BF16),
        )
    ]
    return run_kernel(
        functools.partial(weight_pull_body, n0),
        (n0 + n1,),
        sc,
        ins,
        outs,
        scratch=[pltpu.VMEM((width, rows), BF16)],
        flops=2 * rows * width * (n0 + n1) * chunk,
        moved=rows * width * 4 + (rows + width) * (n0 + n1) * chunk * 2,
    )[0]


def doc_start_rows(sc, docs, positions):
    start = jnp.zeros_like(positions)
    for d in range(docs):
        first = sc[2 + d]
        start = jnp.where(first <= positions, jnp.maximum(start, first), start)
    return start


def doc_start_one(sc, docs, position):
    start = jnp.int32(0)
    for d in range(docs):
        first = sc[2 + d]
        start = jnp.where(first <= position, jnp.maximum(start, first), start)
    return start


def query_rows(sc, docs, block):
    first = sc[1] + block * QB
    position = first + lax.broadcasted_iota(jnp.int32, (1, QB), 1)
    start = doc_start_rows(sc, docs, position)
    return (
        jnp.concatenate([position, position], 1),
        jnp.concatenate([start, start], 1),
        doc_start_one(sc, docs, first),
    )


def head_stack(rows, scale):
    value = rows.astype(F32)
    if scale != 1.0:
        value = value * scale
    lane = lax.broadcasted_iota(jnp.int32, value.shape, 1)
    return jnp.concatenate(
        [jnp.where(lane < HEAD_DIM, value, 0.0), jnp.where(lane >= HEAD_DIM, value, 0.0)], 0
    ).astype(BF16)


def place_rows(sc, s, rows):
    return pl.ds(pl.multiple_of((sc[0] ^ s) * rows, rows), rows)


def spread(sc, pieces, first_col, cols, straight=None, flipped=None):
    for s, piece in enumerate(pieces):
        value = piece[s] if len(piece.shape) == 3 and piece.shape[0] > 1 else None
        if value is None:
            value = piece[0] if len(piece.shape) == 3 else piece[...]
        value = value[:, first_col : first_col + cols]
        at = place_rows(sc, s, value.shape[0])
        if straight is not None:
            straight[at, :] = value
        if flipped is not None:
            flipped[:, at] = value.T


def block_at(block, size):
    return pl.ds(pl.multiple_of(block * size, size), size)


def masked_scores(keys, queries, first_key, position, start):
    scores = dot_last(keys, queries)
    key_at = first_key + lax.broadcasted_iota(jnp.int32, (KB, 1), 0)
    return jnp.where((key_at >= start) & (key_at <= position), scores, NEG)


def flash_step(keys_ref, values_ref, queries, block, first_key, position, start, acc, carry):
    top, total = carry
    scores = masked_scores(keys_ref[block_at(block, KB), :], queries, first_key, position, start)
    top_new = jnp.maximum(top, jnp.max(scores, 0, keepdims=True))
    expo = jnp.exp(scores - top_new)
    shrink = jnp.exp(top - top_new)
    total = total * shrink + jnp.sum(expo, 0, keepdims=True)
    expo = expo.astype(BF16)
    for h in range(2):
        lanes = slice(h * QB, (h + 1) * QB)
        rows = slice(h * HEAD_DIM, (h + 1) * HEAD_DIM)
        values = values_ref[rows, block_at(block, KB)]
        acc[rows, :] = acc[rows, :] * shrink[:, lanes] + dot(values, expo[:, lanes])
    return top_new, total


def attend_own_body(docs, sc, p0, p1, p2, p3, acc, top_ref, total_ref, q_all, k_all, v_flip):
    block = pl.program_id(0)
    cols = q_all.shape[1]

    @pl.when(block == 0)
    def _():
        pieces = (p0, p1, p2, p3)
        spread(sc, pieces, 0, cols, straight=q_all)
        spread(sc, pieces, cols, cols, straight=k_all)
        spread(sc, pieces, 2 * cols, cols, flipped=v_flip)

    position, start, lowest = query_rows(sc, docs, block)
    queries = head_stack(q_all[block_at(block, QB), :], HEAD_DIM**-0.5)
    acc[...] = jnp.zeros_like(acc)
    least = jnp.maximum(lowest - sc[1], 0) // KB
    last = ((block + 1) * QB - 1) // KB

    def step(back, carry):
        at = last - back
        return flash_step(
            k_all, v_flip, queries, at, sc[1] + at * KB, position, start, acc, carry
        )

    top, total = lax.fori_loop(
        0,
        last - least + 1,
        step,
        (jnp.full((1, 2 * QB), NEG, F32), jnp.zeros((1, 2 * QB), F32)),
    )
    for h in range(2):
        top_ref[h : h + 1, :] = top[:, h * QB : (h + 1) * QB]
        total_ref[h : h + 1, :] = total[:, h * QB : (h + 1) * QB]


def piece_specs(pieces):
    out = []
    for array in pieces:
        dims = array.shape
        out.append((whole((1,) + dims[1:]) if len(dims) == 3 else whole(dims), array))
    return out


def attend_own(sc, docs, pieces):
    rows, cols = pieces[1].shape[0], pieces[1].shape[1] // 3
    span = GROUP * rows
    stat = (pl.BlockSpec((8, QB), lambda j, sc: (0, j)), shape((8, span), F32))
    return run_kernel(
        functools.partial(attend_own_body, docs),
        (span // QB,),
        sc,
        piece_specs(pieces),
        [(pl.BlockSpec((cols, QB), lambda j, sc: (0, j)), shape((cols, span), F32)), stat, stat],
        scratch=[
            pltpu.VMEM((span, cols), BF16),
            pltpu.VMEM((span, cols), BF16),
            pltpu.VMEM((cols, span), BF16),
        ],
        flops=span * span * cols * 2,
        moved=span * cols * 10,
    )


def attend_back_body(
    docs, sc, p0, p1, p2, p3, kv, acc_in, top_in, total_in, mixed, out, log_total, q_all, k_all, v_flip, acc
):
    block = pl.program_id(0)
    cols = q_all.shape[1]
    span = q_all.shape[0]

    @pl.when(block == 0)
    def _():
        spread(sc, (p0, p1, p2, p3), 0, cols, straight=q_all)
        spread(sc, (kv,) * GROUP, 0, cols, straight=k_all)
        spread(sc, (kv,) * GROUP, cols, cols, flipped=v_flip)

    position, start, lowest = query_rows(sc, docs, block)
    queries = head_stack(q_all[block_at(block, QB), :], HEAD_DIM**-0.5)
    acc[...] = acc_in[...]
    before = sc[1] - span
    least = jnp.maximum(lowest - before, 0) // KB

    def step(at, carry):
        return flash_step(k_all, v_flip, queries, at, before + at * KB, position, start, acc, carry)

    top, total = lax.fori_loop(
        least,
        span // KB,
        step,
        (
            jnp.concatenate([top_in[h : h + 1, :] for h in range(2)], 1),
            jnp.concatenate([total_in[h : h + 1, :] for h in range(2)], 1),
        ),
    )
    sums = top + jnp.log(total)
    share = 1.0 / total
    parts = []
    for h in range(2):
        lanes = slice(h * QB, (h + 1) * QB)
        log_total[h : h + 1, :] = sums[:, lanes]
        parts.append(acc[h * HEAD_DIM : (h + 1) * HEAD_DIM, :] * share[:, lanes])
    value = jnp.concatenate(parts, 0).T
    out[...] = value
    mixed[0] = value.astype(BF16)


def slot_spec(rows, cols):
    per = rows // QB
    return pl.BlockSpec((1, QB, cols), lambda j, sc: ((j // per) ^ sc[0], j % per, 0))


def attend_back(sc, docs, pieces, kv, acc, top, total):
    rows, cols = pieces[1].shape[0], pieces[1].shape[1] // 3
    span = GROUP * rows
    stat = pl.BlockSpec((8, QB), lambda j, sc: (0, j))
    ins = piece_specs(pieces) + [
        (whole(kv.shape), kv),
        (pl.BlockSpec((cols, QB), lambda j, sc: (0, j)), acc),
        (stat, top),
        (stat, total),
    ]
    outs = [
        (slot_spec(rows, cols), shape((GROUP, rows, cols), BF16)),
        (pl.BlockSpec((QB, cols), lambda j, sc: (j, 0)), shape((span, cols), F32)),
        (stat, shape((8, span), F32)),
    ]
    return run_kernel(
        functools.partial(attend_back_body, docs),
        (span // QB,),
        sc,
        ins,
        outs,
        scratch=[
            pltpu.VMEM((span, cols), BF16),
            pltpu.VMEM((span, cols), BF16),
            pltpu.VMEM((cols, span), BF16),
            pltpu.VMEM((cols, QB), F32),
        ],
        flops=span * span * cols * 2,
        moved=span * cols * 16,
    )


def pull_step(block, first_key, position, start, queries, grads, log_rows, delta, refs):
    k_all, v_all, k_flip, grad_k, grad_v, grad_q = refs
    at = block_at(block, KB)
    scores = masked_scores(k_all[at, :], queries, first_key, position, start)
    probs = jnp.exp(scores - log_rows)
    grad_probs = dot_last(v_all[at, :], grads)
    grad_scores = (probs * (grad_probs - delta)).astype(BF16)
    grad_v[at, :] += dot(probs.astype(BF16), grads)
    grad_k[at, :] += dot(grad_scores, queries)
    for h in range(2):
        rows = slice(h * HEAD_DIM, (h + 1) * HEAD_DIM)
        grad_q[rows, :] += dot(k_flip[rows, at], grad_scores[:, h * QB : (h + 1) * QB])


def pull_rows(block, q_all, g_all, out, log_total):
    queries = head_stack(q_all[block_at(block, QB), :], HEAD_DIM**-0.5)
    grad_rows = g_all[block_at(block, QB), :]
    grads = head_stack(grad_rows, 1.0)
    flipped = (grad_rows.astype(F32) * out[...]).T
    delta = jnp.concatenate(
        [
            jnp.sum(flipped[h * HEAD_DIM : (h + 1) * HEAD_DIM, :], 0, keepdims=True)
            for h in range(2)
        ],
        1,
    )
    log_rows = jnp.concatenate([log_total[h : h + 1, :] for h in range(2)], 1)
    return queries, grads, log_rows, delta


def pull_back_body(
    docs, sc, p0, p1, p2, p3, g0, g1, g2, g3, kv, out, log_total, grad_q, grad_kv,
    q_all, g_all, k_all, v_all, k_flip, grad_k, grad_v
):
    block = pl.program_id(0)
    span, cols = q_all.shape
    before = sc[1] - span

    @pl.when(block == 0)
    def _():
        spread(sc, (p0, p1, p2, p3), 0, cols, straight=q_all)
        spread(sc, (g0, g1, g2, g3), 0, cols, straight=g_all)
        spread(sc, (kv,) * GROUP, 0, cols, straight=k_all, flipped=k_flip)
        spread(sc, (kv,) * GROUP, cols, cols, straight=v_all)
        grad_k[...] = jnp.zeros_like(grad_k)
        grad_v[...] = jnp.zeros_like(grad_v)

    grad_q[...] = jnp.zeros_like(grad_q)
    position, start, lowest = query_rows(sc, docs, block)

    @pl.when(lowest < sc[1])
    def _():
        queries, grads, log_rows, delta = pull_rows(block, q_all, g_all, out, log_total)

        def step(at, carry):
            pull_step(
                at,
                before + at * KB,
                position,
                start,
                queries,
                grads,
                log_rows,
                delta,
                (k_all, v_all, k_flip, grad_k, grad_v, grad_q),
            )
            return carry

        lax.fori_loop(jnp.maximum(lowest - before, 0) // KB, span // KB, step, 0)

    @pl.when(block == pl.num_programs(0) - 1)
    def _():
        for s in range(GROUP):
            at = place_rows(sc, s, span // GROUP)
            grad_kv[s, :, :cols] = grad_k[at, :].astype(BF16)
            grad_kv[s, :, cols:] = grad_v[at, :].astype(BF16)


def pull_back(sc, docs, pieces, grads, kv, out, log_total):
    rows, cols = pieces[1].shape[0], pieces[1].shape[1] // 3
    span = GROUP * rows
    ins = piece_specs(pieces) + piece_specs(grads) + [
        (whole(kv.shape), kv),
        (pl.BlockSpec((QB, cols), lambda j, sc: (j, 0)), out),
        (pl.BlockSpec((8, QB), lambda j, sc: (0, j)), log_total),
    ]
    outs = [
        (pl.BlockSpec((cols, QB), lambda j, sc: (0, j)), shape((cols, span), F32)),
        (whole((GROUP, rows, 2 * cols)), shape((GROUP, rows, 2 * cols), BF16)),
    ]
    low = pltpu.VMEM((span, cols), BF16)
    return run_kernel(
        functools.partial(pull_back_body, docs),
        (span // QB,),
        sc,
        ins,
        outs,
        scratch=[
            low,
            low,
            low,
            low,
            pltpu.VMEM((cols, span), BF16),
            pltpu.VMEM((span, cols), F32),
            pltpu.VMEM((span, cols), F32),
        ],
        flops=span * span * cols * 4,
        moved=span * cols * 20,
    )


def pull_own_body(
    docs, sc, p0, p1, p2, p3, g0, g1, g2, g3, out, log_total, grad_q_in, grad_q_out, grad_kv,
    q_all, g_all, k_all, v_all, k_flip, grad_k, grad_v, grad_q
):
    block = pl.program_id(0)
    span, cols = q_all.shape

    @pl.when(block == 0)
    def _():
        pieces = (p0, p1, p2, p3)
        spread(sc, pieces, 0, cols, straight=q_all)
        spread(sc, (g0, g1, g2, g3), 0, cols, straight=g_all)
        spread(sc, pieces, cols, cols, straight=k_all, flipped=k_flip)
        spread(sc, pieces, 2 * cols, cols, straight=v_all)
        grad_k[...] = jnp.zeros_like(grad_k)
        grad_v[...] = jnp.zeros_like(grad_v)

    grad_q[...] = grad_q_in[...]
    position, start, lowest = query_rows(sc, docs, block)
    queries, grads, log_rows, delta = pull_rows(block, q_all, g_all, out, log_total)

    def step(at, carry):
        pull_step(
            at,
            sc[1] + at * KB,
            position,
            start,
            queries,
            grads,
            log_rows,
            delta,
            (k_all, v_all, k_flip, grad_k, grad_v, grad_q),
        )
        return carry

    last = ((block + 1) * QB - 1) // KB
    lax.fori_loop(jnp.maximum(lowest - sc[1], 0) // KB, last + 1, step, 0)
    grad_q_out[0] = (grad_q[...] * HEAD_DIM**-0.5).T.astype(BF16)

    @pl.when(block == pl.num_programs(0) - 1)
    def _():
        for s in range(GROUP):
            at = place_rows(sc, s, span // GROUP)
            grad_kv[s, :, :cols] = grad_k[at, :]
            grad_kv[s, :, cols:] = grad_v[at, :]


def pull_own(sc, docs, pieces, grads, out, log_total, grad_q):
    rows, cols = pieces[1].shape[0], pieces[1].shape[1] // 3
    span = GROUP * rows
    ins = piece_specs(pieces) + piece_specs(grads) + [
        (pl.BlockSpec((QB, cols), lambda j, sc: (j, 0)), out),
        (pl.BlockSpec((8, QB), lambda j, sc: (0, j)), log_total),
        (pl.BlockSpec((cols, QB), lambda j, sc: (0, j)), grad_q),
    ]
    outs = [
        (slot_spec(rows, cols), shape((GROUP, rows, cols), BF16)),
        (whole((GROUP, rows, 2 * cols)), shape((GROUP, rows, 2 * cols), F32)),
    ]
    low = pltpu.VMEM((span, cols), BF16)
    return run_kernel(
        functools.partial(pull_own_body, docs),
        (span // QB,),
        sc,
        ins,
        outs,
        scratch=[
            low,
            low,
            low,
            low,
            pltpu.VMEM((cols, span), BF16),
            pltpu.VMEM((span, cols), F32),
            pltpu.VMEM((span, cols), F32),
            pltpu.VMEM((cols, QB), F32),
        ],
        flops=span * span * cols * 5,
        moved=span * cols * 24,
    )


def swap_tp(value):
    return lax.ppermute(value, "tp", [(0, 1), (1, 0)])


def swap_fsdp(value, s):
    return lax.ppermute(value, "fsdp", [(i, i ^ s) for i in range(lax.axis_size("fsdp"))])


def shift_fsdp(value, by):
    size = lax.axis_size("fsdp")
    return lax.ppermute(value, "fsdp", [(i, i + by) for i in range(size) if 0 <= i + by < size])


def butterfly(value):
    s = 1
    while s < lax.axis_size("fsdp"):
        value = value + swap_fsdp(value, s)
        s *= 2
    return value


def trade(pieces):
    return [pieces] + [swap_fsdp(pieces[s], s) for s in range(1, GROUP)]


def gather(shard):
    return lax.all_gather(shard, "fsdp", axis=0, tiled=True)


def scatter_sum(full):
    return lax.psum_scatter(full, "fsdp", scatter_dimension=0, tiled=True)


def shards(
    tokens,
    cotangent,
    segments,
    doc_batch,
    ln1_gain,
    ln1_bias,
    w_qkv,
    b_qv,
    w_out,
    b_out,
    ln2_gain,
    ln2_bias,
    w_fc,
    b_fc,
    w_proj,
    b_proj,
):
    rows, width = tokens.shape
    depth = w_qkv.shape[1]
    out_cols = w_out.shape[1]
    units = w_fc.shape[2]
    cols = out_cols // GROUP
    docs = doc_batch.shape[0]
    me = lax.axis_index("fsdp")
    total_rows = rows * lax.axis_size("fsdp")

    def pack_qkv(l):
        return w_qkv[l].reshape(depth, 3, GROUP, cols).transpose(0, 2, 1, 3).reshape(depth, 3 * out_cols)

    def pack_rest(l):
        return [w_out[l].T, w_fc[l], w_proj[l].T]

    fc_at, proj_at = out_cols, out_cols + units
    rest_cols = out_cols + 2 * units
    full_a = gather(pack_qkv(0))
    full_b = gather(jnp.concatenate(pack_rest(0) + [pack_qkv(1)], 1))
    full_c = gather(jnp.concatenate(pack_rest(1), 1))
    qkv_of = ((full_a, 0), (full_b, rest_cols))
    rest_of = (full_b, full_c)

    doc_ids = jnp.arange(docs, dtype=jnp.int32)
    is_doc = segments[:, None] == doc_ids[None, :]
    doc_tokens = butterfly(jnp.sum(is_doc.astype(jnp.int32), 0))
    doc_first = jnp.cumsum(doc_tokens) - doc_tokens
    in_batch = doc_batch[:, None] == jnp.arange(MB, dtype=jnp.int32)[None, :]
    counts = jnp.sum(jnp.where(in_batch, doc_tokens[:, None], 0), 0)
    doc_count = jnp.sum(jnp.where(in_batch, counts[None, :], 0), 1)
    row_count = jnp.sum(jnp.where(is_doc, doc_count[None, :], 0), 1).astype(F32)
    row_weight = total_rows / (MB * row_count)
    sc = jnp.concatenate(
        [jnp.stack([me % GROUP, (me // GROUP) * (GROUP * rows)]).astype(jnp.int32), doc_first]
    )

    def bias_qkv(l):
        three = jnp.stack([b_qv[l, 0], jnp.zeros_like(b_qv[l, 0]), b_qv[l, 1]])
        return three.reshape(3, GROUP, cols).transpose(1, 0, 2).reshape(1, 3 * out_cols)

    def row(vector):
        return vector.reshape(1, vector.shape[0])

    stream, sums = tokens, None
    stored = []
    for l in range(LAYERS):
        weights, first = qkv_of[l]
        stream, low_one, pieces = norm_qkv(
            sc, stream, sums, row(ln1_gain[l]), row(ln1_bias[l]), weights, first // (3 * cols), bias_qkv(l)
        )
        pieces = trade(pieces)
        kv = jnp.stack([pieces[0][0, :, cols:]] + [piece[:, cols:] for piece in pieces[1:]])
        kv_back = shift_fsdp(kv, GROUP)
        acc, top, total = attend_own(sc, docs, pieces)
        mixed, out, log_total = attend_back(sc, docs, pieces, kv_back, acc, top, total)
        mixed = trade(mixed)
        mixed_full, part = out_proj(sc, mixed[0], mixed[1:], rest_of[l])
        middle, low_two, hidden, act, part_two = feed(
            sc,
            stream,
            part,
            swap_tp(part),
            row(b_out[l]),
            row(ln2_gain[l]),
            row(ln2_bias[l]),
            rest_of[l],
            fc_at,
            proj_at,
            row(b_fc[l]),
        )
        stored.append(
            (stream, low_one, pieces, kv_back, out, log_total, mixed_full, middle, low_two, hidden, act)
        )
        stream, sums = middle, (part_two, swap_tp(part_two), row(b_proj[l]))
    own, got, badd = sums
    outputs = (stream + (own.astype(F32) + got.astype(F32)) + badd).astype(BF16)

    grad = cotangent.astype(F32) * row_weight[:, None]
    small = [None] * LAYERS
    large = [None] * LAYERS
    for l in range(LAYERS - 1, -1, -1):
        stream, low_one, pieces, kv_back, out, log_total, mixed_full, middle, low_two, hidden, act = stored[l]
        low_proj, sum_bproj, grad_hidden, sum_bfc, part = feed_pull(
            sc, grad, hidden, rest_of[l], fc_at, proj_at
        )
        got = swap_tp(part)
        feed_grads = scatter_sum(weight_pull(sc, low_two, grad_hidden, low_proj, act))
        grad, low_out, grad_mixed, sum_gain_two, sum_bias_two, sum_bout = mid_pull(
            sc, grad, part, got, middle, row(ln2_gain[l]), rest_of[l], out_cols
        )
        grad_mixed = trade(grad_mixed)
        grad_q, grad_kv_back = pull_back(sc, docs, pieces, grad_mixed, kv_back, out, log_total)
        grad_kv_got = shift_fsdp(grad_kv_back, -GROUP)
        grad_q, grad_kv = pull_own(sc, docs, pieces, grad_mixed, out, log_total, grad_q)
        grad_pieces = jnp.concatenate([grad_q, (grad_kv + grad_kv_got.astype(F32)).astype(BF16)], 2)
        grad_pieces = trade(grad_pieces)
        weights, first = qkv_of[l]
        grad_qkv, part, sum_bqkv = qkv_pull(
            sc, grad_pieces[0], grad_pieces[1:], weights, first // (3 * out_cols)
        )
        got = swap_tp(part)
        attn_grads = scatter_sum(weight_pull(sc, low_one, grad_qkv, low_out, mixed_full))
        grad, sum_gain_one, sum_bias_one = first_pull(sc, grad, part, got, stream, row(ln1_gain[l]))
        sums = [sum_gain_one, sum_bias_one, sum_bqkv, sum_bout, sum_gain_two, sum_bias_two, sum_bfc, sum_bproj]
        small[l] = butterfly(jnp.concatenate([jnp.sum(value, 0) for value in sums]))
        large[l] = (feed_grads, attn_grads)

    def small_parts(vector):
        ends, at = [], 0
        for size in (width, width, 3 * out_cols, width, width, width, units, width):
            ends.append(vector[at : at + size])
            at += size
        three = ends[2].reshape(GROUP, 3, cols).transpose(1, 0, 2).reshape(3, out_cols)
        ends[2] = three[0::2]
        return ends

    small = [small_parts(vector) for vector in small]

    def stack_small(member):
        return jnp.stack([small[l][member] for l in range(LAYERS)])

    grad_wqkv = jnp.stack(
        [
            large[l][1][:, : 3 * out_cols]
            .reshape(depth, GROUP, 3, cols)
            .transpose(0, 2, 1, 3)
            .reshape(depth, 3, out_cols)
            for l in range(LAYERS)
        ]
    ).astype(F32)
    grad_wout = jnp.stack([large[l][1][:, 3 * out_cols :].T for l in range(LAYERS)]).astype(F32)
    grad_wfc = jnp.stack([large[l][0][:, :units] for l in range(LAYERS)]).astype(F32)
    grad_wproj = jnp.stack([large[l][0][:, units:].T for l in range(LAYERS)]).astype(F32)

    return (
        outputs,
        grad,
        stack_small(0),
        stack_small(1),
        grad_wqkv,
        stack_small(2),
        grad_wout,
        stack_small(3),
        stack_small(4),
        stack_small(5),
        grad_wfc,
        stack_small(6),
        grad_wproj,
        stack_small(7),
    )


def solution(mesh):
    placed = (
        P("fsdp", None),
        P("fsdp", None),
        P("fsdp"),
        P(),
        P(),
        P(),
        P(None, "fsdp", None, "tp"),
        P(None, None, "tp"),
        P(None, "tp", "fsdp"),
        P(),
        P(),
        P(),
        P(None, "fsdp", "tp"),
        P(None, "tp"),
        P(None, "tp", "fsdp"),
        P(),
    )
    return jax.shard_map(
        shards,
        mesh=mesh,
        in_specs=placed,
        out_specs=(
            P("fsdp", None),
            P("fsdp", None),
            P(),
            P(),
            P(None, "fsdp", None, "tp"),
            P(None, None, "tp"),
            P(None, "tp", "fsdp"),
            P(),
            P(),
            P(),
            P(None, "fsdp", "tp"),
            P(None, "tp"),
            P(None, "tp", "fsdp"),
            P(),
        ),
        check_vma=False,
    )
```

```python
import functools

import jax
import jax.numpy as jnp
from jax import lax
from jax.experimental import pallas as pl
from jax.experimental.pallas import tpu as pltpu
from jax.sharding import PartitionSpec as P

HEAD_DIM = 64
LAYERS = 2
MB = 3
REACH = 4

EPS = 1e-05
GROUP = REACH
QB = 256
LN_ROWS = 128
ACT_ROWS = 128
KB = 256
NEG = -1e30
F32 = jnp.float32
BF16 = jnp.bfloat16
VMEM_BYTES = 56 * 1024 * 1024
LAST = (((1,), (1,)), ((), ()))
FIRST = (((0,), (0,)), ((), ()))


def dot(left, right):
    return jnp.dot(left, right, preferred_element_type=F32)


def dot_last(left, right):
    return lax.dot_general(left, right, LAST, preferred_element_type=F32)


def shape(dims, dtype):
    return jax.ShapeDtypeStruct(dims, dtype)


def whole(dims):
    return pl.BlockSpec(dims, lambda *_: (0,) * len(dims))


def run_kernel(body, grid, scalars, ins, outs, scratch=(), flops=0, moved=0):
    return pl.pallas_call(
        body,
        grid_spec=pltpu.PrefetchScalarGridSpec(
            num_scalar_prefetch=1,
            grid=grid,
            in_specs=[spec for spec, _ in ins],
            out_specs=[spec for spec, _ in outs],
            scratch_shapes=list(scratch),
        ),
        out_shape=[out for _, out in outs],
        compiler_params=pltpu.CompilerParams(
            vmem_limit_bytes=VMEM_BYTES, dimension_semantics=("arbitrary",) * len(grid)
        ),
        cost_estimate=pl.CostEstimate(flops=flops, bytes_accessed=moved, transcendentals=0),
    )(scalars, *[array for _, array in ins])


def each_rows(count, chunk, body):
    def step(at, carry):
        body(pl.ds(pl.multiple_of(at * chunk, chunk), chunk))
        return carry

    lax.fori_loop(0, count // chunk, step, 0)


def norm_parts(rows):
    centred = rows - jnp.mean(rows, -1, keepdims=True)
    inv_scale = lax.rsqrt(jnp.mean(centred * centred, -1, keepdims=True) + EPS)
    return centred * inv_scale, inv_scale


def norm_pull(grad_rows, unit_rows, inv_scale, gain):
    scaled = grad_rows * gain
    return inv_scale * (
        scaled
        - jnp.mean(scaled, -1, keepdims=True)
        - unit_rows * jnp.mean(scaled * unit_rows, -1, keepdims=True)
    )


def eight_rows(rows):
    return jnp.sum(rows.reshape(rows.shape[0] // 8, 8, rows.shape[1]), 0)


def norm_qkv_body(summed, sc, *refs):
    if summed:
        base, own, got, badd, gain, bias, w, bq, stream, low, piece = refs
    else:
        base, gain, bias, w, bq, stream, low, piece = refs

    @pl.when(pl.program_id(0) == 0)
    def _():
        def rows(at):
            value = base[at, :].astype(F32)
            if summed:
                value = value + (own[at, :].astype(F32) + got[at, :].astype(F32)) + badd[...]
            stream[at, :] = value
            unit, _ = norm_parts(value)
            low[at, :] = (unit * gain[...] + bias[...]).astype(BF16)

        each_rows(base.shape[0], LN_ROWS, rows)

    piece[0] = (dot(low[...], w[...]) + bq[...]).astype(BF16)


def norm_qkv(sc, base, sums, gain, bias, weights, first_block, bq):
    rows, width = base.shape
    cols = bq.shape[1] // GROUP
    ins = [(whole(base.shape), base)]
    if sums is not None:
        own, got, badd = sums
        ins += [(whole(own.shape), own), (whole(got.shape), got), (whole(badd.shape), badd)]
    ins += [
        (whole(gain.shape), gain),
        (whole(bias.shape), bias),
        (pl.BlockSpec((width, cols), lambda s, sc: (0, first_block + (sc[0] ^ s))), weights),
        (pl.BlockSpec((1, cols), lambda s, sc: (0, sc[0] ^ s)), bq),
    ]
    outs = [
        (whole((rows, width)), shape((rows, width), F32)),
        (whole((rows, width)), shape((rows, width), BF16)),
        (pl.BlockSpec((1, rows, cols), lambda s, sc: (s, 0, 0)), shape((GROUP, rows, cols), BF16)),
    ]
    return run_kernel(
        functools.partial(norm_qkv_body, sums is not None),
        (GROUP,),
        sc,
        ins,
        outs,
        flops=2 * rows * width * cols * GROUP,
        moved=rows * width * 12 + width * cols * GROUP * 2,
    )


def out_proj_body(sc, p0, p1, p2, p3, w, full, partial):
    cols = p1.shape[1]
    for s, piece in enumerate((p0, p1, p2, p3)):
        value = piece[0] if s == 0 else piece[...]
        full[:, pl.ds(pl.multiple_of((sc[0] ^ s) * cols, cols), cols)] = value
    tile = 256
    for at in range(0, partial.shape[1], tile):
        partial[:, at : at + tile] = dot_last(full[...], w[at : at + tile, :]).astype(BF16)


def out_proj(sc, mixed_all, got, weights):
    rows, cols = got[0].shape
    width = weights.shape[0]
    ins = [(whole((1, rows, cols)), mixed_all)]
    ins += [(whole((rows, cols)), piece) for piece in got]
    ins += [(whole((width, GROUP * cols)), weights)]
    outs = [
        (whole((rows, GROUP * cols)), shape((rows, GROUP * cols), BF16)),
        (whole((rows, width)), shape((rows, width), BF16)),
    ]
    return run_kernel(
        out_proj_body,
        (1,),
        sc,
        ins,
        outs,
        flops=2 * rows * width * GROUP * cols,
        moved=rows * width * 4 + width * GROUP * cols * 2,
    )


def gelu_rows(value):
    return 0.5 * value * (1.0 + jnp.tanh(0.7978845608028654 * (value + 0.044715 * value * value * value)))


def gelu_slope(value):
    square = value * value
    top = jnp.tanh(0.7978845608028654 * (value + 0.044715 * square * value))
    inner = 0.7978845608028654 * (1.0 + 3.0 * 0.044715 * square)
    return 0.5 * (1.0 + top) + 0.5 * value * (1.0 - top * top) * inner


def feed_body(
    sc, base, own, got, badd, gain, bias, fc, bfc, proj, middle, low, hidden, act, partial, total
):
    at_chunk = pl.program_id(0)

    @pl.when(at_chunk == 0)
    def _():
        def rows(at):
            value = base[at, :] + (own[at, :].astype(F32) + got[at, :].astype(F32)) + badd[...]
            middle[at, :] = value
            unit, _ = norm_parts(value)
            low[at, :] = (unit * gain[...] + bias[...]).astype(BF16)

        each_rows(base.shape[0], LN_ROWS, rows)

    hidden[...] = dot(low[...], fc[...]) + bfc[...]

    def rows_act(at):
        act[at, :] = gelu_rows(hidden[at, :]).astype(BF16)

    each_rows(hidden.shape[0], ACT_ROWS, rows_act)
    part = dot_last(act[...], proj[...])

    @pl.when(at_chunk == 0)
    def _():
        total[...] = part

    @pl.when(at_chunk > 0)
    def _():
        total[...] += part

    @pl.when(at_chunk == pl.num_programs(0) - 1)
    def _():
        partial[...] = total[...].astype(BF16)


def feed(sc, base, own, got, badd, gain, bias, weights, fc_at, proj_at, bfc):
    rows, width = base.shape
    units, chunk = bfc.shape[1], 512
    ins = [
        (whole(base.shape), base),
        (whole(own.shape), own),
        (whole(got.shape), got),
        (whole(badd.shape), badd),
        (whole(gain.shape), gain),
        (whole(bias.shape), bias),
        (pl.BlockSpec((width, chunk), lambda j, sc: (0, fc_at // chunk + j)), weights),
        (pl.BlockSpec((1, chunk), lambda j, sc: (0, j)), bfc),
        (pl.BlockSpec((width, chunk), lambda j, sc: (0, proj_at // chunk + j)), weights),
    ]
    outs = [
        (whole((rows, width)), shape((rows, width), F32)),
        (whole((rows, width)), shape((rows, width), BF16)),
        (pl.BlockSpec((rows, chunk), lambda j, sc: (0, j)), shape((rows, units), F32)),
        (pl.BlockSpec((rows, chunk), lambda j, sc: (0, j)), shape((rows, units), BF16)),
        (whole((rows, width)), shape((rows, width), BF16)),
    ]
    return run_kernel(
        feed_body,
        (units // chunk,),
        sc,
        ins,
        outs,
        scratch=[pltpu.VMEM((rows, width), F32)],
        flops=4 * rows * width * units,
        moved=rows * width * 16 + width * units * 4 + rows * units * 6,
    )


def feed_pull_body(sc, grad, hidden, proj, fc, low, sum_low, slope_grad, sum_hidden, partial, total, grad_act):
    at_chunk = pl.program_id(0)

    @pl.when(at_chunk == 0)
    def _():
        sum_low[...] = jnp.zeros_like(sum_low)

        def rows(at):
            value = grad[at, :].astype(BF16)
            low[at, :] = value
            sum_low[...] += eight_rows(value.astype(F32))

        each_rows(grad.shape[0], LN_ROWS, rows)

    grad_act[...] = dot(low[...], proj[...])
    sum_hidden[...] = jnp.zeros_like(sum_hidden)

    def rows_slope(at):
        value = (grad_act[at, :] * gelu_slope(hidden[at, :])).astype(BF16)
        slope_grad[at, :] = value
        sum_hidden[...] += eight_rows(value.astype(F32))

    each_rows(grad.shape[0], ACT_ROWS, rows_slope)
    part = dot_last(slope_grad[...], fc[...])

    @pl.when(at_chunk == 0)
    def _():
        total[...] = part

    @pl.when(at_chunk > 0)
    def _():
        total[...] += part

    @pl.when(at_chunk == pl.num_programs(0) - 1)
    def _():
        partial[...] = total[...].astype(BF16)


def feed_pull(sc, grad, hidden, weights, fc_at, proj_at):
    rows, width = grad.shape
    units, chunk = hidden.shape[1], 512
    ins = [
        (whole(grad.shape), grad),
        (pl.BlockSpec((rows, chunk), lambda j, sc: (0, j)), hidden),
        (pl.BlockSpec((width, chunk), lambda j, sc: (0, proj_at // chunk + j)), weights),
        (pl.BlockSpec((width, chunk), lambda j, sc: (0, fc_at // chunk + j)), weights),
    ]
    outs = [
        (whole((rows, width)), shape((rows, width), BF16)),
        (whole((8, width)), shape((8, width), F32)),
        (pl.BlockSpec((rows, chunk), lambda j, sc: (0, j)), shape((rows, units), BF16)),
        (pl.BlockSpec((8, chunk), lambda j, sc: (0, j)), shape((8, units), F32)),
        (whole((rows, width)), shape((rows, width), BF16)),
    ]
    return run_kernel(
        feed_pull_body,
        (units // chunk,),
        sc,
        ins,
        outs,
        scratch=[pltpu.VMEM((rows, width), F32), pltpu.VMEM((rows, chunk), F32)],
        flops=4 * rows * width * units,
        moved=rows * width * 8 + width * units * 4 + rows * units * 6,
    )


def norm_pull_rows(at, grad, own, got, inputs, gain, grad_new, sum_gain, sum_bias):
    grad_rows = own[at, :].astype(F32) + got[at, :].astype(F32)
    unit, inv_scale = norm_parts(inputs[at, :])
    value = grad[at, :] + norm_pull(grad_rows, unit, inv_scale, gain[...])
    grad_new[at, :] = value
    sum_gain[...] += eight_rows(grad_rows * unit)
    sum_bias[...] += eight_rows(grad_rows)
    return value


def mid_pull_body(sc, grad, own, got, inputs, gain, w, grad_new, low, pieces, sum_gain, sum_bias, sum_low, mixed):
    for total in (sum_gain, sum_bias, sum_low):
        total[...] = jnp.zeros_like(total)

    def rows(at):
        value = norm_pull_rows(at, grad, own, got, inputs, gain, grad_new, sum_gain, sum_bias)
        value = value.astype(BF16)
        low[at, :] = value
        sum_low[...] += eight_rows(value.astype(F32))

    each_rows(grad.shape[0], LN_ROWS, rows)
    mixed[...] = dot(low[...], w[...]).astype(BF16)
    cols = pieces.shape[2]
    for s in range(GROUP):
        pieces[s] = mixed[:, pl.ds(pl.multiple_of((sc[0] ^ s) * cols, cols), cols)]


def mid_pull(sc, grad, own, got, inputs, gain, weights, out_cols):
    rows, width = grad.shape
    cols = out_cols // GROUP
    ins = [
        (whole(grad.shape), grad),
        (whole(own.shape), own),
        (whole(got.shape), got),
        (whole(inputs.shape), inputs),
        (whole(gain.shape), gain),
        (whole((width, out_cols)), weights),
    ]
    sums = (whole((8, width)), shape((8, width), F32))
    outs = [
        (whole((rows, width)), shape((rows, width), F32)),
        (whole((rows, width)), shape((rows, width), BF16)),
        (whole((GROUP, rows, cols)), shape((GROUP, rows, cols), BF16)),
        sums,
        sums,
        sums,
    ]
    return run_kernel(
        mid_pull_body,
        (1,),
        sc,
        ins,
        outs,
        scratch=[pltpu.VMEM((rows, out_cols), BF16)],
        flops=2 * rows * width * out_cols,
        moved=rows * width * 18 + width * out_cols * 2,
    )


def qkv_pull_body(sc, p0, p1, p2, p3, w, full, partial, sums):
    cols = p1.shape[1]
    for s, piece in enumerate((p0, p1, p2, p3)):
        value = piece[0] if s == 0 else piece[...]
        full[:, pl.ds(pl.multiple_of((sc[0] ^ s) * cols, cols), cols)] = value
    sums[...] = jnp.zeros_like(sums)

    def rows(at):
        sums[...] += eight_rows(full[at, :].astype(F32))

    each_rows(full.shape[0], LN_ROWS, rows)
    tile = 256
    for at in range(0, partial.shape[1], tile):
        partial[:, at : at + tile] = dot_last(full[...], w[at : at + tile, :]).astype(BF16)


def qkv_pull(sc, own, got, weights, block_at):
    rows, cols = got[0].shape
    width, total = weights.shape[0], GROUP * cols
    ins = [(whole((1, rows, cols)), own)]
    ins += [(whole((rows, cols)), piece) for piece in got]
    ins += [(pl.BlockSpec((width, total), lambda j, sc: (0, block_at)), weights)]
    outs = [
        (whole((rows, total)), shape((rows, total), BF16)),
        (whole((rows, width)), shape((rows, width), BF16)),
        (whole((8, total)), shape((8, total), F32)),
    ]
    return run_kernel(
        qkv_pull_body,
        (1,),
        sc,
        ins,
        outs,
        flops=2 * rows * width * total,
        moved=rows * width * 6 + width * total * 2,
    )


def first_pull_body(sc, grad, own, got, inputs, gain, grad_new, sum_gain, sum_bias):
    for total in (sum_gain, sum_bias):
        total[...] = jnp.zeros_like(total)

    def rows(at):
        norm_pull_rows(at, grad, own, got, inputs, gain, grad_new, sum_gain, sum_bias)

    each_rows(grad.shape[0], LN_ROWS, rows)


def first_pull(sc, grad, own, got, inputs, gain):
    rows, width = grad.shape
    arrays = (grad, own, got, inputs, gain)
    sums = (whole((8, width)), shape((8, width), F32))
    return run_kernel(
        first_pull_body,
        (1,),
        sc,
        [(whole(array.shape), array) for array in arrays],
        [(whole((rows, width)), shape((rows, width), F32)), sums, sums],
        moved=rows * width * 16,
    )


def flip_slots(sc, span, source, plain, flipped):
    plain[...] = source[...].T
    width = plain.shape[0]
    groups = lax.axis_size("fsdp") // GROUP
    depth = width // (GROUP * groups)
    mine = sc[1] // span
    slot = 0
    for s in (0, 2, 1, 3):
        for onward in range(groups):
            owner = lax.rem(mine + onward, groups) * GROUP + (sc[0] ^ s)
            flipped[slot * depth : (slot + 1) * depth, :] = plain[
                pl.ds(pl.multiple_of(owner * depth, depth), depth), :
            ]
            slot += 1


def weight_pull_body(first_steps, sc, x0, g0, x1, g1, keep, send, plain, flipped):
    at = pl.program_id(0)
    half = keep.shape[0]
    span = GROUP * x0.shape[0]

    @pl.when(at == 0)
    def _():
        flip_slots(sc, span, x0, plain, flipped)

    @pl.when(at == first_steps)
    def _():
        flip_slots(sc, span, x1, plain, flipped)

    @pl.when(at < first_steps)
    def _():
        keep[...] = dot(flipped[:half, :], g0[...]).astype(BF16)
        send[...] = dot(flipped[half:, :], g0[...]).astype(BF16)

    @pl.when(at >= first_steps)
    def _():
        keep[...] = dot(flipped[:half, :], g1[...]).astype(BF16)
        send[...] = dot(flipped[half:, :], g1[...]).astype(BF16)


def weight_pull(sc, x0, g0, x1, g1):
    rows, width = x0.shape
    chunk = 512
    n0, n1 = g0.shape[1] // chunk, g1.shape[1] // chunk
    ins = [
        (whole(x0.shape), x0),
        (pl.BlockSpec((rows, chunk), lambda j, sc: (0, jnp.minimum(j, n0 - 1))), g0),
        (whole(x1.shape), x1),
        (pl.BlockSpec((rows, chunk), lambda j, sc: (0, jnp.maximum(j - n0, 0))), g1),
    ]
    half = (
        pl.BlockSpec((width // 2, chunk), lambda j, sc: (0, j)),
        shape((width // 2, (n0 + n1) * chunk), BF16),
    )
    return run_kernel(
        functools.partial(weight_pull_body, n0),
        (n0 + n1,),
        sc,
        ins,
        [half, half],
        scratch=[pltpu.VMEM((width, rows), BF16), pltpu.VMEM((width, rows), BF16)],
        flops=2 * rows * width * (n0 + n1) * chunk,
        moved=rows * width * 4 + (rows + width) * (n0 + n1) * chunk * 2,
    )


ROWS = 256
MESH = pl.DeviceIdType.MESH


class Links:
    def __init__(self, send, recv):
        self.send, self.recv, self.used = send, recv, 0
        self.me = lax.axis_index("fsdp")
        self.place = lax.rem(self.me, GROUP)
        self.group = self.me // GROUP
        self.groups = lax.axis_size("fsdp") // GROUP
        self.other = 1 - lax.axis_index("tp")

    def peer(self, s):
        return {"fsdp": self.group * GROUP + (self.place ^ s)}

    def beyond(self, by, s):
        return {"fsdp": lax.rem(self.group + by, self.groups) * GROUP + (self.place ^ s)}

    def copy(self, source, target, device):
        at = self.used
        self.used += 1
        return pltpu.make_async_remote_copy(
            src_ref=source,
            dst_ref=target,
            send_sem=self.send.at[at],
            recv_sem=self.recv.at[at],
            device_id=device,
            device_id_type=MESH,
        )

    def swap(self, source, target):
        return self.copy(source, target, {"tp": self.other})

    def greet(self, devices):
        barrier = pltpu.get_barrier_semaphore()
        for device in devices:
            pl.semaphore_signal(barrier, inc=1, device_id=device, device_id_type=MESH)
        pl.semaphore_wait(barrier, len(devices))


def columns(place, cols):
    return pl.ds(pl.multiple_of(place * cols, cols), cols)


def tiles(count, size, body):
    def step(at, carry):
        body(pl.ds(pl.multiple_of(at * size, size), size))
        return carry

    lax.fori_loop(0, count // size, step, 0)


def rows_within(first, body):
    def step(at, carry):
        body(pl.ds(pl.multiple_of(first + at * LN_ROWS, LN_ROWS), LN_ROWS))
        return carry

    lax.fori_loop(0, ROWS // LN_ROWS, step, 0)


def out_rows(rows, mixed, w, target):
    def tile(at):
        target[rows, at] = dot_last(mixed[rows, :], w[at, :]).astype(BF16)

    tiles(w.shape[0], 256, tile)


def norm_rows(first, base, sums, gain, bias, stream, low):
    def body(at):
        value = base[at, :].astype(F32)
        if sums is not None:
            own, got, badd = sums
            value = value + (own[at, :].astype(F32) + got[at, :].astype(F32)) + badd[...]
        stream[at, :] = value
        unit, _ = norm_parts(value)
        low[at, :] = (unit * gain[...] + bias[...]).astype(BF16)

    rows_within(first, body)


def feed_rows(rows, low, fc, bfc, hidden, act, proj, target):
    def tile(at):
        value = dot(low[rows, :], fc[:, at]) + bfc[:, at]
        hidden[rows, at] = value
        act[rows, at] = gelu_rows(value).astype(BF16)

    tiles(fc.shape[1], 512, tile)

    def tile_out(at):
        target[rows, at] = dot_last(act[rows, :], proj[at, :]).astype(BF16)

    tiles(proj.shape[0], 256, tile_out)


def send_qkv(links, low, w, bq, ready, pieces, kv_back, kept):
    cols = bq.shape[1] // GROUP
    copies = []
    order = (2, 3, 1, 0)
    chunks = low.shape[0] // ROWS
    for c in range(chunks):
        rows = pl.ds(c * ROWS, ROWS)
        across = {
            s: links.copy(ready.at[s, rows], pieces.at[s, rows], links.peer(s)) for s in order if s
        }
        onward = {
            s: links.copy(
                ready.at[s, rows, pl.ds(cols // 3, 2 * cols // 3)],
                kv_back.at[s, rows],
                links.beyond(1, s),
            )
            for s in order
        }
        own = pltpu.make_async_copy(ready.at[0, rows], pieces.at[0, rows], kept.at[c])
        copies.append((across, onward, own))
    last = links.group == links.groups - 1

    def start(c):
        rows = pl.ds(c * ROWS, ROWS)
        across, onward, own = copies[c]
        for s in order:
            at = columns(links.place ^ s, cols)
            ready[s, rows, :] = (dot(low[rows, :], w[:, at]) + bq[:, at]).astype(BF16)
            if s:
                across[s].start()
            else:
                own.start()

            @pl.when(jnp.logical_not(last))
            def _():
                onward[s].start()

    def finish():
        for across, onward, own in copies:
            own.wait()
            for s in order:
                if s:
                    across[s].wait()

                @pl.when(jnp.logical_not(last))
                def _():
                    onward[s].wait_send()

                @pl.when(links.group > 0)
                def _():
                    onward[s].wait_recv()

    return start, finish


def qkv_copies(rows):
    return rows // ROWS * (2 * GROUP - 1)


def first_body(
    base, gain, bias, w_all, bq, stream, low, pieces, kv_back, w, ready, send, recv, load, kept
):
    links = Links(send, recv)
    loaded = pltpu.make_async_copy(w_all, w, load.at[0])
    loaded.start()
    links.greet(
        [links.peer(s) for s in range(1, GROUP)]
        + [links.beyond(1, s) for s in range(GROUP)]
        + [links.beyond(links.groups - 1, s) for s in range(GROUP)]
    )
    start, finish = send_qkv(links, low, w, bq, ready, pieces, kv_back, kept)
    chunks = base.shape[0] // ROWS
    for c in range(chunks):
        norm_rows(c * ROWS, base, None, gain, bias, stream, low)
        if c == 0:
            loaded.wait()
        start(c)
    finish()


ANY = pl.BlockSpec(memory_space=pl.ANY)
VMEM = pl.BlockSpec(memory_space=pltpu.VMEM)


def run_links(body, name, ins, outs, scratch, flops, moved):
    return pl.pallas_call(
        body,
        in_specs=[spec for spec, _ in ins],
        out_specs=[spec for spec, _ in outs],
        out_shape=[out for _, out in outs],
        scratch_shapes=list(scratch),
        compiler_params=pltpu.CompilerParams(
            vmem_limit_bytes=VMEM_BYTES, collective_id=name, has_side_effects=True
        ),
        cost_estimate=pl.CostEstimate(flops=flops, bytes_accessed=moved, transcendentals=0),
    )(*[array for _, array in ins])


def first_segment(base, gain, bias, weights, bq):
    rows, width = base.shape
    total = bq.shape[1]
    cols = total // GROUP
    copies = pltpu.SemaphoreType.DMA((qkv_copies(rows),))
    return run_links(
        first_body,
        0,
        [(VMEM, base), (VMEM, gain), (VMEM, bias), (ANY, weights), (VMEM, bq)],
        [
            (VMEM, shape((rows, width), F32)),
            (VMEM, shape((rows, width), BF16)),
            (ANY, shape((GROUP, rows, cols), BF16)),
            (ANY, shape((GROUP, rows, 2 * cols // 3), BF16)),
        ],
        [
            pltpu.VMEM((width, total), BF16),
            pltpu.VMEM((GROUP, rows, cols), BF16),
            copies,
            copies,
            pltpu.SemaphoreType.DMA((1,)),
            pltpu.SemaphoreType.DMA((rows // ROWS,)),
        ],
        flops=2 * rows * width * total,
        moved=rows * width * 8 + width * total * 2,
    )


def trade_mixed(links, mixed_all, mixed):
    cols = mixed_all.shape[2]
    copies = []
    for c in range(mixed.shape[0] // ROWS):
        rows = pl.ds(c * ROWS, ROWS)
        copies.append(
            [
                links.copy(
                    mixed_all.at[s, rows],
                    mixed.at[rows, columns(links.place, cols)],
                    links.peer(s),
                )
                for s in (2, 3, 1)
            ]
        )

    def start():
        for chunk in copies:
            for one in chunk:
                one.start()
        mixed[:, columns(links.place, cols)] = mixed_all[0]

    def wait(c):
        for one in copies[c]:
            one.wait_recv()

    def finish():
        for chunk in copies:
            for one in chunk:
                one.wait_send()

    return start, wait, finish


def between_body(
    at, mixed_all, base, bout, gain_two, bias_two, bfc, bproj, gain, bias, bq, rest, qkv,
    mixed, middle, low_two, hidden, act, stream, low, pieces, kv_back,
    w_out, w_fc, w_proj, w_qkv, part, got, part_two, got_two, ready, send, recv, load, kept
):
    fc_at, proj_at, first = at
    links = Links(send, recv)
    loads = [
        pltpu.make_async_copy(source.at[:, pl.ds(start, target.shape[1])], target, load.at[i])
        for i, (source, start, target) in enumerate(
            ((rest, 0, w_out), (rest, fc_at, w_fc), (rest, proj_at, w_proj), (qkv, first, w_qkv))
        )
    ]
    for one in loads:
        one.start()
    links.greet(
        [links.peer(s) for s in range(1, GROUP)]
        + [links.beyond(1, s) for s in range(GROUP)]
        + [links.beyond(links.groups - 1, s) for s in range(GROUP)]
        + [{"tp": links.other}]
    )
    chunks = [pl.ds(c * ROWS, ROWS) for c in range(base.shape[0] // ROWS)]
    start_mixed, wait_mixed, finish_mixed = trade_mixed(links, mixed_all, mixed)
    swaps = [links.swap(part.at[rows], got.at[rows]) for rows in chunks]
    swaps_two = [links.swap(part_two.at[rows], got_two.at[rows]) for rows in chunks]
    start_qkv, finish_qkv = send_qkv(links, low, w_qkv, bq, ready, pieces, kv_back, kept)
    start_mixed()
    loads[0].wait()
    for c, rows in enumerate(chunks):
        wait_mixed(c)
        out_rows(rows, mixed, w_out, part)
        swaps[c].start()
    loads[1].wait()
    loads[2].wait()
    for c, rows in enumerate(chunks):
        swaps[c].wait()
        norm_rows(c * ROWS, base, (part, got, bout), gain_two, bias_two, middle, low_two)
        feed_rows(rows, low_two, w_fc, bfc, hidden, act, w_proj, part_two)
        swaps_two[c].start()
    loads[3].wait()
    for c, rows in enumerate(chunks):
        swaps_two[c].wait()
        norm_rows(c * ROWS, middle, (part_two, got_two, bproj), gain, bias, stream, low)
        start_qkv(c)
    finish_mixed()
    finish_qkv()


def between_segment(mixed_all, base, vectors, bq, rest, fc_at, proj_at, qkv, first):
    rows, width = base.shape
    total = bq.shape[1]
    cols = total // GROUP
    out_cols = fc_at
    units = proj_at - fc_at
    chunks = rows // ROWS
    copies = pltpu.SemaphoreType.DMA((qkv_copies(rows) + chunks * (GROUP - 1) + 2 * chunks,))
    whole_f32 = (VMEM, shape((rows, width), F32))
    whole_low = (VMEM, shape((rows, width), BF16))
    return run_links(
        functools.partial(between_body, (fc_at, proj_at, first)),
        1,
        [(VMEM, mixed_all), (VMEM, base)]
        + [(VMEM, vector) for vector in vectors]
        + [(VMEM, bq), (ANY, rest), (ANY, qkv)],
        [
            (VMEM, shape((rows, out_cols), BF16)),
            whole_f32,
            whole_low,
            (VMEM, shape((rows, units), F32)),
            (VMEM, shape((rows, units), BF16)),
            whole_f32,
            whole_low,
            (ANY, shape((GROUP, rows, cols), BF16)),
            (ANY, shape((GROUP, rows, 2 * cols // 3), BF16)),
        ],
        [
            pltpu.VMEM((width, out_cols), BF16),
            pltpu.VMEM((width, units), BF16),
            pltpu.VMEM((width, units), BF16),
            pltpu.VMEM((width, total), BF16),
        ]
        + [pltpu.VMEM((rows, width), BF16)] * 4
        + [
            pltpu.VMEM((GROUP, rows, cols), BF16),
            copies,
            copies,
            pltpu.SemaphoreType.DMA((4,)),
            pltpu.SemaphoreType.DMA((chunks,)),
        ],
        flops=2 * rows * width * (total + out_cols + 2 * units),
        moved=rows * width * 20 + rows * units * 6 + width * (total + out_cols + 2 * units) * 2,
    )


def doc_start_rows(sc, docs, positions):
    start = jnp.zeros_like(positions)
    for d in range(docs):
        first = sc[2 + d]
        start = jnp.where(first <= positions, jnp.maximum(start, first), start)
    return start


def doc_start_one(sc, docs, position):
    start = jnp.int32(0)
    for d in range(docs):
        first = sc[2 + d]
        start = jnp.where(first <= position, jnp.maximum(start, first), start)
    return start


def query_rows(sc, docs, block):
    first = sc[1] + block * QB
    position = first + lax.broadcasted_iota(jnp.int32, (1, QB), 1)
    start = doc_start_rows(sc, docs, position)
    return (
        jnp.concatenate([position, position], 1),
        jnp.concatenate([start, start], 1),
        doc_start_one(sc, docs, first),
    )


def head_stack(rows, scale):
    value = rows.astype(F32)
    if scale != 1.0:
        value = value * scale
    lane = lax.broadcasted_iota(jnp.int32, value.shape, 1)
    return jnp.concatenate(
        [jnp.where(lane < HEAD_DIM, value, 0.0), jnp.where(lane >= HEAD_DIM, value, 0.0)], 0
    ).astype(BF16)


def place_rows(sc, s, rows):
    return pl.ds(pl.multiple_of((sc[0] ^ s) * rows, rows), rows)


def spread(sc, pieces, first_col, cols, straight=None, flipped=None):
    for s, piece in enumerate(pieces):
        value = piece[s] if len(piece.shape) == 3 and piece.shape[0] > 1 else None
        if value is None:
            value = piece[0] if len(piece.shape) == 3 else piece[...]
        value = value[:, first_col : first_col + cols]
        at = place_rows(sc, s, value.shape[0])
        if straight is not None:
            straight[at, :] = value
        if flipped is not None:
            flipped[:, at] = value.T


def block_at(block, size):
    return pl.ds(pl.multiple_of(block * size, size), size)


def masked_scores(keys, queries, first_key, position, start):
    scores = dot_last(keys, queries)
    key_at = first_key + lax.broadcasted_iota(jnp.int32, (KB, 1), 0)
    return jnp.where((key_at >= start) & (key_at <= position), scores, NEG)


def flash_step(keys_ref, values_ref, queries, block, first_key, position, start, acc, carry):
    top, total = carry
    scores = masked_scores(keys_ref[block_at(block, KB), :], queries, first_key, position, start)
    top_new = jnp.maximum(top, jnp.max(scores, 0, keepdims=True))
    expo = jnp.exp(scores - top_new)
    shrink = jnp.exp(top - top_new)
    total = total * shrink + jnp.sum(expo, 0, keepdims=True)
    expo = expo.astype(BF16)
    for h in range(2):
        lanes = slice(h * QB, (h + 1) * QB)
        rows = slice(h * HEAD_DIM, (h + 1) * HEAD_DIM)
        values = values_ref[rows, block_at(block, KB)]
        acc[rows, :] = acc[rows, :] * shrink[:, lanes] + dot(values, expo[:, lanes])
    return top_new, total


def attend_body(docs, sc, p0, kv, mixed, out, log_total, q_all, k_all, v_flip, k_back, v_back, acc):
    block = pl.program_id(0)
    span, cols = q_all.shape

    @pl.when(block == 0)
    def _():
        pieces = (p0,) * GROUP
        spread(sc, pieces, 0, cols, straight=q_all)
        spread(sc, pieces, cols, cols, straight=k_all)
        spread(sc, pieces, 2 * cols, cols, flipped=v_flip)
        spread(sc, (kv,) * GROUP, 0, cols, straight=k_back)
        spread(sc, (kv,) * GROUP, cols, cols, flipped=v_back)

    position, start, lowest = query_rows(sc, docs, block)
    queries = head_stack(q_all[block_at(block, QB), :], HEAD_DIM**-0.5)
    acc[...] = jnp.zeros_like(acc)
    least = jnp.maximum(lowest - sc[1], 0) // KB
    last = ((block + 1) * QB - 1) // KB
    before = sc[1] - span

    def step(back, carry):
        at = last - back
        return flash_step(
            k_all, v_flip, queries, at, sc[1] + at * KB, position, start, acc, carry
        )

    def step_back(at, carry):
        return flash_step(
            k_back, v_back, queries, at, before + at * KB, position, start, acc, carry
        )

    carry = (jnp.full((1, 2 * QB), NEG, F32), jnp.zeros((1, 2 * QB), F32))
    carry = lax.fori_loop(0, last - least + 1, step, carry)
    top, total = lax.fori_loop(
        jnp.minimum(jnp.maximum(lowest - before, 0), span) // KB, span // KB, step_back, carry
    )
    sums = top + jnp.log(total)
    share = 1.0 / total
    parts = []
    for h in range(2):
        lanes = slice(h * QB, (h + 1) * QB)
        log_total[h : h + 1, :] = sums[:, lanes]
        parts.append(acc[h * HEAD_DIM : (h + 1) * HEAD_DIM, :] * share[:, lanes])
    value = jnp.concatenate(parts, 0).T
    out[...] = value
    mixed[0] = value.astype(BF16)


def slot_spec(rows, cols):
    per = rows // QB
    return pl.BlockSpec((1, QB, cols), lambda j, sc: ((j // per) ^ sc[0], j % per, 0))


def attend(sc, docs, pieces, kv):
    rows, cols = pieces.shape[1], pieces.shape[2] // 3
    span = GROUP * rows
    stat = (pl.BlockSpec((8, QB), lambda j, sc: (0, j)), shape((8, span), F32))
    low = pltpu.VMEM((span, cols), BF16)
    low_flip = pltpu.VMEM((cols, span), BF16)
    return run_kernel(
        functools.partial(attend_body, docs),
        (span // QB,),
        sc,
        [(whole(pieces.shape), pieces), (whole(kv.shape), kv)],
        [
            (slot_spec(rows, cols), shape((GROUP, rows, cols), BF16)),
            (pl.BlockSpec((QB, cols), lambda j, sc: (j, 0)), shape((span, cols), F32)),
            stat,
        ],
        scratch=[low, low, low_flip, low, low_flip, pltpu.VMEM((cols, QB), F32)],
        flops=span * span * cols * 4,
        moved=span * cols * 20,
    )


def pull_step(block, first_key, position, start, queries, grads, log_rows, delta, refs):
    k_all, v_all, k_flip, grad_k, grad_v, grad_q = refs
    at = block_at(block, KB)
    scores = masked_scores(k_all[at, :], queries, first_key, position, start)
    probs = jnp.exp(scores - log_rows)
    grad_probs = dot_last(v_all[at, :], grads)
    grad_scores = (probs * (grad_probs - delta)).astype(BF16)
    grad_v[at, :] += dot(probs.astype(BF16), grads)
    grad_k[at, :] += dot(grad_scores, queries)
    for h in range(2):
        rows = slice(h * HEAD_DIM, (h + 1) * HEAD_DIM)
        grad_q[rows, :] += dot(k_flip[rows, at], grad_scores[:, h * QB : (h + 1) * QB])


def pull_rows(block, q_all, g_all, out, log_total):
    queries = head_stack(q_all[block_at(block, QB), :], HEAD_DIM**-0.5)
    grad_rows = g_all[block_at(block, QB), :]
    grads = head_stack(grad_rows, 1.0)
    flipped = (grad_rows.astype(F32) * out[...]).T
    delta = jnp.concatenate(
        [
            jnp.sum(flipped[h * HEAD_DIM : (h + 1) * HEAD_DIM, :], 0, keepdims=True)
            for h in range(2)
        ],
        1,
    )
    log_rows = jnp.concatenate([log_total[h : h + 1, :] for h in range(2)], 1)
    return queries, grads, log_rows, delta


def pull_body(
    docs, sc, p0, g0, kv, out, log_total, grad_q_out, grad_kv, grad_kv_back,
    q_all, g_all, k_all, v_all, k_flip, grad_k, grad_v, k_back, v_back, k_back_flip, grad_k_back, grad_v_back, grad_q
):
    block = pl.program_id(0)
    span, cols = q_all.shape
    before = sc[1] - span

    @pl.when(block == 0)
    def _():
        pieces = (p0,) * GROUP
        spread(sc, pieces, 0, cols, straight=q_all)
        spread(sc, (g0,) * GROUP, 0, cols, straight=g_all)
        spread(sc, pieces, cols, cols, straight=k_all, flipped=k_flip)
        spread(sc, pieces, 2 * cols, cols, straight=v_all)
        spread(sc, (kv,) * GROUP, 0, cols, straight=k_back, flipped=k_back_flip)
        spread(sc, (kv,) * GROUP, cols, cols, straight=v_back)
        for total in (grad_k, grad_v, grad_k_back, grad_v_back):
            total[...] = jnp.zeros_like(total)

    grad_q[...] = jnp.zeros_like(grad_q)
    position, start, lowest = query_rows(sc, docs, block)
    queries, grads, log_rows, delta = pull_rows(block, q_all, g_all, out, log_total)

    def step(first, refs, at, carry):
        pull_step(at, first + at * KB, position, start, queries, grads, log_rows, delta, refs)
        return carry

    own_refs = (k_all, v_all, k_flip, grad_k, grad_v, grad_q)
    back_refs = (k_back, v_back, k_back_flip, grad_k_back, grad_v_back, grad_q)
    last = ((block + 1) * QB - 1) // KB
    lax.fori_loop(
        jnp.maximum(lowest - sc[1], 0) // KB, last + 1, functools.partial(step, sc[1], own_refs), 0
    )
    lax.fori_loop(
        jnp.minimum(jnp.maximum(lowest - before, 0), span) // KB,
        span // KB,
        functools.partial(step, before, back_refs),
        0,
    )
    grad_q_out[0] = (grad_q[...] * HEAD_DIM**-0.5).T.astype(BF16)

    @pl.when(block == pl.num_programs(0) - 1)
    def _():
        for s in range(GROUP):
            at = place_rows(sc, s, span // GROUP)
            grad_kv[s, :, :cols] = grad_k[at, :].astype(BF16)
            grad_kv[s, :, cols:] = grad_v[at, :].astype(BF16)
            grad_kv_back[s, :, :cols] = grad_k_back[at, :].astype(BF16)
            grad_kv_back[s, :, cols:] = grad_v_back[at, :].astype(BF16)


def attend_pull(sc, docs, pieces, grads, kv, out, log_total):
    rows, cols = pieces.shape[1], pieces.shape[2] // 3
    span = GROUP * rows
    ins = [
        (whole(pieces.shape), pieces),
        (whole(grads.shape), grads),
        (whole(kv.shape), kv),
        (pl.BlockSpec((QB, cols), lambda j, sc: (j, 0)), out),
        (pl.BlockSpec((8, QB), lambda j, sc: (0, j)), log_total),
    ]
    both = (whole((GROUP, rows, 2 * cols)), shape((GROUP, rows, 2 * cols), BF16))
    low = pltpu.VMEM((span, cols), BF16)
    low_flip = pltpu.VMEM((cols, span), BF16)
    high = pltpu.VMEM((span, cols), F32)
    return run_kernel(
        functools.partial(pull_body, docs),
        (span // QB,),
        sc,
        ins,
        [(slot_spec(rows, cols), shape((GROUP, rows, cols), BF16)), both, both],
        scratch=[low, low, low, low, low_flip, high, high, low, low, low_flip, high, high]
        + [pltpu.VMEM((cols, QB), F32)],
        flops=span * span * cols * 9,
        moved=span * cols * 30,
    )


def swap_tp(value):
    return lax.ppermute(value, "tp", [(0, 1), (1, 0)])


def swap_fsdp(value, s):
    return lax.ppermute(value, "fsdp", [(i, i ^ s) for i in range(lax.axis_size("fsdp"))])


def shift_fsdp(value, by):
    size = lax.axis_size("fsdp")
    return lax.ppermute(value, "fsdp", [(i, i + by) for i in range(size) if 0 <= i + by < size])


def butterfly(value):
    s = 1
    while s < lax.axis_size("fsdp"):
        value = value + swap_fsdp(value, s)
        s *= 2
    return value


def trade(pieces):
    return [pieces] + [swap_fsdp(pieces[s], s) for s in range(1, GROUP)]


def gather(shard):
    return lax.all_gather(shard, "fsdp", axis=0, tiled=True)


def tie(*values):
    return lax.optimization_barrier(values)


class SlotSum:
    def __init__(self, halves):
        self.keep, self.send = halves
        self.groups = lax.axis_size("fsdp") // GROUP

    def add(self, rows):
        total = self.keep[rows].astype(F32)
        for part in self.parts:
            total = total + part[rows].astype(F32)
        return total

    def to_core(self):
        self.parts = [swap_fsdp(self.send, 1)]

    def to_x(self):
        half = self.keep.shape[0] // 2
        self.parts.append(swap_fsdp(self.add(slice(half, None)).astype(BF16), 2))

    def to_groups(self):
        rows = self.keep.shape[0] // 2 // self.groups
        size = lax.axis_size("fsdp")
        self.near = self.add(slice(0, rows))
        self.far = []
        for onward in range(1, self.groups):
            part = self.add(slice(onward * rows, (onward + 1) * rows)).astype(BF16)
            pairs = [(i, (i + GROUP * onward) % size) for i in range(size)]
            self.far.append(lax.ppermute(part, "fsdp", pairs))

    def result(self):
        total = self.near
        for part in self.far:
            total = total + part.astype(F32)
        return total


def shards(
    tokens,
    cotangent,
    segments,
    doc_batch,
    ln1_gain,
    ln1_bias,
    w_qkv,
    b_qv,
    w_out,
    b_out,
    ln2_gain,
    ln2_bias,
    w_fc,
    b_fc,
    w_proj,
    b_proj,
):
    rows, width = tokens.shape
    depth = w_qkv.shape[1]
    out_cols = w_out.shape[1]
    units = w_fc.shape[2]
    cols = out_cols // GROUP
    docs = doc_batch.shape[0]
    me = lax.axis_index("fsdp")
    total_rows = rows * lax.axis_size("fsdp")

    def pack_qkv(l):
        return w_qkv[l].reshape(depth, 3, GROUP, cols).transpose(0, 2, 1, 3).reshape(depth, 3 * out_cols)

    def pack_rest(l):
        return [w_out[l].T, w_fc[l], w_proj[l].T]

    fc_at, proj_at = out_cols, out_cols + units
    rest_cols = out_cols + 2 * units
    full_a = gather(pack_qkv(0))
    full_b = gather(jnp.concatenate(pack_rest(0) + [pack_qkv(1)], 1))
    full_c = gather(jnp.concatenate(pack_rest(1), 1))
    qkv_of = ((full_a, 0), (full_b, rest_cols))
    rest_of = (full_b, full_c)

    doc_ids = jnp.arange(docs, dtype=jnp.int32)
    is_doc = segments[:, None] == doc_ids[None, :]
    doc_tokens = butterfly(jnp.sum(is_doc.astype(jnp.int32), 0))
    doc_first = jnp.cumsum(doc_tokens) - doc_tokens
    in_batch = doc_batch[:, None] == jnp.arange(MB, dtype=jnp.int32)[None, :]
    counts = jnp.sum(jnp.where(in_batch, doc_tokens[:, None], 0), 0)
    doc_count = jnp.sum(jnp.where(in_batch, counts[None, :], 0), 1)
    row_count = jnp.sum(jnp.where(is_doc, doc_count[None, :], 0), 1).astype(F32)
    row_weight = total_rows / (MB * row_count)
    sc = jnp.concatenate(
        [jnp.stack([me % GROUP, (me // GROUP) * (GROUP * rows)]).astype(jnp.int32), doc_first]
    )

    def bias_qkv(l):
        three = jnp.stack([b_qv[l, 0], jnp.zeros_like(b_qv[l, 0]), b_qv[l, 1]])
        return three.reshape(3, GROUP, cols).transpose(1, 0, 2).reshape(1, 3 * out_cols)

    def row(vector):
        return vector.reshape(1, vector.shape[0])

    stored = []
    stream, low_one, pieces, kv_back = first_segment(
        tokens, row(ln1_gain[0]), row(ln1_bias[0]), full_a, bias_qkv(0)
    )
    for l in range(LAYERS):
        mixed, out, log_total = attend(sc, docs, pieces, kv_back)
        if l + 1 < LAYERS:
            vectors = (b_out[l], ln2_gain[l], ln2_bias[l], b_fc[l], b_proj[l], ln1_gain[l + 1], ln1_bias[l + 1])
            mixed_full, middle, low_two, hidden, act, *later = between_segment(
                mixed,
                stream,
                [row(vector) for vector in vectors],
                bias_qkv(l + 1),
                rest_of[l],
                fc_at,
                proj_at,
                *qkv_of[l + 1],
            )
            kept = (stream, low_one, pieces, kv_back)
            stream, low_one, pieces, kv_back = later
        else:
            kept = (stream, low_one, pieces, kv_back)
            mixed = trade(mixed)
            mixed_full, part = out_proj(sc, mixed[0], mixed[1:], rest_of[l])
            middle, low_two, hidden, act, part_two = feed(
                sc,
                stream,
                part,
                swap_tp(part),
                row(b_out[l]),
                row(ln2_gain[l]),
                row(ln2_bias[l]),
                rest_of[l],
                fc_at,
                proj_at,
                row(b_fc[l]),
            )
            stream, sums = middle, (part_two, swap_tp(part_two), row(b_proj[l]))
        stored.append(kept + (out, log_total, mixed_full, middle, low_two, hidden, act))
    own, got, badd = sums
    outputs = (stream + (own.astype(F32) + got.astype(F32)) + badd).astype(BF16)

    grad = cotangent.astype(F32) * row_weight[:, None]
    small = [None] * LAYERS
    large = [None] * LAYERS
    for l in range(LAYERS - 1, -1, -1):
        stream, low_one, pieces, kv_back, out, log_total, mixed_full, middle, low_two, hidden, act = stored[l]
        low_proj, sum_bproj, grad_hidden, sum_bfc, part = feed_pull(
            sc, grad, hidden, rest_of[l], fc_at, proj_at
        )
        got = swap_tp(part)
        halves = weight_pull(sc, low_two, grad_hidden, low_proj, act)
        got, *halves = tie(got, *halves)
        feed_sum = SlotSum(halves)
        feed_sum.to_core()
        if l + 1 < LAYERS:
            attn_sum.to_groups()
        grad, low_out, grad_mixed, sum_gain_two, sum_bias_two, sum_bout = mid_pull(
            sc, grad, part, got, middle, row(ln2_gain[l]), rest_of[l], out_cols
        )
        grad_mixed, feed_sum.parts[0] = tie(grad_mixed, feed_sum.parts[0])
        feed_sum.to_x()
        grad_mixed = jnp.stack([piece if piece.ndim == 2 else piece[0] for piece in trade(grad_mixed)])
        grad_q, grad_kv, grad_kv_back = attend_pull(sc, docs, pieces, grad_mixed, kv_back, out, log_total)
        grad_kv_got = shift_fsdp(grad_kv_back, -GROUP)
        grad_q, feed_sum.parts[1] = tie(grad_q, feed_sum.parts[1])
        feed_sum.to_groups()
        grad_kv = (grad_kv.astype(F32) + grad_kv_got.astype(F32)).astype(BF16)
        grad_pieces = jnp.concatenate([grad_q, grad_kv], 2)
        grad_pieces = trade(grad_pieces)
        weights, first = qkv_of[l]
        grad_qkv, part, sum_bqkv = qkv_pull(
            sc, grad_pieces[0], grad_pieces[1:], weights, first // (3 * out_cols)
        )
        got = swap_tp(part)
        halves = weight_pull(sc, low_one, grad_qkv, low_out, mixed_full)
        got, *halves = tie(got, *halves)
        attn_sum = SlotSum(halves)
        attn_sum.to_core()
        grad, sum_gain_one, sum_bias_one = first_pull(sc, grad, part, got, stream, row(ln1_gain[l]))
        grad, attn_sum.parts[0] = tie(grad, attn_sum.parts[0])
        attn_sum.to_x()
        sums = [sum_gain_one, sum_bias_one, sum_bqkv, sum_bout, sum_gain_two, sum_bias_two, sum_bfc, sum_bproj]
        small[l] = butterfly(jnp.concatenate([jnp.sum(value, 0) for value in sums]))
        large[l] = (feed_sum, attn_sum)
    attn_sum.to_groups()
    large = [[one.result() for one in pair] for pair in large]

    def small_parts(vector):
        ends, at = [], 0
        for size in (width, width, 3 * out_cols, width, width, width, units, width):
            ends.append(vector[at : at + size])
            at += size
        three = ends[2].reshape(GROUP, 3, cols).transpose(1, 0, 2).reshape(3, out_cols)
        ends[2] = three[0::2]
        return ends

    small = [small_parts(vector) for vector in small]

    def stack_small(member):
        return jnp.stack([small[l][member] for l in range(LAYERS)])

    grad_wqkv = jnp.stack(
        [
            large[l][1][:, : 3 * out_cols]
            .reshape(depth, GROUP, 3, cols)
            .transpose(0, 2, 1, 3)
            .reshape(depth, 3, out_cols)
            for l in range(LAYERS)
        ]
    ).astype(F32)
    grad_wout = jnp.stack([large[l][1][:, 3 * out_cols :].T for l in range(LAYERS)]).astype(F32)
    grad_wfc = jnp.stack([large[l][0][:, :units] for l in range(LAYERS)]).astype(F32)
    grad_wproj = jnp.stack([large[l][0][:, units:].T for l in range(LAYERS)]).astype(F32)

    return (
        outputs,
        grad,
        stack_small(0),
        stack_small(1),
        grad_wqkv,
        stack_small(2),
        grad_wout,
        stack_small(3),
        stack_small(4),
        stack_small(5),
        grad_wfc,
        stack_small(6),
        grad_wproj,
        stack_small(7),
    )


def solution(mesh):
    placed = (
        P("fsdp", None),
        P("fsdp", None),
        P("fsdp"),
        P(),
        P(),
        P(),
        P(None, "fsdp", None, "tp"),
        P(None, None, "tp"),
        P(None, "tp", "fsdp"),
        P(),
        P(),
        P(),
        P(None, "fsdp", "tp"),
        P(None, "tp"),
        P(None, "tp", "fsdp"),
        P(),
    )
    return jax.shard_map(
        shards,
        mesh=mesh,
        in_specs=placed,
        out_specs=(
            P("fsdp", None),
            P("fsdp", None),
            P(),
            P(),
            P(None, "fsdp", None, "tp"),
            P(None, None, "tp"),
            P(None, "tp", "fsdp"),
            P(),
            P(),
            P(),
            P(None, "fsdp", "tp"),
            P(None, "tp"),
            P(None, "tp", "fsdp"),
            P(),
        ),
        check_vma=False,
    )
```

```python
import functools

import jax
import jax.numpy as jnp
from jax import lax
from jax.experimental import pallas as pl
from jax.experimental.pallas import tpu as pltpu
from jax.sharding import PartitionSpec as P

HEAD_DIM = 64
LAYERS = 2
MB = 3
REACH = 4

EPS = 1e-05
GROUP = REACH
QB = 256
LN_ROWS = 128
ACT_ROWS = 128
KB = 256
NEG = -1e30
F32 = jnp.float32
BF16 = jnp.bfloat16
VMEM_BYTES = 62 * 1024 * 1024
LAST = (((1,), (1,)), ((), ()))
FIRST = (((0,), (0,)), ((), ()))


def dot(left, right):
    return jnp.dot(left, right, preferred_element_type=F32)


def dot_last(left, right):
    return lax.dot_general(left, right, LAST, preferred_element_type=F32)


def shape(dims, dtype):
    return jax.ShapeDtypeStruct(dims, dtype)


def whole(dims):
    return pl.BlockSpec(dims, lambda *_: (0,) * len(dims))


def run_kernel(body, grid, scalars, ins, outs, scratch=(), flops=0, moved=0):
    return pl.pallas_call(
        body,
        grid_spec=pltpu.PrefetchScalarGridSpec(
            num_scalar_prefetch=1,
            grid=grid,
            in_specs=[spec for spec, _ in ins],
            out_specs=[spec for spec, _ in outs],
            scratch_shapes=list(scratch),
        ),
        out_shape=[out for _, out in outs],
        compiler_params=pltpu.CompilerParams(
            vmem_limit_bytes=VMEM_BYTES, dimension_semantics=("arbitrary",) * len(grid)
        ),
        cost_estimate=pl.CostEstimate(flops=flops, bytes_accessed=moved, transcendentals=0),
    )(scalars, *[array for _, array in ins])


def each_rows(count, chunk, body):
    def step(at, carry):
        body(pl.ds(pl.multiple_of(at * chunk, chunk), chunk))
        return carry

    lax.fori_loop(0, count // chunk, step, 0)


def norm_parts(rows):
    centred = rows - jnp.mean(rows, -1, keepdims=True)
    inv_scale = lax.rsqrt(jnp.mean(centred * centred, -1, keepdims=True) + EPS)
    return centred * inv_scale, inv_scale


def norm_pull(grad_rows, unit_rows, inv_scale, gain):
    scaled = grad_rows * gain
    return inv_scale * (
        scaled
        - jnp.mean(scaled, -1, keepdims=True)
        - unit_rows * jnp.mean(scaled * unit_rows, -1, keepdims=True)
    )


def eight_rows(rows):
    return jnp.sum(rows.reshape(rows.shape[0] // 8, 8, rows.shape[1]), 0)


def gelu_rows(value):
    return 0.5 * value * (1.0 + jnp.tanh(0.7978845608028654 * (value + 0.044715 * value * value * value)))


def gelu_slope(value):
    square = value * value
    top = jnp.tanh(0.7978845608028654 * (value + 0.044715 * square * value))
    inner = 0.7978845608028654 * (1.0 + 3.0 * 0.044715 * square)
    return 0.5 * (1.0 + top) + 0.5 * value * (1.0 - top * top) * inner


def norm_pull_rows(at, grad, own, got, inputs, gain, grad_new, sum_gain, sum_bias):
    grad_rows = own[at, :].astype(F32) + got[at, :].astype(F32)
    unit, inv_scale = norm_parts(inputs[at, :])
    value = grad[at, :] + norm_pull(grad_rows, unit, inv_scale, gain[...])
    grad_new[at, :] = value
    sum_gain[...] += eight_rows(grad_rows * unit)
    sum_bias[...] += eight_rows(grad_rows)
    return value


ROWS = 256
MESH = pl.DeviceIdType.MESH


class Links:
    def __init__(self, send, recv):
        self.send, self.recv, self.used = send, recv, 0
        self.me = lax.axis_index("fsdp")
        self.place = lax.rem(self.me, GROUP)
        self.group = self.me // GROUP
        self.groups = lax.axis_size("fsdp") // GROUP
        self.other = 1 - lax.axis_index("tp")

    def peer(self, s):
        return {"fsdp": self.group * GROUP + (self.place ^ s)}

    def beyond(self, by, s):
        return {"fsdp": lax.rem(self.group + by, self.groups) * GROUP + (self.place ^ s)}

    def copy(self, source, target, device):
        at = self.used
        self.used += 1
        return pltpu.make_async_remote_copy(
            src_ref=source,
            dst_ref=target,
            send_sem=self.send.at[at],
            recv_sem=self.recv.at[at],
            device_id=device,
            device_id_type=MESH,
        )

    def swap(self, source, target):
        return self.copy(source, target, {"tp": self.other})

    def greet(self, devices):
        barrier = pltpu.get_barrier_semaphore()
        for device in devices:
            pl.semaphore_signal(barrier, inc=1, device_id=device, device_id_type=MESH)
        pl.semaphore_wait(barrier, len(devices))


def columns(place, cols):
    return pl.ds(pl.multiple_of(place * cols, cols), cols)


def tiles(count, size, body):
    def step(at, carry):
        body(pl.ds(pl.multiple_of(at * size, size), size))
        return carry

    lax.fori_loop(0, count // size, step, 0)


def rows_within(first, body):
    def step(at, carry):
        body(pl.ds(pl.multiple_of(first + at * LN_ROWS, LN_ROWS), LN_ROWS))
        return carry

    lax.fori_loop(0, ROWS // LN_ROWS, step, 0)


def out_rows(rows, mixed, w, target):
    def tile(at):
        target[rows, at] = dot_last(mixed[rows, :], w[at, :]).astype(BF16)

    tiles(w.shape[0], 256, tile)


def norm_rows(first, base, sums, gain, bias, stream, low):
    def body(at):
        value = base[at, :].astype(F32)
        if sums is not None:
            own, got, badd = sums
            value = value + (own[at, :].astype(F32) + got[at, :].astype(F32)) + badd[...]
        stream[at, :] = value
        unit, _ = norm_parts(value)
        low[at, :] = (unit * gain[...] + bias[...]).astype(BF16)

    rows_within(first, body)


def feed_rows(rows, low, fc, bfc, hidden, act, proj, target):
    def tile(at):
        value = dot(low[rows, :], fc[:, at]) + bfc[:, at]
        hidden[rows, at] = value
        act[rows, at] = gelu_rows(value).astype(BF16)

    tiles(fc.shape[1], 512, tile)

    def tile_out(at):
        target[rows, at] = dot_last(act[rows, :], proj[at, :]).astype(BF16)

    tiles(proj.shape[0], 256, tile_out)


def send_qkv(links, low, w, bq, ready, pieces, kv_back, kept):
    cols = bq.shape[1] // GROUP
    copies = []
    order = (2, 3, 1, 0)
    chunks = low.shape[0] // ROWS
    for c in range(chunks):
        rows = pl.ds(c * ROWS, ROWS)
        across = {
            s: links.copy(ready.at[s, rows], pieces.at[s, rows], links.peer(s)) for s in order if s
        }
        onward = {
            s: links.copy(
                ready.at[s, rows, pl.ds(cols // 3, 2 * cols // 3)],
                kv_back.at[s, rows],
                links.beyond(1, s),
            )
            for s in order
        }
        own = pltpu.make_async_copy(ready.at[0, rows], pieces.at[0, rows], kept.at[c])
        copies.append((across, onward, own))
    last = links.group == links.groups - 1

    def start(c):
        rows = pl.ds(c * ROWS, ROWS)
        across, onward, own = copies[c]
        for s in order:
            at = columns(links.place ^ s, cols)
            ready[s, rows, :] = (dot(low[rows, :], w[:, at]) + bq[:, at]).astype(BF16)
            if s:
                across[s].start()
            else:
                own.start()

            @pl.when(jnp.logical_not(last))
            def _():
                onward[s].start()

    def finish():
        for across, onward, own in copies:
            own.wait()
            for s in order:
                if s:
                    across[s].wait()

                @pl.when(jnp.logical_not(last))
                def _():
                    onward[s].wait_send()

                @pl.when(links.group > 0)
                def _():
                    onward[s].wait_recv()

    return start, finish


def qkv_copies(rows):
    return rows // ROWS * (2 * GROUP - 1)


def first_body(
    base, gain, bias, w_all, bq, stream, low, pieces, kv_back, w, ready, send, recv, load, kept
):
    links = Links(send, recv)
    loaded = pltpu.make_async_copy(w_all, w, load.at[0])
    loaded.start()
    links.greet(
        [links.peer(s) for s in range(1, GROUP)]
        + [links.beyond(1, s) for s in range(GROUP)]
        + [links.beyond(links.groups - 1, s) for s in range(GROUP)]
    )
    start, finish = send_qkv(links, low, w, bq, ready, pieces, kv_back, kept)
    chunks = base.shape[0] // ROWS
    for c in range(chunks):
        norm_rows(c * ROWS, base, None, gain, bias, stream, low)
        if c == 0:
            loaded.wait()
        start(c)
    finish()


ANY = pl.BlockSpec(memory_space=pl.ANY)
VMEM = pl.BlockSpec(memory_space=pltpu.VMEM)


def run_links(body, name, ins, outs, scratch, flops, moved):
    return pl.pallas_call(
        body,
        in_specs=[spec for spec, _ in ins],
        out_specs=[spec for spec, _ in outs],
        out_shape=[out for _, out in outs],
        scratch_shapes=list(scratch),
        compiler_params=pltpu.CompilerParams(
            vmem_limit_bytes=VMEM_BYTES, collective_id=name, has_side_effects=True
        ),
        cost_estimate=pl.CostEstimate(flops=flops, bytes_accessed=moved, transcendentals=0),
    )(*[array for _, array in ins])


def first_segment(base, gain, bias, weights, bq):
    rows, width = base.shape
    total = bq.shape[1]
    cols = total // GROUP
    copies = pltpu.SemaphoreType.DMA((qkv_copies(rows),))
    return run_links(
        first_body,
        0,
        [(VMEM, base), (VMEM, gain), (VMEM, bias), (ANY, weights), (VMEM, bq)],
        [
            (VMEM, shape((rows, width), F32)),
            (VMEM, shape((rows, width), BF16)),
            (ANY, shape((GROUP, rows, cols), BF16)),
            (ANY, shape((GROUP, rows, 2 * cols // 3), BF16)),
        ],
        [
            pltpu.VMEM((width, total), BF16),
            pltpu.VMEM((GROUP, rows, cols), BF16),
            copies,
            copies,
            pltpu.SemaphoreType.DMA((1,)),
            pltpu.SemaphoreType.DMA((rows // ROWS,)),
        ],
        flops=2 * rows * width * total,
        moved=rows * width * 8 + width * total * 2,
    )


def trade_mixed(links, mixed_all, mixed):
    cols = mixed_all.shape[2]
    copies = []
    for c in range(mixed.shape[0] // ROWS):
        rows = pl.ds(c * ROWS, ROWS)
        copies.append(
            [
                links.copy(
                    mixed_all.at[s, rows],
                    mixed.at[rows, columns(links.place, cols)],
                    links.peer(s),
                )
                for s in (2, 3, 1)
            ]
        )

    def start():
        for chunk in copies:
            for one in chunk:
                one.start()
        mixed[:, columns(links.place, cols)] = mixed_all[0]

    def wait(c):
        for one in copies[c]:
            one.wait_recv()

    def finish():
        for chunk in copies:
            for one in chunk:
                one.wait_send()

    return start, wait, finish


def between_body(
    at, mixed_all, base, bout, gain_two, bias_two, bfc, bproj, gain, bias, bq, rest, qkv,
    mixed, middle, low_two, hidden, act, stream, low, pieces, kv_back,
    w_out, w_fc, w_proj, w_qkv, part, got, part_two, got_two, ready, send, recv, load, kept
):
    fc_at, proj_at, first = at
    links = Links(send, recv)
    loads = [
        pltpu.make_async_copy(source.at[:, pl.ds(start, target.shape[1])], target, load.at[i])
        for i, (source, start, target) in enumerate(
            ((rest, 0, w_out), (rest, fc_at, w_fc), (rest, proj_at, w_proj), (qkv, first, w_qkv))
        )
    ]
    for one in loads:
        one.start()
    links.greet(
        [links.peer(s) for s in range(1, GROUP)]
        + [links.beyond(1, s) for s in range(GROUP)]
        + [links.beyond(links.groups - 1, s) for s in range(GROUP)]
        + [{"tp": links.other}]
    )
    chunks = [pl.ds(c * ROWS, ROWS) for c in range(base.shape[0] // ROWS)]
    start_mixed, wait_mixed, finish_mixed = trade_mixed(links, mixed_all, mixed)
    swaps = [links.swap(part.at[rows], got.at[rows]) for rows in chunks]
    swaps_two = [links.swap(part_two.at[rows], got_two.at[rows]) for rows in chunks]
    start_qkv, finish_qkv = send_qkv(links, low, w_qkv, bq, ready, pieces, kv_back, kept)
    start_mixed()
    loads[0].wait()
    for c, rows in enumerate(chunks):
        wait_mixed(c)
        out_rows(rows, mixed, w_out, part)
        swaps[c].start()
    loads[1].wait()
    loads[2].wait()
    for c, rows in enumerate(chunks):
        swaps[c].wait()
        norm_rows(c * ROWS, base, (part, got, bout), gain_two, bias_two, middle, low_two)
        feed_rows(rows, low_two, w_fc, bfc, hidden, act, w_proj, part_two)
        swaps_two[c].start()
    loads[3].wait()
    for c, rows in enumerate(chunks):
        swaps_two[c].wait()
        norm_rows(c * ROWS, middle, (part_two, got_two, bproj), gain, bias, stream, low)
        start_qkv(c)
    finish_mixed()
    finish_qkv()


def between_segment(mixed_all, base, vectors, bq, rest, fc_at, proj_at, qkv, first):
    rows, width = base.shape
    total = bq.shape[1]
    cols = total // GROUP
    out_cols = fc_at
    units = proj_at - fc_at
    chunks = rows // ROWS
    copies = pltpu.SemaphoreType.DMA((qkv_copies(rows) + chunks * (GROUP - 1) + 2 * chunks,))
    whole_f32 = (VMEM, shape((rows, width), F32))
    whole_low = (VMEM, shape((rows, width), BF16))
    return run_links(
        functools.partial(between_body, (fc_at, proj_at, first)),
        1,
        [(VMEM, mixed_all), (VMEM, base)]
        + [(VMEM, vector) for vector in vectors]
        + [(VMEM, bq), (ANY, rest), (ANY, qkv)],
        [
            (VMEM, shape((rows, out_cols), BF16)),
            whole_f32,
            whole_low,
            (VMEM, shape((rows, units), F32)),
            (VMEM, shape((rows, units), BF16)),
            whole_f32,
            whole_low,
            (ANY, shape((GROUP, rows, cols), BF16)),
            (ANY, shape((GROUP, rows, 2 * cols // 3), BF16)),
        ],
        [
            pltpu.VMEM((width, out_cols), BF16),
            pltpu.VMEM((width, units), BF16),
            pltpu.VMEM((width, units), BF16),
            pltpu.VMEM((width, total), BF16),
        ]
        + [pltpu.VMEM((rows, width), BF16)] * 4
        + [
            pltpu.VMEM((GROUP, rows, cols), BF16),
            copies,
            copies,
            pltpu.SemaphoreType.DMA((4,)),
            pltpu.SemaphoreType.DMA((chunks,)),
        ],
        flops=2 * rows * width * (total + out_cols + 2 * units),
        moved=rows * width * 20 + rows * units * 6 + width * (total + out_cols + 2 * units) * 2,
    )


def pull_qkv_rows(first, back, links, full, back_got, w, target, sums):
    cols = full.shape[1] // GROUP
    rows = pl.ds(first, ROWS)

    @pl.when(links.group < links.groups - 1)
    def _():
        for s in range(GROUP):
            at = pl.ds(
                pl.multiple_of((links.place ^ s) * cols + cols // 3, cols // 3), 2 * cols // 3
            )
            full[rows, at] = (full[rows, at].astype(F32) + back_got[s, rows].astype(F32)).astype(BF16)

    def tile(at):
        target[rows, at] = dot_last(full[rows, :], w[at, :]).astype(BF16)

    tiles(w.shape[0], 256, tile)

    def body(at):
        sums[...] += eight_rows(full[at, :].astype(F32))

    rows_within(first, body)


def trade_pulls(links, grad_q, grad_kv, grad_kv_back, full, back_got):
    part = grad_q.shape[2]
    copies = []
    for c in range(full.shape[0] // ROWS):
        rows = pl.ds(c * ROWS, ROWS)
        across, back = [], []
        for s in (2, 3, 1):
            for source, start, size in ((grad_kv, part, 2 * part), (grad_q, 0, part)):
                at = pl.ds(pl.multiple_of(links.place * 3 * part + start, part), size)
                across.append(
                    links.copy(source.at[s, rows], full.at[rows, at], links.peer(s))
                )
        for s in (2, 3, 1, 0):
            back.append(
                links.copy(
                    grad_kv_back.at[s, rows],
                    back_got.at[s, rows],
                    links.beyond(links.groups - 1, s),
                )
            )
        copies.append((across, back))

    def start():
        for across, back in copies:
            for one in across:
                one.start()

            @pl.when(links.group > 0)
            def _():
                for one in back:
                    one.start()

        first = pl.multiple_of(links.place * 3 * part, part)
        full[:, pl.ds(first, part)] = grad_q[0]
        full[:, pl.ds(pl.multiple_of(first + part, part), 2 * part)] = grad_kv[0]

    def wait(c):
        across, back = copies[c]
        for one in across:
            one.wait_recv()

        @pl.when(links.group < links.groups - 1)
        def _():
            for one in back:
                one.wait_recv()

    def finish():
        for across, back in copies:
            for one in across:
                one.wait_send()

            @pl.when(links.group > 0)
            def _():
                for one in back:
                    one.wait_send()

    return start, wait, finish


def pull_copies(rows):
    return rows // ROWS * (2 * (GROUP - 1) + GROUP)


def pull_norm_rows(first, grad, own, got, inputs, gain, grad_new, sums, low=None):
    def body(at):
        value = norm_pull_rows(at, grad, own, got, inputs, gain, grad_new, sums[0], sums[1])
        if low is not None:
            value = value.astype(BF16)
            low[at, :] = value
            sums[2][...] += eight_rows(value.astype(F32))

    rows_within(first, body)


def round_rows(first, grad, low, sums):
    def body(at):
        value = grad[at, :].astype(BF16)
        low[at, :] = value
        sums[...] += eight_rows(value.astype(F32))

    rows_within(first, body)


def pull_feed_rows(rows, low, proj, hidden, grad_hidden, sums, fc, target):
    def tile(at):
        value = dot(low[rows, :], proj[:, at]) * gelu_slope(hidden[rows, at])
        value = value.astype(BF16)
        grad_hidden[rows, at] = value
        sums[:, at] += eight_rows(value.astype(F32))

    tiles(proj.shape[1], 512, tile)

    def tile_out(at):
        target[rows, at] = dot_last(grad_hidden[rows, :], fc[at, :]).astype(BF16)

    tiles(fc.shape[0], 256, tile_out)


def send_mixed_pull(links, low, w, ready, pieces, kept):
    cols = ready.shape[2]
    copies = []
    for c in range(low.shape[0] // ROWS):
        rows = pl.ds(c * ROWS, ROWS)
        across = {
            s: links.copy(ready.at[s, rows], pieces.at[s, rows], links.peer(s))
            for s in range(1, GROUP)
        }
        copies.append((across, pltpu.make_async_copy(ready.at[0, rows], pieces.at[0, rows], kept.at[c])))

    def start(c):
        rows = pl.ds(c * ROWS, ROWS)
        across, own = copies[c]
        for s in (2, 3, 1, 0):
            at = columns(links.place ^ s, cols)
            ready[s, rows, :] = dot(low[rows, :], w[:, at]).astype(BF16)
            (across[s] if s else own).start()

    def finish():
        for across, own in copies:
            own.wait()
            for one in across.values():
                one.wait()

    return start, finish


def load_columns(plan, load):
    copies = []
    for i, (source, start, target) in enumerate(plan):
        if start is not None:
            source = source.at[:, pl.ds(start, target.shape[1])]
        copies.append(pltpu.make_async_copy(source, target, load.at[i]))
    for one in copies:
        one.start()
    return copies


def turn_body(
    at, mixed_all, base_in, grad_in, bout, gain_two, bias_two, bfc, rest,
    mixed, middle, low_two, act, part_two, low_proj, sum_proj, grad_hidden, sum_fc, grad_new, low_out,
    sum_gain, sum_bias, sum_out, pieces, stay0, go0, stay1, go1,
    w_out, w_fc, w_proj, base, grad, hidden, part, got, part_three, got_three, ready,
    plain, flipped, away0, away1, met0, met1, send, recv, load, kept
):
    fc_at, proj_at = at
    links = Links(send, recv)
    loads = load_columns(
        (
            (rest, 0, w_out),
            (base_in, None, base),
            (grad_in, None, grad),
            (rest, fc_at, w_fc),
            (rest, proj_at, w_proj),
        ),
        load,
    )
    links.greet([links.peer(s) for s in range(1, GROUP)] + [{"tp": links.other}])
    chunks = [pl.ds(c * ROWS, ROWS) for c in range(base.shape[0] // ROWS)]
    start_mixed, wait_mixed, finish_mixed = trade_mixed(links, mixed_all, mixed)
    swaps = [links.swap(part.at[rows], got.at[rows]) for rows in chunks]
    swaps_three = [links.swap(part_three.at[rows], got_three.at[rows]) for rows in chunks]
    start_pull, finish_pull = send_mixed_pull(links, low_out, w_out, ready, pieces, kept)
    core_sums = (
        CoreSum(links, stay0, go0, away0, met0),
        CoreSum(links, stay1, go1, away1, met1),
    )
    start_mixed()
    for total in (sum_proj, sum_fc, sum_gain, sum_bias, sum_out):
        total[...] = jnp.zeros_like(total)
    loads[0].wait()
    for c, rows in enumerate(chunks):
        wait_mixed(c)
        out_rows(rows, mixed, w_out, part)
        swaps[c].start()
    for one in loads[1:]:
        one.wait()
    for c in range(len(chunks)):
        round_rows(c * ROWS, grad, low_proj, sum_proj)
    for c, rows in enumerate(chunks):
        swaps[c].wait()
        norm_rows(c * ROWS, base, (part, got, bout), gain_two, bias_two, middle, low_two)

        def tile(at):
            value = dot(low_two[rows, :], w_fc[:, at]) + bfc[:, at]
            hidden[rows, at] = value
            act[rows, at] = gelu_rows(value).astype(BF16)

        tiles(w_fc.shape[1], 512, tile)
        pull_feed_rows(rows, low_proj, w_proj, hidden, grad_hidden, sum_fc, w_fc, part_three)
        swaps_three[c].start()
    core_sums[0].multiply(low_two, grad_hidden, plain, flipped)
    core_sums[1].multiply(low_proj, act, plain, flipped)
    for rows in chunks:

        def tile_out(at):
            part_two[rows, at] = dot_last(act[rows, :], w_proj[at, :]).astype(BF16)

        tiles(w_proj.shape[0], 256, tile_out)
    for c, rows in enumerate(chunks):
        swaps_three[c].wait()
        pull_norm_rows(
            c * ROWS, grad, part_three, got_three, middle, gain_two, grad_new, (sum_gain, sum_bias, sum_out), low_out
        )
        start_pull(c)
    for one in core_sums:
        one.add()
    finish_mixed()
    finish_pull()


def turn_segment(mixed_all, base, grad, vectors, rest, fc_at, proj_at):
    rows, width = base.shape
    out_cols, units = fc_at, proj_at - fc_at
    cols = out_cols // GROUP
    chunks = rows // ROWS
    copies = pltpu.SemaphoreType.DMA((2 * chunks * (GROUP - 1) + 2 * chunks + 2,))
    high = (VMEM, shape((rows, width), F32))
    low = (VMEM, shape((rows, width), BF16))
    sums = (VMEM, shape((8, width), F32))
    return run_links(
        functools.partial(turn_body, (fc_at, proj_at)),
        2,
        [(VMEM, mixed_all), (ANY, base), (ANY, grad)]
        + [(VMEM, vector) for vector in vectors]
        + [(ANY, rest)],
        [
            (VMEM, shape((rows, out_cols), BF16)),
            high,
            low,
            (VMEM, shape((rows, units), BF16)),
            low,
            low,
            sums,
            (VMEM, shape((rows, units), BF16)),
            (VMEM, shape((8, units), F32)),
            high,
            low,
            sums,
            sums,
            sums,
            (ANY, shape((GROUP, rows, cols), BF16)),
        ]
        + [(VMEM, shape((width // 4, units), BF16))] * 4,
        [
            pltpu.VMEM((width, out_cols), BF16),
            pltpu.VMEM((width, units), BF16),
            pltpu.VMEM((width, units), BF16),
            pltpu.VMEM((rows, width), F32),
            pltpu.VMEM((rows, width), F32),
            pltpu.VMEM((rows, units), F32),
        ]
        + [pltpu.VMEM((rows, width), BF16)] * 4
        + [
            pltpu.VMEM((GROUP, rows, cols), BF16),
        ]
        + [pltpu.VMEM((width, rows), BF16)] * 2
        + [pltpu.VMEM((width // 2, units), BF16)] * 4
        + [
            copies,
            copies,
            pltpu.SemaphoreType.DMA((5,)),
            pltpu.SemaphoreType.DMA((chunks,)),
        ],
        flops=2 * rows * width * (2 * out_cols + 4 * units),
        moved=rows * width * 22 + rows * units * 4 + width * (out_cols + 2 * units) * 2,
    )


def pull_both_body(
    at, grad_q, grad_kv, grad_kv_back, gain, gain_two, qkv, rest, grad_in, stream_in, hidden_in, middle_in,
    stay0_in, met0_in, stay1_in, go1,
    full, sum_qkv, sum_gain_one, sum_bias_one, low_proj, sum_proj, grad_hidden, sum_fc, grad_new, low_out,
    sum_gain, sum_bias, sum_out, pieces, total0, total1,
    w_qkv, w_out, w_fc, w_proj, grad, stream, hidden, middle, grad_mid, back_got,
    part, got, part_two, got_two, ready,
    stay0, met0, far0, came0, stay1, met1, far1, came1, send, recv, load, kept
):
    first, fc_at, proj_at = at
    links = Links(send, recv)
    loads = load_columns(
        (
            (qkv, first, w_qkv),
            (grad_in, None, grad),
            (stream_in, None, stream),
            (rest, proj_at, w_proj),
            (hidden_in, None, hidden),
            (rest, fc_at, w_fc),
            (middle_in, None, middle),
            (rest, 0, w_out),
            (stay0_in, None, stay0),
            (met0_in, None, met0),
            (stay1_in, None, stay1),
        ),
        load,
    )
    links.greet(
        [links.peer(s) for s in range(1, GROUP)]
        + [links.beyond(1, s) for s in range(GROUP)]
        + [links.beyond(links.groups - 1, s) for s in range(GROUP)]
        + [{"tp": links.other}]
        + group_greets(links)
    )
    chunks = [pl.ds(c * ROWS, ROWS) for c in range(grad.shape[0] // ROWS)]
    start_pulls, wait_pulls, finish_pulls = trade_pulls(
        links, grad_q, grad_kv, grad_kv_back, full, back_got
    )
    swaps = [links.swap(part.at[rows], got.at[rows]) for rows in chunks]
    swaps_two = [links.swap(part_two.at[rows], got_two.at[rows]) for rows in chunks]
    start_pull, finish_pull = send_mixed_pull(links, low_out, w_out, ready, pieces, kept)
    late_x = links.copy(go1, met1, links.peer(2))
    group_sums = (
        GroupSum(links, stay0, met0, far0, came0, total0),
        GroupSum(links, stay1, met1, far1, came1, total1),
    )
    start_pulls()
    for total in (sum_qkv, sum_gain_one, sum_bias_one, sum_proj, sum_fc, sum_gain, sum_bias, sum_out):
        total[...] = jnp.zeros_like(total)
    for one in loads:
        one.wait()
    group_sums[0].add()
    for c, rows in enumerate(chunks):
        wait_pulls(c)
        if c == len(chunks) - 1:
            late_x.start()
            group_sums[0].start()
        pull_qkv_rows(c * ROWS, None, links, full, back_got, w_qkv, part, sum_qkv)
        swaps[c].start()
    for c, rows in enumerate(chunks):
        swaps[c].wait()
        pull_norm_rows(
            c * ROWS, grad, part, got, stream, gain, grad_mid, (sum_gain_one, sum_bias_one)
        )
        round_rows(c * ROWS, grad_mid, low_proj, sum_proj)
        pull_feed_rows(rows, low_proj, w_proj, hidden, grad_hidden, sum_fc, w_fc, part_two)
        swaps_two[c].start()
    late_x.wait()
    group_sums[1].add()
    group_sums[1].start()
    for c, rows in enumerate(chunks):
        swaps_two[c].wait()
        pull_norm_rows(
            c * ROWS, grad_mid, part_two, got_two, middle, gain_two, grad_new, (sum_gain, sum_bias, sum_out), low_out
        )
        start_pull(c)
    finish_pulls()
    finish_pull()
    for one in group_sums:
        one.finish()


def pull_both_segment(pulls, gain, gain_two, qkv, first, rest, fc_at, proj_at, grad, stream, hidden, middle, sums_in):
    rows, width = grad.shape
    out_cols, units = fc_at, proj_at - fc_at
    cols = out_cols // GROUP
    total = 3 * out_cols
    chunks = rows // ROWS
    groups = lax.axis_size("fsdp") // GROUP
    stay = sums_in[0]
    copies = pltpu.SemaphoreType.DMA((pull_copies(rows) + chunks * (GROUP - 1) + 2 * chunks + 2 * groups - 1,))
    high = (VMEM, shape((rows, width), F32))
    low = (VMEM, shape((rows, width), BF16))
    sums = (VMEM, shape((8, width), F32))
    return run_links(
        functools.partial(pull_both_body, (first, fc_at, proj_at)),
        3,
        [(VMEM, pull) for pull in pulls]
        + [(VMEM, gain), (VMEM, gain_two)]
        + [(ANY, array) for array in (qkv, rest, grad, stream, hidden, middle)]
        + [(ANY, array) for array in sums_in],
        [
            (VMEM, shape((rows, total), BF16)),
            (VMEM, shape((8, total), F32)),
            sums,
            sums,
            low,
            sums,
            (VMEM, shape((rows, units), BF16)),
            (VMEM, shape((8, units), F32)),
            high,
            low,
            sums,
            sums,
            sums,
            (ANY, shape((GROUP, rows, cols), BF16)),
        ]
        + [(VMEM, shape((stay.shape[0] // groups, stay.shape[1]), F32))] * 2,
        [
            pltpu.VMEM((width, total), BF16),
            pltpu.VMEM((width, out_cols), BF16),
            pltpu.VMEM((width, units), BF16),
            pltpu.VMEM((width, units), BF16),
            pltpu.VMEM((rows, width), F32),
            pltpu.VMEM((rows, width), F32),
            pltpu.VMEM((rows, units), F32),
            pltpu.VMEM((rows, width), F32),
            pltpu.VMEM((rows, width), F32),
            pltpu.VMEM((GROUP, rows, 2 * cols), BF16),
        ]
        + [pltpu.VMEM((rows, width), BF16)] * 4
        + [
            pltpu.VMEM((GROUP, rows, cols), BF16),
        ]
        + ([pltpu.VMEM(stay.shape, BF16)] + group_scratch(stay, groups, True)) * 2
        + [
            copies,
            copies,
            pltpu.SemaphoreType.DMA((11,)),
            pltpu.SemaphoreType.DMA((chunks,)),
        ],
        flops=2 * rows * width * (total + out_cols + 2 * units),
        moved=rows * width * 22 + rows * units * 6 + width * (total + out_cols + 2 * units) * 2,
    )


def pull_last_body(
    first, grad_q, grad_kv, grad_kv_back, gain, qkv, grad_in, stream_in,
    low_two_in, grad_hidden_in, low_proj_in, act_in, low_one_in, low_out_in, mixed_in, stay0_in, met0_in, stay1_in, met1_in,
    full, sum_qkv, sum_gain, sum_bias, grad_new, total0, total1, total2, total3, total4, total5,
    w_qkv, grad, stream, back_got, part, got, left, right, wide, narrow, plain, flipped,
    stay0, met0, far0, came0, stay1, met1, far1, came1,
    away2, gone2, stay2, go2, met2, far2, came2,
    away3, gone3, stay3, go3, met3, far3, came3,
    away4, gone4, stay4, go4, met4, far4, came4,
    away5, gone5, stay5, go5, met5, far5, came5,
    send, recv, load
):
    links = Links(send, recv)
    loads = load_columns(
        (
            (low_two_in, None, left),
            (grad_hidden_in, None, wide),
            (stay0_in, None, stay0),
            (met0_in, None, met0),
            (stay1_in, None, stay1),
            (met1_in, None, met1),
            (low_proj_in, None, right),
            (qkv, first, w_qkv),
            (grad_in, None, grad),
            (stream_in, None, stream),
            (mixed_in, None, narrow),
        ),
        load,
    )
    again = [
        pltpu.make_async_copy(source, target, load.at[len(loads) + i])
        for i, (source, target) in enumerate(((act_in, wide), (low_one_in, left), (low_out_in, right)))
    ]
    links.greet(
        [links.peer(s) for s in range(1, GROUP)]
        + [links.beyond(1, s) for s in range(GROUP)]
        + [links.beyond(links.groups - 1, s) for s in range(GROUP)]
        + [{"tp": links.other}]
        + group_greets(links)
    )
    chunks = [pl.ds(c * ROWS, ROWS) for c in range(grad.shape[0] // ROWS)]
    start_pulls, wait_pulls, finish_pulls = trade_pulls(
        links, grad_q, grad_kv, grad_kv_back, full, back_got
    )
    swaps = [links.swap(part.at[rows], got.at[rows]) for rows in chunks]
    parts = (
        (away2, gone2, stay2, go2, met2),
        (away3, gone3, stay3, go3, met3),
        (away4, gone4, stay4, go4, met4),
        (away5, gone5, stay5, go5, met5),
    )
    core_sums = [CoreSum(links, stay, go, away, gone) for away, gone, stay, go, _ in parts]
    over_x = [links.copy(go, met, links.peer(2)) for _, _, _, go, met in parts]
    group_sums = [
        GroupSum(links, *refs)
        for refs in (
            (stay0, met0, far0, came0, total0),
            (stay1, met1, far1, came1, total1),
            (stay2, met2, far2, came2, total2),
            (stay3, met3, far3, came3, total3),
            (stay4, met4, far4, came4, total4),
            (stay5, met5, far5, came5, total5),
        )
    ]
    start_pulls()
    for total in (sum_qkv, sum_gain, sum_bias):
        total[...] = jnp.zeros_like(total)
    loads[0].wait()
    loads[1].wait()
    core_sums[0].multiply(left, wide, plain, flipped)
    again[0].start()
    again[1].start()
    for one in loads[2:]:
        one.wait()
    group_sums[0].add()
    group_sums[1].add()
    again[0].wait()
    core_sums[1].multiply(right, wide, plain, flipped)
    again[2].start()
    core_sums[0].add()
    core_sums[1].add()
    for c, rows in enumerate(chunks):
        wait_pulls(c)
        if c == len(chunks) - 1:
            over_x[0].start()
            group_sums[0].start()
            group_sums[1].start()
            over_x[1].start()
        pull_qkv_rows(c * ROWS, None, links, full, back_got, w_qkv, part, sum_qkv)
        swaps[c].start()
    again[1].wait()
    again[2].wait()
    core_sums[2].multiply(left, full, plain, flipped)
    core_sums[3].multiply(right, narrow, plain, flipped)
    for c, rows in enumerate(chunks):
        swaps[c].wait()
        pull_norm_rows(c * ROWS, grad, part, got, stream, gain, grad_new, (sum_gain, sum_bias))
    for at in (2, 3):
        core_sums[at].add()
        over_x[at].start()
    for at in range(4):
        over_x[at].wait()
        group_sums[2 + at].add()
        group_sums[2 + at].start()
    finish_pulls()
    for one in group_sums:
        one.finish()


def pull_last_segment(pulls, gain, qkv, first, grad, stream, factors, sums_in):
    rows, width = grad.shape
    cols = pulls[0].shape[2]
    total = 3 * GROUP * cols
    units = factors[1].shape[1]
    chunks = rows // ROWS
    groups = lax.axis_size("fsdp") // GROUP
    copies = pltpu.SemaphoreType.DMA((pull_copies(rows) + chunks + 8 + 6 * (groups - 1),))
    sums = (VMEM, shape((8, width), F32))
    sizes = [sums_in[0].shape[1], sums_in[2].shape[1], units, units, total, GROUP * cols]
    quarter = width // 4
    scratch = []
    for at, size in enumerate(sizes):
        stay = shape((quarter, size), BF16)
        if at >= 2:
            scratch += [pltpu.VMEM((2 * quarter, size), BF16)] * 2
            scratch += [pltpu.VMEM(stay.shape, BF16)]
        scratch += [pltpu.VMEM(stay.shape, BF16)] + group_scratch(stay, groups, True)
    return run_links(
        functools.partial(pull_last_body, first),
        4,
        [(VMEM, pull) for pull in pulls]
        + [(VMEM, gain)]
        + [(ANY, array) for array in (qkv, grad, stream, *factors, *sums_in)],
        [
            (VMEM, shape((rows, total), BF16)),
            (VMEM, shape((8, total), F32)),
            sums,
            sums,
            (VMEM, shape((rows, width), F32)),
        ]
        + [(VMEM, shape((quarter // groups, size), F32)) for size in sizes],
        [
            pltpu.VMEM((width, total), BF16),
            pltpu.VMEM((rows, width), F32),
            pltpu.VMEM((rows, width), F32),
            pltpu.VMEM((GROUP, rows, 2 * cols), BF16),
            pltpu.VMEM((rows, width), BF16),
            pltpu.VMEM((rows, width), BF16),
            pltpu.VMEM((rows, width), BF16),
            pltpu.VMEM((rows, width), BF16),
            pltpu.VMEM((rows, units), BF16),
            pltpu.VMEM((rows, GROUP * cols), BF16),
            pltpu.VMEM((width, rows), BF16),
            pltpu.VMEM((width, rows), BF16),
        ]
        + scratch
        + [copies, copies, pltpu.SemaphoreType.DMA((14,))],
        flops=2 * rows * width * total * 2 + 4 * rows * width * units,
        moved=rows * width * 24 + rows * units * 4 + width * total * 2,
    )


def flip_slots(links, source, plain, flipped):
    plain[...] = source[...].T
    depth = plain.shape[0] // (GROUP * links.groups)
    slot = 0
    for s in (0, 2, 1, 3):
        for onward in range(links.groups):
            owner = lax.rem(links.group + onward, links.groups) * GROUP + (links.place ^ s)
            flipped[slot * depth : (slot + 1) * depth, :] = plain[
                pl.ds(pl.multiple_of(owner * depth, depth), depth), :
            ]
            slot += 1


class CoreSum:
    def __init__(self, links, stay, go, away, got):
        self.links, self.stay, self.go, self.away, self.got = links, stay, go, away, got
        self.copy = links.copy(away, got, links.peer(1))

    def multiply(self, x, g, plain, flipped):
        flip_slots(self.links, x, plain, flipped)
        quarter = self.stay.shape[0]

        def far(at):
            self.away[:, at] = dot(flipped[2 * quarter :, :], g[:, at]).astype(BF16)

        def near(at):
            self.stay[:, at] = dot(flipped[:quarter, :], g[:, at]).astype(BF16)
            self.go[:, at] = dot(flipped[quarter : 2 * quarter, :], g[:, at]).astype(BF16)

        tiles(g.shape[1], 512, far)
        self.copy.start()
        tiles(g.shape[1], 512, near)

    def add(self):
        self.copy.wait()
        quarter = self.stay.shape[0]
        chunk = 16
        for target, first in ((self.go, quarter), (self.stay, 0)):

            def body(at):
                from_row = pl.ds(pl.multiple_of(at.start + first, chunk), chunk)
                total = target[at, :].astype(F32) + self.got[from_row, :].astype(F32)
                target[at, :] = total.astype(BF16)

            each_rows(quarter, chunk, body)


def weight_pull_body(x0, g0, x1, g1, stay0, go0, stay1, go1, plain, flipped, away0, got0, away1, got1, send, recv):
    links = Links(send, recv)
    links.greet([links.peer(1)])
    first = CoreSum(links, stay0, go0, away0, got0)
    second = CoreSum(links, stay1, go1, away1, got1)
    first.multiply(x0, g0, plain, flipped)
    second.multiply(x1, g1, plain, flipped)
    first.add()
    second.add()


def weight_pull(name, x0, g0, x1, g1):
    rows, width = x0.shape
    sizes = (g0.shape[1], g1.shape[1])
    quarter = [(VMEM, shape((width // 4, size), BF16)) for size in sizes]
    half = [pltpu.VMEM((width // 2, size), BF16) for size in sizes]
    return run_links(
        weight_pull_body,
        name,
        [(VMEM, array) for array in (x0, g0, x1, g1)],
        [quarter[0], quarter[0], quarter[1], quarter[1]],
        [pltpu.VMEM((width, rows), BF16), pltpu.VMEM((width, rows), BF16)]
        + [half[0], half[0], half[1], half[1]]
        + [pltpu.SemaphoreType.DMA((2,)), pltpu.SemaphoreType.DMA((2,))],
        flops=2 * rows * width * sum(sizes),
        moved=rows * width * 4 + (rows + width) * sum(sizes) * 2,
    )


class GroupSum:
    def __init__(self, links, stay, met, far, came, result):
        self.stay, self.met, self.far, self.came, self.result = stay, met, far, came, result
        self.depth = result.shape[0]
        self.copies = []
        for onward in range(1, links.groups):
            rows = pl.ds((onward - 1) * self.depth, self.depth)
            self.copies.append(links.copy(far.at[rows], came.at[rows], links.beyond(onward, 0)))

    def add(self):
        chunk = 16

        def near(at):
            self.result[at, :] = self.stay[at, :].astype(F32) + self.met[at, :].astype(F32)

        each_rows(self.depth, chunk, near)

        def far(at):
            from_row = pl.ds(pl.multiple_of(at.start + self.depth, chunk), chunk)
            total = self.stay[from_row, :].astype(F32) + self.met[from_row, :].astype(F32)
            self.far[at, :] = total.astype(BF16)

        each_rows(self.far.shape[0], chunk, far)

    def start(self):
        for one in self.copies:
            one.start()

    def finish(self):
        for one in self.copies:
            one.wait()
        chunk = 16

        def body(at):
            total = self.result[at, :]
            for onward in range(len(self.copies)):
                from_row = pl.ds(pl.multiple_of(at.start + onward * self.depth, chunk), chunk)
                total = total + self.came[from_row, :].astype(F32)
            self.result[at, :] = total

        each_rows(self.depth, chunk, body)


def group_scratch(stay, groups, met):
    rows, size = stay.shape
    far = pltpu.VMEM((rows - rows // groups, size), BF16)
    return ([pltpu.VMEM((rows, size), BF16)] if met else []) + [far, far]


def group_greets(links):
    return [links.beyond(onward, 0) for onward in range(2, links.groups - 1)]


def doc_start_rows(sc, docs, positions):
    start = jnp.zeros_like(positions)
    for d in range(docs):
        first = sc[2 + d]
        start = jnp.where(first <= positions, jnp.maximum(start, first), start)
    return start


def doc_start_one(sc, docs, position):
    start = jnp.int32(0)
    for d in range(docs):
        first = sc[2 + d]
        start = jnp.where(first <= position, jnp.maximum(start, first), start)
    return start


def query_rows(sc, docs, block):
    first = sc[1] + block * QB
    position = first + lax.broadcasted_iota(jnp.int32, (1, QB), 1)
    start = doc_start_rows(sc, docs, position)
    return (
        jnp.concatenate([position, position], 1),
        jnp.concatenate([start, start], 1),
        doc_start_one(sc, docs, first),
    )


def head_stack(rows, scale):
    value = rows.astype(F32)
    if scale != 1.0:
        value = value * scale
    lane = lax.broadcasted_iota(jnp.int32, value.shape, 1)
    return jnp.concatenate(
        [jnp.where(lane < HEAD_DIM, value, 0.0), jnp.where(lane >= HEAD_DIM, value, 0.0)], 0
    ).astype(BF16)


def place_rows(sc, s, rows):
    return pl.ds(pl.multiple_of((sc[0] ^ s) * rows, rows), rows)


def spread(sc, pieces, first_col, cols, straight=None, flipped=None):
    for s, piece in enumerate(pieces):
        value = piece[s] if len(piece.shape) == 3 and piece.shape[0] > 1 else None
        if value is None:
            value = piece[0] if len(piece.shape) == 3 else piece[...]
        value = value[:, first_col : first_col + cols]
        at = place_rows(sc, s, value.shape[0])
        if straight is not None:
            straight[at, :] = value
        if flipped is not None:
            flipped[:, at] = value.T


def block_at(block, size):
    return pl.ds(pl.multiple_of(block * size, size), size)


def masked_scores(keys, queries, first_key, position, start):
    scores = dot_last(keys, queries)
    key_at = first_key + lax.broadcasted_iota(jnp.int32, (KB, 1), 0)
    return jnp.where((key_at >= start) & (key_at <= position), scores, NEG)


def flash_step(keys_ref, values_ref, queries, block, first_key, position, start, acc, carry):
    top, total = carry
    scores = masked_scores(keys_ref[block_at(block, KB), :], queries, first_key, position, start)
    top_new = jnp.maximum(top, jnp.max(scores, 0, keepdims=True))
    expo = jnp.exp(scores - top_new)
    shrink = jnp.exp(top - top_new)
    total = total * shrink + jnp.sum(expo, 0, keepdims=True)
    expo = expo.astype(BF16)
    for h in range(2):
        lanes = slice(h * QB, (h + 1) * QB)
        rows = slice(h * HEAD_DIM, (h + 1) * HEAD_DIM)
        values = values_ref[rows, block_at(block, KB)]
        acc[rows, :] = acc[rows, :] * shrink[:, lanes] + dot(values, expo[:, lanes])
    return top_new, total


def attend_body(docs, sc, p0, kv, mixed, out, log_total, q_all, k_all, v_flip, k_back, v_back, acc):
    block = pl.program_id(0)
    span, cols = q_all.shape

    @pl.when(block == 0)
    def _():
        pieces = (p0,) * GROUP
        spread(sc, pieces, 0, cols, straight=q_all)
        spread(sc, pieces, cols, cols, straight=k_all)
        spread(sc, pieces, 2 * cols, cols, flipped=v_flip)
        spread(sc, (kv,) * GROUP, 0, cols, straight=k_back)
        spread(sc, (kv,) * GROUP, cols, cols, flipped=v_back)

    position, start, lowest = query_rows(sc, docs, block)
    queries = head_stack(q_all[block_at(block, QB), :], HEAD_DIM**-0.5)
    acc[...] = jnp.zeros_like(acc)
    least = jnp.maximum(lowest - sc[1], 0) // KB
    last = ((block + 1) * QB - 1) // KB
    before = sc[1] - span

    def step(back, carry):
        at = last - back
        return flash_step(
            k_all, v_flip, queries, at, sc[1] + at * KB, position, start, acc, carry
        )

    def step_back(at, carry):
        return flash_step(
            k_back, v_back, queries, at, before + at * KB, position, start, acc, carry
        )

    carry = (jnp.full((1, 2 * QB), NEG, F32), jnp.zeros((1, 2 * QB), F32))
    carry = lax.fori_loop(0, last - least + 1, step, carry)
    top, total = lax.fori_loop(
        jnp.minimum(jnp.maximum(lowest - before, 0), span) // KB, span // KB, step_back, carry
    )
    sums = top + jnp.log(total)
    share = 1.0 / total
    parts = []
    for h in range(2):
        lanes = slice(h * QB, (h + 1) * QB)
        log_total[h : h + 1, :] = sums[:, lanes]
        parts.append(acc[h * HEAD_DIM : (h + 1) * HEAD_DIM, :] * share[:, lanes])
    value = jnp.concatenate(parts, 0).T
    out[...] = value
    mixed[0] = value.astype(BF16)


def slot_spec(rows, cols):
    per = rows // QB
    return pl.BlockSpec((1, QB, cols), lambda j, sc: ((j // per) ^ sc[0], j % per, 0))


def attend(sc, docs, pieces, kv):
    rows, cols = pieces.shape[1], pieces.shape[2] // 3
    span = GROUP * rows
    stat = (pl.BlockSpec((8, QB), lambda j, sc: (0, j)), shape((8, span), F32))
    low = pltpu.VMEM((span, cols), BF16)
    low_flip = pltpu.VMEM((cols, span), BF16)
    return run_kernel(
        functools.partial(attend_body, docs),
        (span // QB,),
        sc,
        [(whole(pieces.shape), pieces), (whole(kv.shape), kv)],
        [
            (slot_spec(rows, cols), shape((GROUP, rows, cols), BF16)),
            (pl.BlockSpec((QB, cols), lambda j, sc: (j, 0)), shape((span, cols), F32)),
            stat,
        ],
        scratch=[low, low, low_flip, low, low_flip, pltpu.VMEM((cols, QB), F32)],
        flops=span * span * cols * 4,
        moved=span * cols * 20,
    )


def pull_step(block, first_key, position, start, queries, grads, log_rows, delta, refs):
    k_all, v_all, k_flip, grad_k, grad_v, grad_q = refs
    at = block_at(block, KB)
    scores = masked_scores(k_all[at, :], queries, first_key, position, start)
    probs = jnp.exp(scores - log_rows)
    grad_probs = dot_last(v_all[at, :], grads)
    grad_scores = (probs * (grad_probs - delta)).astype(BF16)
    grad_v[at, :] += dot(probs.astype(BF16), grads)
    grad_k[at, :] += dot(grad_scores, queries)
    for h in range(2):
        rows = slice(h * HEAD_DIM, (h + 1) * HEAD_DIM)
        grad_q[rows, :] += dot(k_flip[rows, at], grad_scores[:, h * QB : (h + 1) * QB])


def pull_rows(block, q_all, g_all, out, log_total):
    queries = head_stack(q_all[block_at(block, QB), :], HEAD_DIM**-0.5)
    grad_rows = g_all[block_at(block, QB), :]
    grads = head_stack(grad_rows, 1.0)
    flipped = (grad_rows.astype(F32) * out[...]).T
    delta = jnp.concatenate(
        [
            jnp.sum(flipped[h * HEAD_DIM : (h + 1) * HEAD_DIM, :], 0, keepdims=True)
            for h in range(2)
        ],
        1,
    )
    log_rows = jnp.concatenate([log_total[h : h + 1, :] for h in range(2)], 1)
    return queries, grads, log_rows, delta


def pull_body(
    docs, sc, p0, g0, kv, out, log_total, grad_q_out, grad_kv, grad_kv_back,
    q_all, g_all, k_all, v_all, k_flip, grad_k, grad_v, k_back, v_back, k_back_flip, grad_k_back, grad_v_back, grad_q
):
    block = pl.program_id(0)
    span, cols = q_all.shape
    before = sc[1] - span

    @pl.when(block == 0)
    def _():
        pieces = (p0,) * GROUP
        spread(sc, pieces, 0, cols, straight=q_all)
        spread(sc, (g0,) * GROUP, 0, cols, straight=g_all)
        spread(sc, pieces, cols, cols, straight=k_all, flipped=k_flip)
        spread(sc, pieces, 2 * cols, cols, straight=v_all)
        spread(sc, (kv,) * GROUP, 0, cols, straight=k_back, flipped=k_back_flip)
        spread(sc, (kv,) * GROUP, cols, cols, straight=v_back)
        for total in (grad_k, grad_v, grad_k_back, grad_v_back):
            total[...] = jnp.zeros_like(total)

    grad_q[...] = jnp.zeros_like(grad_q)
    position, start, lowest = query_rows(sc, docs, block)
    queries, grads, log_rows, delta = pull_rows(block, q_all, g_all, out, log_total)

    def step(first, refs, at, carry):
        pull_step(at, first + at * KB, position, start, queries, grads, log_rows, delta, refs)
        return carry

    own_refs = (k_all, v_all, k_flip, grad_k, grad_v, grad_q)
    back_refs = (k_back, v_back, k_back_flip, grad_k_back, grad_v_back, grad_q)
    last = ((block + 1) * QB - 1) // KB
    lax.fori_loop(
        jnp.maximum(lowest - sc[1], 0) // KB, last + 1, functools.partial(step, sc[1], own_refs), 0
    )
    lax.fori_loop(
        jnp.minimum(jnp.maximum(lowest - before, 0), span) // KB,
        span // KB,
        functools.partial(step, before, back_refs),
        0,
    )
    grad_q_out[0] = (grad_q[...] * HEAD_DIM**-0.5).T.astype(BF16)

    @pl.when(block == pl.num_programs(0) - 1)
    def _():
        for s in range(GROUP):
            at = place_rows(sc, s, span // GROUP)
            grad_kv[s, :, :cols] = grad_k[at, :].astype(BF16)
            grad_kv[s, :, cols:] = grad_v[at, :].astype(BF16)
            grad_kv_back[s, :, :cols] = grad_k_back[at, :].astype(BF16)
            grad_kv_back[s, :, cols:] = grad_v_back[at, :].astype(BF16)


def attend_pull(sc, docs, pieces, grads, kv, out, log_total):
    rows, cols = pieces.shape[1], pieces.shape[2] // 3
    span = GROUP * rows
    ins = [
        (whole(pieces.shape), pieces),
        (whole(grads.shape), grads),
        (whole(kv.shape), kv),
        (pl.BlockSpec((QB, cols), lambda j, sc: (j, 0)), out),
        (pl.BlockSpec((8, QB), lambda j, sc: (0, j)), log_total),
    ]
    both = (whole((GROUP, rows, 2 * cols)), shape((GROUP, rows, 2 * cols), BF16))
    low = pltpu.VMEM((span, cols), BF16)
    low_flip = pltpu.VMEM((cols, span), BF16)
    high = pltpu.VMEM((span, cols), F32)
    return run_kernel(
        functools.partial(pull_body, docs),
        (span // QB,),
        sc,
        ins,
        [(slot_spec(rows, cols), shape((GROUP, rows, cols), BF16)), both, both],
        scratch=[low, low, low, low, low_flip, high, high, low, low, low_flip, high, high]
        + [pltpu.VMEM((cols, QB), F32)],
        flops=span * span * cols * 9,
        moved=span * cols * 30,
    )


def swap_tp(value):
    return lax.ppermute(value, "tp", [(0, 1), (1, 0)])


def swap_fsdp(value, s):
    return lax.ppermute(value, "fsdp", [(i, i ^ s) for i in range(lax.axis_size("fsdp"))])


def shift_fsdp(value, by):
    size = lax.axis_size("fsdp")
    return lax.ppermute(value, "fsdp", [(i, i + by) for i in range(size) if 0 <= i + by < size])


def butterfly(value):
    s = 1
    while s < lax.axis_size("fsdp"):
        value = value + swap_fsdp(value, s)
        s *= 2
    return value


def trade(pieces):
    return [pieces] + [swap_fsdp(pieces[s], s) for s in range(1, GROUP)]


def gather(shard):
    return lax.all_gather(shard, "fsdp", axis=0, tiled=True)


def tie(*values):
    return lax.optimization_barrier(values)


def shards(
    tokens,
    cotangent,
    segments,
    doc_batch,
    ln1_gain,
    ln1_bias,
    w_qkv,
    b_qv,
    w_out,
    b_out,
    ln2_gain,
    ln2_bias,
    w_fc,
    b_fc,
    w_proj,
    b_proj,
):
    rows, width = tokens.shape
    depth = w_qkv.shape[1]
    out_cols = w_out.shape[1]
    units = w_fc.shape[2]
    cols = out_cols // GROUP
    docs = doc_batch.shape[0]
    me = lax.axis_index("fsdp")
    total_rows = rows * lax.axis_size("fsdp")

    def pack_qkv(l):
        return w_qkv[l].reshape(depth, 3, GROUP, cols).transpose(0, 2, 1, 3).reshape(depth, 3 * out_cols)

    def pack_rest(l):
        return [w_out[l].T, w_fc[l], w_proj[l].T]

    fc_at, proj_at = out_cols, out_cols + units
    rest_cols = out_cols + 2 * units
    full_a = gather(pack_qkv(0))
    full_b = gather(jnp.concatenate(pack_rest(0) + [pack_qkv(1)], 1))
    full_c = gather(jnp.concatenate(pack_rest(1), 1))
    qkv_of = ((full_a, 0), (full_b, rest_cols))
    rest_of = (full_b, full_c)

    doc_ids = jnp.arange(docs, dtype=jnp.int32)
    is_doc = segments[:, None] == doc_ids[None, :]
    doc_tokens = butterfly(jnp.sum(is_doc.astype(jnp.int32), 0))
    doc_first = jnp.cumsum(doc_tokens) - doc_tokens
    in_batch = doc_batch[:, None] == jnp.arange(MB, dtype=jnp.int32)[None, :]
    counts = jnp.sum(jnp.where(in_batch, doc_tokens[:, None], 0), 0)
    doc_count = jnp.sum(jnp.where(in_batch, counts[None, :], 0), 1)
    row_count = jnp.sum(jnp.where(is_doc, doc_count[None, :], 0), 1).astype(F32)
    row_weight = total_rows / (MB * row_count)
    sc = jnp.concatenate(
        [jnp.stack([me % GROUP, (me // GROUP) * (GROUP * rows)]).astype(jnp.int32), doc_first]
    )

    def bias_qkv(l):
        three = jnp.stack([b_qv[l, 0], jnp.zeros_like(b_qv[l, 0]), b_qv[l, 1]])
        return three.reshape(3, GROUP, cols).transpose(1, 0, 2).reshape(1, 3 * out_cols)

    def row(vector):
        return vector.reshape(1, vector.shape[0])

    stored = []
    stream, low_one, pieces, kv_back = first_segment(
        tokens, row(ln1_gain[0]), row(ln1_bias[0]), full_a, bias_qkv(0)
    )
    for l in range(LAYERS - 1):
        mixed, out, log_total = attend(sc, docs, pieces, kv_back)
        vectors = (b_out[l], ln2_gain[l], ln2_bias[l], b_fc[l], b_proj[l], ln1_gain[l + 1], ln1_bias[l + 1])
        mixed_full, middle, low_two, hidden, act, *later = between_segment(
            mixed,
            stream,
            [row(vector) for vector in vectors],
            bias_qkv(l + 1),
            rest_of[l],
            fc_at,
            proj_at,
            *qkv_of[l + 1],
        )
        stored.append(
            (stream, low_one, pieces, kv_back, out, log_total, mixed_full, middle, low_two, hidden, act)
        )
        stream, low_one, pieces, kv_back = later

    l = LAYERS - 1
    mixed, out, log_total = attend(sc, docs, pieces, kv_back)
    grad = cotangent.astype(F32) * row_weight[:, None]
    (
        mixed_full,
        middle,
        low_two,
        act,
        part_two,
        low_proj,
        sum_bproj,
        grad_hidden,
        sum_bfc,
        grad,
        low_out,
        sum_gain_two,
        sum_bias_two,
        sum_bout,
        grad_mixed,
        *feed_parts,
    ) = turn_segment(
        mixed,
        stream,
        grad,
        [row(vector) for vector in (b_out[l], ln2_gain[l], ln2_bias[l], b_fc[l])],
        rest_of[l],
        fc_at,
        proj_at,
    )
    other_two = swap_tp(part_two)
    outputs = (middle + (part_two.astype(F32) + other_two.astype(F32)) + b_proj[l][None]).astype(BF16)

    stay0, go0, stay1, go1 = feed_parts
    met0 = swap_fsdp(go0, 2)
    grad_mixed, stay0 = tie(grad_mixed, stay0)
    pulls = attend_pull(sc, docs, pieces, grad_mixed, kv_back, out, log_total)
    *pulls, met0 = tie(*pulls, met0)
    sums_one = [sum_bout, sum_gain_two, sum_bias_two, sum_bfc, sum_bproj]
    low_one_kept, low_out_kept, mixed_kept = low_one, low_out, mixed_full
    (stream_below, low_one, pieces, kv_back, out, log_total, mixed_full, middle, low_two, hidden, act) = stored[0]
    weights, first = qkv_of[1]
    (
        grad_qkv,
        sum_bqkv,
        sum_gain_one,
        sum_bias_one,
        low_proj,
        sum_bproj,
        grad_hidden,
        sum_bfc,
        grad,
        low_out,
        sum_gain_two,
        sum_bias_two,
        sum_bout,
        grad_mixed,
        *feed_totals,
    ) = pull_both_segment(
        pulls,
        row(ln1_gain[1]),
        row(ln2_gain[0]),
        weights,
        first,
        rest_of[0],
        fc_at,
        proj_at,
        grad,
        stream,
        hidden,
        middle,
        [stay0, met0, stay1, go1],
    )
    stay0, go0, stay1, go1 = weight_pull(5, low_one_kept, grad_qkv, low_out_kept, mixed_kept)
    met0, met1 = swap_fsdp(go0, 2), swap_fsdp(go1, 2)

    def join_small(sums):
        return butterfly(jnp.concatenate([jnp.sum(value, 0) for value in sums]))

    small_one = join_small([sum_gain_one, sum_bias_one, sum_bqkv] + sums_one)
    grad_mixed, stay0 = tie(grad_mixed, stay0)
    pulls = attend_pull(sc, docs, pieces, grad_mixed, kv_back, out, log_total)
    *pulls, met0, met1 = tie(*pulls, met0, met1)
    sums_zero = [sum_bout, sum_gain_two, sum_bias_two, sum_bfc, sum_bproj]
    weights, first = qkv_of[0]
    grad_qkv, sum_bqkv, sum_gain_one, sum_bias_one, grad, *totals = pull_last_segment(
        pulls,
        row(ln1_gain[0]),
        weights,
        first,
        grad,
        stream_below,
        [low_two, grad_hidden, low_proj, act, low_one, low_out, mixed_full],
        [stay0, met0, stay1, met1],
    )
    small_zero = join_small([sum_gain_one, sum_bias_one, sum_bqkv] + sums_zero)
    small = [small_zero, small_one]
    large = [totals[2:], feed_totals + totals[:2]]

    def small_parts(vector):
        ends, at = [], 0
        for size in (width, width, 3 * out_cols, width, width, width, units, width):
            ends.append(vector[at : at + size])
            at += size
        three = ends[2].reshape(GROUP, 3, cols).transpose(1, 0, 2).reshape(3, out_cols)
        ends[2] = three[0::2]
        return ends

    small = [small_parts(vector) for vector in small]

    def stack_small(member):
        return jnp.stack([small[l][member] for l in range(LAYERS)])

    grad_wqkv = jnp.stack(
        [
            large[l][2]
            .reshape(depth, GROUP, 3, cols)
            .transpose(0, 2, 1, 3)
            .reshape(depth, 3, out_cols)
            for l in range(LAYERS)
        ]
    )
    grad_wout = jnp.stack([large[l][3].T for l in range(LAYERS)])
    grad_wfc = jnp.stack([large[l][0] for l in range(LAYERS)])
    grad_wproj = jnp.stack([large[l][1].T for l in range(LAYERS)])

    return (
        outputs,
        grad,
        stack_small(0),
        stack_small(1),
        grad_wqkv,
        stack_small(2),
        grad_wout,
        stack_small(3),
        stack_small(4),
        stack_small(5),
        grad_wfc,
        stack_small(6),
        grad_wproj,
        stack_small(7),
    )


def solution(mesh):
    placed = (
        P("fsdp", None),
        P("fsdp", None),
        P("fsdp"),
        P(),
        P(),
        P(),
        P(None, "fsdp", None, "tp"),
        P(None, None, "tp"),
        P(None, "tp", "fsdp"),
        P(),
        P(),
        P(),
        P(None, "fsdp", "tp"),
        P(None, "tp"),
        P(None, "tp", "fsdp"),
        P(),
    )
    return jax.shard_map(
        shards,
        mesh=mesh,
        in_specs=placed,
        out_specs=(
            P("fsdp", None),
            P("fsdp", None),
            P(),
            P(),
            P(None, "fsdp", None, "tp"),
            P(None, None, "tp"),
            P(None, "tp", "fsdp"),
            P(),
            P(),
            P(),
            P(None, "fsdp", "tp"),
            P(None, "tp"),
            P(None, "tp", "fsdp"),
            P(),
        ),
        check_vma=False,
    )
```

```python
import functools

import jax
import jax.numpy as jnp
from jax import lax
from jax.experimental import pallas as pl
from jax.experimental.pallas import tpu as pltpu
from jax.sharding import PartitionSpec as P

HEAD_DIM = 64
LAYERS = 2
MB = 3
REACH = 4

EPS = 1e-05
GROUP = REACH
QB = 512
PULL_QB = 256
LN_ROWS = 128
ACT_ROWS = 128
KB = 512
PULL_KB = 256
NEG = -1e30
F32 = jnp.float32
BF16 = jnp.bfloat16
VMEM_BYTES = 62 * 1024 * 1024
LAST = (((1,), (1,)), ((), ()))
FIRST = (((0,), (0,)), ((), ()))


def dot(left, right):
    return jnp.dot(left, right, preferred_element_type=F32)


def dot_last(left, right):
    return lax.dot_general(left, right, LAST, preferred_element_type=F32)


def shape(dims, dtype):
    return jax.ShapeDtypeStruct(dims, dtype)


def whole(dims):
    return pl.BlockSpec(dims, lambda *_: (0,) * len(dims))


def run_kernel(body, grid, scalars, ins, outs, scratch=(), flops=0, moved=0):
    return pl.pallas_call(
        body,
        grid_spec=pltpu.PrefetchScalarGridSpec(
            num_scalar_prefetch=1,
            grid=grid,
            in_specs=[spec for spec, _ in ins],
            out_specs=[spec for spec, _ in outs],
            scratch_shapes=list(scratch),
        ),
        out_shape=[out for _, out in outs],
        compiler_params=pltpu.CompilerParams(
            vmem_limit_bytes=VMEM_BYTES, dimension_semantics=("arbitrary",) * len(grid)
        ),
        cost_estimate=pl.CostEstimate(flops=flops, bytes_accessed=moved, transcendentals=0),
    )(scalars, *[array for _, array in ins])


def each_rows(count, chunk, body):
    def step(at, carry):
        body(pl.ds(pl.multiple_of(at * chunk, chunk), chunk))
        return carry

    lax.fori_loop(0, count // chunk, step, 0)


def norm_parts(rows):
    centred = rows - jnp.mean(rows, -1, keepdims=True)
    inv_scale = lax.rsqrt(jnp.mean(centred * centred, -1, keepdims=True) + EPS)
    return centred * inv_scale, inv_scale


def norm_pull(grad_rows, unit_rows, inv_scale, gain):
    scaled = grad_rows * gain
    return inv_scale * (
        scaled
        - jnp.mean(scaled, -1, keepdims=True)
        - unit_rows * jnp.mean(scaled * unit_rows, -1, keepdims=True)
    )


def eight_rows(rows):
    return jnp.sum(rows.reshape(rows.shape[0] // 8, 8, rows.shape[1]), 0)


def gelu_rows(value):
    return 0.5 * value * (1.0 + jnp.tanh(0.7978845608028654 * (value + 0.044715 * value * value * value)))


def gelu_slope(value):
    square = value * value
    top = jnp.tanh(0.7978845608028654 * (value + 0.044715 * square * value))
    inner = 0.7978845608028654 * (1.0 + 3.0 * 0.044715 * square)
    return 0.5 * (1.0 + top) + 0.5 * value * (1.0 - top * top) * inner


def norm_pull_rows(at, grad, own, got, inputs, gain, grad_new, sum_gain, sum_bias):
    grad_rows = own[at, :].astype(F32) + got[at, :].astype(F32)
    unit, inv_scale = norm_parts(inputs[at, :])
    value = grad[at, :] + norm_pull(grad_rows, unit, inv_scale, gain[...])
    grad_new[at, :] = value
    sum_gain[...] += eight_rows(grad_rows * unit)
    sum_bias[...] += eight_rows(grad_rows)
    return value


ROWS = 256
MESH = pl.DeviceIdType.MESH


class Links:
    def __init__(self, send, recv):
        self.send, self.recv, self.used = send, recv, 0
        self.me = lax.axis_index("fsdp")
        self.place = lax.rem(self.me, GROUP)
        self.group = self.me // GROUP
        self.groups = lax.axis_size("fsdp") // GROUP
        self.other = 1 - lax.axis_index("tp")

    def peer(self, s):
        return {"fsdp": self.group * GROUP + (self.place ^ s)}

    def beyond(self, by, s):
        return {"fsdp": lax.rem(self.group + by, self.groups) * GROUP + (self.place ^ s)}

    def copy(self, source, target, device):
        at = self.used
        self.used += 1
        return pltpu.make_async_remote_copy(
            src_ref=source,
            dst_ref=target,
            send_sem=self.send.at[at],
            recv_sem=self.recv.at[at],
            device_id=device,
            device_id_type=MESH,
        )

    def swap(self, source, target):
        return self.copy(source, target, {"tp": self.other})

    def greet(self, devices):
        barrier = pltpu.get_barrier_semaphore()
        for device in devices:
            pl.semaphore_signal(barrier, inc=1, device_id=device, device_id_type=MESH)
        pl.semaphore_wait(barrier, len(devices))


def columns(place, cols):
    return pl.ds(pl.multiple_of(place * cols, cols), cols)


def tiles(count, size, body):
    def step(at, carry):
        body(pl.ds(pl.multiple_of(at * size, size), size))
        return carry

    lax.fori_loop(0, count // size, step, 0)


def rows_within(first, body):
    def step(at, carry):
        body(pl.ds(pl.multiple_of(first + at * LN_ROWS, LN_ROWS), LN_ROWS))
        return carry

    lax.fori_loop(0, ROWS // LN_ROWS, step, 0)


def out_rows(rows, mixed, w, target):
    def tile(at):
        target[rows, at] = dot_last(mixed[rows, :], w[at, :]).astype(BF16)

    tiles(w.shape[0], 256, tile)


def norm_rows(first, base, sums, gain, bias, stream, low):
    def body(at):
        value = base[at, :].astype(F32)
        if sums is not None:
            own, got, badd = sums
            value = value + (own[at, :].astype(F32) + got[at, :].astype(F32)) + badd[...]
        stream[at, :] = value
        unit, _ = norm_parts(value)
        low[at, :] = (unit * gain[...] + bias[...]).astype(BF16)

    rows_within(first, body)


def feed_rows(rows, low, fc, bfc, hidden, act, proj, target):
    def tile(at):
        value = dot(low[rows, :], fc[:, at]) + bfc[:, at]
        hidden[rows, at] = value
        act[rows, at] = gelu_rows(value).astype(BF16)

    tiles(fc.shape[1], 512, tile)

    def tile_out(at):
        target[rows, at] = dot_last(act[rows, :], proj[at, :]).astype(BF16)

    tiles(proj.shape[0], 256, tile_out)


def send_qkv(links, low, w, bq, ready, pieces, kv_back, kept):
    cols = bq.shape[1] // GROUP
    copies = []
    order = (2, 3, 1, 0)
    chunks = low.shape[0] // ROWS
    for c in range(chunks):
        rows = pl.ds(c * ROWS, ROWS)
        across = {
            s: links.copy(ready.at[s, rows], pieces.at[links.place, rows], links.peer(s)) for s in order if s
        }
        onward = {
            s: links.copy(
                ready.at[s, rows, pl.ds(cols // 3, 2 * cols // 3)],
                kv_back.at[links.place, rows],
                links.beyond(1, s),
            )
            for s in order
        }
        own = pltpu.make_async_copy(ready.at[0, rows], pieces.at[links.place, rows], kept.at[c])
        copies.append((across, onward, own))
    last = links.group == links.groups - 1

    def start(c):
        rows = pl.ds(c * ROWS, ROWS)
        across, onward, own = copies[c]
        for s in order:
            at = columns(links.place ^ s, cols)
            ready[s, rows, :] = (dot(low[rows, :], w[:, at]) + bq[:, at]).astype(BF16)
            if s:
                across[s].start()
            else:
                own.start()

            @pl.when(jnp.logical_not(last))
            def _():
                onward[s].start()

    def finish():
        for across, onward, own in copies:
            own.wait()
            for s in order:
                if s:
                    across[s].wait()

                @pl.when(jnp.logical_not(last))
                def _():
                    onward[s].wait_send()

                @pl.when(links.group > 0)
                def _():
                    onward[s].wait_recv()

    return start, finish


def qkv_copies(rows):
    return rows // ROWS * (2 * GROUP - 1)


class ShardGather:
    def __init__(self, links, shard, full):
        self.depth = shard.shape[0]
        self.links, self.shard, self.full = links, shard, full
        groups = range(links.groups)
        self.along = [
            links.copy(shard, full.at[self.rows(0, 0)], links.beyond(onward, 0)) for onward in groups[1:]
        ]
        self.over_x = [self.relay(onward, 0, links.peer(2)) for onward in groups]
        self.over_core = [
            [self.relay(onward, s, links.peer(1)) for onward in groups] for s in (0, 2)
        ]

    def rows(self, back, s):
        links = self.links
        group = lax.rem(links.group + links.groups - back, links.groups)
        owner = group * GROUP + (links.place ^ s)
        return pl.ds(pl.multiple_of(owner * self.depth, self.depth), self.depth)

    def relay(self, back, s, device):
        rows = self.rows(back, s)
        own = back == 0 and s == 0
        return self.links.copy(self.shard if own else self.full.at[rows], self.full.at[rows], device)

    def start(self):
        for one in self.along:
            one.start()
        self.over_x[0].start()
        self.over_core[0][0].start()
        self.full[self.rows(0, 0), :] = self.shard[...]

    def pass_x(self):
        for onward, one in enumerate(self.along, 1):
            one.wait_recv()
            self.over_x[onward].start()
            self.over_core[0][onward].start()

    def pass_core(self):
        for one, last in zip(self.over_x, self.over_core[1]):
            one.wait_recv()
            last.start()

    def arrive(self):
        for one in self.over_core[0] + self.over_core[1]:
            one.wait_recv()

    def finish(self):
        for one in self.along + self.over_x + self.over_core[0] + self.over_core[1]:
            one.wait_send()


def gather_copies():
    groups = lax.axis_size("fsdp") // GROUP
    return 4 * groups - 1


class RowSum:
    def __init__(self, links, held, came, far):
        self.held, self.came, self.far = held, came, far
        self.near = [links.copy(held.at[i], came.at[i], links.peer(i + 1)) for i in range(2)]
        self.along = [
            links.copy(held.at[2], far.at[onward - 1], links.beyond(onward, 0))
            for onward in range(1, links.groups)
        ]

    def step(self, i):
        self.near[i].wait()
        self.held[i + 1] = self.held[i] + self.came[i]

    def finish(self):
        total = self.held[2]
        for at, one in enumerate(self.along):
            one.wait()
            total = total + self.far[at]
        return total


def count_docs(segments, counts):
    for d in range(counts.shape[0]):
        found = jnp.where(segments[...] == d, 1.0, 0.0).astype(F32)
        total = jnp.sum(jnp.sum(found, 0, keepdims=True), 1, keepdims=True)
        counts[d : d + 1, :] = jnp.broadcast_to(total, (1, counts.shape[1]))


def first_body(
    base, gain, bias, shard, bq, segments, stream, low, w, tokens, first, pieces, kv_back,
    ready, held, came, far, send, recv, kept
):
    links = Links(send, recv)
    gathered = ShardGather(links, shard, w)
    counted = RowSum(links, held, came, far)
    start, finish = send_qkv(links, low, w, bq, ready, pieces, kv_back, kept)
    count_docs(segments, held.at[0])
    links.greet(
        [links.peer(s) for s in range(1, GROUP)]
        + [links.beyond(1, s) for s in range(GROUP)]
        + [links.beyond(links.groups - 1, s) for s in range(GROUP)]
        + group_greets(links)
    )
    gathered.start()
    counted.near[0].start()
    chunks = base.shape[0] // ROWS
    for c in range(chunks):
        norm_rows(c * ROWS, base, None, gain, bias, stream, low)
    counted.step(0)
    counted.near[1].start()
    gathered.pass_x()
    counted.step(1)
    for one in counted.along:
        one.start()
    gathered.pass_core()
    gathered.arrive()
    for c in range(chunks):
        start(c)
    total = counted.finish()
    tokens[...] = total
    begin = jnp.zeros((1, total.shape[1]), F32)
    for d in range(total.shape[0]):
        first[d : d + 1, :] = begin
        begin = begin + total[d : d + 1, :]
    gathered.finish()
    finish()


ANY = pl.BlockSpec(memory_space=pl.ANY)
VMEM = pl.BlockSpec(memory_space=pltpu.VMEM)


def run_links(body, name, ins, outs, scratch, flops, moved):
    return pl.pallas_call(
        body,
        in_specs=[spec for spec, _ in ins],
        out_specs=[spec for spec, _ in outs],
        out_shape=[out for _, out in outs],
        scratch_shapes=list(scratch),
        compiler_params=pltpu.CompilerParams(
            vmem_limit_bytes=VMEM_BYTES, collective_id=name, has_side_effects=True
        ),
        cost_estimate=pl.CostEstimate(flops=flops, bytes_accessed=moved, transcendentals=0),
    )(*[array for _, array in ins])


def first_segment(base, gain, bias, shard, bq, segments, docs):
    rows, width = base.shape
    total = bq.shape[1]
    cols = total // GROUP
    groups = lax.axis_size("fsdp") // GROUP
    copies = pltpu.SemaphoreType.DMA((qkv_copies(rows) + gather_copies() + groups + 1,))
    counts = (VMEM, shape((docs, 128), F32))
    return run_links(
        first_body,
        0,
        [(VMEM, array) for array in (base, gain, bias, shard, bq, segments)],
        [
            (VMEM, shape((rows, width), F32)),
            (VMEM, shape((rows, width), BF16)),
            (VMEM, shape((width, total), BF16)),
            counts,
            counts,
            (ANY, shape((GROUP, rows, cols), BF16)),
            (ANY, shape((GROUP, rows, 2 * cols // 3), BF16)),
        ],
        [
            pltpu.VMEM((GROUP, rows, cols), BF16),
            pltpu.VMEM((3, docs, 128), F32),
            pltpu.VMEM((2, docs, 128), F32),
            pltpu.VMEM((groups - 1, docs, 128), F32),
            copies,
            copies,
            pltpu.SemaphoreType.DMA((rows // ROWS,)),
        ],
        flops=2 * rows * width * total,
        moved=rows * width * 8 + width * total * 2,
    )


def trade_mixed(links, mixed_all, mixed):
    cols = mixed_all.shape[2]
    copies = []
    for c in range(mixed.shape[0] // ROWS):
        rows = pl.ds(c * ROWS, ROWS)
        copies.append(
            [
                links.copy(
                    mixed_all.at[links.place ^ s, rows],
                    mixed.at[rows, columns(links.place, cols)],
                    links.peer(s),
                )
                for s in (2, 3, 1)
            ]
        )

    def start():
        for chunk in copies:
            for one in chunk:
                one.start()
        mixed[:, columns(links.place, cols)] = mixed_all[links.place]

    def wait(c):
        for one in copies[c]:
            one.wait_recv()

    def finish():
        for chunk in copies:
            for one in chunk:
                one.wait_send()

    return start, wait, finish


def between_body(
    at, mixed_all, base, bout, gain_two, bias_two, bfc, bproj, gain, bias, bq, rest, shard,
    mixed, middle, low_two, hidden, act, stream, low, w_qkv, pieces, kv_back,
    w_out, w_fc, w_proj, part, got, part_two, got_two, ready, send, recv, load, kept
):
    out_at, fc_at, proj_at = at
    links = Links(send, recv)
    loads = [
        pltpu.make_async_copy(source.at[:, pl.ds(start, target.shape[1])], target, load.at[i])
        for i, (source, start, target) in enumerate(
            ((rest, out_at, w_out), (rest, fc_at, w_fc), (rest, proj_at, w_proj))
        )
    ]
    for one in loads:
        one.start()
    links.greet(
        [links.peer(s) for s in range(1, GROUP)]
        + [links.beyond(1, s) for s in range(GROUP)]
        + [links.beyond(links.groups - 1, s) for s in range(GROUP)]
        + [{"tp": links.other}]
        + group_greets(links)
    )
    gathered = ShardGather(links, shard, w_qkv)
    chunks = [pl.ds(c * ROWS, ROWS) for c in range(base.shape[0] // ROWS)]
    start_mixed, wait_mixed, finish_mixed = trade_mixed(links, mixed_all, mixed)
    swaps = [links.swap(part.at[rows], got.at[rows]) for rows in chunks]
    swaps_two = [links.swap(part_two.at[rows], got_two.at[rows]) for rows in chunks]
    start_qkv, finish_qkv = send_qkv(links, low, w_qkv, bq, ready, pieces, kv_back, kept)
    start_mixed()
    gathered.start()
    loads[0].wait()
    for c, rows in enumerate(chunks):
        wait_mixed(c)
        out_rows(rows, mixed, w_out, part)
        swaps[c].start()
    loads[1].wait()
    loads[2].wait()
    for c, rows in enumerate(chunks):
        swaps[c].wait()
        norm_rows(c * ROWS, base, (part, got, bout), gain_two, bias_two, middle, low_two)
        feed_rows(rows, low_two, w_fc, bfc, hidden, act, w_proj, part_two)
        swaps_two[c].start()
        (gathered.pass_core if c else gathered.pass_x)()
    gathered.arrive()
    for c, rows in enumerate(chunks):
        swaps_two[c].wait()
        norm_rows(c * ROWS, middle, (part_two, got_two, bproj), gain, bias, stream, low)
        start_qkv(c)
    finish_mixed()
    gathered.finish()
    finish_qkv()


def between_segment(mixed_all, base, vectors, bq, rest, at, units, shard):
    rows, width = base.shape
    total = bq.shape[1]
    cols = total // GROUP
    out_cols = at[1] - at[0]
    chunks = rows // ROWS
    copies = pltpu.SemaphoreType.DMA((qkv_copies(rows) + chunks * (GROUP - 1) + 2 * chunks + gather_copies(),))
    whole_f32 = (VMEM, shape((rows, width), F32))
    whole_low = (VMEM, shape((rows, width), BF16))
    return run_links(
        functools.partial(between_body, at),
        1,
        [(VMEM, mixed_all), (VMEM, base)]
        + [(VMEM, vector) for vector in vectors]
        + [(VMEM, bq), (ANY, rest), (VMEM, shard)],
        [
            (VMEM, shape((rows, out_cols), BF16)),
            whole_f32,
            whole_low,
            (VMEM, shape((rows, units), F32)),
            (VMEM, shape((rows, units), BF16)),
            whole_f32,
            whole_low,
            (VMEM, shape((width, total), BF16)),
            (ANY, shape((GROUP, rows, cols), BF16)),
            (ANY, shape((GROUP, rows, 2 * cols // 3), BF16)),
        ],
        [
            pltpu.VMEM((width, out_cols), BF16),
            pltpu.VMEM((width, units), BF16),
            pltpu.VMEM((width, units), BF16),
        ]
        + [pltpu.VMEM((rows, width), BF16)] * 4
        + [
            pltpu.VMEM((GROUP, rows, cols), BF16),
            copies,
            copies,
            pltpu.SemaphoreType.DMA((3,)),
            pltpu.SemaphoreType.DMA((chunks,)),
        ],
        flops=2 * rows * width * (total + out_cols + 2 * units),
        moved=rows * width * 20 + rows * units * 6 + width * (total + out_cols + 2 * units) * 2,
    )


def pull_qkv_rows(first, back, links, full, back_got, w, target, sums):
    cols = full.shape[1] // GROUP
    rows = pl.ds(first, ROWS)

    @pl.when(links.group < links.groups - 1)
    def _():
        for s in range(GROUP):
            at = pl.ds(
                pl.multiple_of((links.place ^ s) * cols + cols // 3, cols // 3), 2 * cols // 3
            )
            full[rows, at] = (full[rows, at].astype(F32) + back_got[s, rows].astype(F32)).astype(BF16)

    def tile(at):
        target[rows, at] = dot_last(full[rows, :], w[at, :]).astype(BF16)

    tiles(w.shape[0], 256, tile)

    def body(at):
        sums[...] += eight_rows(full[at, :].astype(F32))

    rows_within(first, body)


def trade_pulls(links, grad_q, grad_kv, grad_kv_back, full, back_got):
    part = grad_q.shape[2]
    copies = []
    for c in range(full.shape[0] // ROWS):
        rows = pl.ds(c * ROWS, ROWS)
        across, back = [], []
        for s in (2, 3, 1):
            for source, start, size in ((grad_kv, part, 2 * part), (grad_q, 0, part)):
                at = pl.ds(pl.multiple_of(links.place * 3 * part + start, part), size)
                across.append(
                    links.copy(source.at[links.place ^ s, rows], full.at[rows, at], links.peer(s))
                )
        for s in (2, 3, 1, 0):
            back.append(
                links.copy(
                    grad_kv_back.at[links.place ^ s, rows],
                    back_got.at[s, rows],
                    links.beyond(links.groups - 1, s),
                )
            )
        copies.append((across, back))

    def start():
        for across, back in copies:
            for one in across:
                one.start()

            @pl.when(links.group > 0)
            def _():
                for one in back:
                    one.start()

        first = pl.multiple_of(links.place * 3 * part, part)
        full[:, pl.ds(first, part)] = grad_q[links.place]
        full[:, pl.ds(pl.multiple_of(first + part, part), 2 * part)] = grad_kv[links.place]

    def wait(c):
        across, back = copies[c]
        for one in across:
            one.wait_recv()

        @pl.when(links.group < links.groups - 1)
        def _():
            for one in back:
                one.wait_recv()

    def finish():
        for across, back in copies:
            for one in across:
                one.wait_send()

            @pl.when(links.group > 0)
            def _():
                for one in back:
                    one.wait_send()

    return start, wait, finish


def pull_copies(rows):
    return rows // ROWS * (2 * (GROUP - 1) + GROUP)


def pull_norm_rows(first, grad, own, got, inputs, gain, grad_new, sums, low=None):
    def body(at):
        value = norm_pull_rows(at, grad, own, got, inputs, gain, grad_new, sums[0], sums[1])
        if low is not None:
            value = value.astype(BF16)
            low[at, :] = value
            sums[2][...] += eight_rows(value.astype(F32))

    rows_within(first, body)


def round_rows(first, grad, low, sums):
    def body(at):
        value = grad[at, :].astype(BF16)
        low[at, :] = value
        sums[...] += eight_rows(value.astype(F32))

    rows_within(first, body)


def pull_feed_rows(rows, low, proj, hidden, held, grad_hidden, sums, fc, target):
    def tile(at):
        value = dot(low[rows, :], proj[:, at]) * gelu_slope(hidden[held, at])
        value = value.astype(BF16)
        grad_hidden[rows, at] = value
        sums[:, at] += eight_rows(value.astype(F32))

    tiles(proj.shape[1], 512, tile)

    def tile_out(at):
        target[rows, at] = dot_last(grad_hidden[rows, :], fc[at, :]).astype(BF16)

    tiles(fc.shape[0], 256, tile_out)


def send_mixed_pull(links, low, w, ready, pieces, kept):
    cols = ready.shape[2]
    copies = []
    for c in range(low.shape[0] // ROWS):
        rows = pl.ds(c * ROWS, ROWS)
        across = {
            s: links.copy(ready.at[s, rows], pieces.at[links.place, rows], links.peer(s))
            for s in range(1, GROUP)
        }
        own = pltpu.make_async_copy(ready.at[0, rows], pieces.at[links.place, rows], kept.at[c])
        copies.append((across, own))

    def start(c):
        rows = pl.ds(c * ROWS, ROWS)
        across, own = copies[c]
        for s in (2, 3, 1, 0):
            at = columns(links.place ^ s, cols)
            ready[s, rows, :] = dot(low[rows, :], w[:, at]).astype(BF16)
            (across[s] if s else own).start()

    def finish():
        for across, own in copies:
            own.wait()
            for one in across.values():
                one.wait()

    return start, finish


def load_columns(plan, load):
    copies = []
    for i, (source, start, target) in enumerate(plan):
        if start is not None:
            source = source.at[:, pl.ds(start, target.shape[1])]
        copies.append(pltpu.make_async_copy(source, target, load.at[i]))
    for one in copies:
        one.start()
    return copies


def turn_body(
    at, mixed_all, base_in, grad_in, bout, gain_two, bias_two, bfc, rest,
    mixed, middle, low_two, act, part_two, low_proj, sum_proj, grad_hidden, sum_fc, grad_new, low_out,
    sum_gain, sum_bias, sum_out, pieces, stay0, go0, stay1, go1,
    w_out, w_fc, w_proj, base, grad, hidden, part, got, part_three, got_three, ready,
    plain, flipped, away0, away1, met0, met1, send, recv, load, kept
):
    out_at, fc_at, proj_at = at
    links = Links(send, recv)
    loads = load_columns(
        (
            (rest, out_at, w_out),
            (base_in, None, base),
            (grad_in, None, grad),
            (rest, fc_at, w_fc),
            (rest, proj_at, w_proj),
        ),
        load,
    )
    links.greet([links.peer(s) for s in range(1, GROUP)] + [{"tp": links.other}])
    chunks = [pl.ds(c * ROWS, ROWS) for c in range(base.shape[0] // ROWS)]
    start_mixed, wait_mixed, finish_mixed = trade_mixed(links, mixed_all, mixed)
    swaps = [links.swap(part.at[rows], got.at[rows]) for rows in chunks]
    swaps_three = [links.swap(part_three.at[rows], got_three.at[rows]) for rows in chunks]
    start_pull, finish_pull = send_mixed_pull(links, low_out, w_out, ready, pieces, kept)
    core_sums = (
        CoreSum(links, stay0, go0, away0, met0),
        CoreSum(links, stay1, go1, away1, met1),
    )
    start_mixed()
    for total in (sum_proj, sum_fc, sum_gain, sum_bias, sum_out):
        total[...] = jnp.zeros_like(total)
    loads[0].wait()
    for c, rows in enumerate(chunks):
        wait_mixed(c)
        out_rows(rows, mixed, w_out, part)
        swaps[c].start()
    for one in loads[1:]:
        one.wait()
    for c in range(len(chunks)):
        round_rows(c * ROWS, grad, low_proj, sum_proj)
    for c, rows in enumerate(chunks):
        swaps[c].wait()
        norm_rows(c * ROWS, base, (part, got, bout), gain_two, bias_two, middle, low_two)

        def tile(at):
            value = dot(low_two[rows, :], w_fc[:, at]) + bfc[:, at]
            hidden[rows, at] = value
            act[rows, at] = gelu_rows(value).astype(BF16)

        tiles(w_fc.shape[1], 512, tile)
        pull_feed_rows(
            rows, low_proj, w_proj, hidden, rows, grad_hidden, sum_fc, w_fc, part_three
        )
        swaps_three[c].start()
    core_sums[0].multiply(low_two, grad_hidden, plain, flipped)
    core_sums[1].multiply(low_proj, act, plain, flipped)
    for rows in chunks:

        def tile_out(at):
            part_two[rows, at] = dot_last(act[rows, :], w_proj[at, :]).astype(BF16)

        tiles(w_proj.shape[0], 256, tile_out)
    for c, rows in enumerate(chunks):
        swaps_three[c].wait()
        pull_norm_rows(
            c * ROWS, grad, part_three, got_three, middle, gain_two, grad_new, (sum_gain, sum_bias, sum_out), low_out
        )
        start_pull(c)
    for one in core_sums:
        one.add()
    finish_mixed()
    finish_pull()


def turn_segment(mixed_all, base, grad, vectors, rest, at, units):
    rows, width = base.shape
    out_cols = at[1] - at[0]
    cols = out_cols // GROUP
    chunks = rows // ROWS
    copies = pltpu.SemaphoreType.DMA((2 * chunks * (GROUP - 1) + 2 * chunks + 2,))
    high = (VMEM, shape((rows, width), F32))
    low = (VMEM, shape((rows, width), BF16))
    sums = (VMEM, shape((8, width), F32))
    return run_links(
        functools.partial(turn_body, at),
        2,
        [(VMEM, mixed_all), (ANY, base), (ANY, grad)]
        + [(VMEM, vector) for vector in vectors]
        + [(ANY, rest)],
        [
            (VMEM, shape((rows, out_cols), BF16)),
            high,
            low,
            (VMEM, shape((rows, units), BF16)),
            low,
            low,
            sums,
            (VMEM, shape((rows, units), BF16)),
            (VMEM, shape((8, units), F32)),
            high,
            low,
            sums,
            sums,
            sums,
            (ANY, shape((GROUP, rows, cols), BF16)),
        ]
        + [(VMEM, shape((width // 4, units), BF16))] * 4,
        [
            pltpu.VMEM((width, out_cols), BF16),
            pltpu.VMEM((width, units), BF16),
            pltpu.VMEM((width, units), BF16),
            pltpu.VMEM((rows, width), F32),
            pltpu.VMEM((rows, width), F32),
            pltpu.VMEM((rows, units), F32),
        ]
        + [pltpu.VMEM((rows, width), BF16)] * 4
        + [
            pltpu.VMEM((GROUP, rows, cols), BF16),
        ]
        + [pltpu.VMEM((width, rows), BF16)] * 2
        + [pltpu.VMEM((width // 2, units), BF16)] * 4
        + [
            copies,
            copies,
            pltpu.SemaphoreType.DMA((5,)),
            pltpu.SemaphoreType.DMA((chunks,)),
        ],
        flops=2 * rows * width * (2 * out_cols + 4 * units),
        moved=rows * width * 22 + rows * units * 4 + width * (out_cols + 2 * units) * 2,
    )


def pull_both_body(
    at, grad_q, grad_kv, grad_kv_back, gain, gain_two, qkv, rest, grad_in, stream_in, hidden_in, middle_in,
    stay0_in, met0_in, stay1_in, go1, low_two_in, act_in,
    full, sum_qkv, sum_gain_one, sum_bias_one, low_proj, sum_proj, grad_hidden, sum_fc, grad_new, low_out,
    sum_gain, sum_bias, sum_out, pieces, total0, total1, near2, *refs
):
    groups = lax.axis_size("fsdp") // GROUP
    far2, (stay3, go3), refs = refs[: groups - 1], refs[groups - 1 : groups + 1], refs[groups + 1 :]
    (w_qkv, w_out, w_fc, w_proj, grad, stream, hidden, back_got, part, got, part_two, got_two, ready,
    stay0, met0, far0, came0, stay1, met1, far1, came1,
    left, wide, plain, flipped, stay2, go2, met2, away, gone2, gone3, send, recv, load, kept) = refs
    out_at, fc_at, proj_at = at
    links = Links(send, recv)
    loads = load_columns(
        (
            (qkv, None, w_qkv),
            (grad_in, None, grad),
            (stream_in, None, stream),
            (rest, proj_at, w_proj),
            (hidden_in.at[pl.ds(0, ROWS)], None, hidden),
            (rest, fc_at, w_fc),
            (rest, out_at, w_out),
            (stay0_in, None, stay0),
            (met0_in, None, met0),
            (stay1_in, None, stay1),
            (low_two_in, None, left),
            (act_in, None, wide),
        ),
        load,
    )
    middle = stream
    load_middle = pltpu.make_async_copy(middle_in, middle, load.at[len(loads)])
    links.greet(
        [links.peer(s) for s in range(1, GROUP)]
        + [links.beyond(1, s) for s in range(GROUP)]
        + [links.beyond(links.groups - 1, s) for s in range(GROUP)]
        + [{"tp": links.other}]
        + group_greets(links)
    )
    chunks = [pl.ds(c * ROWS, ROWS) for c in range(grad.shape[0] // ROWS)]
    start_pulls, wait_pulls, finish_pulls = trade_pulls(
        links, grad_q, grad_kv, grad_kv_back, full, back_got
    )
    swaps = [links.swap(part.at[rows], got.at[rows]) for rows in chunks]
    swaps_two = [links.swap(part_two.at[rows], got_two.at[rows]) for rows in chunks]
    start_pull, finish_pull = send_mixed_pull(links, low_out, w_out, ready, pieces, kept)
    late_x = links.copy(go1, met1, links.peer(2))
    group_sums = (
        GroupSum(links, stay0, met0, far0, came0, total0),
        GroupSum(links, stay1, met1, far1, came1, total1),
    )
    core_sums = (
        CoreSum(links, stay2, go2, away, gone2),
        CoreSum(links, stay3, go3, away, gone3),
    )
    feed_x = links.copy(go2, met2, links.peer(2))
    start_pulls()
    late_x.start()
    for total in (sum_qkv, sum_gain_one, sum_bias_one, sum_proj, sum_fc, sum_gain, sum_bias, sum_out):
        total[...] = jnp.zeros_like(total)
    for one in loads:
        one.wait()
    group_sums[0].add()
    group_sums[0].start()
    for c, rows in enumerate(chunks):
        wait_pulls(c)
        pull_qkv_rows(c * ROWS, None, links, full, back_got, w_qkv, part, sum_qkv)
        swaps[c].start()
    for c, rows in enumerate(chunks):
        swaps[c].wait()
        pull_norm_rows(
            c * ROWS, grad, part, got, stream, gain, grad_new, (sum_gain_one, sum_bias_one)
        )
        if c == len(chunks) - 1:
            load_middle.start()
        round_rows(c * ROWS, grad_new, low_proj, sum_proj)
        if c:
            load_hidden.wait()
        pull_feed_rows(
            rows, low_proj, w_proj, hidden, pl.ds(0, ROWS), grad_hidden, sum_fc, w_fc, part_two
        )
        swaps_two[c].start()
        if c + 1 < len(chunks):
            load_hidden = pltpu.make_async_copy(
                hidden_in.at[pl.ds((c + 1) * ROWS, ROWS)], hidden, load.at[len(loads) + 1 + c]
            )
            load_hidden.start()
    core_sums[0].multiply(left, grad_hidden, plain, flipped)
    load_middle.wait()
    late_x.wait()
    group_sums[1].add()
    group_sums[1].start()
    for c, rows in enumerate(chunks):
        swaps_two[c].wait()
        pull_norm_rows(
            c * ROWS, grad_new, part_two, got_two, middle, gain_two, grad_new, (sum_gain, sum_bias, sum_out), low_out
        )
        start_pull(c)
        if c == 0:
            core_sums[0].add()
            feed_x.start()
            core_sums[1].multiply(low_proj, wide, plain, flipped)
    core_sums[1].add()
    feed_x.wait()
    add_slots(stay2, met2, (near2, *far2))
    finish_pulls()
    finish_pull()
    for one in group_sums:
        one.finish()


def pull_both_segment(pulls, gain, gain_two, qkv, rest, at, units, grad, stream, hidden, middle, sums_in, factors):
    rows, width = grad.shape
    out_cols = at[1] - at[0]
    cols = out_cols // GROUP
    total = 3 * out_cols
    chunks = rows // ROWS
    groups = lax.axis_size("fsdp") // GROUP
    stay = sums_in[0]
    copies = pltpu.SemaphoreType.DMA((pull_copies(rows) + chunks * (GROUP - 1) + 2 * chunks + 2 * groups + 2,))
    high = (VMEM, shape((rows, width), F32))
    low = (VMEM, shape((rows, width), BF16))
    sums = (VMEM, shape((8, width), F32))
    return run_links(
        functools.partial(pull_both_body, at),
        3,
        [(VMEM, pull) for pull in pulls]
        + [(VMEM, gain), (VMEM, gain_two)]
        + [(ANY, array) for array in (qkv, rest, grad, stream, hidden, middle)]
        + [(ANY, array) for array in (*sums_in, *factors)],
        [
            (VMEM, shape((rows, total), BF16)),
            (VMEM, shape((8, total), F32)),
            sums,
            sums,
            low,
            sums,
            (VMEM, shape((rows, units), BF16)),
            (VMEM, shape((8, units), F32)),
            high,
            low,
            sums,
            sums,
            sums,
            (ANY, shape((GROUP, rows, cols), BF16)),
        ]
        + [(VMEM, shape((stay.shape[0] // groups, stay.shape[1]), F32))] * 2
        + [(VMEM, shape((width // 4 // groups, units), F32))]
        + [(VMEM, shape((width // 4 // groups, units), BF16))] * (groups - 1)
        + [(VMEM, shape((width // 4, units), BF16))] * 2,
        [
            pltpu.VMEM((width, total), BF16),
            pltpu.VMEM((width, out_cols), BF16),
            pltpu.VMEM((width, units), BF16),
            pltpu.VMEM((width, units), BF16),
            pltpu.VMEM((rows, width), F32),
            pltpu.VMEM((rows, width), F32),
            pltpu.VMEM((ROWS, units), F32),
            pltpu.VMEM((GROUP, rows, 2 * cols), BF16),
        ]
        + [pltpu.VMEM((rows, width), BF16)] * 4
        + [
            pltpu.VMEM((GROUP, rows, cols), BF16),
        ]
        + ([pltpu.VMEM(stay.shape, BF16)] + group_scratch(stay, groups, True)) * 2
        + [pltpu.VMEM((rows, width), BF16), pltpu.VMEM((rows, units), BF16)]
        + [pltpu.VMEM((width, rows), BF16)] * 2
        + [pltpu.VMEM((width // 4, units), BF16)] * 3
        + [pltpu.VMEM((width // 2, units), BF16)] * 3
        + [
            copies,
            copies,
            pltpu.SemaphoreType.DMA((12 + chunks,)),
            pltpu.SemaphoreType.DMA((chunks,)),
        ],
        flops=2 * rows * width * (total + out_cols + 2 * units),
        moved=rows * width * 22 + rows * units * 6 + width * (total + out_cols + 2 * units) * 2,
    )


def add_slots(stay, met, slots):
    chunk = 16
    depth = slots[0].shape[0]
    for at, slot in enumerate(slots):

        def body(rows):
            from_row = pl.ds(pl.multiple_of(rows.start + at * depth, chunk), chunk)
            total = stay[from_row, :].astype(F32) + met[from_row, :].astype(F32)
            slot[rows, :] = total.astype(slot.dtype)

        each_rows(depth, chunk, body)


def pack_sums(sums, target, first):
    width = target.shape[1]
    at = first
    for one in sums:
        total = jnp.sum(one[...], 0, keepdims=True)
        for start in range(0, total.shape[1], width):
            size = min(width, total.shape[1] - start)
            target[at : at + 1, :size] = total[:, start : start + size]
            at += 1


def finish_body(small, fc1, proj1, out1, proj0, out0, near, *refs):
    *came, gain1, bias1, bqv, bout, gain2, bias2, bfc, bproj, wfc, wproj, wout = refs
    fc0 = near[...]
    for one in came:
        fc0 = fc0 + one[...].astype(F32)
    width = small.shape[1]
    cols = bqv.shape[2] // GROUP
    wfc[0] = fc0
    wfc[1] = fc1[...]
    for l, proj, out in ((0, proj0, out0), (1, proj1, out1)):
        at = l * (small.shape[0] // 2)
        for target, where in ((gain1, 0), (bias1, 1), (bout, 4), (gain2, 5), (bias2, 6), (bproj, 9)):
            target[l : l + 1, :] = small[at + where : at + where + 1, :]
        for i in range(bfc.shape[1] // width):
            bfc[l : l + 1, i * width : (i + 1) * width] = small[at + 7 + i : at + 8 + i, :]
        for place in range(GROUP):
            for i in range(2):
                where = place * 3 * cols + 2 * i * cols
                line, lane = at + 2 + where // width, where % width
                bqv[l, i : i + 1, place * cols : (place + 1) * cols] = small[
                    line : line + 1, lane : lane + cols
                ]
        wproj[l] = proj[...].T
        wout[l] = out[...].T


def finish(small, totals, near, came, out_cols, units):
    depth, width = totals[0].shape[0], small.shape[1]
    vector = shape((LAYERS, width), F32)
    outs = [vector, vector, shape((LAYERS, 2, out_cols), F32), vector, vector, vector]
    outs += [shape((LAYERS, units), F32), vector, shape((LAYERS, depth, units), F32)]
    outs += [shape((LAYERS, units, depth), F32), shape((LAYERS, out_cols, depth), F32)]
    return pl.pallas_call(
        finish_body,
        in_specs=[VMEM] * (2 + len(totals) + len(came)),
        out_specs=[VMEM] * len(outs),
        out_shape=outs,
        compiler_params=pltpu.CompilerParams(vmem_limit_bytes=VMEM_BYTES),
    )(small, *totals, near, *came)


def pull_last_body(
    grad_q, grad_kv, grad_kv_back, gain, qkv, grad_in, stream_in,
    low_one1_in, grad_qkv1_in, low_out1_in, mixed1_in, low_one_in, low_out_in, mixed_in, stay0_in, met0_in,
    gain1, bias1, bqkv1, bout1, gain2_1, bias2_1, bfc1, bproj1, bout0, gain2_0, bias2_0, bfc0, bproj0,
    grad_new, small, total0, total1, total2, total3, total4,
    full, sum_qkv, sum_gain, sum_bias, held, came, far, w_qkv, grad, stream, back_got, part, got,
    left1, wide1, right1, narrow1, left, right, narrow, plain, flipped,
    stay0, met0, far0, came0,
    away1, gone1, stay1, go1, met1, far1, came1,
    away2, gone2, stay2, go2, met2, far2, came2,
    away3, gone3, stay3, go3, met3, far3, came3,
    away4, gone4, stay4, go4, met4, far4, came4,
    send, recv, load
):
    links = Links(send, recv)
    loads = load_columns(
        (
            (low_one1_in, None, left1),
            (grad_qkv1_in, None, wide1),
            (low_out1_in, None, right1),
            (mixed1_in, None, narrow1),
            (stay0_in, None, stay0),
            (met0_in, None, met0),
            (qkv, None, w_qkv),
            (grad_in, None, grad),
            (stream_in, None, stream),
            (low_one_in, None, left),
            (low_out_in, None, right),
            (mixed_in, None, narrow),
        ),
        load,
    )
    links.greet(
        [links.peer(s) for s in range(1, GROUP)]
        + [links.beyond(1, s) for s in range(GROUP)]
        + [links.beyond(links.groups - 1, s) for s in range(GROUP)]
        + [{"tp": links.other}]
        + group_greets(links)
    )
    chunks = [pl.ds(c * ROWS, ROWS) for c in range(grad.shape[0] // ROWS)]
    start_pulls, wait_pulls, finish_pulls = trade_pulls(
        links, grad_q, grad_kv, grad_kv_back, full, back_got
    )
    swaps = [links.swap(part.at[rows], got.at[rows]) for rows in chunks]
    parts = (
        (away1, gone1, stay1, go1, met1, far1, came1, total1),
        (away2, gone2, stay2, go2, met2, far2, came2, total2),
        (away3, gone3, stay3, go3, met3, far3, came3, total3),
        (away4, gone4, stay4, go4, met4, far4, came4, total4),
    )
    core_sums, over_x, group_sums, spans = [], [], [], []
    for at, (away, gone, stay, go, met, *rest) in enumerate(parts):
        core_sums.append(CoreSum(links, stay, go, away, gone))
        size = stay.shape[1]
        step = size if at % 2 else size // 2
        spans.append([])
        for start in range(0, size, step):
            place = pl.ds(start, step)
            spans[at].append(len(over_x))
            over_x.append(links.copy(go.at[:, place], met.at[:, place], links.peer(2)))
            group_sums.append(GroupSum(links, *[ref.at[:, place] for ref in (stay, met, *rest)]))
    early_sum = GroupSum(links, stay0, met0, far0, came0, total0)
    smalls = RowSum(links, held, came, far)
    sums_one = (gain1, bias1, bqkv1, bout1, gain2_1, bias2_1, bfc1, bproj1)
    sums_zero = (sum_gain, sum_bias, sum_qkv, bout0, gain2_0, bias2_0, bfc0, bproj0)
    start_pulls()
    for total in (sum_qkv, sum_gain, sum_bias):
        total[...] = jnp.zeros_like(total)
    for one in loads:
        one.wait()
    early_sum.add()
    early_sum.start()
    core_sums[0].multiply(left1, wide1, plain, flipped)
    core_sums[1].multiply(right1, narrow1, plain, flipped)
    held[0] = jnp.zeros(held.shape[1:], F32)
    pack_sums(sums_one, held.at[0], held.shape[1] // 2)
    core_sums[0].add()
    core_sums[1].add()
    for at in spans[0] + spans[1]:
        over_x[at].start()
    for c, rows in enumerate(chunks):
        wait_pulls(c)
        pull_qkv_rows(c * ROWS, None, links, full, back_got, w_qkv, part, sum_qkv)
        swaps[c].start()
    core_sums[2].multiply(left, full, plain, flipped)
    core_sums[3].multiply(right, narrow, plain, flipped)
    core_sums[2].add()
    for at in spans[2]:
        over_x[at].start()
    core_sums[3].add()
    for at in spans[3]:
        over_x[at].start()
    for c, rows in enumerate(chunks):
        swaps[c].wait()
        pull_norm_rows(c * ROWS, grad, part, got, stream, gain, grad_new, (sum_gain, sum_bias))
    pack_sums(sums_zero, held.at[0], 0)
    smalls.near[0].start()
    smalls.step(0)
    smalls.near[1].start()
    for at, one in enumerate(group_sums):
        over_x[at].wait()
        one.add()
        one.start()
        if at == 3:
            smalls.step(1)
            for far_one in smalls.along:
                far_one.start()
    finish_pulls()
    small[...] = smalls.finish()
    early_sum.finish()
    for one in group_sums:
        one.finish()


def pull_last_segment(pulls, gain, qkv, grad, stream, factors, sums_in, smalls):
    rows, width = grad.shape
    cols = pulls[0].shape[2]
    out_cols = GROUP * cols
    total = 3 * out_cols
    units = sums_in[0].shape[1]
    chunks = rows // ROWS
    groups = lax.axis_size("fsdp") // GROUP
    copies = pltpu.SemaphoreType.DMA(
        (pull_copies(rows) + chunks + 10 + 7 * (groups - 1) + groups + 1,)
    )
    sizes = [total, out_cols, total, out_cols]
    quarter = width // 4
    scratch = []
    for size in sizes:
        stay = shape((quarter, size), BF16)
        scratch += [pltpu.VMEM((2 * quarter, size), BF16)] * 2
        scratch += [pltpu.VMEM(stay.shape, BF16)]
        scratch += [pltpu.VMEM(stay.shape, BF16)] + group_scratch(stay, groups, True)
    low = pltpu.VMEM((rows, width), BF16)
    high = pltpu.VMEM((rows, width), F32)
    mixed = pltpu.VMEM((rows, out_cols), BF16)
    flip = pltpu.VMEM((width, rows), BF16)
    eight = pltpu.VMEM((8, width), F32)
    return run_links(
        pull_last_body,
        4,
        [(VMEM, pull) for pull in pulls]
        + [(VMEM, gain)]
        + [(ANY, array) for array in (qkv, grad, stream, *factors, *sums_in)]
        + [(VMEM, array) for array in smalls],
        [(VMEM, shape((rows, width), F32)), (VMEM, shape((24, width), F32))]
        + [(VMEM, shape((quarter // groups, size), F32)) for size in [units] + sizes],
        [
            pltpu.VMEM((rows, total), BF16),
            pltpu.VMEM((8, total), F32),
            eight,
            eight,
            pltpu.VMEM((3, 24, width), F32),
            pltpu.VMEM((2, 24, width), F32),
            pltpu.VMEM((groups - 1, 24, width), F32),
            pltpu.VMEM((width, total), BF16),
            high,
            high,
            pltpu.VMEM((GROUP, rows, 2 * cols), BF16),
            low,
            low,
            low,
            pltpu.VMEM((rows, total), BF16),
            low,
            mixed,
            low,
            low,
            mixed,
            flip,
            flip,
            pltpu.VMEM((quarter, units), BF16),
        ]
        + group_scratch(shape((quarter, units), BF16), groups, True)
        + scratch
        + [copies, copies, pltpu.SemaphoreType.DMA((12,))],
        flops=2 * rows * width * (3 * total + 2 * out_cols),
        moved=rows * width * 24 + width * total * 2,
    )


def flip_slots(links, source, plain, flipped):
    plain[...] = source[...].T
    depth = plain.shape[0] // (GROUP * links.groups)
    slot = 0
    for s in (0, 2, 1, 3):
        for onward in range(links.groups):
            owner = lax.rem(links.group + onward, links.groups) * GROUP + (links.place ^ s)
            flipped[slot * depth : (slot + 1) * depth, :] = plain[
                pl.ds(pl.multiple_of(owner * depth, depth), depth), :
            ]
            slot += 1


class CoreSum:
    def __init__(self, links, stay, go, away, got):
        self.links, self.stay, self.go, self.away, self.got = links, stay, go, away, got
        self.copy = links.copy(away, got, links.peer(1))
        self.sent = False

    def release(self):
        self.copy.wait_send()
        self.sent = True

    def multiply(self, x, g, plain, flipped):
        flip_slots(self.links, x, plain, flipped)
        quarter = self.stay.shape[0]

        def far(at):
            self.away[:, at] = dot(flipped[2 * quarter :, :], g[:, at]).astype(BF16)

        def near(at):
            self.stay[:, at] = dot(flipped[:quarter, :], g[:, at]).astype(BF16)
            self.go[:, at] = dot(flipped[quarter : 2 * quarter, :], g[:, at]).astype(BF16)

        tiles(g.shape[1], 512, far)
        self.copy.start()
        tiles(g.shape[1], 512, near)

    def add(self):
        if not self.sent:
            self.release()
        self.copy.wait_recv()
        quarter = self.stay.shape[0]
        chunk = 16
        for target, first in ((self.go, quarter), (self.stay, 0)):

            def body(at):
                from_row = pl.ds(pl.multiple_of(at.start + first, chunk), chunk)
                total = target[at, :].astype(F32) + self.got[from_row, :].astype(F32)
                target[at, :] = total.astype(BF16)

            each_rows(quarter, chunk, body)


class GroupSum:
    def __init__(self, links, stay, met, far, came, result):
        self.stay, self.met, self.far, self.came, self.result = stay, met, far, came, result
        self.depth = result.shape[0]
        self.copies = []
        for onward in range(1, links.groups):
            rows = pl.ds((onward - 1) * self.depth, self.depth)
            self.copies.append(links.copy(far.at[rows], came.at[rows], links.beyond(onward, 0)))

    def add(self):
        chunk = 16

        def near(at):
            self.result[at, :] = self.stay[at, :].astype(F32) + self.met[at, :].astype(F32)

        each_rows(self.depth, chunk, near)

        def far(at):
            from_row = pl.ds(pl.multiple_of(at.start + self.depth, chunk), chunk)
            total = self.stay[from_row, :].astype(F32) + self.met[from_row, :].astype(F32)
            self.far[at, :] = total.astype(BF16)

        each_rows(self.far.shape[0], chunk, far)

    def start(self):
        for one in self.copies:
            one.start()

    def finish(self):
        for one in self.copies:
            one.wait()
        chunk = 16

        def body(at):
            total = self.result[at, :]
            for onward in range(len(self.copies)):
                from_row = pl.ds(pl.multiple_of(at.start + onward * self.depth, chunk), chunk)
                total = total + self.came[from_row, :].astype(F32)
            self.result[at, :] = total

        each_rows(self.depth, chunk, body)


def group_scratch(stay, groups, met):
    rows, size = stay.shape
    far = pltpu.VMEM((rows - rows // groups, size), BF16)
    return ([pltpu.VMEM((rows, size), BF16)] if met else []) + [far, far]


def group_greets(links):
    return [links.beyond(onward, 0) for onward in range(2, links.groups - 1)]


def doc_start_rows(sc, docs, positions):
    start = jnp.zeros_like(positions)
    for d in range(docs):
        first = sc[2 + d]
        start = jnp.where(first <= positions, jnp.maximum(start, first), start)
    return start


def doc_start_one(sc, docs, position):
    start = jnp.int32(0)
    for d in range(docs):
        first = sc[2 + d]
        start = jnp.where(first <= position, jnp.maximum(start, first), start)
    return start


def query_rows(sc, docs, block, size):
    first = sc[1] + block * size
    position = first + lax.broadcasted_iota(jnp.int32, (1, size), 1)
    start = doc_start_rows(sc, docs, position)
    return (
        jnp.concatenate([position, position], 1),
        jnp.concatenate([start, start], 1),
        doc_start_one(sc, docs, first),
    )


def head_stack(rows, scale):
    value = rows.astype(F32)
    if scale != 1.0:
        value = value * scale
    lane = lax.broadcasted_iota(jnp.int32, value.shape, 1)
    return jnp.concatenate(
        [jnp.where(lane < HEAD_DIM, value, 0.0), jnp.where(lane >= HEAD_DIM, value, 0.0)], 0
    ).astype(BF16)


def block_at(block, size):
    return pl.ds(pl.multiple_of(block * size, size), size)


def masked_scores(keys, queries, first_key, position, start):
    scores = dot_last(keys, queries)
    key_at = first_key + lax.broadcasted_iota(jnp.int32, (keys.shape[0], 1), 0)
    return jnp.where((key_at >= start) & (key_at <= position), scores, NEG)


def flash_step(keys, values_ref, queries, at, first_key, position, start, acc, carry):
    top, total = carry
    scores = masked_scores(keys, queries, first_key, position, start)
    top_new = jnp.maximum(top, jnp.max(scores, 0, keepdims=True))
    expo = jnp.exp(scores - top_new)
    shrink = jnp.exp(top - top_new)
    total = total * shrink + jnp.sum(expo, 0, keepdims=True)
    expo = expo.astype(BF16)
    for h in range(2):
        lanes = slice(h * QB, (h + 1) * QB)
        rows = slice(h * HEAD_DIM, (h + 1) * HEAD_DIM)
        acc[rows, :] = acc[rows, :] * shrink[:, lanes] + dot(values_ref[rows, at], expo[:, lanes])
    return top_new, total


def attend_body(docs, sc, qkv, kv, mixed, out, log_total, v_flip, v_back, acc):
    block = pl.program_id(0)
    span, cols = out.shape[0] * pl.num_programs(0), out.shape[1]
    rows = qkv.shape[0]

    @pl.when(block == 0)
    def _():
        for first in range(0, rows, QB):
            v_flip[:, first : first + QB] = qkv[first : first + QB, 2 * cols :].T
            v_back[:, first : first + QB] = kv[first : first + QB, cols:].T

    position, start, lowest = query_rows(sc, docs, block, QB)
    queries = head_stack(qkv[block_at(block, QB), :cols], HEAD_DIM**-0.5)
    acc[...] = jnp.zeros_like(acc)
    least = jnp.maximum(lowest - sc[1], 0) // KB
    last = ((block + 1) * QB - 1) // KB
    before = sc[1] - span

    def step(back, carry):
        at = block_at(last - back, KB)
        keys = qkv[at, cols : 2 * cols]
        first_key = sc[1] + (last - back) * KB
        return flash_step(keys, v_flip, queries, at, first_key, position, start, acc, carry)

    def step_back(where, carry):
        at = block_at(where, KB)
        return flash_step(
            kv[at, :cols], v_back, queries, at, before + where * KB, position, start, acc, carry
        )

    carry = (jnp.full((1, 2 * QB), NEG, F32), jnp.zeros((1, 2 * QB), F32))
    carry = lax.fori_loop(0, last - least + 1, step, carry)
    top, total = lax.fori_loop(
        jnp.minimum(jnp.maximum(lowest - before, 0), span) // KB, span // KB, step_back, carry
    )
    sums = top + jnp.log(total)
    share = 1.0 / total
    parts = []
    for h in range(2):
        lanes = slice(h * QB, (h + 1) * QB)
        log_total[h : h + 1, :] = sums[:, lanes]
        parts.append(acc[h * HEAD_DIM : (h + 1) * HEAD_DIM, :] * share[:, lanes])
    value = jnp.concatenate(parts, 0).T
    out[...] = value
    mixed[...] = value.astype(BF16)


def attend(sc, docs, pieces, kv):
    rows, cols = pieces.shape[1], pieces.shape[2] // 3
    span = GROUP * rows
    low_flip = pltpu.VMEM((cols, span), BF16)
    block = pl.BlockSpec((QB, cols), lambda j, sc: (j, 0))
    mixed, out, log_total = run_kernel(
        functools.partial(attend_body, docs),
        (span // QB,),
        sc,
        [
            (whole((span, 3 * cols)), pieces.reshape(span, 3 * cols)),
            (whole((span, 2 * cols)), kv.reshape(span, 2 * cols)),
        ],
        [
            (block, shape((span, cols), BF16)),
            (block, shape((span, cols), F32)),
            (pl.BlockSpec((8, QB), lambda j, sc: (0, j)), shape((8, span), F32)),
        ],
        scratch=[low_flip, low_flip, pltpu.VMEM((cols, QB), F32)],
        flops=span * span * cols * 4,
        moved=span * cols * 20,
    )
    return mixed.reshape(GROUP, rows, cols), out, log_total


def pull_step(keys, values, at, first_key, position, start, queries, grads, log_rows, delta, refs):
    k_flip, grad_k, grad_v, grad_q = refs
    scores = masked_scores(keys, queries, first_key, position, start)
    probs = jnp.exp(scores - log_rows)
    grad_probs = dot_last(values, grads)
    grad_scores = (probs * (grad_probs - delta)).astype(BF16)
    grad_v[at, :] += dot(probs.astype(BF16), grads)
    grad_k[at, :] += dot(grad_scores, queries)
    size = grad_q.shape[1]
    for h in range(2):
        rows = slice(h * HEAD_DIM, (h + 1) * HEAD_DIM)
        grad_q[rows, :] += dot(k_flip[rows, at], grad_scores[:, h * size : (h + 1) * size])


def pull_body(
    docs, sc, qkv, grad_mixed, kv, out, log_total, grad_q_out, grad_kv, grad_kv_back,
    k_flip, grad_k, grad_v, k_back_flip, grad_k_back, grad_v_back, grad_q
):
    block = pl.program_id(0)
    span, cols = qkv.shape[0], out.shape[1]
    size = out.shape[0]
    before = sc[1] - span

    @pl.when(block == 0)
    def _():
        for first in range(0, span, PULL_KB):
            k_flip[:, first : first + PULL_KB] = qkv[first : first + PULL_KB, cols : 2 * cols].T
            k_back_flip[:, first : first + PULL_KB] = kv[first : first + PULL_KB, :cols].T
        for total in (grad_k, grad_v, grad_k_back, grad_v_back):
            total[...] = jnp.zeros_like(total)

    grad_q[...] = jnp.zeros_like(grad_q)
    position, start, lowest = query_rows(sc, docs, block, size)
    queries = head_stack(qkv[block_at(block, size), :cols], HEAD_DIM**-0.5)
    grad_rows = grad_mixed[block_at(block, size), :]
    grads = head_stack(grad_rows, 1.0)
    flipped = (grad_rows.astype(F32) * out[...]).T
    heads = [slice(h * HEAD_DIM, (h + 1) * HEAD_DIM) for h in range(2)]
    delta = jnp.concatenate([jnp.sum(flipped[rows, :], 0, keepdims=True) for rows in heads], 1)
    log_rows = jnp.concatenate([log_total[h : h + 1, :] for h in range(2)], 1)

    def step(where, carry):
        at = block_at(where, PULL_KB)
        pull_step(
            qkv[at, cols : 2 * cols], qkv[at, 2 * cols :], at, sc[1] + where * PULL_KB,
            position, start, queries, grads, log_rows, delta, (k_flip, grad_k, grad_v, grad_q),
        )
        return carry

    def step_back(where, carry):
        at = block_at(where, PULL_KB)
        pull_step(
            kv[at, :cols], kv[at, cols:], at, before + where * PULL_KB,
            position, start, queries, grads, log_rows, delta, (k_back_flip, grad_k_back, grad_v_back, grad_q),
        )
        return carry

    last = ((block + 1) * size - 1) // PULL_KB
    lax.fori_loop(jnp.maximum(lowest - sc[1], 0) // PULL_KB, last + 1, step, 0)
    lax.fori_loop(
        jnp.minimum(jnp.maximum(lowest - before, 0), span) // PULL_KB, span // PULL_KB, step_back, 0
    )
    grad_q_out[...] = (grad_q[...] * HEAD_DIM**-0.5).T.astype(BF16)

    @pl.when(block == pl.num_programs(0) - 1)
    def _():
        grad_kv[:, :cols] = grad_k[...].astype(BF16)
        grad_kv[:, cols:] = grad_v[...].astype(BF16)
        grad_kv_back[:, :cols] = grad_k_back[...].astype(BF16)
        grad_kv_back[:, cols:] = grad_v_back[...].astype(BF16)


def attend_pull(sc, docs, pieces, grads, kv, out, log_total):
    rows, cols = pieces.shape[1], pieces.shape[2] // 3
    span = GROUP * rows
    block = pl.BlockSpec((PULL_QB, cols), lambda j, sc: (j, 0))
    both = (whole((span, 2 * cols)), shape((span, 2 * cols), BF16))
    low_flip = pltpu.VMEM((cols, span), BF16)
    high = pltpu.VMEM((span, cols), F32)
    parts = run_kernel(
        functools.partial(pull_body, docs),
        (span // PULL_QB,),
        sc,
        [
            (whole((span, 3 * cols)), pieces.reshape(span, 3 * cols)),
            (whole((span, cols)), grads.reshape(span, cols)),
            (whole((span, 2 * cols)), kv.reshape(span, 2 * cols)),
            (block, out),
            (pl.BlockSpec((8, PULL_QB), lambda j, sc: (0, j)), log_total),
        ],
        [(block, shape((span, cols), BF16)), both, both],
        scratch=[low_flip, high, high, low_flip, high, high, pltpu.VMEM((cols, PULL_QB), F32)],
        flops=span * span * cols * 9,
        moved=span * cols * 30,
    )
    return [part.reshape(GROUP, rows, part.shape[1]) for part in parts]


def swap_tp(value):
    return lax.ppermute(value, "tp", [(0, 1), (1, 0)])


def swap_fsdp(value, s):
    return lax.ppermute(value, "fsdp", [(i, i ^ s) for i in range(lax.axis_size("fsdp"))])


def shift_fsdp(value, by):
    size = lax.axis_size("fsdp")
    return lax.ppermute(value, "fsdp", [(i, i + by) for i in range(size) if 0 <= i + by < size])


def gather(shard):
    return lax.all_gather(shard, "fsdp", axis=0, tiled=True)


def tie(*values):
    return lax.optimization_barrier(values)


def shards(
    tokens,
    cotangent,
    segments,
    doc_batch,
    ln1_gain,
    ln1_bias,
    w_qkv,
    b_qv,
    w_out,
    b_out,
    ln2_gain,
    ln2_bias,
    w_fc,
    b_fc,
    w_proj,
    b_proj,
):
    rows, width = tokens.shape
    depth = w_qkv.shape[1]
    out_cols = w_out.shape[1]
    units = w_fc.shape[2]
    cols = out_cols // GROUP
    docs = doc_batch.shape[0]
    me = lax.axis_index("fsdp")
    total_rows = rows * lax.axis_size("fsdp")

    def pack_qkv(l):
        return w_qkv[l].reshape(depth, 3, GROUP, cols).transpose(0, 2, 1, 3).reshape(depth, 3 * out_cols)

    def pack_rest(l):
        return [w_out[l].T, w_fc[l], w_proj[l].T]

    rest = gather(jnp.concatenate(pack_rest(0) + pack_rest(1), 1))

    def rest_at(l):
        first = l * (out_cols + 2 * units)
        return (first, first + out_cols, first + out_cols + units)

    def bias_qkv(l):
        three = jnp.stack([b_qv[l, 0], jnp.zeros_like(b_qv[l, 0]), b_qv[l, 1]])
        return three.reshape(3, GROUP, cols).transpose(1, 0, 2).reshape(1, 3 * out_cols)

    def row(vector):
        return vector.reshape(1, vector.shape[0])

    stored = []
    stream, low_one, full_qkv, doc_tokens, doc_first, pieces, kv_back = first_segment(
        tokens,
        row(ln1_gain[0]),
        row(ln1_bias[0]),
        pack_qkv(0),
        bias_qkv(0),
        segments.reshape(rows // 128, 128),
        docs,
    )
    qkv_of = [full_qkv]
    doc_tokens, doc_first = (value[:, 0].astype(jnp.int32) for value in (doc_tokens, doc_first))
    sc = jnp.concatenate(
        [jnp.stack([me % GROUP, (me // GROUP) * (GROUP * rows)]).astype(jnp.int32), doc_first]
    )
    doc_ids = jnp.arange(docs, dtype=jnp.int32)
    is_doc = segments[:, None] == doc_ids[None, :]
    in_batch = doc_batch[:, None] == jnp.arange(MB, dtype=jnp.int32)[None, :]
    counts = jnp.sum(jnp.where(in_batch, doc_tokens[:, None], 0), 0)
    doc_count = jnp.sum(jnp.where(in_batch, counts[None, :], 0), 1)
    row_count = jnp.sum(jnp.where(is_doc, doc_count[None, :], 0), 1).astype(F32)
    row_weight = total_rows / (MB * row_count)
    for l in range(LAYERS - 1):
        mixed, out, log_total = attend(sc, docs, pieces, kv_back)
        vectors = (b_out[l], ln2_gain[l], ln2_bias[l], b_fc[l], b_proj[l], ln1_gain[l + 1], ln1_bias[l + 1])
        mixed_full, middle, low_two, hidden, act, *later = between_segment(
            mixed,
            stream,
            [row(vector) for vector in vectors],
            bias_qkv(l + 1),
            rest,
            rest_at(l),
            units,
            pack_qkv(l + 1),
        )
        stored.append(
            (stream, low_one, pieces, kv_back, out, log_total, mixed_full, middle, low_two, hidden, act)
        )
        stream, low_one, full_qkv, pieces, kv_back = later
        qkv_of.append(full_qkv)

    l = LAYERS - 1
    mixed, out, log_total = attend(sc, docs, pieces, kv_back)
    grad = cotangent.astype(F32) * row_weight[:, None]
    (
        mixed_full,
        middle,
        low_two,
        act,
        part_two,
        low_proj,
        sum_bproj,
        grad_hidden,
        sum_bfc,
        grad,
        low_out,
        sum_gain_two,
        sum_bias_two,
        sum_bout,
        grad_mixed,
        *feed_parts,
    ) = turn_segment(
        mixed,
        stream,
        grad,
        [row(vector) for vector in (b_out[l], ln2_gain[l], ln2_bias[l], b_fc[l])],
        rest,
        rest_at(l),
        units,
    )
    other_two = swap_tp(part_two)
    outputs = (middle + (part_two.astype(F32) + other_two.astype(F32)) + b_proj[l][None]).astype(BF16)

    stay0, go0, stay1, go1 = feed_parts
    met0 = swap_fsdp(go0, 2)
    grad_mixed, stay0 = tie(grad_mixed, stay0)
    pulls = attend_pull(sc, docs, pieces, grad_mixed, kv_back, out, log_total)
    *pulls, met0 = tie(*pulls, met0)
    sums_one = [sum_bout, sum_gain_two, sum_bias_two, sum_bfc, sum_bproj]
    low_one_kept, low_out_kept, mixed_kept = low_one, low_out, mixed_full
    (stream_below, low_one, pieces, kv_back, out, log_total, mixed_full, middle, low_two, hidden, act) = stored[0]
    (
        grad_qkv,
        sum_bqkv,
        sum_gain_one,
        sum_bias_one,
        low_proj,
        sum_bproj,
        grad_hidden,
        sum_bfc,
        grad,
        low_out,
        sum_gain_two,
        sum_bias_two,
        sum_bout,
        grad_mixed,
        *later,
    ) = pull_both_segment(
        pulls,
        row(ln1_gain[1]),
        row(ln2_gain[0]),
        qkv_of[1],
        rest,
        rest_at(0),
        units,
        grad,
        stream,
        hidden,
        middle,
        [stay0, met0, stay1, go1],
        [low_two, act],
    )
    feed_totals, near, far, (stay0, go0) = later[:2], later[2], later[3:-2], later[-2:]
    came = []
    for onward, value in enumerate(far, 1):
        size = lax.axis_size("fsdp")
        pairs = [(i, (i + GROUP * onward) % size) for i in range(size)]
        came.append(lax.ppermute(value, "fsdp", pairs))
    met0 = swap_fsdp(go0, 2)
    sums_one = [sum_gain_one, sum_bias_one, sum_bqkv] + sums_one
    pulls = attend_pull(sc, docs, pieces, grad_mixed, kv_back, out, log_total)
    *pulls, came, met0 = tie(*pulls, came, met0)
    sums_zero = [sum_bout, sum_gain_two, sum_bias_two, sum_bfc, sum_bproj]
    grad, small, proj0, qkv1, out1, qkv0, out0 = pull_last_segment(
        pulls,
        row(ln1_gain[0]),
        qkv_of[0],
        grad,
        stream_below,
        [low_one_kept, grad_qkv, low_out_kept, mixed_kept, low_one, low_out, mixed_full],
        [stay0, met0],
        sums_one + sums_zero,
    )
    gain1, bias1, bqv, bout, gain2, bias2, bfc, bproj, grad_wfc, grad_wproj, grad_wout = finish(
        small, [*feed_totals, out1, proj0, out0], near, came, out_cols, units
    )
    grad_wqkv = jnp.stack(
        [
            value.reshape(depth, GROUP, 3, cols).transpose(0, 2, 1, 3).reshape(depth, 3, out_cols)
            for value in (qkv0, qkv1)
        ]
    )

    return (
        outputs,
        grad,
        gain1,
        bias1,
        grad_wqkv,
        bqv,
        grad_wout,
        bout,
        gain2,
        bias2,
        grad_wfc,
        bfc,
        grad_wproj,
        bproj,
    )


def solution(mesh):
    placed = (
        P("fsdp", None),
        P("fsdp", None),
        P("fsdp"),
        P(),
        P(),
        P(),
        P(None, "fsdp", None, "tp"),
        P(None, None, "tp"),
        P(None, "tp", "fsdp"),
        P(),
        P(),
        P(),
        P(None, "fsdp", "tp"),
        P(None, "tp"),
        P(None, "tp", "fsdp"),
        P(),
    )
    return jax.shard_map(
        shards,
        mesh=mesh,
        in_specs=placed,
        out_specs=(
            P("fsdp", None),
            P("fsdp", None),
            P(),
            P(),
            P(None, "fsdp", None, "tp"),
            P(None, None, "tp"),
            P(None, "tp", "fsdp"),
            P(),
            P(),
            P(),
            P(None, "fsdp", "tp"),
            P(None, "tp"),
            P(None, "tp", "fsdp"),
            P(),
        ),
        check_vma=False,
    )
```

```python
import functools

import jax
import jax.numpy as jnp
from jax import lax
from jax.experimental import pallas as pl
from jax.experimental.pallas import tpu as pltpu
from jax.sharding import PartitionSpec as P

HEAD_DIM = 64
LAYERS = 2
MB = 3
REACH = 4

EPS = 1e-05
GROUP = REACH
QB = 512
PULL_QB = 256
LN_ROWS = 128
ACT_ROWS = 128
KB = 512
PULL_KB = 256
NEG = -1e30
F32 = jnp.float32
BF16 = jnp.bfloat16
VMEM_BYTES = 62 * 1024 * 1024
LAST = (((1,), (1,)), ((), ()))
FIRST = (((0,), (0,)), ((), ()))


def dot(left, right):
    return jnp.dot(left, right, preferred_element_type=F32)


def dot_last(left, right):
    return lax.dot_general(left, right, LAST, preferred_element_type=F32)


def shape(dims, dtype):
    return jax.ShapeDtypeStruct(dims, dtype)


def whole(dims):
    return pl.BlockSpec(dims, lambda *_: (0,) * len(dims))


def run_kernel(body, grid, scalars, ins, outs, scratch=(), flops=0, moved=0):
    return pl.pallas_call(
        body,
        grid_spec=pltpu.PrefetchScalarGridSpec(
            num_scalar_prefetch=1,
            grid=grid,
            in_specs=[spec for spec, _ in ins],
            out_specs=[spec for spec, _ in outs],
            scratch_shapes=list(scratch),
        ),
        out_shape=[out for _, out in outs],
        compiler_params=pltpu.CompilerParams(
            vmem_limit_bytes=VMEM_BYTES, dimension_semantics=("arbitrary",) * len(grid)
        ),
        cost_estimate=pl.CostEstimate(flops=flops, bytes_accessed=moved, transcendentals=0),
    )(scalars, *[array for _, array in ins])


def each_rows(count, chunk, body):
    def step(at, carry):
        body(pl.ds(pl.multiple_of(at * chunk, chunk), chunk))
        return carry

    lax.fori_loop(0, count // chunk, step, 0)


def norm_parts(rows):
    centred = rows - jnp.mean(rows, -1, keepdims=True)
    inv_scale = lax.rsqrt(jnp.mean(centred * centred, -1, keepdims=True) + EPS)
    return centred * inv_scale, inv_scale


def norm_pull(grad_rows, unit_rows, inv_scale, gain):
    scaled = grad_rows * gain
    return inv_scale * (
        scaled
        - jnp.mean(scaled, -1, keepdims=True)
        - unit_rows * jnp.mean(scaled * unit_rows, -1, keepdims=True)
    )


def eight_rows(rows):
    return jnp.sum(rows.reshape(rows.shape[0] // 8, 8, rows.shape[1]), 0)


def gelu_rows(value):
    return 0.5 * value * (1.0 + jnp.tanh(0.7978845608028654 * (value + 0.044715 * value * value * value)))


def gelu_slope(value):
    square = value * value
    top = jnp.tanh(0.7978845608028654 * (value + 0.044715 * square * value))
    inner = 0.7978845608028654 * (1.0 + 3.0 * 0.044715 * square)
    return 0.5 * (1.0 + top) + 0.5 * value * (1.0 - top * top) * inner


def norm_pull_rows(at, grad, own, got, inputs, gain, grad_new, sum_gain, sum_bias):
    grad_rows = own[at, :].astype(F32) + got[at, :].astype(F32)
    unit, inv_scale = norm_parts(inputs[at, :])
    value = grad[at, :] + norm_pull(grad_rows, unit, inv_scale, gain[...])
    grad_new[at, :] = value
    sum_gain[...] += eight_rows(grad_rows * unit)
    sum_bias[...] += eight_rows(grad_rows)
    return value


CHUNK = [256]
SIZES = (256, 128, 256, 128, 256)
MESH = pl.DeviceIdType.MESH


class Links:
    def __init__(self, send, recv):
        self.send, self.recv, self.used = send, recv, 0
        self.me = lax.axis_index("fsdp")
        self.place = lax.rem(self.me, GROUP)
        self.group = self.me // GROUP
        self.groups = lax.axis_size("fsdp") // GROUP
        self.other = 1 - lax.axis_index("tp")

    def peer(self, s):
        return {"fsdp": self.group * GROUP + (self.place ^ s)}

    def beyond(self, by, s):
        return {"fsdp": lax.rem(self.group + by, self.groups) * GROUP + (self.place ^ s)}

    def copy(self, source, target, device):
        at = self.used
        self.used += 1
        return pltpu.make_async_remote_copy(
            src_ref=source,
            dst_ref=target,
            send_sem=self.send.at[at],
            recv_sem=self.recv.at[at],
            device_id=device,
            device_id_type=MESH,
        )

    def swap(self, source, target):
        return self.copy(source, target, {"tp": self.other})

    def greet(self, devices):
        barrier = pltpu.get_barrier_semaphore()
        for device in devices:
            pl.semaphore_signal(barrier, inc=1, device_id=device, device_id_type=MESH)
        pl.semaphore_wait(barrier, len(devices))


def columns(place, cols):
    return pl.ds(pl.multiple_of(place * cols, cols), cols)


def tiles(count, size, body):
    def step(at, carry):
        body(pl.ds(pl.multiple_of(at * size, size), size))
        return carry

    lax.fori_loop(0, count // size, step, 0)


def rows_within(first, body):
    def step(at, carry):
        body(pl.ds(pl.multiple_of(first + at * LN_ROWS, LN_ROWS), LN_ROWS))
        return carry

    lax.fori_loop(0, CHUNK[0] // LN_ROWS, step, 0)


def out_rows(rows, mixed, w, target):
    def tile(at):
        target[rows, at] = dot_last(mixed[rows, :], w[at, :]).astype(BF16)

    tiles(w.shape[0], 256, tile)


def norm_rows(first, base, sums, gain, bias, stream, low):
    def body(at):
        value = base[at, :].astype(F32)
        if sums is not None:
            own, got, badd = sums
            value = value + (own[at, :].astype(F32) + got[at, :].astype(F32)) + badd[...]
        stream[at, :] = value
        unit, _ = norm_parts(value)
        low[at, :] = (unit * gain[...] + bias[...]).astype(BF16)

    rows_within(first, body)


def feed_rows(rows, low, fc, bfc, hidden, act, proj, target):
    def tile(at):
        value = dot(low[rows, :], fc[:, at]) + bfc[:, at]
        hidden[rows, at] = value
        act[rows, at] = gelu_rows(value).astype(BF16)

    tiles(fc.shape[1], 512, tile)

    def tile_out(at):
        target[rows, at] = dot_last(act[rows, :], proj[at, :]).astype(BF16)

    tiles(proj.shape[0], 256, tile_out)


def send_qkv(links, low, w, bq, ready, pieces, kv_back, kept):
    cols = bq.shape[1] // GROUP
    copies = []
    order = (2, 3, 1, 0)
    chunks = low.shape[0] // CHUNK[0]
    for c in range(chunks):
        rows = pl.ds(c * CHUNK[0], CHUNK[0])
        across = {
            s: links.copy(ready.at[s, rows], pieces.at[links.place, rows], links.peer(s)) for s in order if s
        }
        onward = {
            s: links.copy(
                ready.at[s, rows, pl.ds(cols // 3, 2 * cols // 3)],
                kv_back.at[links.place, rows],
                links.beyond(1, s),
            )
            for s in order
        }
        own = pltpu.make_async_copy(ready.at[0, rows], pieces.at[links.place, rows], kept.at[c])
        copies.append((across, onward, own))
    last = links.group == links.groups - 1

    def start(c):
        rows = pl.ds(c * CHUNK[0], CHUNK[0])
        across, onward, own = copies[c]
        for s in order:
            at = columns(links.place ^ s, cols)
            ready[s, rows, :] = (dot(low[rows, :], w[:, at]) + bq[:, at]).astype(BF16)
            if s:
                across[s].start()
            else:
                own.start()

            @pl.when(jnp.logical_not(last))
            def _():
                onward[s].start()

    def finish():
        for across, onward, own in copies:
            own.wait()
            for s in order:
                if s:
                    across[s].wait()

                @pl.when(jnp.logical_not(last))
                def _():
                    onward[s].wait_send()

                @pl.when(links.group > 0)
                def _():
                    onward[s].wait_recv()

    return start, finish


def qkv_copies(rows):
    return rows // CHUNK[0] * (2 * GROUP - 1)


class ShardGather:
    def __init__(self, links, shard, full):
        self.depth = shard.shape[0]
        self.links, self.shard, self.full = links, shard, full
        groups = range(links.groups)
        self.along = [
            links.copy(shard, full.at[self.rows(0, 0)], links.beyond(onward, 0)) for onward in groups[1:]
        ]
        self.over_x = [self.relay(onward, 0, links.peer(2)) for onward in groups]
        self.over_core = [
            [self.relay(onward, s, links.peer(1)) for onward in groups] for s in (0, 2)
        ]

    def rows(self, back, s):
        links = self.links
        group = lax.rem(links.group + links.groups - back, links.groups)
        owner = group * GROUP + (links.place ^ s)
        return pl.ds(pl.multiple_of(owner * self.depth, self.depth), self.depth)

    def relay(self, back, s, device):
        rows = self.rows(back, s)
        own = back == 0 and s == 0
        return self.links.copy(self.shard if own else self.full.at[rows], self.full.at[rows], device)

    def start(self):
        for one in self.along:
            one.start()
        self.over_x[0].start()
        self.over_core[0][0].start()
        self.full[self.rows(0, 0), :] = self.shard[...]

    def pass_x(self):
        for onward, one in enumerate(self.along, 1):
            one.wait_recv()
            self.over_x[onward].start()
            self.over_core[0][onward].start()

    def pass_core(self):
        for one, last in zip(self.over_x, self.over_core[1]):
            one.wait_recv()
            last.start()

    def arrive(self):
        for one in self.over_core[0] + self.over_core[1]:
            one.wait_recv()

    def finish(self):
        for one in self.along + self.over_x + self.over_core[0] + self.over_core[1]:
            one.wait_send()


def gather_copies():
    groups = lax.axis_size("fsdp") // GROUP
    return 4 * groups - 1


class RowSum:
    def __init__(self, links, held, came, far):
        self.held, self.came, self.far = held, came, far
        self.near = [links.copy(held.at[i], came.at[i], links.peer(i + 1)) for i in range(2)]
        self.along = [
            links.copy(held.at[2], far.at[onward - 1], links.beyond(onward, 0))
            for onward in range(1, links.groups)
        ]

    def step(self, i):
        self.near[i].wait()
        self.held[i + 1] = self.held[i] + self.came[i]

    def finish(self):
        total = self.held[2]
        for at, one in enumerate(self.along):
            one.wait()
            total = total + self.far[at]
        return total


def count_docs(segments, counts):
    for d in range(counts.shape[0]):
        found = jnp.where(segments[...] == d, 1.0, 0.0).astype(F32)
        total = jnp.sum(jnp.sum(found, 0, keepdims=True), 1, keepdims=True)
        counts[d : d + 1, :] = jnp.broadcast_to(total, (1, counts.shape[1]))


def first_body(
    base, gain, bias, shard, bq, segments, stream, low, w, tokens, first, pieces, kv_back,
    ready, held, came, far, send, recv, kept
):
    links = Links(send, recv)
    gathered = ShardGather(links, shard, w)
    counted = RowSum(links, held, came, far)
    start, finish = send_qkv(links, low, w, bq, ready, pieces, kv_back, kept)
    count_docs(segments, held.at[0])
    links.greet(
        [links.peer(s) for s in range(1, GROUP)]
        + [links.beyond(1, s) for s in range(GROUP)]
        + [links.beyond(links.groups - 1, s) for s in range(GROUP)]
        + group_greets(links)
    )
    gathered.start()
    counted.near[0].start()
    chunks = base.shape[0] // CHUNK[0]
    for c in range(chunks):
        norm_rows(c * CHUNK[0], base, None, gain, bias, stream, low)
    counted.step(0)
    counted.near[1].start()
    gathered.pass_x()
    counted.step(1)
    for one in counted.along:
        one.start()
    gathered.pass_core()
    gathered.arrive()
    for c in range(chunks):
        start(c)
    total = counted.finish()
    tokens[...] = total
    begin = jnp.zeros((1, total.shape[1]), F32)
    for d in range(total.shape[0]):
        first[d : d + 1, :] = begin
        begin = begin + total[d : d + 1, :]
    gathered.finish()
    finish()


ANY = pl.BlockSpec(memory_space=pl.ANY)
VMEM = pl.BlockSpec(memory_space=pltpu.VMEM)


def run_links(body, name, ins, outs, scratch, flops, moved):
    return pl.pallas_call(
        body,
        in_specs=[spec for spec, _ in ins],
        out_specs=[spec for spec, _ in outs],
        out_shape=[out for _, out in outs],
        scratch_shapes=list(scratch),
        compiler_params=pltpu.CompilerParams(
            vmem_limit_bytes=VMEM_BYTES, collective_id=name, has_side_effects=True
        ),
        cost_estimate=pl.CostEstimate(flops=flops, bytes_accessed=moved, transcendentals=0),
    )(*[array for _, array in ins])


def first_segment(base, gain, bias, shard, bq, segments, docs):
    CHUNK[0] = SIZES[0]
    rows, width = base.shape
    total = bq.shape[1]
    cols = total // GROUP
    groups = lax.axis_size("fsdp") // GROUP
    copies = pltpu.SemaphoreType.DMA((qkv_copies(rows) + gather_copies() + groups + 1,))
    counts = (VMEM, shape((docs, 128), F32))
    return run_links(
        first_body,
        0,
        [(VMEM, array) for array in (base, gain, bias, shard, bq, segments)],
        [
            (VMEM, shape((rows, width), F32)),
            (VMEM, shape((rows, width), BF16)),
            (VMEM, shape((width, total), BF16)),
            counts,
            counts,
            (ANY, shape((GROUP, rows, cols), BF16)),
            (ANY, shape((GROUP, rows, 2 * cols // 3), BF16)),
        ],
        [
            pltpu.VMEM((GROUP, rows, cols), BF16),
            pltpu.VMEM((3, docs, 128), F32),
            pltpu.VMEM((2, docs, 128), F32),
            pltpu.VMEM((groups - 1, docs, 128), F32),
            copies,
            copies,
            pltpu.SemaphoreType.DMA((rows // CHUNK[0],)),
        ],
        flops=2 * rows * width * total,
        moved=rows * width * 8 + width * total * 2,
    )


def trade_mixed(links, mixed_all, mixed):
    cols = mixed_all.shape[2]
    copies = []
    for c in range(mixed.shape[0] // CHUNK[0]):
        rows = pl.ds(c * CHUNK[0], CHUNK[0])
        copies.append(
            [
                links.copy(
                    mixed_all.at[links.place ^ s, rows],
                    mixed.at[rows, columns(links.place, cols)],
                    links.peer(s),
                )
                for s in (2, 3, 1)
            ]
        )

    def start():
        for chunk in copies:
            for one in chunk:
                one.start()
        mixed[:, columns(links.place, cols)] = mixed_all[links.place]

    def wait(c):
        for one in copies[c]:
            one.wait_recv()

    def finish():
        for chunk in copies:
            for one in chunk:
                one.wait_send()

    return start, wait, finish


def between_body(
    at, mixed_all, base, bout, gain_two, bias_two, bfc, bproj, gain, bias, bq, rest, shard,
    mixed, middle, low_two, hidden, act, stream, low, w_qkv, pieces, kv_back,
    w_out, w_fc, w_proj, part, got, part_two, got_two, ready, send, recv, load, kept
):
    out_at, fc_at, proj_at = at
    links = Links(send, recv)
    loads = [
        pltpu.make_async_copy(source.at[:, pl.ds(start, target.shape[1])], target, load.at[i])
        for i, (source, start, target) in enumerate(
            ((rest, out_at, w_out), (rest, fc_at, w_fc), (rest, proj_at, w_proj))
        )
    ]
    for one in loads:
        one.start()
    links.greet(
        [links.peer(s) for s in range(1, GROUP)]
        + [links.beyond(1, s) for s in range(GROUP)]
        + [links.beyond(links.groups - 1, s) for s in range(GROUP)]
        + [{"tp": links.other}]
        + group_greets(links)
    )
    gathered = ShardGather(links, shard, w_qkv)
    chunks = [pl.ds(c * CHUNK[0], CHUNK[0]) for c in range(base.shape[0] // CHUNK[0])]
    start_mixed, wait_mixed, finish_mixed = trade_mixed(links, mixed_all, mixed)
    swaps = [links.swap(part.at[rows], got.at[rows]) for rows in chunks]
    swaps_two = [links.swap(part_two.at[rows], got_two.at[rows]) for rows in chunks]
    start_qkv, finish_qkv = send_qkv(links, low, w_qkv, bq, ready, pieces, kv_back, kept)
    start_mixed()
    gathered.start()
    loads[0].wait()
    for c, rows in enumerate(chunks):
        wait_mixed(c)
        out_rows(rows, mixed, w_out, part)
        swaps[c].start()
    loads[1].wait()
    loads[2].wait()
    for c, rows in enumerate(chunks):
        swaps[c].wait()
        norm_rows(c * CHUNK[0], base, (part, got, bout), gain_two, bias_two, middle, low_two)
        feed_rows(rows, low_two, w_fc, bfc, hidden, act, w_proj, part_two)
        swaps_two[c].start()
        if c == 0:
            gathered.pass_x()
        if c == 1:
            gathered.pass_core()
    gathered.arrive()
    for c, rows in enumerate(chunks):
        swaps_two[c].wait()
        norm_rows(c * CHUNK[0], middle, (part_two, got_two, bproj), gain, bias, stream, low)
        start_qkv(c)
    finish_mixed()
    gathered.finish()
    finish_qkv()


def between_segment(mixed_all, base, vectors, bq, rest, at, units, shard):
    CHUNK[0] = SIZES[1]
    rows, width = base.shape
    total = bq.shape[1]
    cols = total // GROUP
    out_cols = at[1] - at[0]
    chunks = rows // CHUNK[0]
    copies = pltpu.SemaphoreType.DMA((qkv_copies(rows) + chunks * (GROUP - 1) + 2 * chunks + gather_copies(),))
    whole_f32 = (VMEM, shape((rows, width), F32))
    whole_low = (VMEM, shape((rows, width), BF16))
    return run_links(
        functools.partial(between_body, at),
        1,
        [(VMEM, mixed_all), (VMEM, base)]
        + [(VMEM, vector) for vector in vectors]
        + [(VMEM, bq), (ANY, rest), (VMEM, shard)],
        [
            (VMEM, shape((rows, out_cols), BF16)),
            whole_f32,
            whole_low,
            (VMEM, shape((rows, units), F32)),
            (VMEM, shape((rows, units), BF16)),
            whole_f32,
            whole_low,
            (VMEM, shape((width, total), BF16)),
            (ANY, shape((GROUP, rows, cols), BF16)),
            (ANY, shape((GROUP, rows, 2 * cols // 3), BF16)),
        ],
        [
            pltpu.VMEM((width, out_cols), BF16),
            pltpu.VMEM((width, units), BF16),
            pltpu.VMEM((width, units), BF16),
        ]
        + [pltpu.VMEM((rows, width), BF16)] * 4
        + [
            pltpu.VMEM((GROUP, rows, cols), BF16),
            copies,
            copies,
            pltpu.SemaphoreType.DMA((3,)),
            pltpu.SemaphoreType.DMA((chunks,)),
        ],
        flops=2 * rows * width * (total + out_cols + 2 * units),
        moved=rows * width * 20 + rows * units * 6 + width * (total + out_cols + 2 * units) * 2,
    )


def pull_qkv_rows(first, back, links, full, back_got, w, target, sums):
    cols = full.shape[1] // GROUP
    rows = pl.ds(first, CHUNK[0])

    @pl.when(links.group < links.groups - 1)
    def _():
        for s in range(GROUP):
            at = pl.ds(
                pl.multiple_of((links.place ^ s) * cols + cols // 3, cols // 3), 2 * cols // 3
            )
            full[rows, at] = (full[rows, at].astype(F32) + back_got[s, rows].astype(F32)).astype(BF16)

    def tile(at):
        target[rows, at] = dot_last(full[rows, :], w[at, :]).astype(BF16)

    tiles(w.shape[0], 256, tile)

    def body(at):
        sums[...] += eight_rows(full[at, :].astype(F32))

    rows_within(first, body)


def trade_pulls(links, grad_q, grad_kv, grad_kv_back, full, back_got):
    part = grad_q.shape[2]
    copies = []
    for c in range(full.shape[0] // CHUNK[0]):
        rows = pl.ds(c * CHUNK[0], CHUNK[0])
        across, back = [], []
        for s in (2, 3, 1):
            for source, start, size in ((grad_kv, part, 2 * part), (grad_q, 0, part)):
                at = pl.ds(pl.multiple_of(links.place * 3 * part + start, part), size)
                across.append(
                    links.copy(source.at[links.place ^ s, rows], full.at[rows, at], links.peer(s))
                )
        for s in (2, 3, 1, 0):
            back.append(
                links.copy(
                    grad_kv_back.at[links.place ^ s, rows],
                    back_got.at[s, rows],
                    links.beyond(links.groups - 1, s),
                )
            )
        copies.append((across, back))

    def start():
        for across, back in copies:
            for one in across:
                one.start()

            @pl.when(links.group > 0)
            def _():
                for one in back:
                    one.start()

        first = pl.multiple_of(links.place * 3 * part, part)
        full[:, pl.ds(first, part)] = grad_q[links.place]
        full[:, pl.ds(pl.multiple_of(first + part, part), 2 * part)] = grad_kv[links.place]

    def wait(c):
        across, back = copies[c]
        for one in across:
            one.wait_recv()

        @pl.when(links.group < links.groups - 1)
        def _():
            for one in back:
                one.wait_recv()

    def finish():
        for across, back in copies:
            for one in across:
                one.wait_send()

            @pl.when(links.group > 0)
            def _():
                for one in back:
                    one.wait_send()

    return start, wait, finish


def pull_copies(rows):
    return rows // CHUNK[0] * (2 * (GROUP - 1) + GROUP)


def pull_norm_rows(first, grad, own, got, inputs, gain, grad_new, sums, low=None):
    def body(at):
        value = norm_pull_rows(at, grad, own, got, inputs, gain, grad_new, sums[0], sums[1])
        if low is not None:
            value = value.astype(BF16)
            low[at, :] = value
            sums[2][...] += eight_rows(value.astype(F32))

    rows_within(first, body)


def round_rows(first, grad, low, sums):
    def body(at):
        value = grad[at, :].astype(BF16)
        low[at, :] = value
        sums[...] += eight_rows(value.astype(F32))

    rows_within(first, body)


def pull_feed_rows(rows, low, proj, hidden, held, grad_hidden, sums, fc, target):
    def tile(at):
        value = dot(low[rows, :], proj[:, at]) * gelu_slope(hidden[held, at])
        value = value.astype(BF16)
        grad_hidden[rows, at] = value
        sums[:, at] += eight_rows(value.astype(F32))

    tiles(proj.shape[1], 512, tile)

    def tile_out(at):
        target[rows, at] = dot_last(grad_hidden[rows, :], fc[at, :]).astype(BF16)

    tiles(fc.shape[0], 256, tile_out)


def send_mixed_pull(links, low, w, ready, pieces, kept):
    cols = ready.shape[2]
    copies = []
    for c in range(low.shape[0] // CHUNK[0]):
        rows = pl.ds(c * CHUNK[0], CHUNK[0])
        across = {
            s: links.copy(ready.at[s, rows], pieces.at[links.place, rows], links.peer(s))
            for s in range(1, GROUP)
        }
        own = pltpu.make_async_copy(ready.at[0, rows], pieces.at[links.place, rows], kept.at[c])
        copies.append((across, own))

    def start(c):
        rows = pl.ds(c * CHUNK[0], CHUNK[0])
        across, own = copies[c]
        for s in (2, 3, 1, 0):
            at = columns(links.place ^ s, cols)
            ready[s, rows, :] = dot(low[rows, :], w[:, at]).astype(BF16)
            (across[s] if s else own).start()

    def finish():
        for across, own in copies:
            own.wait()
            for one in across.values():
                one.wait()

    return start, finish


def load_columns(plan, load):
    copies = []
    for i, (source, start, target) in enumerate(plan):
        if start is not None:
            source = source.at[:, pl.ds(start, target.shape[1])]
        copies.append(pltpu.make_async_copy(source, target, load.at[i]))
    for one in copies:
        one.start()
    return copies


def turn_body(
    at, mixed_all, base_in, grad_in, bout, gain_two, bias_two, bfc, rest,
    mixed, middle, low_two, act, part_two, low_proj, sum_proj, grad_hidden, sum_fc, grad_new, low_out,
    sum_gain, sum_bias, sum_out, pieces, stay0, go0, stay1, go1,
    w_out, w_fc, w_proj, base, grad, hidden, part, got, part_three, got_three, ready,
    plain, flipped, away0, away1, met0, met1, send, recv, load, kept
):
    out_at, fc_at, proj_at = at
    links = Links(send, recv)
    loads = load_columns(
        (
            (rest, out_at, w_out),
            (base_in, None, base),
            (grad_in, None, grad),
            (rest, fc_at, w_fc),
            (rest, proj_at, w_proj),
        ),
        load,
    )
    links.greet([links.peer(s) for s in range(1, GROUP)] + [{"tp": links.other}])
    chunks = [pl.ds(c * CHUNK[0], CHUNK[0]) for c in range(base.shape[0] // CHUNK[0])]
    start_mixed, wait_mixed, finish_mixed = trade_mixed(links, mixed_all, mixed)
    swaps = [links.swap(part.at[rows], got.at[rows]) for rows in chunks]
    swaps_three = [links.swap(part_three.at[rows], got_three.at[rows]) for rows in chunks]
    start_pull, finish_pull = send_mixed_pull(links, low_out, w_out, ready, pieces, kept)
    core_sums = (
        CoreSum(links, stay0, go0, away0, met0),
        CoreSum(links, stay1, go1, away1, met1),
    )
    start_mixed()
    for total in (sum_proj, sum_fc, sum_gain, sum_bias, sum_out):
        total[...] = jnp.zeros_like(total)
    loads[0].wait()
    for c, rows in enumerate(chunks):
        wait_mixed(c)
        out_rows(rows, mixed, w_out, part)
        swaps[c].start()
    for one in loads[1:]:
        one.wait()
    for c in range(len(chunks)):
        round_rows(c * CHUNK[0], grad, low_proj, sum_proj)
    for c, rows in enumerate(chunks):
        swaps[c].wait()
        norm_rows(c * CHUNK[0], base, (part, got, bout), gain_two, bias_two, middle, low_two)

        def tile(at):
            value = dot(low_two[rows, :], w_fc[:, at]) + bfc[:, at]
            hidden[rows, at] = value
            act[rows, at] = gelu_rows(value).astype(BF16)

        tiles(w_fc.shape[1], 512, tile)
        pull_feed_rows(
            rows, low_proj, w_proj, hidden, rows, grad_hidden, sum_fc, w_fc, part_three
        )
        swaps_three[c].start()
    core_sums[0].multiply(low_two, grad_hidden, plain, flipped)
    core_sums[1].multiply(low_proj, act, plain, flipped)
    for rows in chunks:

        def tile_out(at):
            part_two[rows, at] = dot_last(act[rows, :], w_proj[at, :]).astype(BF16)

        tiles(w_proj.shape[0], 256, tile_out)
    for c, rows in enumerate(chunks):
        swaps_three[c].wait()
        pull_norm_rows(
            c * CHUNK[0], grad, part_three, got_three, middle, gain_two, grad_new, (sum_gain, sum_bias, sum_out), low_out
        )
        start_pull(c)
    for one in core_sums:
        one.add()
    finish_mixed()
    finish_pull()


def turn_segment(mixed_all, base, grad, vectors, rest, at, units):
    CHUNK[0] = SIZES[2]
    rows, width = base.shape
    out_cols = at[1] - at[0]
    cols = out_cols // GROUP
    chunks = rows // CHUNK[0]
    copies = pltpu.SemaphoreType.DMA((2 * chunks * (GROUP - 1) + 2 * chunks + 2,))
    high = (VMEM, shape((rows, width), F32))
    low = (VMEM, shape((rows, width), BF16))
    sums = (VMEM, shape((8, width), F32))
    return run_links(
        functools.partial(turn_body, at),
        2,
        [(VMEM, mixed_all), (ANY, base), (ANY, grad)]
        + [(VMEM, vector) for vector in vectors]
        + [(ANY, rest)],
        [
            (VMEM, shape((rows, out_cols), BF16)),
            high,
            low,
            (VMEM, shape((rows, units), BF16)),
            low,
            low,
            sums,
            (VMEM, shape((rows, units), BF16)),
            (VMEM, shape((8, units), F32)),
            high,
            low,
            sums,
            sums,
            sums,
            (ANY, shape((GROUP, rows, cols), BF16)),
        ]
        + [(VMEM, shape((width // 4, units), BF16))] * 4,
        [
            pltpu.VMEM((width, out_cols), BF16),
            pltpu.VMEM((width, units), BF16),
            pltpu.VMEM((width, units), BF16),
            pltpu.VMEM((rows, width), F32),
            pltpu.VMEM((rows, width), F32),
            pltpu.VMEM((rows, units), F32),
        ]
        + [pltpu.VMEM((rows, width), BF16)] * 4
        + [
            pltpu.VMEM((GROUP, rows, cols), BF16),
        ]
        + [pltpu.VMEM((width, rows), BF16)] * 2
        + [pltpu.VMEM((width // 2, units), BF16)] * 4
        + [
            copies,
            copies,
            pltpu.SemaphoreType.DMA((5,)),
            pltpu.SemaphoreType.DMA((chunks,)),
        ],
        flops=2 * rows * width * (2 * out_cols + 4 * units),
        moved=rows * width * 22 + rows * units * 4 + width * (out_cols + 2 * units) * 2,
    )


def pull_both_body(
    at, grad_q, grad_kv, grad_kv_back, gain, gain_two, qkv, rest, grad_in, stream_in, hidden_in, middle_in,
    stay0_in, met0_in, stay1_in, go1, low_two_in, act_in,
    full, sum_qkv, sum_gain_one, sum_bias_one, low_proj, sum_proj, grad_hidden, sum_fc, grad_new, low_out,
    sum_gain, sum_bias, sum_out, pieces, total0, total1, near2, *refs
):
    groups = lax.axis_size("fsdp") // GROUP
    far2, (stay3, go3), refs = refs[: groups - 1], refs[groups - 1 : groups + 1], refs[groups + 1 :]
    (w_qkv, w_out, w_fc, w_proj, grad, stream, hidden, back_got, part, got, part_two, got_two, ready,
    stay0, met0, far0, came0, stay1, met1, far1, came1,
    left, wide, plain, flipped, stay2, go2, met2, away, gone2, gone3, send, recv, load, kept) = refs
    out_at, fc_at, proj_at = at
    links = Links(send, recv)
    loads = load_columns(
        (
            (qkv, None, w_qkv),
            (grad_in, None, grad),
            (stream_in, None, stream),
            (rest, proj_at, w_proj),
            (hidden_in.at[pl.ds(0, CHUNK[0])], None, hidden),
            (rest, fc_at, w_fc),
            (rest, out_at, w_out),
            (stay0_in, None, stay0),
            (met0_in, None, met0),
            (stay1_in, None, stay1),
            (low_two_in, None, left),
            (act_in, None, wide),
        ),
        load,
    )
    middle = stream
    load_middle = pltpu.make_async_copy(middle_in, middle, load.at[len(loads)])
    links.greet(
        [links.peer(s) for s in range(1, GROUP)]
        + [links.beyond(1, s) for s in range(GROUP)]
        + [links.beyond(links.groups - 1, s) for s in range(GROUP)]
        + [{"tp": links.other}]
        + group_greets(links)
    )
    chunks = [pl.ds(c * CHUNK[0], CHUNK[0]) for c in range(grad.shape[0] // CHUNK[0])]
    start_pulls, wait_pulls, finish_pulls = trade_pulls(
        links, grad_q, grad_kv, grad_kv_back, full, back_got
    )
    swaps = [links.swap(part.at[rows], got.at[rows]) for rows in chunks]
    swaps_two = [links.swap(part_two.at[rows], got_two.at[rows]) for rows in chunks]
    start_pull, finish_pull = send_mixed_pull(links, low_out, w_out, ready, pieces, kept)
    late_x = links.copy(go1, met1, links.peer(2))
    group_sums = (
        GroupSum(links, stay0, met0, far0, came0, total0),
        GroupSum(links, stay1, met1, far1, came1, total1),
    )
    core_sums = (
        CoreSum(links, stay2, go2, away, gone2),
        CoreSum(links, stay3, go3, away, gone3),
    )
    feed_x = links.copy(go2, met2, links.peer(2))
    start_pulls()
    for total in (sum_qkv, sum_gain_one, sum_bias_one, sum_proj, sum_fc, sum_gain, sum_bias, sum_out):
        total[...] = jnp.zeros_like(total)
    for one in loads:
        one.wait()
    for c, rows in enumerate(chunks):
        wait_pulls(c)
        if c == len(chunks) // 2:
            late_x.start()
            group_sums[0].send(0)
        pull_qkv_rows(c * CHUNK[0], None, links, full, back_got, w_qkv, part, sum_qkv)
        swaps[c].start()
    for c, rows in enumerate(chunks):
        swaps[c].wait()
        pull_norm_rows(
            c * CHUNK[0], grad, part, got, stream, gain, grad_new, (sum_gain_one, sum_bias_one)
        )
        if c == len(chunks) - 1:
            load_middle.start()
        round_rows(c * CHUNK[0], grad_new, low_proj, sum_proj)
        if c:
            load_hidden.wait()
        pull_feed_rows(
            rows, low_proj, w_proj, hidden, pl.ds(0, CHUNK[0]), grad_hidden, sum_fc, w_fc, part_two
        )
        swaps_two[c].start()
        if c + 1 < len(chunks):
            load_hidden = pltpu.make_async_copy(
                hidden_in.at[pl.ds((c + 1) * CHUNK[0], CHUNK[0])], hidden, load.at[len(loads) + 1 + c]
            )
            load_hidden.start()
    core_sums[0].multiply(left, grad_hidden, plain, flipped)
    load_middle.wait()
    for c, rows in enumerate(chunks):
        swaps_two[c].wait()
        pull_norm_rows(
            c * CHUNK[0], grad_new, part_two, got_two, middle, gain_two, grad_new, (sum_gain, sum_bias, sum_out), low_out
        )
        start_pull(c)
        if c == 0:
            core_sums[0].add()
            feed_x.start()
            late_x.wait()
            group_sums[1].send(0)
            group_sums[0].pass_on(0)
            core_sums[1].multiply(low_proj, wide, plain, flipped)
    group_sums[1].pass_on(0)
    core_sums[1].add()
    feed_x.wait()
    add_slots(stay2, met2, (near2, *far2))
    finish_pulls()
    finish_pull()
    for one in group_sums:
        one.finish(2)


def pull_both_segment(pulls, gain, gain_two, qkv, rest, at, units, grad, stream, hidden, middle, sums_in, factors):
    CHUNK[0] = SIZES[3]
    rows, width = grad.shape
    out_cols = at[1] - at[0]
    cols = out_cols // GROUP
    total = 3 * out_cols
    chunks = rows // CHUNK[0]
    groups = lax.axis_size("fsdp") // GROUP
    stay = sums_in[0]
    copies = pltpu.SemaphoreType.DMA((pull_copies(rows) + chunks * (GROUP - 1) + 2 * chunks + 2 * groups + 2,))
    high = (VMEM, shape((rows, width), F32))
    low = (VMEM, shape((rows, width), BF16))
    sums = (VMEM, shape((8, width), F32))
    return run_links(
        functools.partial(pull_both_body, at),
        3,
        [(VMEM, pull) for pull in pulls]
        + [(VMEM, gain), (VMEM, gain_two)]
        + [(ANY, array) for array in (qkv, rest, grad, stream, hidden, middle)]
        + [(ANY, array) for array in (*sums_in, *factors)],
        [
            (VMEM, shape((rows, total), BF16)),
            (VMEM, shape((8, total), F32)),
            sums,
            sums,
            low,
            sums,
            (VMEM, shape((rows, units), BF16)),
            (VMEM, shape((8, units), F32)),
            high,
            low,
            sums,
            sums,
            sums,
            (ANY, shape((GROUP, rows, cols), BF16)),
        ]
        + [(VMEM, shape((stay.shape[0] // groups, stay.shape[1]), F32))] * 2
        + [(VMEM, shape((width // 4 // groups, units), F32))]
        + [(VMEM, shape((width // 4 // groups, units), BF16))] * (groups - 1)
        + [(VMEM, shape((width // 4, units), BF16))] * 2,
        [
            pltpu.VMEM((width, total), BF16),
            pltpu.VMEM((width, out_cols), BF16),
            pltpu.VMEM((width, units), BF16),
            pltpu.VMEM((width, units), BF16),
            pltpu.VMEM((rows, width), F32),
            pltpu.VMEM((rows, width), F32),
            pltpu.VMEM((CHUNK[0], units), F32),
            pltpu.VMEM((GROUP, rows, 2 * cols), BF16),
        ]
        + [pltpu.VMEM((rows, width), BF16)] * 4
        + [
            pltpu.VMEM((GROUP, rows, cols), BF16),
        ]
        + ([pltpu.VMEM(stay.shape, BF16)] + group_scratch(stay, groups, True)) * 2
        + [pltpu.VMEM((rows, width), BF16), pltpu.VMEM((rows, units), BF16)]
        + [pltpu.VMEM((width, rows), BF16)] * 2
        + [pltpu.VMEM((width // 4, units), BF16)] * 3
        + [pltpu.VMEM((width // 2, units), BF16)] * 3
        + [
            copies,
            copies,
            pltpu.SemaphoreType.DMA((12 + chunks,)),
            pltpu.SemaphoreType.DMA((chunks,)),
        ],
        flops=2 * rows * width * (total + out_cols + 2 * units),
        moved=rows * width * 22 + rows * units * 6 + width * (total + out_cols + 2 * units) * 2,
    )


def add_slots(stay, met, slots):
    chunk = 16
    depth = slots[0].shape[0]
    for at, slot in enumerate(slots):

        def body(rows):
            from_row = pl.ds(pl.multiple_of(rows.start + at * depth, chunk), chunk)
            total = stay[from_row, :].astype(F32) + met[from_row, :].astype(F32)
            slot[rows, :] = total.astype(slot.dtype)

        each_rows(depth, chunk, body)


def pack_sums(sums, target, first):
    width = target.shape[1]
    at = first
    for one in sums:
        total = jnp.sum(one[...], 0, keepdims=True)
        for start in range(0, total.shape[1], width):
            size = min(width, total.shape[1] - start)
            target[at : at + 1, :size] = total[:, start : start + size]
            at += 1


def pack_body(wqkv, bqv, wout, wfc, wproj, rest, qkv0, qkv1, bq0, bq1):
    cols = bqv.shape[2] // GROUP
    at = 0
    for l in range(LAYERS):
        for part in (wout, wfc, wproj):
            size = part.shape[2]
            rest[:, at : at + size] = part[l]
            at += size
    for l, (qkv, bq) in enumerate(((qkv0, bq0), (qkv1, bq1))):
        bq[...] = jnp.zeros_like(bq)
        for place in range(GROUP):
            here = slice(place * cols, (place + 1) * cols)
            for c in range(3):
                where = (3 * place + c) * cols
                qkv[:, where : where + cols] = wqkv[l, c, :, here]
                if c != 1:
                    bq[:, where : where + cols] = bqv[l, c // 2 : c // 2 + 1, here]


def pack(w_qkv, b_qv, w_out, w_fc, w_proj):
    depth, out_cols, units = w_fc.shape[1], w_out.shape[1], w_fc.shape[2]
    rest = LAYERS * (out_cols + 2 * units)
    outs = [shape((depth, rest), BF16)] + [shape((depth, 3 * out_cols), BF16)] * 2
    outs += [shape((1, 3 * out_cols), F32)] * 2
    return pl.pallas_call(
        pack_body,
        in_specs=[VMEM] * 5,
        out_specs=[VMEM] * 5,
        out_shape=outs,
        compiler_params=pltpu.CompilerParams(vmem_limit_bytes=VMEM_BYTES),
    )(
        w_qkv.transpose(0, 2, 1, 3),
        b_qv,
        w_out.transpose(0, 2, 1),
        w_fc,
        w_proj.transpose(0, 2, 1),
    )


def finish_body(small, fc1, proj1, qkv1, out1, proj0, qkv0, out0, near, *refs):
    *came, grad_in, middle, own, other, bproj_in, outputs, grad, gain1, bias1, bqv, bout, gain2, bias2, bfc, bproj, wfc, wproj, wout, wqkv = refs
    def rows(at):
        grad[at, :] = grad_in[at, :]
        total = own[at, :].astype(F32) + other[at, :].astype(F32)
        outputs[at, :] = (middle[at, :] + total + bproj_in[...]).astype(BF16)

    each_rows(grad.shape[0], LN_ROWS, rows)
    fc0 = near[...]
    for one in came:
        fc0 = fc0 + one[...].astype(F32)
    width = small.shape[1]
    cols = bqv.shape[2] // GROUP
    wfc[0] = fc0
    wfc[1] = fc1[...]
    for l, proj, qkv, out in ((0, proj0, qkv0, out0), (1, proj1, qkv1, out1)):
        at = l * (small.shape[0] // 2)
        for target, where in ((gain1, 0), (bias1, 1), (bout, 4), (gain2, 5), (bias2, 6), (bproj, 9)):
            target[l : l + 1, :] = small[at + where : at + where + 1, :]
        for i in range(bfc.shape[1] // width):
            bfc[l : l + 1, i * width : (i + 1) * width] = small[at + 7 + i : at + 8 + i, :]
        for place in range(GROUP):
            for i in range(2):
                where = place * 3 * cols + 2 * i * cols
                line, lane = at + 2 + where // width, where % width
                bqv[l, i : i + 1, place * cols : (place + 1) * cols] = small[
                    line : line + 1, lane : lane + cols
                ]
        wproj[l] = proj[...]
        wout[l] = out[...]
        for place in range(GROUP):
            for c in range(3):
                at = (3 * place + c) * cols
                wqkv[l, c, :, place * cols : (place + 1) * cols] = qkv[:, at : at + cols]


def finish(small, totals, near, came, last, out_cols, units):
    depth, width = totals[0].shape[0], small.shape[1]
    vector = shape((LAYERS, width), F32)
    grad = last[0].shape
    outs = [shape(grad, BF16), shape(grad, F32)]
    outs += [vector, vector, shape((LAYERS, 2, out_cols), F32), vector, vector, vector]
    outs += [shape((LAYERS, units), F32), vector, shape((LAYERS, depth, units), F32)]
    outs += [shape((LAYERS, depth, units), F32), shape((LAYERS, depth, out_cols), F32)]
    outs += [shape((LAYERS, 3, depth, out_cols), F32)]
    return pl.pallas_call(
        finish_body,
        in_specs=[VMEM] * (2 + len(totals) + len(came) + len(last)),
        out_specs=[VMEM] * len(outs),
        out_shape=outs,
        compiler_params=pltpu.CompilerParams(vmem_limit_bytes=VMEM_BYTES),
    )(small, *totals, near, *came, *last)


def pull_last_body(
    grad_q, grad_kv, grad_kv_back, gain, qkv, grad_in, stream_in,
    low_one1_in, grad_qkv1_in, low_out1_in, mixed1_in, low_one_in, low_out_in, mixed_in, stay0_in, met0_in,
    gain1, bias1, bqkv1, bout1, gain2_1, bias2_1, bfc1, bproj1, bout0, gain2_0, bias2_0, bfc0, bproj0,
    grad_new, small, total0, total1, total2, total3, total4,
    full, sum_qkv, sum_gain, sum_bias, held, came, far, w_qkv, grad, stream, back_got, part, got,
    left1, wide1, right1, narrow1, left, right, narrow, plain, flipped,
    stay0, met0, far0, came0,
    away1, gone1, stay1, go1, met1, far1, came1,
    away2, gone2, stay2, go2, met2, far2, came2,
    away3, gone3, stay3, go3, met3, far3, came3,
    away4, gone4, stay4, go4, met4, far4, came4,
    send, recv, load
):
    links = Links(send, recv)
    loads = load_columns(
        (
            (low_one1_in, None, left1),
            (grad_qkv1_in, None, wide1),
            (low_out1_in, None, right1),
            (mixed1_in, None, narrow1),
            (stay0_in, None, stay0),
            (met0_in, None, met0),
            (qkv, None, w_qkv),
            (grad_in, None, grad),
            (stream_in, None, stream),
            (low_one_in, None, left),
            (low_out_in, None, right),
            (mixed_in, None, narrow),
        ),
        load,
    )
    links.greet(
        [links.peer(s) for s in range(1, GROUP)]
        + [links.beyond(1, s) for s in range(GROUP)]
        + [links.beyond(links.groups - 1, s) for s in range(GROUP)]
        + [{"tp": links.other}]
        + group_greets(links)
    )
    chunks = [pl.ds(c * CHUNK[0], CHUNK[0]) for c in range(grad.shape[0] // CHUNK[0])]
    start_pulls, wait_pulls, finish_pulls = trade_pulls(
        links, grad_q, grad_kv, grad_kv_back, full, back_got
    )
    swaps = [links.swap(part.at[rows], got.at[rows]) for rows in chunks]
    parts = (
        (away1, gone1, stay1, go1, met1, far1, came1, total1),
        (away2, gone2, stay2, go2, met2, far2, came2, total2),
        (away3, gone3, stay3, go3, met3, far3, came3, total3),
        (away4, gone4, stay4, go4, met4, far4, came4, total4),
    )
    core_sums, over_x, group_sums, spans = [], [], [], []
    for at, (away, gone, stay, go, met, *rest) in enumerate(parts):
        core_sums.append(CoreSum(links, stay, go, away, gone))
        size = stay.shape[1]
        step = size if at % 2 else size // 2
        spans.append([])
        for start in range(0, size, step):
            place = pl.ds(start, step)
            spans[at].append(len(over_x))
            over_x.append(links.copy(go.at[:, place], met.at[:, place], links.peer(2)))
            group_sums.append(GroupSum(links, *[ref.at[:, place] for ref in (stay, met, *rest)]))
    early_sum = GroupSum(links, stay0, met0, far0, came0, total0)
    smalls = RowSum(links, held, came, far)
    sums_one = (gain1, bias1, bqkv1, bout1, gain2_1, bias2_1, bfc1, bproj1)
    sums_zero = (sum_gain, sum_bias, sum_qkv, bout0, gain2_0, bias2_0, bfc0, bproj0)
    start_pulls()
    for total in (sum_qkv, sum_gain, sum_bias):
        total[...] = jnp.zeros_like(total)
    for one in loads:
        one.wait()
    early_sum.send(0)
    core_sums[0].multiply(left1, wide1, plain, flipped)
    core_sums[1].multiply(right1, narrow1, plain, flipped)
    held[0] = jnp.zeros(held.shape[1:], F32)
    pack_sums(sums_one, held.at[0], held.shape[1] // 2)
    core_sums[0].add()
    core_sums[1].add()
    for at in spans[0] + spans[1]:
        over_x[at].start()
    for c, rows in enumerate(chunks):
        wait_pulls(c)
        pull_qkv_rows(c * CHUNK[0], None, links, full, back_got, w_qkv, part, sum_qkv)
        swaps[c].start()
    early_sum.pass_on(0)
    core_sums[2].multiply(left, full, plain, flipped)
    core_sums[3].multiply(right, narrow, plain, flipped)
    core_sums[2].add()
    for at in spans[2]:
        over_x[at].start()
    core_sums[3].add()
    for at in spans[3]:
        over_x[at].start()
    for c, rows in enumerate(chunks):
        swaps[c].wait()
        pull_norm_rows(c * CHUNK[0], grad, part, got, stream, gain, grad_new, (sum_gain, sum_bias))
    pack_sums(sums_zero, held.at[0], 0)
    smalls.near[0].start()
    smalls.step(0)
    smalls.near[1].start()
    for at, one in enumerate(group_sums):
        over_x[at].wait()
        one.send(0)
        if at:
            group_sums[at - 1].pass_on(0)
        if at == 3:
            smalls.step(1)
            for far_one in smalls.along:
                far_one.start()
    group_sums[-1].pass_on(0)
    finish_pulls()
    small[...] = smalls.finish()
    early_sum.finish(2)
    for one in group_sums:
        one.finish(2)


def pull_last_segment(pulls, gain, qkv, grad, stream, factors, sums_in, smalls):
    CHUNK[0] = SIZES[4]
    rows, width = grad.shape
    cols = pulls[0].shape[2]
    out_cols = GROUP * cols
    total = 3 * out_cols
    units = sums_in[0].shape[1]
    chunks = rows // CHUNK[0]
    groups = lax.axis_size("fsdp") // GROUP
    copies = pltpu.SemaphoreType.DMA(
        (pull_copies(rows) + chunks + 10 + 7 * (groups - 1) + groups + 1,)
    )
    sizes = [total, out_cols, total, out_cols]
    quarter = width // 4
    scratch = []
    for size in sizes:
        stay = shape((quarter, size), BF16)
        scratch += [pltpu.VMEM((2 * quarter, size), BF16)] * 2
        scratch += [pltpu.VMEM(stay.shape, BF16)]
        scratch += [pltpu.VMEM(stay.shape, BF16)] + group_scratch(stay, groups, True)
    low = pltpu.VMEM((rows, width), BF16)
    high = pltpu.VMEM((rows, width), F32)
    mixed = pltpu.VMEM((rows, out_cols), BF16)
    flip = pltpu.VMEM((width, rows), BF16)
    eight = pltpu.VMEM((8, width), F32)
    return run_links(
        pull_last_body,
        4,
        [(VMEM, pull) for pull in pulls]
        + [(VMEM, gain)]
        + [(ANY, array) for array in (qkv, grad, stream, *factors, *sums_in)]
        + [(VMEM, array) for array in smalls],
        [(VMEM, shape((rows, width), F32)), (VMEM, shape((24, width), F32))]
        + [(VMEM, shape((quarter // groups, size), F32)) for size in [units] + sizes],
        [
            pltpu.VMEM((rows, total), BF16),
            pltpu.VMEM((8, total), F32),
            eight,
            eight,
            pltpu.VMEM((3, 24, width), F32),
            pltpu.VMEM((2, 24, width), F32),
            pltpu.VMEM((groups - 1, 24, width), F32),
            pltpu.VMEM((width, total), BF16),
            high,
            high,
            pltpu.VMEM((GROUP, rows, 2 * cols), BF16),
            low,
            low,
            low,
            pltpu.VMEM((rows, total), BF16),
            low,
            mixed,
            low,
            low,
            mixed,
            flip,
            flip,
            pltpu.VMEM((quarter, units), BF16),
        ]
        + group_scratch(shape((quarter, units), BF16), groups, True)
        + scratch
        + [copies, copies, pltpu.SemaphoreType.DMA((12,))],
        flops=2 * rows * width * (3 * total + 2 * out_cols),
        moved=rows * width * 24 + width * total * 2,
    )


def halving_order(count):
    order = [0]
    bit = count // 2
    while bit:
        order = order + [at + bit for at in order]
        bit //= 2
    return order


def flip_slots(links, source, plain, flipped):
    plain[...] = source[...].T
    depth = plain.shape[0] // (GROUP * links.groups)
    slot = 0
    for s in (0, 2, 1, 3):
        for other in halving_order(links.groups):
            owner = (links.group ^ other) * GROUP + (links.place ^ s)
            flipped[slot * depth : (slot + 1) * depth, :] = plain[
                pl.ds(pl.multiple_of(owner * depth, depth), depth), :
            ]
            slot += 1


class CoreSum:
    def __init__(self, links, stay, go, away, got):
        self.links, self.stay, self.go, self.away, self.got = links, stay, go, away, got
        self.copy = links.copy(away, got, links.peer(1))
        self.sent = False

    def release(self):
        self.copy.wait_send()
        self.sent = True

    def multiply(self, x, g, plain, flipped):
        flip_slots(self.links, x, plain, flipped)
        quarter = self.stay.shape[0]

        def far(at):
            self.away[:, at] = dot(flipped[2 * quarter :, :], g[:, at]).astype(BF16)

        def near(at):
            self.stay[:, at] = dot(flipped[:quarter, :], g[:, at]).astype(BF16)
            self.go[:, at] = dot(flipped[quarter : 2 * quarter, :], g[:, at]).astype(BF16)

        tiles(g.shape[1], 512, far)
        self.copy.start()
        tiles(g.shape[1], 512, near)

    def add(self):
        if not self.sent:
            self.release()
        self.copy.wait_recv()
        quarter = self.stay.shape[0]
        chunk = 16
        for target, first in ((self.go, quarter), (self.stay, 0)):

            def body(at):
                from_row = pl.ds(pl.multiple_of(at.start + first, chunk), chunk)
                total = target[at, :].astype(F32) + self.got[from_row, :].astype(F32)
                target[at, :] = total.astype(BF16)

            each_rows(quarter, chunk, body)


class GroupSum:
    def __init__(self, links, stay, met, far, came, result):
        self.stay, self.met, self.far, self.came, self.result = stay, met, far, came, result
        self.depth = result.shape[0]
        self.copies, self.counts = [], []
        first, count, bit = 0, links.groups // 2, 1
        while count:
            rows = pl.ds(first * self.depth, count * self.depth)
            device = {"fsdp": (links.group ^ bit) * GROUP + links.place}
            self.copies.append(links.copy(far.at[rows], came.at[rows], device))
            self.counts.append((first, count))
            first, count, bit = first + count, count // 2, bit * 2

    def add(self, step, target, target_first, first, count):
        chunk = 16

        def body(at):
            def rows(slot):
                return pl.ds(pl.multiple_of(at.start + slot * self.depth, chunk), chunk)

            total = self.stay[rows(first), :].astype(F32) + self.met[rows(first), :].astype(F32)
            for came_first, _ in self.counts[:step]:
                total = total + self.came[rows(came_first + first), :].astype(F32)
            target[rows(target_first), :] = total.astype(target.dtype)

        each_rows(count * self.depth, chunk, body)

    def send(self, step):
        first, count = self.counts[step]
        self.add(step, self.far, first, count, count)
        self.copies[step].start()

    def pass_on(self, step):
        self.copies[step].wait()
        self.send(step + 1)

    def finish(self, sent=1):
        for step in range(sent, len(self.copies)):
            self.pass_on(step - 1)
        self.copies[-1].wait()
        self.add(len(self.copies), self.result, 0, 0, 1)


def group_scratch(stay, groups, met):
    rows, size = stay.shape
    far = pltpu.VMEM((rows - rows // groups, size), BF16)
    return ([pltpu.VMEM((rows, size), BF16)] if met else []) + [far, far]


def group_greets(links):
    return [links.beyond(onward, 0) for onward in range(2, links.groups - 1)]


def doc_start_rows(sc, docs, positions):
    start = jnp.zeros_like(positions)
    for d in range(docs):
        first = sc[2 + d]
        start = jnp.where(first <= positions, jnp.maximum(start, first), start)
    return start


def doc_start_one(sc, docs, position):
    start = jnp.int32(0)
    for d in range(docs):
        first = sc[2 + d]
        start = jnp.where(first <= position, jnp.maximum(start, first), start)
    return start


def query_rows(sc, docs, block, size):
    first = sc[1] + block * size
    position = first + lax.broadcasted_iota(jnp.int32, (1, size), 1)
    start = doc_start_rows(sc, docs, position)
    return (
        jnp.concatenate([position, position], 1),
        jnp.concatenate([start, start], 1),
        doc_start_one(sc, docs, first),
    )


def head_stack(rows, scale):
    value = rows.astype(F32)
    if scale != 1.0:
        value = value * scale
    lane = lax.broadcasted_iota(jnp.int32, value.shape, 1)
    return jnp.concatenate(
        [jnp.where(lane < HEAD_DIM, value, 0.0), jnp.where(lane >= HEAD_DIM, value, 0.0)], 0
    ).astype(BF16)


def block_at(block, size):
    return pl.ds(pl.multiple_of(block * size, size), size)


def masked_scores(keys, queries, first_key, position, start):
    scores = dot_last(keys, queries)
    key_at = first_key + lax.broadcasted_iota(jnp.int32, (keys.shape[0], 1), 0)
    return jnp.where((key_at >= start) & (key_at <= position), scores, NEG)


def flash_step(keys, values_ref, queries, at, first_key, position, start, acc, carry):
    top, total = carry
    scores = masked_scores(keys, queries, first_key, position, start)
    top_new = jnp.maximum(top, jnp.max(scores, 0, keepdims=True))
    expo = jnp.exp(scores - top_new)
    shrink = jnp.exp(top - top_new)
    total = total * shrink + jnp.sum(expo, 0, keepdims=True)
    expo = expo.astype(BF16)
    for h in range(2):
        lanes = slice(h * QB, (h + 1) * QB)
        rows = slice(h * HEAD_DIM, (h + 1) * HEAD_DIM)
        acc[rows, :] = acc[rows, :] * shrink[:, lanes] + dot(values_ref[rows, at], expo[:, lanes])
    return top_new, total


def attend_body(docs, sc, qkv, kv, mixed, out, log_total, v_flip, v_back, acc):
    block = pl.program_id(0)
    span, cols = out.shape[0] * pl.num_programs(0), out.shape[1]
    rows = qkv.shape[0]

    @pl.when(block == 0)
    def _():
        for first in range(0, rows, QB):
            v_flip[:, first : first + QB] = qkv[first : first + QB, 2 * cols :].T
            v_back[:, first : first + QB] = kv[first : first + QB, cols:].T

    position, start, lowest = query_rows(sc, docs, block, QB)
    queries = head_stack(qkv[block_at(block, QB), :cols], HEAD_DIM**-0.5)
    acc[...] = jnp.zeros_like(acc)
    least = jnp.maximum(lowest - sc[1], 0) // KB
    last = ((block + 1) * QB - 1) // KB
    before = sc[1] - span

    def step(back, carry):
        at = block_at(last - back, KB)
        keys = qkv[at, cols : 2 * cols]
        first_key = sc[1] + (last - back) * KB
        return flash_step(keys, v_flip, queries, at, first_key, position, start, acc, carry)

    def step_back(where, carry):
        at = block_at(where, KB)
        return flash_step(
            kv[at, :cols], v_back, queries, at, before + where * KB, position, start, acc, carry
        )

    carry = (jnp.full((1, 2 * QB), NEG, F32), jnp.zeros((1, 2 * QB), F32))
    carry = lax.fori_loop(0, last - least + 1, step, carry)
    top, total = lax.fori_loop(
        jnp.minimum(jnp.maximum(lowest - before, 0), span) // KB, span // KB, step_back, carry
    )
    sums = top + jnp.log(total)
    share = 1.0 / total
    parts = []
    for h in range(2):
        lanes = slice(h * QB, (h + 1) * QB)
        log_total[h : h + 1, :] = sums[:, lanes]
        parts.append(acc[h * HEAD_DIM : (h + 1) * HEAD_DIM, :] * share[:, lanes])
    value = jnp.concatenate(parts, 0).T
    out[...] = value
    mixed[...] = value.astype(BF16)


def attend(sc, docs, pieces, kv):
    rows, cols = pieces.shape[1], pieces.shape[2] // 3
    span = GROUP * rows
    low_flip = pltpu.VMEM((cols, span), BF16)
    block = pl.BlockSpec((QB, cols), lambda j, sc: (j, 0))
    mixed, out, log_total = run_kernel(
        functools.partial(attend_body, docs),
        (span // QB,),
        sc,
        [
            (whole((span, 3 * cols)), pieces.reshape(span, 3 * cols)),
            (whole((span, 2 * cols)), kv.reshape(span, 2 * cols)),
        ],
        [
            (block, shape((span, cols), BF16)),
            (block, shape((span, cols), F32)),
            (pl.BlockSpec((8, QB), lambda j, sc: (0, j)), shape((8, span), F32)),
        ],
        scratch=[low_flip, low_flip, pltpu.VMEM((cols, QB), F32)],
        flops=span * span * cols * 4,
        moved=span * cols * 20,
    )
    return mixed.reshape(GROUP, rows, cols), out, log_total


def pull_step(keys, values, at, first_key, position, start, queries, grads, log_rows, delta, refs):
    k_flip, grad_k, grad_v, grad_q = refs
    scores = masked_scores(keys, queries, first_key, position, start)
    probs = jnp.exp(scores - log_rows)
    grad_probs = dot_last(values, grads)
    grad_scores = (probs * (grad_probs - delta)).astype(BF16)
    grad_v[at, :] += dot(probs.astype(BF16), grads)
    grad_k[at, :] += dot(grad_scores, queries)
    size = grad_q.shape[1]
    for h in range(2):
        rows = slice(h * HEAD_DIM, (h + 1) * HEAD_DIM)
        grad_q[rows, :] += dot(k_flip[rows, at], grad_scores[:, h * size : (h + 1) * size])


def pull_body(
    docs, sc, qkv, grad_mixed, kv, out, log_total, grad_q_out, grad_kv, grad_kv_back,
    k_flip, grad_k, grad_v, k_back_flip, grad_k_back, grad_v_back, grad_q
):
    block = pl.program_id(0)
    span, cols = qkv.shape[0], out.shape[1]
    size = out.shape[0]
    before = sc[1] - span

    @pl.when(block == 0)
    def _():
        for first in range(0, span, PULL_KB):
            k_flip[:, first : first + PULL_KB] = qkv[first : first + PULL_KB, cols : 2 * cols].T
            k_back_flip[:, first : first + PULL_KB] = kv[first : first + PULL_KB, :cols].T
        for total in (grad_k, grad_v, grad_k_back, grad_v_back):
            total[...] = jnp.zeros_like(total)

    grad_q[...] = jnp.zeros_like(grad_q)
    position, start, lowest = query_rows(sc, docs, block, size)
    queries = head_stack(qkv[block_at(block, size), :cols], HEAD_DIM**-0.5)
    grad_rows = grad_mixed[block_at(block, size), :]
    grads = head_stack(grad_rows, 1.0)
    flipped = (grad_rows.astype(F32) * out[...]).T
    heads = [slice(h * HEAD_DIM, (h + 1) * HEAD_DIM) for h in range(2)]
    delta = jnp.concatenate([jnp.sum(flipped[rows, :], 0, keepdims=True) for rows in heads], 1)
    log_rows = jnp.concatenate([log_total[h : h + 1, :] for h in range(2)], 1)

    def step(where, carry):
        at = block_at(where, PULL_KB)
        pull_step(
            qkv[at, cols : 2 * cols], qkv[at, 2 * cols :], at, sc[1] + where * PULL_KB,
            position, start, queries, grads, log_rows, delta, (k_flip, grad_k, grad_v, grad_q),
        )
        return carry

    def step_back(where, carry):
        at = block_at(where, PULL_KB)
        pull_step(
            kv[at, :cols], kv[at, cols:], at, before + where * PULL_KB,
            position, start, queries, grads, log_rows, delta, (k_back_flip, grad_k_back, grad_v_back, grad_q),
        )
        return carry

    last = ((block + 1) * size - 1) // PULL_KB
    lax.fori_loop(jnp.maximum(lowest - sc[1], 0) // PULL_KB, last + 1, step, 0)
    lax.fori_loop(
        jnp.minimum(jnp.maximum(lowest - before, 0), span) // PULL_KB, span // PULL_KB, step_back, 0
    )
    grad_q_out[...] = (grad_q[...] * HEAD_DIM**-0.5).T.astype(BF16)

    @pl.when(block == pl.num_programs(0) - 1)
    def _():
        grad_kv[:, :cols] = grad_k[...].astype(BF16)
        grad_kv[:, cols:] = grad_v[...].astype(BF16)
        grad_kv_back[:, :cols] = grad_k_back[...].astype(BF16)
        grad_kv_back[:, cols:] = grad_v_back[...].astype(BF16)


def attend_pull(sc, docs, pieces, grads, kv, out, log_total):
    rows, cols = pieces.shape[1], pieces.shape[2] // 3
    span = GROUP * rows
    block = pl.BlockSpec((PULL_QB, cols), lambda j, sc: (j, 0))
    both = (whole((span, 2 * cols)), shape((span, 2 * cols), BF16))
    low_flip = pltpu.VMEM((cols, span), BF16)
    high = pltpu.VMEM((span, cols), F32)
    parts = run_kernel(
        functools.partial(pull_body, docs),
        (span // PULL_QB,),
        sc,
        [
            (whole((span, 3 * cols)), pieces.reshape(span, 3 * cols)),
            (whole((span, cols)), grads.reshape(span, cols)),
            (whole((span, 2 * cols)), kv.reshape(span, 2 * cols)),
            (block, out),
            (pl.BlockSpec((8, PULL_QB), lambda j, sc: (0, j)), log_total),
        ],
        [(block, shape((span, cols), BF16)), both, both],
        scratch=[low_flip, high, high, low_flip, high, high, pltpu.VMEM((cols, PULL_QB), F32)],
        flops=span * span * cols * 9,
        moved=span * cols * 30,
    )
    return [part.reshape(GROUP, rows, part.shape[1]) for part in parts]


def swap_tp(value):
    return lax.ppermute(value, "tp", [(0, 1), (1, 0)])


def swap_fsdp(value, s):
    return lax.ppermute(value, "fsdp", [(i, i ^ s) for i in range(lax.axis_size("fsdp"))])


def shift_fsdp(value, by):
    size = lax.axis_size("fsdp")
    return lax.ppermute(value, "fsdp", [(i, i + by) for i in range(size) if 0 <= i + by < size])


def gather(shard):
    return lax.all_gather(shard, "fsdp", axis=0, tiled=True)


def tie(*values):
    return lax.optimization_barrier(values)


def shards(
    tokens,
    cotangent,
    segments,
    doc_batch,
    ln1_gain,
    ln1_bias,
    w_qkv,
    b_qv,
    w_out,
    b_out,
    ln2_gain,
    ln2_bias,
    w_fc,
    b_fc,
    w_proj,
    b_proj,
):
    rows, width = tokens.shape
    depth = w_qkv.shape[1]
    out_cols = w_out.shape[1]
    units = w_fc.shape[2]
    cols = out_cols // GROUP
    docs = doc_batch.shape[0]
    me = lax.axis_index("fsdp")
    total_rows = rows * lax.axis_size("fsdp")

    rest, *packed = pack(w_qkv, b_qv, w_out, w_fc, w_proj)
    rest = gather(rest)
    shards_qkv, bias_qkv = packed[:LAYERS], packed[LAYERS:]

    def rest_at(l):
        first = l * (out_cols + 2 * units)
        return (first, first + out_cols, first + out_cols + units)

    def row(vector):
        return vector.reshape(1, vector.shape[0])

    stored = []
    stream, low_one, full_qkv, doc_tokens, doc_first, pieces, kv_back = first_segment(
        tokens,
        row(ln1_gain[0]),
        row(ln1_bias[0]),
        shards_qkv[0],
        bias_qkv[0],
        segments.reshape(rows // 128, 128),
        docs,
    )
    qkv_of = [full_qkv]
    doc_tokens, doc_first = (value[:, 0].astype(jnp.int32) for value in (doc_tokens, doc_first))
    sc = jnp.concatenate(
        [jnp.stack([me % GROUP, (me // GROUP) * (GROUP * rows)]).astype(jnp.int32), doc_first]
    )
    doc_ids = jnp.arange(docs, dtype=jnp.int32)
    is_doc = segments[:, None] == doc_ids[None, :]
    in_batch = doc_batch[:, None] == jnp.arange(MB, dtype=jnp.int32)[None, :]
    counts = jnp.sum(jnp.where(in_batch, doc_tokens[:, None], 0), 0)
    doc_count = jnp.sum(jnp.where(in_batch, counts[None, :], 0), 1)
    row_count = jnp.sum(jnp.where(is_doc, doc_count[None, :], 0), 1).astype(F32)
    row_weight = total_rows / (MB * row_count)
    for l in range(LAYERS - 1):
        mixed, out, log_total = attend(sc, docs, pieces, kv_back)
        vectors = (b_out[l], ln2_gain[l], ln2_bias[l], b_fc[l], b_proj[l], ln1_gain[l + 1], ln1_bias[l + 1])
        mixed_full, middle, low_two, hidden, act, *later = between_segment(
            mixed,
            stream,
            [row(vector) for vector in vectors],
            bias_qkv[l + 1],
            rest,
            rest_at(l),
            units,
            shards_qkv[l + 1],
        )
        stored.append(
            (stream, low_one, pieces, kv_back, out, log_total, mixed_full, middle, low_two, hidden, act)
        )
        stream, low_one, full_qkv, pieces, kv_back = later
        qkv_of.append(full_qkv)

    l = LAYERS - 1
    mixed, out, log_total = attend(sc, docs, pieces, kv_back)
    grad = cotangent.astype(F32) * row_weight[:, None]
    (
        mixed_full,
        middle,
        low_two,
        act,
        part_two,
        low_proj,
        sum_bproj,
        grad_hidden,
        sum_bfc,
        grad,
        low_out,
        sum_gain_two,
        sum_bias_two,
        sum_bout,
        grad_mixed,
        *feed_parts,
    ) = turn_segment(
        mixed,
        stream,
        grad,
        [row(vector) for vector in (b_out[l], ln2_gain[l], ln2_bias[l], b_fc[l])],
        rest,
        rest_at(l),
        units,
    )
    last = [middle, part_two, swap_tp(part_two), row(b_proj[l])]

    stay0, go0, stay1, go1 = feed_parts
    met0 = swap_fsdp(go0, 2)
    grad_mixed, stay0 = tie(grad_mixed, stay0)
    pulls = attend_pull(sc, docs, pieces, grad_mixed, kv_back, out, log_total)
    *pulls, met0 = tie(*pulls, met0)
    sums_one = [sum_bout, sum_gain_two, sum_bias_two, sum_bfc, sum_bproj]
    low_one_kept, low_out_kept, mixed_kept = low_one, low_out, mixed_full
    (stream_below, low_one, pieces, kv_back, out, log_total, mixed_full, middle, low_two, hidden, act) = stored[0]
    (
        grad_qkv,
        sum_bqkv,
        sum_gain_one,
        sum_bias_one,
        low_proj,
        sum_bproj,
        grad_hidden,
        sum_bfc,
        grad,
        low_out,
        sum_gain_two,
        sum_bias_two,
        sum_bout,
        grad_mixed,
        *later,
    ) = pull_both_segment(
        pulls,
        row(ln1_gain[1]),
        row(ln2_gain[0]),
        qkv_of[1],
        rest,
        rest_at(0),
        units,
        grad,
        stream,
        hidden,
        middle,
        [stay0, met0, stay1, go1],
        [low_two, act],
    )
    feed_totals, near, far, (stay0, go0) = later[:2], later[2], later[3:-2], later[-2:]
    came = []
    others = halving_order(lax.axis_size("fsdp") // GROUP)[1:]
    for other, value in zip(others, far):
        came.append(swap_fsdp(value, GROUP * other))
    met0 = swap_fsdp(go0, 2)
    sums_one = [sum_gain_one, sum_bias_one, sum_bqkv] + sums_one
    pulls = attend_pull(sc, docs, pieces, grad_mixed, kv_back, out, log_total)
    *pulls, came, met0 = tie(*pulls, came, met0)
    sums_zero = [sum_bout, sum_gain_two, sum_bias_two, sum_bfc, sum_bproj]
    grad, small, proj0, qkv1, out1, qkv0, out0 = pull_last_segment(
        pulls,
        row(ln1_gain[0]),
        qkv_of[0],
        grad,
        stream_below,
        [low_one_kept, grad_qkv, low_out_kept, mixed_kept, low_one, low_out, mixed_full],
        [stay0, met0],
        sums_one + sums_zero,
    )
    (
        outputs,
        grad,
        gain1,
        bias1,
        bqv,
        bout,
        gain2,
        bias2,
        bfc,
        bproj,
        grad_wfc,
        grad_wproj,
        grad_wout,
        grad_wqkv,
    ) = finish(
        small, [*feed_totals, qkv1, out1, proj0, qkv0, out0], near, came, [grad, *last], out_cols, units
    )
    grad_wproj = grad_wproj.transpose(0, 2, 1)
    grad_wout = grad_wout.transpose(0, 2, 1)
    grad_wqkv = grad_wqkv.transpose(0, 2, 1, 3)

    return (
        outputs,
        grad,
        gain1,
        bias1,
        grad_wqkv,
        bqv,
        grad_wout,
        bout,
        gain2,
        bias2,
        grad_wfc,
        bfc,
        grad_wproj,
        bproj,
    )


def solution(mesh):
    placed = (
        P("fsdp", None),
        P("fsdp", None),
        P("fsdp"),
        P(),
        P(),
        P(),
        P(None, "fsdp", None, "tp"),
        P(None, None, "tp"),
        P(None, "tp", "fsdp"),
        P(),
        P(),
        P(),
        P(None, "fsdp", "tp"),
        P(None, "tp"),
        P(None, "tp", "fsdp"),
        P(),
    )
    return jax.shard_map(
        shards,
        mesh=mesh,
        in_specs=placed,
        out_specs=(
            P("fsdp", None),
            P("fsdp", None),
            P(),
            P(),
            P(None, "fsdp", None, "tp"),
            P(None, None, "tp"),
            P(None, "tp", "fsdp"),
            P(),
            P(),
            P(),
            P(None, "fsdp", "tp"),
            P(None, "tp"),
            P(None, "tp", "fsdp"),
            P(),
        ),
        check_vma=False,
    )
```

```python
import functools

import jax
import jax.numpy as jnp
from jax import lax
from jax.experimental import pallas as pl
from jax.experimental.pallas import tpu as pltpu
from jax.sharding import PartitionSpec as P

HEAD_DIM = 64
LAYERS = 2
MB = 3
REACH = 4
TAIL = 768

EPS = 1e-05
GROUP = REACH
QB = 512
PULL_QB = 256
LN_ROWS = 128
ACT_ROWS = 128
KB = 512
PULL_KB = 256
NEG = -1e30
F32 = jnp.float32
BF16 = jnp.bfloat16
VMEM_BYTES = 62 * 1024 * 1024
LAST = (((1,), (1,)), ((), ()))
FIRST = (((0,), (0,)), ((), ()))


def dot(left, right):
    return jnp.dot(left, right, preferred_element_type=F32)


def dot_last(left, right):
    return lax.dot_general(left, right, LAST, preferred_element_type=F32)


def shape(dims, dtype):
    return jax.ShapeDtypeStruct(dims, dtype)


def whole(dims):
    return pl.BlockSpec(dims, lambda *_: (0,) * len(dims))


def run_kernel(body, grid, scalars, ins, outs, scratch=(), flops=0, moved=0):
    return pl.pallas_call(
        body,
        grid_spec=pltpu.PrefetchScalarGridSpec(
            num_scalar_prefetch=1,
            grid=grid,
            in_specs=[spec for spec, _ in ins],
            out_specs=[spec for spec, _ in outs],
            scratch_shapes=list(scratch),
        ),
        out_shape=[out for _, out in outs],
        compiler_params=pltpu.CompilerParams(
            vmem_limit_bytes=VMEM_BYTES, dimension_semantics=("arbitrary",) * len(grid)
        ),
        cost_estimate=pl.CostEstimate(flops=flops, bytes_accessed=moved, transcendentals=0),
    )(scalars, *[array for _, array in ins])


def each_rows(count, chunk, body):
    def step(at, carry):
        body(pl.ds(pl.multiple_of(at * chunk, chunk), chunk))
        return carry

    lax.fori_loop(0, count // chunk, step, 0)


def norm_parts(rows):
    centred = rows - jnp.mean(rows, -1, keepdims=True)
    inv_scale = lax.rsqrt(jnp.mean(centred * centred, -1, keepdims=True) + EPS)
    return centred * inv_scale, inv_scale


def norm_pull(grad_rows, unit_rows, inv_scale, gain):
    scaled = grad_rows * gain
    return inv_scale * (
        scaled
        - jnp.mean(scaled, -1, keepdims=True)
        - unit_rows * jnp.mean(scaled * unit_rows, -1, keepdims=True)
    )


def eight_rows(rows):
    return jnp.sum(rows.reshape(rows.shape[0] // 8, 8, rows.shape[1]), 0)


def gelu_rows(value):
    return 0.5 * value * (1.0 + jnp.tanh(0.7978845608028654 * (value + 0.044715 * value * value * value)))


def gelu_slope(value):
    square = value * value
    top = jnp.tanh(0.7978845608028654 * (value + 0.044715 * square * value))
    inner = 0.7978845608028654 * (1.0 + 3.0 * 0.044715 * square)
    return 0.5 * (1.0 + top) + 0.5 * value * (1.0 - top * top) * inner


def norm_pull_rows(at, grad, own, got, inputs, gain, grad_new, sum_gain, sum_bias):
    grad_rows = own[at, :].astype(F32) + got[at, :].astype(F32)
    unit, inv_scale = norm_parts(inputs[at, :])
    value = grad[at, :] + norm_pull(grad_rows, unit, inv_scale, gain[...])
    grad_new[at, :] = value
    sum_gain[...] += eight_rows(grad_rows * unit)
    sum_bias[...] += eight_rows(grad_rows)
    return value


CHUNK = [256]
SIZES = (256, 128, 256, 128, 256)
MESH = pl.DeviceIdType.MESH


class Links:
    def __init__(self, send, recv):
        self.send, self.recv, self.used = send, recv, 0
        self.me = lax.axis_index("fsdp")
        self.place = lax.rem(self.me, GROUP)
        self.group = self.me // GROUP
        self.groups = lax.axis_size("fsdp") // GROUP
        self.other = 1 - lax.axis_index("tp")

    def peer(self, s):
        return {"fsdp": self.group * GROUP + (self.place ^ s)}

    def beyond(self, by, s):
        return {"fsdp": lax.rem(self.group + by, self.groups) * GROUP + (self.place ^ s)}

    def copy(self, source, target, device):
        at = self.used
        self.used += 1
        return pltpu.make_async_remote_copy(
            src_ref=source,
            dst_ref=target,
            send_sem=self.send.at[at],
            recv_sem=self.recv.at[at],
            device_id=device,
            device_id_type=MESH,
        )

    def swap(self, source, target):
        return self.copy(source, target, {"tp": self.other})

    def greet(self, devices):
        barrier = pltpu.get_barrier_semaphore()
        for device in devices:
            pl.semaphore_signal(barrier, inc=1, device_id=device, device_id_type=MESH)
        pl.semaphore_wait(barrier, len(devices))


def columns(place, cols):
    return pl.ds(pl.multiple_of(place * cols, cols), cols)


def tiles(count, size, body):
    def step(at, carry):
        body(pl.ds(pl.multiple_of(at * size, size), size))
        return carry

    lax.fori_loop(0, count // size, step, 0)


def rows_within(first, body):
    def step(at, carry):
        body(pl.ds(pl.multiple_of(first + at * LN_ROWS, LN_ROWS), LN_ROWS))
        return carry

    lax.fori_loop(0, CHUNK[0] // LN_ROWS, step, 0)


def out_rows(rows, mixed, w, target):
    def tile(at):
        target[rows, at] = dot_last(mixed[rows, :], w[at, :]).astype(BF16)

    tiles(w.shape[0], 256, tile)


def norm_rows(first, base, sums, gain, bias, stream, low):
    def body(at):
        value = base[at, :].astype(F32)
        if sums is not None:
            own, got, badd = sums
            value = value + (own[at, :].astype(F32) + got[at, :].astype(F32)) + badd[...]
        stream[at, :] = value
        unit, _ = norm_parts(value)
        low[at, :] = (unit * gain[...] + bias[...]).astype(BF16)

    rows_within(first, body)


def feed_rows(rows, low, fc, bfc, hidden, act, proj, target):
    def tile(at):
        value = dot(low[rows, :], fc[:, at]) + bfc[:, at]
        hidden[rows, at] = value
        act[rows, at] = gelu_rows(value).astype(BF16)

    tiles(fc.shape[1], 512, tile)

    def tile_out(at):
        target[rows, at] = dot_last(act[rows, :], proj[at, :]).astype(BF16)

    tiles(proj.shape[0], 256, tile_out)


def send_qkv(links, low, w, bq, ready, pieces, kv_back, kept):
    cols = bq.shape[1] // GROUP
    copies = []
    order = (2, 3, 1, 0)
    chunks = low.shape[0] // CHUNK[0]
    for c in range(chunks):
        rows = pl.ds(c * CHUNK[0], CHUNK[0])
        across = {
            s: links.copy(ready.at[s, rows], pieces.at[links.place, rows], links.peer(s)) for s in order if s
        }
        onward = {
            s: links.copy(
                ready.at[s, rows, pl.ds(cols // 3, 2 * cols // 3)],
                kv_back.at[links.place, rows],
                links.beyond(1, s),
            )
            for s in order
        }
        own = pltpu.make_async_copy(ready.at[0, rows], pieces.at[links.place, rows], kept.at[c])
        copies.append((across, onward, own))
    last = links.group == links.groups - 1

    def start(c):
        rows = pl.ds(c * CHUNK[0], CHUNK[0])
        across, onward, own = copies[c]
        for s in order:
            at = columns(links.place ^ s, cols)
            ready[s, rows, :] = (dot(low[rows, :], w[:, at]) + bq[:, at]).astype(BF16)
            if s:
                across[s].start()
            else:
                own.start()

            @pl.when(jnp.logical_not(last))
            def _():
                onward[s].start()

    def finish():
        for across, onward, own in copies:
            own.wait()
            for s in order:
                if s:
                    across[s].wait()

                @pl.when(jnp.logical_not(last))
                def _():
                    onward[s].wait_send()

                @pl.when(links.group > 0)
                def _():
                    onward[s].wait_recv()

    return start, finish


def qkv_copies(rows):
    return rows // CHUNK[0] * (2 * GROUP - 1)


class ShardGather:
    def __init__(self, links, shard, full):
        self.depth = shard.shape[0]
        self.links, self.shard, self.full = links, shard, full
        self.steps, held = [], [0]
        bit = links.groups // 2
        while bit:
            device = {"fsdp": (links.group ^ bit) * GROUP + links.place}
            self.steps.append({block: self.relay(block, 0, device) for block in held})
            held = held + [block ^ bit for block in held]
            bit //= 2
        self.held = held
        self.over_x = {block: self.relay(block, 0, links.peer(2)) for block in held}
        self.over_core = [
            {block: self.relay(block, s, links.peer(1)) for block in held} for s in (0, 2)
        ]

    def rows(self, block, s):
        owner = (self.links.group ^ block) * GROUP + (self.links.place ^ s)
        return pl.ds(pl.multiple_of(owner * self.depth, self.depth), self.depth)

    def relay(self, block, s, device):
        rows = self.rows(block, s)
        own = block == 0 and s == 0
        return self.links.copy(self.shard if own else self.full.at[rows], self.full.at[rows], device)

    def spread(self, block, step):
        for later in self.steps[step:]:
            later[block].start()
        self.over_x[block].start()
        self.over_core[0][block].start()

    def start(self):
        self.spread(0, 0)
        self.full[self.rows(0, 0), :] = self.shard[...]

    def pass_x(self):
        bit = self.links.groups // 2
        for step, copies in enumerate(self.steps):
            for block, one in copies.items():
                one.wait_recv()
                self.spread(block ^ bit, step + 1)
            bit //= 2

    def pass_core(self):
        for block in self.held:
            self.over_x[block].wait_recv()
            self.over_core[1][block].start()

    def arrive(self):
        for copies in self.over_core:
            for one in copies.values():
                one.wait_recv()

    def finish(self):
        for copies in (*self.steps, self.over_x, *self.over_core):
            for one in copies.values():
                one.wait_send()


def gather_copies():
    groups = lax.axis_size("fsdp") // GROUP
    return 4 * groups - 1


class RowSum:
    def __init__(self, links, held, came, far):
        self.held, self.came, self.far = held, came, far
        self.near = [links.copy(held.at[i], came.at[i], links.peer(i + 1)) for i in range(2)]
        self.along = [
            links.copy(held.at[2], far.at[onward - 1], links.beyond(onward, 0))
            for onward in range(1, links.groups)
        ]

    def step(self, i):
        self.near[i].wait()
        self.held[i + 1] = self.held[i] + self.came[i]

    def finish(self):
        total = self.held[2]
        for at, one in enumerate(self.along):
            one.wait()
            total = total + self.far[at]
        return total


def count_docs(segments, counts):
    for d in range(counts.shape[0]):
        found = jnp.where(segments[...] == d, 1.0, 0.0).astype(F32)
        total = jnp.sum(jnp.sum(found, 0, keepdims=True), 1, keepdims=True)
        counts[d : d + 1, :] = jnp.broadcast_to(total, (1, counts.shape[1]))


def first_body(
    base, gain, bias, shard, bq, segments, stream, low, w, tokens, first, pieces, kv_back,
    ready, held, came, far, send, recv, kept, flush
):
    links = Links(send, recv)
    gathered = ShardGather(links, shard, w)
    counted = RowSum(links, held, came, far)
    start, finish = send_qkv(links, low, w, bq, ready, pieces, kv_back, kept)
    count_docs(segments, held.at[0])
    links.greet(
        [links.peer(s) for s in range(1, GROUP)]
        + [links.beyond(1, s) for s in range(GROUP)]
        + [links.beyond(links.groups - 1, s) for s in range(GROUP)]
        + group_greets(links)
    )
    gathered.start()
    counted.near[0].start()
    chunks = base.shape[0] // CHUNK[0]
    for c in range(chunks):
        norm_rows(c * CHUNK[0], base, None, gain, bias, stream, low)
    flush(0, 1)
    counted.step(0)
    counted.near[1].start()
    gathered.pass_x()
    counted.step(1)
    for one in counted.along:
        one.start()
    gathered.pass_core()
    gathered.arrive()
    flush(2)
    for c in range(chunks):
        start(c)
    total = counted.finish()
    tokens[...] = total
    begin = jnp.zeros((1, total.shape[1]), F32)
    for d in range(total.shape[0]):
        first[d : d + 1, :] = begin
        begin = begin + total[d : d + 1, :]
    gathered.finish()
    finish()


ANY = pl.BlockSpec(memory_space=pl.ANY)
VMEM = pl.BlockSpec(memory_space=pltpu.VMEM)


def run_links(body, name, ins, outs, scratch, flops, moved, late=()):
    def with_flush(*refs):
        n_in, n_out = len(ins), len(outs)
        given = refs[:n_in]
        held = list(refs[n_in : n_in + n_out])
        rest = refs[n_in + n_out : len(refs) - len(late) - 1]
        twins, done = refs[len(refs) - len(late) - 1 : -1], refs[-1]
        copies = {}
        for i, (at, twin) in enumerate(zip(late, twins)):
            copies[at] = pltpu.make_async_copy(twin, held[at], done.at[i])
            held[at] = twin
        started = []

        def flush(*which):
            for at in which:
                copies[at].start()
                started.append(at)

        body(*given, *held, *rest, flush=flush)
        flush(*[at for at in late if at not in started])
        for at in late:
            copies[at].wait()

    twins = [pltpu.VMEM(outs[at][1].shape, outs[at][1].dtype) for at in late]
    twins.append(pltpu.SemaphoreType.DMA((max(1, len(late)),)))
    return pl.pallas_call(
        with_flush,
        in_specs=[spec for spec, _ in ins],
        out_specs=[ANY if at in late else spec for at, (spec, _) in enumerate(outs)],
        out_shape=[out for _, out in outs],
        scratch_shapes=list(scratch) + twins,
        compiler_params=pltpu.CompilerParams(
            vmem_limit_bytes=VMEM_BYTES, collective_id=name, has_side_effects=True
        ),
        cost_estimate=pl.CostEstimate(flops=flops, bytes_accessed=moved, transcendentals=0),
    )(*[array for _, array in ins])


def first_segment(base, gain, bias, shard, bq, segments, docs):
    CHUNK[0] = SIZES[0]
    rows, width = base.shape
    total = bq.shape[1]
    cols = total // GROUP
    groups = lax.axis_size("fsdp") // GROUP
    copies = pltpu.SemaphoreType.DMA((qkv_copies(rows) + gather_copies() + groups + 1,))
    counts = (VMEM, shape((docs, 128), F32))
    return run_links(
        first_body,
        0,
        [(VMEM, array) for array in (base, gain, bias, shard, bq, segments)],
        [
            (VMEM, shape((rows, width), F32)),
            (VMEM, shape((rows, width), BF16)),
            (VMEM, shape((width, total), BF16)),
            counts,
            counts,
            (ANY, shape((GROUP, rows, cols), BF16)),
            (ANY, shape((GROUP, rows, 2 * cols // 3), BF16)),
        ],
        [
            pltpu.VMEM((GROUP, rows, cols), BF16),
            pltpu.VMEM((3, docs, 128), F32),
            pltpu.VMEM((2, docs, 128), F32),
            pltpu.VMEM((groups - 1, docs, 128), F32),
            copies,
            copies,
            pltpu.SemaphoreType.DMA((rows // CHUNK[0],)),
        ],
        flops=2 * rows * width * total,
        moved=rows * width * 8 + width * total * 2,
        late=(0, 1, 2),
    )


def trade_mixed(links, mixed_all, mixed):
    cols = mixed_all.shape[2]
    copies = []
    for c in range(mixed.shape[0] // CHUNK[0]):
        rows = pl.ds(c * CHUNK[0], CHUNK[0])
        copies.append(
            [
                links.copy(
                    mixed_all.at[links.place ^ s, rows],
                    mixed.at[rows, columns(links.place, cols)],
                    links.peer(s),
                )
                for s in (2, 3, 1)
            ]
        )

    def start():
        for chunk in copies:
            for one in chunk:
                one.start()
        mixed[:, columns(links.place, cols)] = mixed_all[links.place]

    def wait(c):
        for one in copies[c]:
            one.wait_recv()

    def finish():
        for chunk in copies:
            for one in chunk:
                one.wait_send()

    return start, wait, finish


def between_body(
    at, mixed_all, base, bout, gain_two, bias_two, bfc, bproj, gain, bias, bq, rest, shard,
    mixed, middle, low_two, hidden, act, stream, low, w_qkv, pieces, kv_back,
    w_out, w_fc, w_proj, part, got, part_two, got_two, ready, send, recv, load, kept, flush
):
    out_at, fc_at, proj_at = at
    links = Links(send, recv)
    loads = [
        pltpu.make_async_copy(source.at[:, pl.ds(start, target.shape[1])], target, load.at[i])
        for i, (source, start, target) in enumerate(
            ((rest, out_at, w_out), (rest, fc_at, w_fc), (rest, proj_at, w_proj))
        )
    ]
    for one in loads:
        one.start()
    links.greet(
        [links.peer(s) for s in range(1, GROUP)]
        + [links.beyond(1, s) for s in range(GROUP)]
        + [links.beyond(links.groups - 1, s) for s in range(GROUP)]
        + [{"tp": links.other}]
        + group_greets(links)
    )
    total = bq.shape[1]
    gathered, tail = (
        ShardGather(links, shard.at[:, place], w_qkv.at[:, place])
        for place in (pl.ds(0, total), pl.ds(total, TAIL))
    )
    chunks = [pl.ds(c * CHUNK[0], CHUNK[0]) for c in range(base.shape[0] // CHUNK[0])]
    start_mixed, wait_mixed, finish_mixed = trade_mixed(links, mixed_all, mixed)
    swaps = [links.swap(part.at[rows], got.at[rows]) for rows in chunks]
    swaps_two = [links.swap(part_two.at[rows], got_two.at[rows]) for rows in chunks]
    start_qkv, finish_qkv = send_qkv(links, low, w_qkv, bq, ready, pieces, kv_back, kept)
    start_mixed()
    gathered.start()
    tail.start()
    loads[0].wait()
    for c, rows in enumerate(chunks):
        wait_mixed(c)
        out_rows(rows, mixed, w_out, part)
        swaps[c].start()
    loads[1].wait()
    loads[2].wait()
    for c, rows in enumerate(chunks):
        swaps[c].wait()
        norm_rows(c * CHUNK[0], base, (part, got, bout), gain_two, bias_two, middle, low_two)
        feed_rows(rows, low_two, w_fc, bfc, hidden, act, w_proj, part_two)
        swaps_two[c].start()
        if c == 0:
            gathered.pass_x()
        if c == 1:
            tail.pass_x()
    gathered.pass_core()
    flush(0, 1, 2, 3, 4)
    gathered.arrive()
    for c, rows in enumerate(chunks):
        swaps_two[c].wait()
        norm_rows(c * CHUNK[0], middle, (part_two, got_two, bproj), gain, bias, stream, low)
        start_qkv(c)
        if c == 1:
            tail.pass_core()
    tail.arrive()
    flush(7)
    finish_mixed()
    gathered.finish()
    tail.finish()
    finish_qkv()


def between_segment(mixed_all, base, vectors, bq, rest, at, units, shard):
    CHUNK[0] = SIZES[1]
    rows, width = base.shape
    total = bq.shape[1]
    cols = total // GROUP
    out_cols = at[1] - at[0]
    chunks = rows // CHUNK[0]
    copies = pltpu.SemaphoreType.DMA((qkv_copies(rows) + chunks * (GROUP - 1) + 2 * chunks + 2 * gather_copies(),))
    whole_f32 = (VMEM, shape((rows, width), F32))
    whole_low = (VMEM, shape((rows, width), BF16))
    return run_links(
        functools.partial(between_body, at),
        1,
        [(VMEM, mixed_all), (VMEM, base)]
        + [(VMEM, vector) for vector in vectors]
        + [(VMEM, bq), (ANY, rest), (VMEM, shard)],
        [
            (VMEM, shape((rows, out_cols), BF16)),
            whole_f32,
            whole_low,
            (VMEM, shape((rows, units), F32)),
            (VMEM, shape((rows, units), BF16)),
            whole_f32,
            whole_low,
            (VMEM, shape((width, shard.shape[1]), BF16)),
            (ANY, shape((GROUP, rows, cols), BF16)),
            (ANY, shape((GROUP, rows, 2 * cols // 3), BF16)),
        ],
        [
            pltpu.VMEM((width, out_cols), BF16),
            pltpu.VMEM((width, units), BF16),
            pltpu.VMEM((width, units), BF16),
        ]
        + [pltpu.VMEM((rows, width), BF16)] * 4
        + [
            pltpu.VMEM((GROUP, rows, cols), BF16),
            copies,
            copies,
            pltpu.SemaphoreType.DMA((3,)),
            pltpu.SemaphoreType.DMA((chunks,)),
        ],
        flops=2 * rows * width * (total + out_cols + 2 * units),
        moved=rows * width * 20 + rows * units * 6 + width * (total + out_cols + 2 * units) * 2,
        late=tuple(range(8)),
    )


def pull_qkv_rows(first, back, links, full, back_got, w, target, sums):
    cols = full.shape[1] // GROUP
    rows = pl.ds(first, CHUNK[0])

    @pl.when(links.group < links.groups - 1)
    def _():
        for s in range(GROUP):
            at = pl.ds(
                pl.multiple_of((links.place ^ s) * cols + cols // 3, cols // 3), 2 * cols // 3
            )
            full[rows, at] = (full[rows, at].astype(F32) + back_got[s, rows].astype(F32)).astype(BF16)

    def tile(at):
        target[rows, at] = dot_last(full[rows, :], w[at, :]).astype(BF16)

    tiles(w.shape[0], 256, tile)

    def body(at):
        sums[...] += eight_rows(full[at, :].astype(F32))

    rows_within(first, body)


def trade_pulls(links, grad_q, grad_kv, grad_kv_back, full, back_got):
    part = grad_q.shape[2]
    copies = []
    for c in range(full.shape[0] // CHUNK[0]):
        rows = pl.ds(c * CHUNK[0], CHUNK[0])
        across, back = [], []
        for s in (2, 3, 1):
            for source, start, size in ((grad_kv, part, 2 * part), (grad_q, 0, part)):
                at = pl.ds(pl.multiple_of(links.place * 3 * part + start, part), size)
                across.append(
                    links.copy(source.at[links.place ^ s, rows], full.at[rows, at], links.peer(s))
                )
        for s in (2, 3, 1, 0):
            back.append(
                links.copy(
                    grad_kv_back.at[links.place ^ s, rows],
                    back_got.at[s, rows],
                    links.beyond(links.groups - 1, s),
                )
            )
        copies.append((across, back))

    def start():
        for across, back in copies:
            for one in across:
                one.start()

            @pl.when(links.group > 0)
            def _():
                for one in back:
                    one.start()

        first = pl.multiple_of(links.place * 3 * part, part)
        full[:, pl.ds(first, part)] = grad_q[links.place]
        full[:, pl.ds(pl.multiple_of(first + part, part), 2 * part)] = grad_kv[links.place]

    def wait(c):
        across, back = copies[c]
        for one in across:
            one.wait_recv()

        @pl.when(links.group < links.groups - 1)
        def _():
            for one in back:
                one.wait_recv()

    def finish():
        for across, back in copies:
            for one in across:
                one.wait_send()

            @pl.when(links.group > 0)
            def _():
                for one in back:
                    one.wait_send()

    return start, wait, finish


def pull_copies(rows):
    return rows // CHUNK[0] * (2 * (GROUP - 1) + GROUP)


def pull_norm_rows(first, grad, own, got, inputs, gain, grad_new, sums, low=None):
    def body(at):
        value = norm_pull_rows(at, grad, own, got, inputs, gain, grad_new, sums[0], sums[1])
        if low is not None:
            value = value.astype(BF16)
            low[at, :] = value
            sums[2][...] += eight_rows(value.astype(F32))

    rows_within(first, body)


def round_rows(first, grad, low, sums):
    def body(at):
        value = grad[at, :].astype(BF16)
        low[at, :] = value
        sums[...] += eight_rows(value.astype(F32))

    rows_within(first, body)


def pull_feed_rows(rows, low, proj, hidden, held, grad_hidden, sums, fc, target):
    def tile(at):
        value = dot(low[rows, :], proj[:, at]) * gelu_slope(hidden[held, at])
        value = value.astype(BF16)
        grad_hidden[rows, at] = value
        sums[:, at] += eight_rows(value.astype(F32))

    tiles(proj.shape[1], 512, tile)

    def tile_out(at):
        target[rows, at] = dot_last(grad_hidden[rows, :], fc[at, :]).astype(BF16)

    tiles(fc.shape[0], 256, tile_out)


def send_mixed_pull(links, low, w, ready, pieces, kept):
    cols = ready.shape[2]
    copies = []
    for c in range(low.shape[0] // CHUNK[0]):
        rows = pl.ds(c * CHUNK[0], CHUNK[0])
        across = {
            s: links.copy(ready.at[s, rows], pieces.at[links.place, rows], links.peer(s))
            for s in range(1, GROUP)
        }
        own = pltpu.make_async_copy(ready.at[0, rows], pieces.at[links.place, rows], kept.at[c])
        copies.append((across, own))

    def start(c):
        rows = pl.ds(c * CHUNK[0], CHUNK[0])
        across, own = copies[c]
        for s in (2, 3, 1, 0):
            at = columns(links.place ^ s, cols)
            ready[s, rows, :] = dot(low[rows, :], w[:, at]).astype(BF16)
            (across[s] if s else own).start()

    def finish():
        for across, own in copies:
            own.wait()
            for one in across.values():
                one.wait()

    return start, finish


def load_columns(plan, load):
    copies = []
    for i, (source, start, target) in enumerate(plan):
        if start is not None:
            source = source.at[:, pl.ds(start, target.shape[1])]
        copies.append(pltpu.make_async_copy(source, target, load.at[i]))
    for one in copies:
        one.start()
    return copies


def turn_body(
    at, mixed_all, base_in, grad_in, bout, gain_two, bias_two, bfc, rest, last,
    mixed, middle, low_two, act, part_two, low_proj, sum_proj, grad_hidden, sum_fc, grad_new, low_out,
    sum_gain, sum_bias, sum_out, pieces, stay0, go0, stay1, go1,
    w_out, w_fc, w_proj, base, grad, hidden, part, got, part_three, got_three, ready,
    plain, flipped, away0, away1, met0, met1, send, recv, load, kept, flush
):
    out_at, fc_at, proj_at = at
    links = Links(send, recv)
    loads = load_columns(
        (
            (rest, out_at, w_out),
            (base_in, None, base),
            (grad_in, None, grad),
            (rest, fc_at, w_fc),
            (rest, proj_at, w_proj.at[:, pl.ds(0, w_proj.shape[1] - TAIL)]),
            (last, last.shape[1] - TAIL, w_proj.at[:, pl.ds(w_proj.shape[1] - TAIL, TAIL)]),
        ),
        load,
    )
    links.greet([links.peer(s) for s in range(1, GROUP)] + [{"tp": links.other}])
    chunks = [pl.ds(c * CHUNK[0], CHUNK[0]) for c in range(base.shape[0] // CHUNK[0])]
    start_mixed, wait_mixed, finish_mixed = trade_mixed(links, mixed_all, mixed)
    swaps = [links.swap(part.at[rows], got.at[rows]) for rows in chunks]
    swaps_three = [links.swap(part_three.at[rows], got_three.at[rows]) for rows in chunks]
    start_pull, finish_pull = send_mixed_pull(links, low_out, w_out, ready, pieces, kept)
    core_sums = (
        CoreSum(links, stay0, go0, away0, met0),
        CoreSum(links, stay1, go1, away1, met1),
    )
    start_mixed()
    for total in (sum_proj, sum_fc, sum_gain, sum_bias, sum_out):
        total[...] = jnp.zeros_like(total)
    loads[0].wait()
    for c, rows in enumerate(chunks):
        wait_mixed(c)
        out_rows(rows, mixed, w_out, part)
        swaps[c].start()
    for one in loads[1:]:
        one.wait()
    for c in range(len(chunks)):
        round_rows(c * CHUNK[0], grad, low_proj, sum_proj)
    for c, rows in enumerate(chunks):
        swaps[c].wait()
        norm_rows(c * CHUNK[0], base, (part, got, bout), gain_two, bias_two, middle, low_two)

        def tile(at):
            value = dot(low_two[rows, :], w_fc[:, at]) + bfc[:, at]
            hidden[rows, at] = value
            act[rows, at] = gelu_rows(value).astype(BF16)

        tiles(w_fc.shape[1], 512, tile)
        pull_feed_rows(
            rows, low_proj, w_proj, hidden, rows, grad_hidden, sum_fc, w_fc, part_three
        )
        swaps_three[c].start()
    flush(0, 1, 2, 3, 5, 7)
    core_sums[0].multiply(low_two, grad_hidden, plain, flipped)
    core_sums[1].multiply(low_proj, act, plain, flipped)
    for rows in chunks:

        def tile_out(at):
            part_two[rows, at] = dot_last(act[rows, :], w_proj[at, :]).astype(BF16)

        tiles(w_proj.shape[0], 256, tile_out)
    flush(4)
    for c, rows in enumerate(chunks):
        swaps_three[c].wait()
        pull_norm_rows(
            c * CHUNK[0], grad, part_three, got_three, middle, gain_two, grad_new, (sum_gain, sum_bias, sum_out), low_out
        )
        start_pull(c)
    for one in core_sums:
        one.add()
    finish_mixed()
    finish_pull()


def turn_segment(mixed_all, base, grad, vectors, rest, last, at, units):
    CHUNK[0] = SIZES[2]
    rows, width = base.shape
    out_cols = at[1] - at[0]
    cols = out_cols // GROUP
    chunks = rows // CHUNK[0]
    copies = pltpu.SemaphoreType.DMA((2 * chunks * (GROUP - 1) + 2 * chunks + 2,))
    high = (VMEM, shape((rows, width), F32))
    low = (VMEM, shape((rows, width), BF16))
    sums = (VMEM, shape((8, width), F32))
    return run_links(
        functools.partial(turn_body, at),
        2,
        [(VMEM, mixed_all), (ANY, base), (ANY, grad)]
        + [(VMEM, vector) for vector in vectors]
        + [(ANY, rest), (ANY, last)],
        [
            (VMEM, shape((rows, out_cols), BF16)),
            high,
            low,
            (VMEM, shape((rows, units), BF16)),
            low,
            low,
            sums,
            (VMEM, shape((rows, units), BF16)),
            (VMEM, shape((8, units), F32)),
            high,
            low,
            sums,
            sums,
            sums,
            (ANY, shape((GROUP, rows, cols), BF16)),
        ]
        + [(VMEM, shape((width // 4, units), BF16))] * 4,
        [
            pltpu.VMEM((width, out_cols), BF16),
            pltpu.VMEM((width, units), BF16),
            pltpu.VMEM((width, units), BF16),
            pltpu.VMEM((rows, width), F32),
            pltpu.VMEM((rows, width), F32),
            pltpu.VMEM((rows, units), F32),
        ]
        + [pltpu.VMEM((rows, width), BF16)] * 4
        + [
            pltpu.VMEM((GROUP, rows, cols), BF16),
        ]
        + [pltpu.VMEM((width, rows), BF16)] * 2
        + [pltpu.VMEM((width // 2, units), BF16)] * 4
        + [
            copies,
            copies,
            pltpu.SemaphoreType.DMA((6,)),
            pltpu.SemaphoreType.DMA((chunks,)),
        ],
        flops=2 * rows * width * (2 * out_cols + 4 * units),
        moved=rows * width * 22 + rows * units * 4 + width * (out_cols + 2 * units) * 2,
        late=(0, 1, 2, 3, 4, 5, 7, 9, 10, 15, 16, 17, 18),
    )


def pull_both_body(
    at, grad_q, grad_kv, grad_kv_back, gain, gain_two, qkv, rest, grad_in, stream_in, hidden_in, middle_in,
    stay0_in, met0_in, stay1_in, go1, low_two_in, act_in,
    full, sum_qkv, sum_gain_one, sum_bias_one, low_proj, sum_proj, grad_hidden, sum_fc, grad_new, low_out,
    sum_gain, sum_bias, sum_out, pieces, total0, total1, near2, *refs, flush
):
    groups = lax.axis_size("fsdp") // GROUP
    far2, (stay3, go3), refs = refs[: groups - 1], refs[groups - 1 : groups + 1], refs[groups + 1 :]
    (w_qkv, w_out, w_fc, w_proj, grad, stream, hidden, back_got, part, got, part_two, got_two, ready,
    stay0, met0, far0, came0, stay1, met1, far1, came1,
    left, wide, plain, flipped, stay2, go2, met2, away, gone2, gone3, send, recv, load, kept) = refs
    out_at, fc_at, proj_at = at
    links = Links(send, recv)
    loads = load_columns(
        (
            (qkv, 0, w_qkv),
            (grad_in, None, grad),
            (stream_in, None, stream),
            (rest, proj_at, w_proj),
            (hidden_in.at[pl.ds(0, CHUNK[0])], None, hidden),
            (rest, fc_at, w_fc),
            (rest, out_at, w_out),
            (stay0_in, None, stay0),
            (met0_in, None, met0),
            (stay1_in, None, stay1),
            (low_two_in, None, left),
            (act_in, None, wide),
        ),
        load,
    )
    middle = stream
    load_middle = pltpu.make_async_copy(middle_in, middle, load.at[len(loads)])
    links.greet(
        [links.peer(s) for s in range(1, GROUP)]
        + [links.beyond(1, s) for s in range(GROUP)]
        + [links.beyond(links.groups - 1, s) for s in range(GROUP)]
        + [{"tp": links.other}]
        + group_greets(links)
    )
    chunks = [pl.ds(c * CHUNK[0], CHUNK[0]) for c in range(grad.shape[0] // CHUNK[0])]
    start_pulls, wait_pulls, finish_pulls = trade_pulls(
        links, grad_q, grad_kv, grad_kv_back, full, back_got
    )
    swaps = [links.swap(part.at[rows], got.at[rows]) for rows in chunks]
    swaps_two = [links.swap(part_two.at[rows], got_two.at[rows]) for rows in chunks]
    start_pull, finish_pull = send_mixed_pull(links, low_out, w_out, ready, pieces, kept)
    late_x = links.copy(go1, met1, links.peer(2))
    group_sums = (
        GroupSum(links, stay0, met0, far0, came0, total0),
        GroupSum(links, stay1, met1, far1, came1, total1),
    )
    core_sums = (
        CoreSum(links, stay2, go2, away, gone2),
        CoreSum(links, stay3, go3, away, gone3),
    )
    feed_x = links.copy(go2, met2, links.peer(2))
    start_pulls()
    for total in (sum_qkv, sum_gain_one, sum_bias_one, sum_proj, sum_fc, sum_gain, sum_bias, sum_out):
        total[...] = jnp.zeros_like(total)
    for one in loads:
        one.wait()
    for c, rows in enumerate(chunks):
        wait_pulls(c)
        if c == len(chunks) // 2:
            late_x.start()
            group_sums[0].send(0)
        pull_qkv_rows(c * CHUNK[0], None, links, full, back_got, w_qkv, part, sum_qkv)
        swaps[c].start()
    flush(0)
    for c, rows in enumerate(chunks):
        swaps[c].wait()
        pull_norm_rows(
            c * CHUNK[0], grad, part, got, stream, gain, grad_new, (sum_gain_one, sum_bias_one)
        )
        if c == len(chunks) - 1:
            load_middle.start()
        round_rows(c * CHUNK[0], grad_new, low_proj, sum_proj)
        if c:
            load_hidden.wait()
        pull_feed_rows(
            rows, low_proj, w_proj, hidden, pl.ds(0, CHUNK[0]), grad_hidden, sum_fc, w_fc, part_two
        )
        swaps_two[c].start()
        if c + 1 < len(chunks):
            load_hidden = pltpu.make_async_copy(
                hidden_in.at[pl.ds((c + 1) * CHUNK[0], CHUNK[0])], hidden, load.at[len(loads) + 1 + c]
            )
            load_hidden.start()
    flush(4, 6)
    core_sums[0].multiply(left, grad_hidden, plain, flipped)
    load_middle.wait()
    for c, rows in enumerate(chunks):
        swaps_two[c].wait()
        pull_norm_rows(
            c * CHUNK[0], grad_new, part_two, got_two, middle, gain_two, grad_new, (sum_gain, sum_bias, sum_out), low_out
        )
        start_pull(c)
        if c == 0:
            core_sums[0].add()
            feed_x.start()
            late_x.wait()
            group_sums[1].send(0)
            group_sums[0].pass_on(0)
            core_sums[1].multiply(low_proj, wide, plain, flipped)
    group_sums[1].pass_on(0)
    core_sums[1].add()
    feed_x.wait()
    add_slots(stay2, met2, (near2, *far2))
    finish_pulls()
    finish_pull()
    for one in group_sums:
        one.finish(2)


def pull_both_segment(pulls, gain, gain_two, qkv, rest, at, units, grad, stream, hidden, middle, sums_in, factors):
    CHUNK[0] = SIZES[3]
    rows, width = grad.shape
    out_cols = at[1] - at[0]
    cols = out_cols // GROUP
    total = 3 * out_cols
    chunks = rows // CHUNK[0]
    groups = lax.axis_size("fsdp") // GROUP
    stay = sums_in[0]
    copies = pltpu.SemaphoreType.DMA((pull_copies(rows) + chunks * (GROUP - 1) + 2 * chunks + 2 * groups + 2,))
    high = (VMEM, shape((rows, width), F32))
    low = (VMEM, shape((rows, width), BF16))
    sums = (VMEM, shape((8, width), F32))
    return run_links(
        functools.partial(pull_both_body, at),
        3,
        [(VMEM, pull) for pull in pulls]
        + [(VMEM, gain), (VMEM, gain_two)]
        + [(ANY, array) for array in (qkv, rest, grad, stream, hidden, middle)]
        + [(ANY, array) for array in (*sums_in, *factors)],
        [
            (VMEM, shape((rows, total), BF16)),
            (VMEM, shape((8, total), F32)),
            sums,
            sums,
            low,
            sums,
            (VMEM, shape((rows, units), BF16)),
            (VMEM, shape((8, units), F32)),
            high,
            low,
            sums,
            sums,
            sums,
            (ANY, shape((GROUP, rows, cols), BF16)),
        ]
        + [(VMEM, shape((stay.shape[0] // groups, stay.shape[1]), F32))] * 2
        + [(VMEM, shape((width // 4 // groups, units), F32))]
        + [(VMEM, shape((width // 4 // groups, units), BF16))] * (groups - 1)
        + [(VMEM, shape((width // 4, units), BF16))] * 2,
        [
            pltpu.VMEM((width, total), BF16),
            pltpu.VMEM((width, out_cols), BF16),
            pltpu.VMEM((width, units), BF16),
            pltpu.VMEM((width, units), BF16),
            pltpu.VMEM((rows, width), F32),
            pltpu.VMEM((rows, width), F32),
            pltpu.VMEM((CHUNK[0], units), F32),
            pltpu.VMEM((GROUP, rows, 2 * cols), BF16),
        ]
        + [pltpu.VMEM((rows, width), BF16)] * 4
        + [
            pltpu.VMEM((GROUP, rows, cols), BF16),
        ]
        + ([pltpu.VMEM(stay.shape, BF16)] + group_scratch(stay, groups, True)) * 2
        + [pltpu.VMEM((rows, width), BF16), pltpu.VMEM((rows, units), BF16)]
        + [pltpu.VMEM((width, rows), BF16)] * 2
        + [pltpu.VMEM((width // 4, units), BF16)] * 3
        + [pltpu.VMEM((width // 2, units), BF16)] * 3
        + [
            copies,
            copies,
            pltpu.SemaphoreType.DMA((12 + chunks,)),
            pltpu.SemaphoreType.DMA((chunks,)),
        ],
        flops=2 * rows * width * (total + out_cols + 2 * units),
        moved=rows * width * 22 + rows * units * 6 + width * (total + out_cols + 2 * units) * 2,
        late=(0, 4, 6, 8, 9),
    )


def add_slots(stay, met, slots):
    chunk = 16
    depth = slots[0].shape[0]
    for at, slot in enumerate(slots):

        def body(rows):
            from_row = pl.ds(pl.multiple_of(rows.start + at * depth, chunk), chunk)
            total = stay[from_row, :].astype(F32) + met[from_row, :].astype(F32)
            slot[rows, :] = total.astype(slot.dtype)

        each_rows(depth, chunk, body)


def pack_sums(sums, target, first):
    width = target.shape[1]
    at = first
    for one in sums:
        total = jnp.sum(one[...], 0, keepdims=True)
        for start in range(0, total.shape[1], width):
            size = min(width, total.shape[1] - start)
            target[at : at + 1, :size] = total[:, start : start + size]
            at += 1


def pack_body(wqkv, bqv, wout, wfc, wproj, rest, qkv0, qkv1, bq0, bq1):
    cols = bqv.shape[2] // GROUP
    at = 0
    for l in range(LAYERS):
        for part in (wout, wfc, wproj):
            size = part.shape[2]
            if part is wproj and l == LAYERS - 1:
                size -= TAIL
            rest[:, at : at + size] = part[l, :, :size]
            at += size
    qkv1[:, qkv1.shape[1] - TAIL :] = wproj[LAYERS - 1, :, wproj.shape[2] - TAIL :]
    for l, (qkv, bq) in enumerate(((qkv0, bq0), (qkv1, bq1))):
        bq[...] = jnp.zeros_like(bq)
        for place in range(GROUP):
            here = slice(place * cols, (place + 1) * cols)
            for c in range(3):
                where = (3 * place + c) * cols
                qkv[:, where : where + cols] = wqkv[l, c, :, here]
                if c != 1:
                    bq[:, where : where + cols] = bqv[l, c // 2 : c // 2 + 1, here]


def pack(w_qkv, b_qv, w_out, w_fc, w_proj):
    depth, out_cols, units = w_fc.shape[1], w_out.shape[1], w_fc.shape[2]
    rest = LAYERS * (out_cols + 2 * units) - TAIL
    outs = [shape((depth, rest), BF16), shape((depth, 3 * out_cols), BF16)]
    outs += [shape((depth, 3 * out_cols + TAIL), BF16)]
    outs += [shape((1, 3 * out_cols), F32)] * 2
    return pl.pallas_call(
        pack_body,
        in_specs=[VMEM] * 5,
        out_specs=[VMEM] * 5,
        out_shape=outs,
        compiler_params=pltpu.CompilerParams(vmem_limit_bytes=VMEM_BYTES),
    )(
        w_qkv.transpose(0, 2, 1, 3),
        b_qv,
        w_out.transpose(0, 2, 1),
        w_fc,
        w_proj.transpose(0, 2, 1),
    )


def finish_body(small, fc1, proj1, qkv1, out1, proj0, qkv0, out0, near, *refs):
    *came, grad_in, middle, own, other, bproj_in, outputs, grad, gain1, bias1, bqv, bout, gain2, bias2, bfc, bproj, wfc, wproj, wout, wqkv = refs
    def rows(at):
        grad[at, :] = grad_in[at, :]
        total = own[at, :].astype(F32) + other[at, :].astype(F32)
        outputs[at, :] = (middle[at, :] + total + bproj_in[...]).astype(BF16)

    each_rows(grad.shape[0], LN_ROWS, rows)
    fc0 = near[...]
    for one in came:
        fc0 = fc0 + one[...].astype(F32)
    width = small.shape[1]
    cols = bqv.shape[2] // GROUP
    wfc[0] = fc0
    wfc[1] = fc1[...]
    for l, proj, qkv, out in ((0, proj0, qkv0, out0), (1, proj1, qkv1, out1)):
        at = l * (small.shape[0] // 2)
        for target, where in ((gain1, 0), (bias1, 1), (bout, 4), (gain2, 5), (bias2, 6), (bproj, 9)):
            target[l : l + 1, :] = small[at + where : at + where + 1, :]
        for i in range(bfc.shape[1] // width):
            bfc[l : l + 1, i * width : (i + 1) * width] = small[at + 7 + i : at + 8 + i, :]
        for place in range(GROUP):
            for i in range(2):
                where = place * 3 * cols + 2 * i * cols
                line, lane = at + 2 + where // width, where % width
                bqv[l, i : i + 1, place * cols : (place + 1) * cols] = small[
                    line : line + 1, lane : lane + cols
                ]
        wproj[l] = proj[...]
        wout[l] = out[...]
        for place in range(GROUP):
            for c in range(3):
                at = (3 * place + c) * cols
                wqkv[l, c, :, place * cols : (place + 1) * cols] = qkv[:, at : at + cols]


def finish(small, totals, near, came, last, out_cols, units):
    depth, width = totals[0].shape[0], small.shape[1]
    vector = shape((LAYERS, width), F32)
    grad = last[0].shape
    outs = [shape(grad, BF16), shape(grad, F32)]
    outs += [vector, vector, shape((LAYERS, 2, out_cols), F32), vector, vector, vector]
    outs += [shape((LAYERS, units), F32), vector, shape((LAYERS, depth, units), F32)]
    outs += [shape((LAYERS, depth, units), F32), shape((LAYERS, depth, out_cols), F32)]
    outs += [shape((LAYERS, 3, depth, out_cols), F32)]
    return pl.pallas_call(
        finish_body,
        in_specs=[VMEM] * (2 + len(totals) + len(came) + len(last)),
        out_specs=[VMEM] * len(outs),
        out_shape=outs,
        compiler_params=pltpu.CompilerParams(vmem_limit_bytes=VMEM_BYTES),
    )(small, *totals, near, *came, *last)


def pull_last_body(
    grad_q, grad_kv, grad_kv_back, gain, qkv, grad_in, stream_in,
    low_one1_in, grad_qkv1_in, low_out1_in, mixed1_in, low_one_in, low_out_in, mixed_in, stay0_in, met0_in,
    gain1, bias1, bqkv1, bout1, gain2_1, bias2_1, bfc1, bproj1, bout0, gain2_0, bias2_0, bfc0, bproj0,
    grad_new, small, total0, total1, total2, total3, total4,
    full, sum_qkv, sum_gain, sum_bias, held, came, far, w_qkv, grad, stream, back_got, part, got,
    left1, wide1, right1, narrow1, left, right, narrow, plain, flipped,
    stay0, met0, far0, came0,
    away1, gone1, stay1, go1, met1, far1, came1,
    away2, gone2, stay2, go2, met2, far2, came2,
    away3, gone3, stay3, go3, met3, far3, came3,
    away4, gone4, stay4, go4, met4, far4, came4,
    send, recv, load, flush
):
    links = Links(send, recv)
    loads = load_columns(
        (
            (low_one1_in, None, left1),
            (grad_qkv1_in, None, wide1),
            (low_out1_in, None, right1),
            (mixed1_in, None, narrow1),
            (stay0_in, None, stay0),
            (met0_in, None, met0),
            (qkv, None, w_qkv),
            (grad_in, None, grad),
            (stream_in, None, stream),
            (low_one_in, None, left),
            (low_out_in, None, right),
            (mixed_in, None, narrow),
        ),
        load,
    )
    links.greet(
        [links.peer(s) for s in range(1, GROUP)]
        + [links.beyond(1, s) for s in range(GROUP)]
        + [links.beyond(links.groups - 1, s) for s in range(GROUP)]
        + [{"tp": links.other}]
        + group_greets(links)
    )
    chunks = [pl.ds(c * CHUNK[0], CHUNK[0]) for c in range(grad.shape[0] // CHUNK[0])]
    start_pulls, wait_pulls, finish_pulls = trade_pulls(
        links, grad_q, grad_kv, grad_kv_back, full, back_got
    )
    swaps = [links.swap(part.at[rows], got.at[rows]) for rows in chunks]
    parts = (
        (away1, gone1, stay1, go1, met1, far1, came1, total1),
        (away2, gone2, stay2, go2, met2, far2, came2, total2),
        (away3, gone3, stay3, go3, met3, far3, came3, total3),
        (away4, gone4, stay4, go4, met4, far4, came4, total4),
    )
    core_sums, over_x, group_sums, spans = [], [], [], []
    for at, (away, gone, stay, go, met, *rest) in enumerate(parts):
        core_sums.append(CoreSum(links, stay, go, away, gone))
        size = stay.shape[1]
        step = size if at % 2 else size // 2
        spans.append([])
        for start in range(0, size, step):
            place = pl.ds(start, step)
            spans[at].append(len(over_x))
            over_x.append(links.copy(go.at[:, place], met.at[:, place], links.peer(2)))
            group_sums.append(GroupSum(links, *[ref.at[:, place] for ref in (stay, met, *rest)]))
    early_sum = GroupSum(links, stay0, met0, far0, came0, total0)
    smalls = RowSum(links, held, came, far)
    sums_one = (gain1, bias1, bqkv1, bout1, gain2_1, bias2_1, bfc1, bproj1)
    sums_zero = (sum_gain, sum_bias, sum_qkv, bout0, gain2_0, bias2_0, bfc0, bproj0)
    start_pulls()
    for total in (sum_qkv, sum_gain, sum_bias):
        total[...] = jnp.zeros_like(total)
    for one in loads:
        one.wait()
    early_sum.send(0)
    core_sums[0].multiply(left1, wide1, plain, flipped)
    core_sums[1].multiply(right1, narrow1, plain, flipped)
    held[0] = jnp.zeros(held.shape[1:], F32)
    pack_sums(sums_one, held.at[0], held.shape[1] // 2)
    core_sums[0].add()
    core_sums[1].add()
    for at in spans[0] + spans[1]:
        over_x[at].start()
    for c, rows in enumerate(chunks):
        wait_pulls(c)
        pull_qkv_rows(c * CHUNK[0], None, links, full, back_got, w_qkv, part, sum_qkv)
        swaps[c].start()
    early_sum.pass_on(0)
    core_sums[2].multiply(left, full, plain, flipped)
    core_sums[3].multiply(right, narrow, plain, flipped)
    core_sums[2].add()
    for at in spans[2]:
        over_x[at].start()
    core_sums[3].add()
    for at in spans[3]:
        over_x[at].start()
    for c, rows in enumerate(chunks):
        swaps[c].wait()
        pull_norm_rows(c * CHUNK[0], grad, part, got, stream, gain, grad_new, (sum_gain, sum_bias))
    flush(0)
    pack_sums(sums_zero, held.at[0], 0)
    smalls.near[0].start()
    smalls.step(0)
    smalls.near[1].start()
    for at, one in enumerate(group_sums):
        over_x[at].wait()
        one.send(0)
        if at:
            group_sums[at - 1].pass_on(0)
        if at == 3:
            smalls.step(1)
            for far_one in smalls.along:
                far_one.start()
    group_sums[-1].pass_on(0)
    finish_pulls()
    small[...] = smalls.finish()
    early_sum.finish(2)
    for one in group_sums:
        one.finish(2)


def pull_last_segment(pulls, gain, qkv, grad, stream, factors, sums_in, smalls):
    CHUNK[0] = SIZES[4]
    rows, width = grad.shape
    cols = pulls[0].shape[2]
    out_cols = GROUP * cols
    total = 3 * out_cols
    units = sums_in[0].shape[1]
    chunks = rows // CHUNK[0]
    groups = lax.axis_size("fsdp") // GROUP
    copies = pltpu.SemaphoreType.DMA(
        (pull_copies(rows) + chunks + 10 + 7 * (groups - 1) + groups + 1,)
    )
    sizes = [total, out_cols, total, out_cols]
    quarter = width // 4
    scratch = []
    for size in sizes:
        stay = shape((quarter, size), BF16)
        scratch += [pltpu.VMEM((2 * quarter, size), BF16)] * 2
        scratch += [pltpu.VMEM(stay.shape, BF16)]
        scratch += [pltpu.VMEM(stay.shape, BF16)] + group_scratch(stay, groups, True)
    low = pltpu.VMEM((rows, width), BF16)
    high = pltpu.VMEM((rows, width), F32)
    mixed = pltpu.VMEM((rows, out_cols), BF16)
    flip = pltpu.VMEM((width, rows), BF16)
    eight = pltpu.VMEM((8, width), F32)
    return run_links(
        pull_last_body,
        4,
        [(VMEM, pull) for pull in pulls]
        + [(VMEM, gain)]
        + [(ANY, array) for array in (qkv, grad, stream, *factors, *sums_in)]
        + [(VMEM, array) for array in smalls],
        [(VMEM, shape((rows, width), F32)), (VMEM, shape((24, width), F32))]
        + [(VMEM, shape((quarter // groups, size), F32)) for size in [units] + sizes],
        [
            pltpu.VMEM((rows, total), BF16),
            pltpu.VMEM((8, total), F32),
            eight,
            eight,
            pltpu.VMEM((3, 24, width), F32),
            pltpu.VMEM((2, 24, width), F32),
            pltpu.VMEM((groups - 1, 24, width), F32),
            pltpu.VMEM((width, total), BF16),
            high,
            high,
            pltpu.VMEM((GROUP, rows, 2 * cols), BF16),
            low,
            low,
            low,
            pltpu.VMEM((rows, total), BF16),
            low,
            mixed,
            low,
            low,
            mixed,
            flip,
            flip,
            pltpu.VMEM((quarter, units), BF16),
        ]
        + group_scratch(shape((quarter, units), BF16), groups, True)
        + scratch
        + [copies, copies, pltpu.SemaphoreType.DMA((12,))],
        flops=2 * rows * width * (3 * total + 2 * out_cols),
        moved=rows * width * 24 + width * total * 2,
        late=(0,),
    )


def halving_order(count):
    order = [0]
    bit = count // 2
    while bit:
        order = order + [at + bit for at in order]
        bit //= 2
    return order


def flip_slots(links, source, plain, flipped):
    plain[...] = source[...].T
    depth = plain.shape[0] // (GROUP * links.groups)
    slot = 0
    for s in (0, 2, 1, 3):
        for other in halving_order(links.groups):
            owner = (links.group ^ other) * GROUP + (links.place ^ s)
            flipped[slot * depth : (slot + 1) * depth, :] = plain[
                pl.ds(pl.multiple_of(owner * depth, depth), depth), :
            ]
            slot += 1


class CoreSum:
    def __init__(self, links, stay, go, away, got):
        self.links, self.stay, self.go, self.away, self.got = links, stay, go, away, got
        self.copy = links.copy(away, got, links.peer(1))
        self.sent = False

    def release(self):
        self.copy.wait_send()
        self.sent = True

    def multiply(self, x, g, plain, flipped):
        flip_slots(self.links, x, plain, flipped)
        quarter = self.stay.shape[0]

        def far(at):
            self.away[:, at] = dot(flipped[2 * quarter :, :], g[:, at]).astype(BF16)

        def near(at):
            self.stay[:, at] = dot(flipped[:quarter, :], g[:, at]).astype(BF16)
            self.go[:, at] = dot(flipped[quarter : 2 * quarter, :], g[:, at]).astype(BF16)

        tiles(g.shape[1], 512, far)
        self.copy.start()
        tiles(g.shape[1], 512, near)

    def add(self):
        if not self.sent:
            self.release()
        self.copy.wait_recv()
        quarter = self.stay.shape[0]
        chunk = 16
        for target, first in ((self.go, quarter), (self.stay, 0)):

            def body(at):
                from_row = pl.ds(pl.multiple_of(at.start + first, chunk), chunk)
                total = target[at, :].astype(F32) + self.got[from_row, :].astype(F32)
                target[at, :] = total.astype(BF16)

            each_rows(quarter, chunk, body)


class GroupSum:
    def __init__(self, links, stay, met, far, came, result):
        self.stay, self.met, self.far, self.came, self.result = stay, met, far, came, result
        self.depth = result.shape[0]
        self.copies, self.counts = [], []
        first, count, bit = 0, links.groups // 2, 1
        while count:
            rows = pl.ds(first * self.depth, count * self.depth)
            device = {"fsdp": (links.group ^ bit) * GROUP + links.place}
            self.copies.append(links.copy(far.at[rows], came.at[rows], device))
            self.counts.append((first, count))
            first, count, bit = first + count, count // 2, bit * 2

    def add(self, step, target, target_first, first, count):
        chunk = 16

        def body(at):
            def rows(slot):
                return pl.ds(pl.multiple_of(at.start + slot * self.depth, chunk), chunk)

            total = self.stay[rows(first), :].astype(F32) + self.met[rows(first), :].astype(F32)
            for came_first, _ in self.counts[:step]:
                total = total + self.came[rows(came_first + first), :].astype(F32)
            target[rows(target_first), :] = total.astype(target.dtype)

        each_rows(count * self.depth, chunk, body)

    def send(self, step):
        first, count = self.counts[step]
        self.add(step, self.far, first, count, count)
        self.copies[step].start()

    def pass_on(self, step):
        self.copies[step].wait()
        self.send(step + 1)

    def finish(self, sent=1):
        for step in range(sent, len(self.copies)):
            self.pass_on(step - 1)
        self.copies[-1].wait()
        self.add(len(self.copies), self.result, 0, 0, 1)


def group_scratch(stay, groups, met):
    rows, size = stay.shape
    far = pltpu.VMEM((rows - rows // groups, size), BF16)
    return ([pltpu.VMEM((rows, size), BF16)] if met else []) + [far, far]


def group_greets(links):
    return [links.beyond(onward, 0) for onward in range(2, links.groups - 1)]


def doc_start_rows(sc, docs, positions):
    start = jnp.zeros_like(positions)
    for d in range(docs):
        first = sc[2 + d]
        start = jnp.where(first <= positions, jnp.maximum(start, first), start)
    return start


def doc_start_one(sc, docs, position):
    start = jnp.int32(0)
    for d in range(docs):
        first = sc[2 + d]
        start = jnp.where(first <= position, jnp.maximum(start, first), start)
    return start


def query_rows(sc, docs, block, size):
    first = sc[1] + block * size
    position = first + lax.broadcasted_iota(jnp.int32, (1, size), 1)
    start = doc_start_rows(sc, docs, position)
    return (
        jnp.concatenate([position, position], 1),
        jnp.concatenate([start, start], 1),
        doc_start_one(sc, docs, first),
    )


def head_stack(rows, scale):
    value = rows.astype(F32)
    if scale != 1.0:
        value = value * scale
    lane = lax.broadcasted_iota(jnp.int32, value.shape, 1)
    return jnp.concatenate(
        [jnp.where(lane < HEAD_DIM, value, 0.0), jnp.where(lane >= HEAD_DIM, value, 0.0)], 0
    ).astype(BF16)


def block_at(block, size):
    return pl.ds(pl.multiple_of(block * size, size), size)


def masked_scores(keys, queries, first_key, position, start):
    scores = dot_last(keys, queries)
    key_at = first_key + lax.broadcasted_iota(jnp.int32, (keys.shape[0], 1), 0)
    return jnp.where((key_at >= start) & (key_at <= position), scores, NEG)


def flash_step(keys, values_ref, queries, at, first_key, position, start, acc, carry):
    top, total = carry
    scores = masked_scores(keys, queries, first_key, position, start)
    top_new = jnp.maximum(top, jnp.max(scores, 0, keepdims=True))
    expo = jnp.exp(scores - top_new)
    shrink = jnp.exp(top - top_new)
    total = total * shrink + jnp.sum(expo, 0, keepdims=True)
    expo = expo.astype(BF16)
    for h in range(2):
        lanes = slice(h * QB, (h + 1) * QB)
        rows = slice(h * HEAD_DIM, (h + 1) * HEAD_DIM)
        acc[rows, :] = acc[rows, :] * shrink[:, lanes] + dot(values_ref[rows, at], expo[:, lanes])
    return top_new, total


def attend_body(docs, sc, qkv, kv, mixed, out, log_total, v_flip, v_back, acc):
    block = pl.program_id(0)
    span, cols = out.shape[0] * pl.num_programs(0), out.shape[1]
    rows = qkv.shape[0]

    @pl.when(block == 0)
    def _():
        for first in range(0, rows, QB):
            v_flip[:, first : first + QB] = qkv[first : first + QB, 2 * cols :].T
            v_back[:, first : first + QB] = kv[first : first + QB, cols:].T

    position, start, lowest = query_rows(sc, docs, block, QB)
    queries = head_stack(qkv[block_at(block, QB), :cols], HEAD_DIM**-0.5)
    acc[...] = jnp.zeros_like(acc)
    least = jnp.maximum(lowest - sc[1], 0) // KB
    last = ((block + 1) * QB - 1) // KB
    before = sc[1] - span

    def step(back, carry):
        at = block_at(last - back, KB)
        keys = qkv[at, cols : 2 * cols]
        first_key = sc[1] + (last - back) * KB
        return flash_step(keys, v_flip, queries, at, first_key, position, start, acc, carry)

    def step_back(where, carry):
        at = block_at(where, KB)
        return flash_step(
            kv[at, :cols], v_back, queries, at, before + where * KB, position, start, acc, carry
        )

    carry = (jnp.full((1, 2 * QB), NEG, F32), jnp.zeros((1, 2 * QB), F32))
    carry = lax.fori_loop(0, last - least + 1, step, carry)
    top, total = lax.fori_loop(
        jnp.minimum(jnp.maximum(lowest - before, 0), span) // KB, span // KB, step_back, carry
    )
    sums = top + jnp.log(total)
    share = 1.0 / total
    parts = []
    for h in range(2):
        lanes = slice(h * QB, (h + 1) * QB)
        log_total[h : h + 1, :] = sums[:, lanes]
        parts.append(acc[h * HEAD_DIM : (h + 1) * HEAD_DIM, :] * share[:, lanes])
    value = jnp.concatenate(parts, 0).T
    out[...] = value
    mixed[...] = value.astype(BF16)


def attend(sc, docs, pieces, kv):
    rows, cols = pieces.shape[1], pieces.shape[2] // 3
    span = GROUP * rows
    low_flip = pltpu.VMEM((cols, span), BF16)
    block = pl.BlockSpec((QB, cols), lambda j, sc: (j, 0))
    mixed, out, log_total = run_kernel(
        functools.partial(attend_body, docs),
        (span // QB,),
        sc,
        [
            (whole((span, 3 * cols)), pieces.reshape(span, 3 * cols)),
            (whole((span, 2 * cols)), kv.reshape(span, 2 * cols)),
        ],
        [
            (block, shape((span, cols), BF16)),
            (block, shape((span, cols), F32)),
            (pl.BlockSpec((8, QB), lambda j, sc: (0, j)), shape((8, span), F32)),
        ],
        scratch=[low_flip, low_flip, pltpu.VMEM((cols, QB), F32)],
        flops=span * span * cols * 4,
        moved=span * cols * 20,
    )
    return mixed.reshape(GROUP, rows, cols), out, log_total


def pull_step(keys, values, at, first_key, position, start, queries, grads, log_rows, delta, refs):
    k_flip, grad_k, grad_v, grad_q = refs
    scores = masked_scores(keys, queries, first_key, position, start)
    probs = jnp.exp(scores - log_rows)
    grad_probs = dot_last(values, grads)
    grad_scores = (probs * (grad_probs - delta)).astype(BF16)
    grad_v[at, :] += dot(probs.astype(BF16), grads)
    grad_k[at, :] += dot(grad_scores, queries)
    size = grad_q.shape[1]
    for h in range(2):
        rows = slice(h * HEAD_DIM, (h + 1) * HEAD_DIM)
        grad_q[rows, :] += dot(k_flip[rows, at], grad_scores[:, h * size : (h + 1) * size])


def pull_body(
    docs, sc, qkv, grad_mixed, kv, out, log_total, grad_q_out, grad_kv, grad_kv_back,
    k_flip, grad_k, grad_v, k_back_flip, grad_k_back, grad_v_back, grad_q
):
    block = pl.program_id(0)
    span, cols = qkv.shape[0], out.shape[1]
    size = out.shape[0]
    before = sc[1] - span

    @pl.when(block == 0)
    def _():
        for first in range(0, span, PULL_KB):
            k_flip[:, first : first + PULL_KB] = qkv[first : first + PULL_KB, cols : 2 * cols].T
            k_back_flip[:, first : first + PULL_KB] = kv[first : first + PULL_KB, :cols].T
        for total in (grad_k, grad_v, grad_k_back, grad_v_back):
            total[...] = jnp.zeros_like(total)

    grad_q[...] = jnp.zeros_like(grad_q)
    position, start, lowest = query_rows(sc, docs, block, size)
    queries = head_stack(qkv[block_at(block, size), :cols], HEAD_DIM**-0.5)
    grad_rows = grad_mixed[block_at(block, size), :]
    grads = head_stack(grad_rows, 1.0)
    flipped = (grad_rows.astype(F32) * out[...]).T
    heads = [slice(h * HEAD_DIM, (h + 1) * HEAD_DIM) for h in range(2)]
    delta = jnp.concatenate([jnp.sum(flipped[rows, :], 0, keepdims=True) for rows in heads], 1)
    log_rows = jnp.concatenate([log_total[h : h + 1, :] for h in range(2)], 1)

    def step(where, carry):
        at = block_at(where, PULL_KB)
        pull_step(
            qkv[at, cols : 2 * cols], qkv[at, 2 * cols :], at, sc[1] + where * PULL_KB,
            position, start, queries, grads, log_rows, delta, (k_flip, grad_k, grad_v, grad_q),
        )
        return carry

    def step_back(where, carry):
        at = block_at(where, PULL_KB)
        pull_step(
            kv[at, :cols], kv[at, cols:], at, before + where * PULL_KB,
            position, start, queries, grads, log_rows, delta, (k_back_flip, grad_k_back, grad_v_back, grad_q),
        )
        return carry

    last = ((block + 1) * size - 1) // PULL_KB
    lax.fori_loop(jnp.maximum(lowest - sc[1], 0) // PULL_KB, last + 1, step, 0)
    lax.fori_loop(
        jnp.minimum(jnp.maximum(lowest - before, 0), span) // PULL_KB, span // PULL_KB, step_back, 0
    )
    grad_q_out[...] = (grad_q[...] * HEAD_DIM**-0.5).T.astype(BF16)

    @pl.when(block == pl.num_programs(0) - 1)
    def _():
        grad_kv[:, :cols] = grad_k[...].astype(BF16)
        grad_kv[:, cols:] = grad_v[...].astype(BF16)
        grad_kv_back[:, :cols] = grad_k_back[...].astype(BF16)
        grad_kv_back[:, cols:] = grad_v_back[...].astype(BF16)


def attend_pull(sc, docs, pieces, grads, kv, out, log_total):
    rows, cols = pieces.shape[1], pieces.shape[2] // 3
    span = GROUP * rows
    block = pl.BlockSpec((PULL_QB, cols), lambda j, sc: (j, 0))
    both = (whole((span, 2 * cols)), shape((span, 2 * cols), BF16))
    low_flip = pltpu.VMEM((cols, span), BF16)
    high = pltpu.VMEM((span, cols), F32)
    parts = run_kernel(
        functools.partial(pull_body, docs),
        (span // PULL_QB,),
        sc,
        [
            (whole((span, 3 * cols)), pieces.reshape(span, 3 * cols)),
            (whole((span, cols)), grads.reshape(span, cols)),
            (whole((span, 2 * cols)), kv.reshape(span, 2 * cols)),
            (block, out),
            (pl.BlockSpec((8, PULL_QB), lambda j, sc: (0, j)), log_total),
        ],
        [(block, shape((span, cols), BF16)), both, both],
        scratch=[low_flip, high, high, low_flip, high, high, pltpu.VMEM((cols, PULL_QB), F32)],
        flops=span * span * cols * 9,
        moved=span * cols * 30,
    )
    return [part.reshape(GROUP, rows, part.shape[1]) for part in parts]


def swap_tp(value):
    return lax.ppermute(value, "tp", [(0, 1), (1, 0)])


def swap_fsdp(value, s):
    return lax.ppermute(value, "fsdp", [(i, i ^ s) for i in range(lax.axis_size("fsdp"))])


def shift_fsdp(value, by):
    size = lax.axis_size("fsdp")
    return lax.ppermute(value, "fsdp", [(i, i + by) for i in range(size) if 0 <= i + by < size])


def gather(shard):
    return lax.all_gather(shard, "fsdp", axis=0, tiled=True)


def tie(*values):
    return lax.optimization_barrier(values)


def shards(
    tokens,
    cotangent,
    segments,
    doc_batch,
    ln1_gain,
    ln1_bias,
    w_qkv,
    b_qv,
    w_out,
    b_out,
    ln2_gain,
    ln2_bias,
    w_fc,
    b_fc,
    w_proj,
    b_proj,
):
    rows, width = tokens.shape
    depth = w_qkv.shape[1]
    out_cols = w_out.shape[1]
    units = w_fc.shape[2]
    cols = out_cols // GROUP
    docs = doc_batch.shape[0]
    me = lax.axis_index("fsdp")
    total_rows = rows * lax.axis_size("fsdp")

    rest, *packed = pack(w_qkv, b_qv, w_out, w_fc, w_proj)
    rest = gather(rest)
    shards_qkv, bias_qkv = packed[:LAYERS], packed[LAYERS:]

    def rest_at(l):
        first = l * (out_cols + 2 * units)
        return (first, first + out_cols, first + out_cols + units)

    def row(vector):
        return vector.reshape(1, vector.shape[0])

    stored = []
    stream, low_one, full_qkv, doc_tokens, doc_first, pieces, kv_back = first_segment(
        tokens,
        row(ln1_gain[0]),
        row(ln1_bias[0]),
        shards_qkv[0],
        bias_qkv[0],
        segments.reshape(rows // 128, 128),
        docs,
    )
    qkv_of = [full_qkv]
    doc_tokens, doc_first = (value[:, 0].astype(jnp.int32) for value in (doc_tokens, doc_first))
    sc = jnp.concatenate(
        [jnp.stack([me % GROUP, (me // GROUP) * (GROUP * rows)]).astype(jnp.int32), doc_first]
    )
    doc_ids = jnp.arange(docs, dtype=jnp.int32)
    is_doc = segments[:, None] == doc_ids[None, :]
    in_batch = doc_batch[:, None] == jnp.arange(MB, dtype=jnp.int32)[None, :]
    counts = jnp.sum(jnp.where(in_batch, doc_tokens[:, None], 0), 0)
    doc_count = jnp.sum(jnp.where(in_batch, counts[None, :], 0), 1)
    row_count = jnp.sum(jnp.where(is_doc, doc_count[None, :], 0), 1).astype(F32)
    row_weight = total_rows / (MB * row_count)
    for l in range(LAYERS - 1):
        mixed, out, log_total = attend(sc, docs, pieces, kv_back)
        vectors = (b_out[l], ln2_gain[l], ln2_bias[l], b_fc[l], b_proj[l], ln1_gain[l + 1], ln1_bias[l + 1])
        mixed_full, middle, low_two, hidden, act, *later = between_segment(
            mixed,
            stream,
            [row(vector) for vector in vectors],
            bias_qkv[l + 1],
            rest,
            rest_at(l),
            units,
            shards_qkv[l + 1],
        )
        stored.append(
            (stream, low_one, pieces, kv_back, out, log_total, mixed_full, middle, low_two, hidden, act)
        )
        stream, low_one, full_qkv, pieces, kv_back = later
        qkv_of.append(full_qkv)

    l = LAYERS - 1
    mixed, out, log_total = attend(sc, docs, pieces, kv_back)
    grad = cotangent.astype(F32) * row_weight[:, None]
    (
        mixed_full,
        middle,
        low_two,
        act,
        part_two,
        low_proj,
        sum_bproj,
        grad_hidden,
        sum_bfc,
        grad,
        low_out,
        sum_gain_two,
        sum_bias_two,
        sum_bout,
        grad_mixed,
        *feed_parts,
    ) = turn_segment(
        mixed,
        stream,
        grad,
        [row(vector) for vector in (b_out[l], ln2_gain[l], ln2_bias[l], b_fc[l])],
        rest,
        qkv_of[l],
        rest_at(l),
        units,
    )
    last = [middle, part_two, swap_tp(part_two), row(b_proj[l])]

    stay0, go0, stay1, go1 = feed_parts
    met0 = swap_fsdp(go0, 2)
    grad_mixed, stay0 = tie(grad_mixed, stay0)
    pulls = attend_pull(sc, docs, pieces, grad_mixed, kv_back, out, log_total)
    *pulls, met0 = tie(*pulls, met0)
    sums_one = [sum_bout, sum_gain_two, sum_bias_two, sum_bfc, sum_bproj]
    low_one_kept, low_out_kept, mixed_kept = low_one, low_out, mixed_full
    (stream_below, low_one, pieces, kv_back, out, log_total, mixed_full, middle, low_two, hidden, act) = stored[0]
    (
        grad_qkv,
        sum_bqkv,
        sum_gain_one,
        sum_bias_one,
        low_proj,
        sum_bproj,
        grad_hidden,
        sum_bfc,
        grad,
        low_out,
        sum_gain_two,
        sum_bias_two,
        sum_bout,
        grad_mixed,
        *later,
    ) = pull_both_segment(
        pulls,
        row(ln1_gain[1]),
        row(ln2_gain[0]),
        qkv_of[1],
        rest,
        rest_at(0),
        units,
        grad,
        stream,
        hidden,
        middle,
        [stay0, met0, stay1, go1],
        [low_two, act],
    )
    feed_totals, near, far, (stay0, go0) = later[:2], later[2], later[3:-2], later[-2:]
    came = []
    others = halving_order(lax.axis_size("fsdp") // GROUP)[1:]
    for other, value in zip(others, far):
        came.append(swap_fsdp(value, GROUP * other))
    met0 = swap_fsdp(go0, 2)
    sums_one = [sum_gain_one, sum_bias_one, sum_bqkv] + sums_one
    pulls = attend_pull(sc, docs, pieces, grad_mixed, kv_back, out, log_total)
    *pulls, came, met0 = tie(*pulls, came, met0)
    sums_zero = [sum_bout, sum_gain_two, sum_bias_two, sum_bfc, sum_bproj]
    grad, small, proj0, qkv1, out1, qkv0, out0 = pull_last_segment(
        pulls,
        row(ln1_gain[0]),
        qkv_of[0],
        grad,
        stream_below,
        [low_one_kept, grad_qkv, low_out_kept, mixed_kept, low_one, low_out, mixed_full],
        [stay0, met0],
        sums_one + sums_zero,
    )
    (
        outputs,
        grad,
        gain1,
        bias1,
        bqv,
        bout,
        gain2,
        bias2,
        bfc,
        bproj,
        grad_wfc,
        grad_wproj,
        grad_wout,
        grad_wqkv,
    ) = finish(
        small, [*feed_totals, qkv1, out1, proj0, qkv0, out0], near, came, [grad, *last], out_cols, units
    )
    grad_wproj = grad_wproj.transpose(0, 2, 1)
    grad_wout = grad_wout.transpose(0, 2, 1)
    grad_wqkv = grad_wqkv.transpose(0, 2, 1, 3)

    return (
        outputs,
        grad,
        gain1,
        bias1,
        grad_wqkv,
        bqv,
        grad_wout,
        bout,
        gain2,
        bias2,
        grad_wfc,
        bfc,
        grad_wproj,
        bproj,
    )


def solution(mesh):
    placed = (
        P("fsdp", None),
        P("fsdp", None),
        P("fsdp"),
        P(),
        P(),
        P(),
        P(None, "fsdp", None, "tp"),
        P(None, None, "tp"),
        P(None, "tp", "fsdp"),
        P(),
        P(),
        P(),
        P(None, "fsdp", "tp"),
        P(None, "tp"),
        P(None, "tp", "fsdp"),
        P(),
    )
    return jax.shard_map(
        shards,
        mesh=mesh,
        in_specs=placed,
        out_specs=(
            P("fsdp", None),
            P("fsdp", None),
            P(),
            P(),
            P(None, "fsdp", None, "tp"),
            P(None, None, "tp"),
            P(None, "tp", "fsdp"),
            P(),
            P(),
            P(),
            P(None, "fsdp", "tp"),
            P(None, "tp"),
            P(None, "tp", "fsdp"),
            P(),
        ),
        check_vma=False,
    )
```

```python
import functools

import jax
import jax.numpy as jnp
from jax import lax
from jax.experimental import pallas as pl
from jax.experimental.pallas import tpu as pltpu
from jax.sharding import PartitionSpec as P

HEAD_DIM = 64
LAYERS = 2
MB = 3
REACH = 4
TAIL = 768

EPS = 1e-05
GROUP = REACH
QB = 512
PULL_QB = 256
LN_ROWS = 128
ACT_ROWS = 128
KB = 512
PULL_KB = 512
NEG = -1e30
F32 = jnp.float32
BF16 = jnp.bfloat16
VMEM_BYTES = 62 * 1024 * 1024
LAST = (((1,), (1,)), ((), ()))
FIRST = (((0,), (0,)), ((), ()))


def dot(left, right):
    return jnp.dot(left, right, preferred_element_type=F32)


def dot_last(left, right):
    return lax.dot_general(left, right, LAST, preferred_element_type=F32)


def shape(dims, dtype):
    return jax.ShapeDtypeStruct(dims, dtype)


def whole(dims):
    return pl.BlockSpec(dims, lambda *_: (0,) * len(dims))


def run_kernel(body, grid, scalars, ins, outs, scratch=(), flops=0, moved=0):
    return pl.pallas_call(
        body,
        grid_spec=pltpu.PrefetchScalarGridSpec(
            num_scalar_prefetch=1,
            grid=grid,
            in_specs=[spec for spec, _ in ins],
            out_specs=[spec for spec, _ in outs],
            scratch_shapes=list(scratch),
        ),
        out_shape=[out for _, out in outs],
        compiler_params=pltpu.CompilerParams(
            vmem_limit_bytes=VMEM_BYTES, dimension_semantics=("arbitrary",) * len(grid)
        ),
        cost_estimate=pl.CostEstimate(flops=flops, bytes_accessed=moved, transcendentals=0),
    )(scalars, *[array for _, array in ins])


def each_rows(count, chunk, body):
    def step(at, carry):
        body(pl.ds(pl.multiple_of(at * chunk, chunk), chunk))
        return carry

    lax.fori_loop(0, count // chunk, step, 0)


def norm_parts(rows):
    centred = rows - jnp.mean(rows, -1, keepdims=True)
    inv_scale = lax.rsqrt(jnp.mean(centred * centred, -1, keepdims=True) + EPS)
    return centred * inv_scale, inv_scale


def norm_pull(grad_rows, unit_rows, inv_scale, gain):
    scaled = grad_rows * gain
    return inv_scale * (
        scaled
        - jnp.mean(scaled, -1, keepdims=True)
        - unit_rows * jnp.mean(scaled * unit_rows, -1, keepdims=True)
    )


def eight_rows(rows):
    return jnp.sum(rows.reshape(rows.shape[0] // 8, 8, rows.shape[1]), 0)


def gelu_rows(value):
    return 0.5 * value * (1.0 + jnp.tanh(0.7978845608028654 * (value + 0.044715 * value * value * value)))


def gelu_slope(value):
    square = value * value
    top = jnp.tanh(0.7978845608028654 * (value + 0.044715 * square * value))
    inner = 0.7978845608028654 * (1.0 + 3.0 * 0.044715 * square)
    return 0.5 * (1.0 + top) + 0.5 * value * (1.0 - top * top) * inner


def norm_pull_rows(at, grad, own, got, inputs, gain, grad_new, sum_gain, sum_bias):
    grad_rows = own[at, :].astype(F32) + got[at, :].astype(F32)
    unit, inv_scale = norm_parts(inputs[at, :])
    value = grad[at, :] + norm_pull(grad_rows, unit, inv_scale, gain[...])
    grad_new[at, :] = value
    sum_gain[...] += eight_rows(grad_rows * unit)
    sum_bias[...] += eight_rows(grad_rows)
    return value


CHUNK = [256]
SIZES = (256, 128, 256, 128, 256)
MESH = pl.DeviceIdType.MESH


class Links:
    def __init__(self, send, recv):
        self.send, self.recv, self.used = send, recv, 0
        self.me = lax.axis_index("fsdp")
        self.place = lax.rem(self.me, GROUP)
        self.group = self.me // GROUP
        self.groups = lax.axis_size("fsdp") // GROUP
        self.other = 1 - lax.axis_index("tp")

    def peer(self, s):
        return {"fsdp": self.group * GROUP + (self.place ^ s)}

    def beyond(self, by, s):
        return {"fsdp": lax.rem(self.group + by, self.groups) * GROUP + (self.place ^ s)}

    def copy(self, source, target, device):
        at = self.used
        self.used += 1
        return pltpu.make_async_remote_copy(
            src_ref=source,
            dst_ref=target,
            send_sem=self.send.at[at],
            recv_sem=self.recv.at[at],
            device_id=device,
            device_id_type=MESH,
        )

    def swap(self, source, target):
        return self.copy(source, target, {"tp": self.other})

    def greet(self, devices):
        barrier = pltpu.get_barrier_semaphore()
        for device in devices:
            pl.semaphore_signal(barrier, inc=1, device_id=device, device_id_type=MESH)
        pl.semaphore_wait(barrier, len(devices))


def columns(place, cols):
    return pl.ds(pl.multiple_of(place * cols, cols), cols)


def tiles(count, size, body):
    def step(at, carry):
        body(pl.ds(pl.multiple_of(at * size, size), size))
        return carry

    lax.fori_loop(0, count // size, step, 0)


def rows_within(first, body):
    def step(at, carry):
        body(pl.ds(pl.multiple_of(first + at * LN_ROWS, LN_ROWS), LN_ROWS))
        return carry

    lax.fori_loop(0, CHUNK[0] // LN_ROWS, step, 0)


def out_rows(rows, mixed, w, target):
    def tile(at):
        target[rows, at] = dot_last(mixed[rows, :], w[at, :]).astype(BF16)

    tiles(w.shape[0], 256, tile)


def norm_rows(first, base, sums, gain, bias, stream, low):
    def body(at):
        value = base[at, :].astype(F32)
        if sums is not None:
            own, got, badd = sums
            value = value + (own[at, :].astype(F32) + got[at, :].astype(F32)) + badd[...]
        stream[at, :] = value
        unit, _ = norm_parts(value)
        low[at, :] = (unit * gain[...] + bias[...]).astype(BF16)

    rows_within(first, body)


def feed_rows(rows, low, fc, bfc, hidden, act, proj, target):
    def tile(at):
        value = dot(low[rows, :], fc[:, at]) + bfc[:, at]
        hidden[rows, at] = value
        act[rows, at] = gelu_rows(value).astype(BF16)

    tiles(fc.shape[1], 512, tile)

    def tile_out(at):
        target[rows, at] = dot_last(act[rows, :], proj[at, :]).astype(BF16)

    tiles(proj.shape[0], 256, tile_out)


def send_qkv(links, low, w, bq, ready, pieces, kv_back, kept):
    cols = bq.shape[1] // GROUP
    copies = []
    order = (2, 3, 1, 0)
    chunks = low.shape[0] // CHUNK[0]
    for c in range(chunks):
        rows = pl.ds(c * CHUNK[0], CHUNK[0])
        across = {
            s: links.copy(ready.at[s, rows], pieces.at[links.place, rows], links.peer(s)) for s in order if s
        }
        onward = {
            s: links.copy(
                ready.at[s, rows, pl.ds(cols // 3, 2 * cols // 3)],
                kv_back.at[links.place, rows],
                links.beyond(1, s),
            )
            for s in order
        }
        own = pltpu.make_async_copy(ready.at[0, rows], pieces.at[links.place, rows], kept.at[c])
        copies.append((across, onward, own))
    last = links.group == links.groups - 1

    def start(c):
        rows = pl.ds(c * CHUNK[0], CHUNK[0])
        across, onward, own = copies[c]
        for s in order:
            at = columns(links.place ^ s, cols)
            ready[s, rows, :] = (dot(low[rows, :], w[:, at]) + bq[:, at]).astype(BF16)
            if s:
                across[s].start()
            else:
                own.start()

            @pl.when(jnp.logical_not(last))
            def _():
                onward[s].start()

    def finish():
        for across, onward, own in copies:
            own.wait()
            for s in order:
                if s:
                    across[s].wait()

                @pl.when(jnp.logical_not(last))
                def _():
                    onward[s].wait_send()

                @pl.when(links.group > 0)
                def _():
                    onward[s].wait_recv()

    return start, finish


def qkv_copies(rows):
    return rows // CHUNK[0] * (2 * GROUP - 1)


class ShardGather:
    def __init__(self, links, shard, full):
        self.depth = shard.shape[0]
        self.links, self.shard, self.full = links, shard, full
        self.steps, held = [], [0]
        bit = links.groups // 2
        while bit:
            device = {"fsdp": (links.group ^ bit) * GROUP + links.place}
            self.steps.append({block: self.relay(block, 0, device) for block in held})
            held = held + [block ^ bit for block in held]
            bit //= 2
        self.held = held
        self.over_x = {block: self.relay(block, 0, links.peer(2)) for block in held}
        self.over_core = [
            {block: self.relay(block, s, links.peer(1)) for block in held} for s in (0, 2)
        ]

    def rows(self, block, s):
        owner = (self.links.group ^ block) * GROUP + (self.links.place ^ s)
        return pl.ds(pl.multiple_of(owner * self.depth, self.depth), self.depth)

    def relay(self, block, s, device):
        rows = self.rows(block, s)
        own = block == 0 and s == 0
        return self.links.copy(self.shard if own else self.full.at[rows], self.full.at[rows], device)

    def spread(self, block, step):
        for later in self.steps[step:]:
            later[block].start()
        self.over_x[block].start()
        self.over_core[0][block].start()

    def start(self):
        self.spread(0, 0)
        self.full[self.rows(0, 0), :] = self.shard[...]

    def pass_x(self):
        bit = self.links.groups // 2
        for step, copies in enumerate(self.steps):
            for block, one in copies.items():
                one.wait_recv()
                self.spread(block ^ bit, step + 1)
            bit //= 2

    def pass_core(self):
        for block in self.held:
            self.over_x[block].wait_recv()
            self.over_core[1][block].start()

    def arrive(self):
        for copies in self.over_core:
            for one in copies.values():
                one.wait_recv()

    def finish(self):
        for copies in (*self.steps, self.over_x, *self.over_core):
            for one in copies.values():
                one.wait_send()


def gather_copies():
    groups = lax.axis_size("fsdp") // GROUP
    return 4 * groups - 1


class RowSum:
    def __init__(self, links, held, came, far):
        self.held, self.came, self.far = held, came, far
        self.near = [links.copy(held.at[i], came.at[i], links.peer(i + 1)) for i in range(2)]
        self.along = [
            links.copy(held.at[2], far.at[onward - 1], links.beyond(onward, 0))
            for onward in range(1, links.groups)
        ]

    def step(self, i):
        self.near[i].wait()
        self.held[i + 1] = self.held[i] + self.came[i]

    def finish(self):
        total = self.held[2]
        for at, one in enumerate(self.along):
            one.wait()
            total = total + self.far[at]
        return total


def count_docs(segments, counts):
    for d in range(counts.shape[0]):
        found = jnp.where(segments[...] == d, 1.0, 0.0).astype(F32)
        total = jnp.sum(jnp.sum(found, 0, keepdims=True), 1, keepdims=True)
        counts[d : d + 1, :] = jnp.broadcast_to(total, (1, counts.shape[1]))


def first_body(
    base, gain, bias, shard, bq, segments, stream, low, w, tokens, first, pieces, kv_back,
    ready, held, came, far, send, recv, kept, flush
):
    links = Links(send, recv)
    gathered = ShardGather(links, shard, w)
    counted = RowSum(links, held, came, far)
    start, finish = send_qkv(links, low, w, bq, ready, pieces, kv_back, kept)
    count_docs(segments, held.at[0])
    links.greet(
        [links.peer(s) for s in range(1, GROUP)]
        + [links.beyond(1, s) for s in range(GROUP)]
        + [links.beyond(links.groups - 1, s) for s in range(GROUP)]
        + group_greets(links)
    )
    gathered.start()
    counted.near[0].start()
    chunks = base.shape[0] // CHUNK[0]
    for c in range(chunks):
        norm_rows(c * CHUNK[0], base, None, gain, bias, stream, low)
    flush(0, 1)
    counted.step(0)
    counted.near[1].start()
    gathered.pass_x()
    counted.step(1)
    for one in counted.along:
        one.start()
    gathered.pass_core()
    gathered.arrive()
    flush(2)
    for c in range(chunks):
        start(c)
    total = counted.finish()
    tokens[...] = total
    begin = jnp.zeros((1, total.shape[1]), F32)
    for d in range(total.shape[0]):
        first[d : d + 1, :] = begin
        begin = begin + total[d : d + 1, :]
    gathered.finish()
    finish()


ANY = pl.BlockSpec(memory_space=pl.ANY)
VMEM = pl.BlockSpec(memory_space=pltpu.VMEM)


def run_links(body, name, ins, outs, scratch, flops, moved, late=()):
    def with_flush(*refs):
        n_in, n_out = len(ins), len(outs)
        given = refs[:n_in]
        held = list(refs[n_in : n_in + n_out])
        rest = refs[n_in + n_out : len(refs) - len(late) - 1]
        twins, done = refs[len(refs) - len(late) - 1 : -1], refs[-1]
        copies = {}
        for i, (at, twin) in enumerate(zip(late, twins)):
            copies[at] = pltpu.make_async_copy(twin, held[at], done.at[i])
            held[at] = twin
        started = []

        def flush(*which):
            for at in which:
                copies[at].start()
                started.append(at)

        body(*given, *held, *rest, flush=flush)
        flush(*[at for at in late if at not in started])
        for at in late:
            copies[at].wait()

    twins = [pltpu.VMEM(outs[at][1].shape, outs[at][1].dtype) for at in late]
    twins.append(pltpu.SemaphoreType.DMA((max(1, len(late)),)))
    return pl.pallas_call(
        with_flush,
        in_specs=[spec for spec, _ in ins],
        out_specs=[ANY if at in late else spec for at, (spec, _) in enumerate(outs)],
        out_shape=[out for _, out in outs],
        scratch_shapes=list(scratch) + twins,
        compiler_params=pltpu.CompilerParams(
            vmem_limit_bytes=VMEM_BYTES, collective_id=name, has_side_effects=True
        ),
        cost_estimate=pl.CostEstimate(flops=flops, bytes_accessed=moved, transcendentals=0),
    )(*[array for _, array in ins])


def first_segment(base, gain, bias, shard, bq, segments, docs):
    CHUNK[0] = SIZES[0]
    rows, width = base.shape
    total = bq.shape[1]
    cols = total // GROUP
    groups = lax.axis_size("fsdp") // GROUP
    copies = pltpu.SemaphoreType.DMA((qkv_copies(rows) + gather_copies() + groups + 1,))
    counts = (VMEM, shape((docs, 128), F32))
    return run_links(
        first_body,
        0,
        [(VMEM, array) for array in (base, gain, bias, shard, bq, segments)],
        [
            (VMEM, shape((rows, width), F32)),
            (VMEM, shape((rows, width), BF16)),
            (VMEM, shape((width, total), BF16)),
            counts,
            counts,
            (ANY, shape((GROUP, rows, cols), BF16)),
            (ANY, shape((GROUP, rows, 2 * cols // 3), BF16)),
        ],
        [
            pltpu.VMEM((GROUP, rows, cols), BF16),
            pltpu.VMEM((3, docs, 128), F32),
            pltpu.VMEM((2, docs, 128), F32),
            pltpu.VMEM((groups - 1, docs, 128), F32),
            copies,
            copies,
            pltpu.SemaphoreType.DMA((rows // CHUNK[0],)),
        ],
        flops=2 * rows * width * total,
        moved=rows * width * 8 + width * total * 2,
        late=(0, 1, 2),
    )


def trade_mixed(links, mixed_all, mixed):
    cols = mixed_all.shape[2]
    copies = []
    for c in range(mixed.shape[0] // CHUNK[0]):
        rows = pl.ds(c * CHUNK[0], CHUNK[0])
        copies.append(
            [
                links.copy(
                    mixed_all.at[links.place ^ s, rows],
                    mixed.at[rows, columns(links.place, cols)],
                    links.peer(s),
                )
                for s in (2, 3, 1)
            ]
        )

    def start():
        for chunk in copies:
            for one in chunk:
                one.start()
        mixed[:, columns(links.place, cols)] = mixed_all[links.place]

    def wait(c):
        for one in copies[c]:
            one.wait_recv()

    def finish():
        for chunk in copies:
            for one in chunk:
                one.wait_send()

    return start, wait, finish


def between_body(
    at, mixed_all, base, bout, gain_two, bias_two, bfc, bproj, gain, bias, bq, rest, shard,
    mixed, middle, low_two, hidden, act, stream, low, w_qkv, pieces, kv_back,
    w_out, w_fc, w_proj, part, got, part_two, got_two, ready, send, recv, load, kept, flush
):
    out_at, fc_at, proj_at = at
    links = Links(send, recv)
    loads = [
        pltpu.make_async_copy(source.at[:, pl.ds(start, target.shape[1])], target, load.at[i])
        for i, (source, start, target) in enumerate(
            ((rest, out_at, w_out), (rest, fc_at, w_fc), (rest, proj_at, w_proj))
        )
    ]
    for one in loads:
        one.start()
    links.greet(
        [links.peer(s) for s in range(1, GROUP)]
        + [links.beyond(1, s) for s in range(GROUP)]
        + [links.beyond(links.groups - 1, s) for s in range(GROUP)]
        + [{"tp": links.other}]
        + group_greets(links)
    )
    total = bq.shape[1]
    gathered, tail = (
        ShardGather(links, shard.at[:, place], w_qkv.at[:, place])
        for place in (pl.ds(0, total), pl.ds(total, TAIL))
    )
    chunks = [pl.ds(c * CHUNK[0], CHUNK[0]) for c in range(base.shape[0] // CHUNK[0])]
    start_mixed, wait_mixed, finish_mixed = trade_mixed(links, mixed_all, mixed)
    swaps = [links.swap(part.at[rows], got.at[rows]) for rows in chunks]
    swaps_two = [links.swap(part_two.at[rows], got_two.at[rows]) for rows in chunks]
    start_qkv, finish_qkv = send_qkv(links, low, w_qkv, bq, ready, pieces, kv_back, kept)
    start_mixed()
    gathered.start()
    tail.start()
    loads[0].wait()
    for c, rows in enumerate(chunks):
        wait_mixed(c)
        out_rows(rows, mixed, w_out, part)
        swaps[c].start()
    loads[1].wait()
    loads[2].wait()
    for c, rows in enumerate(chunks):
        swaps[c].wait()
        norm_rows(c * CHUNK[0], base, (part, got, bout), gain_two, bias_two, middle, low_two)
        feed_rows(rows, low_two, w_fc, bfc, hidden, act, w_proj, part_two)
        swaps_two[c].start()
        if c == 0:
            gathered.pass_x()
        if c == 1:
            tail.pass_x()
    gathered.pass_core()
    flush(0, 1, 2, 3, 4)
    gathered.arrive()
    for c, rows in enumerate(chunks):
        swaps_two[c].wait()
        norm_rows(c * CHUNK[0], middle, (part_two, got_two, bproj), gain, bias, stream, low)
        start_qkv(c)
        if c == 1:
            tail.pass_core()
    tail.arrive()
    flush(7)
    finish_mixed()
    gathered.finish()
    tail.finish()
    finish_qkv()


def between_segment(mixed_all, base, vectors, bq, rest, at, units, shard):
    CHUNK[0] = SIZES[1]
    rows, width = base.shape
    total = bq.shape[1]
    cols = total // GROUP
    out_cols = at[1] - at[0]
    chunks = rows // CHUNK[0]
    copies = pltpu.SemaphoreType.DMA((qkv_copies(rows) + chunks * (GROUP - 1) + 2 * chunks + 2 * gather_copies(),))
    whole_f32 = (VMEM, shape((rows, width), F32))
    whole_low = (VMEM, shape((rows, width), BF16))
    return run_links(
        functools.partial(between_body, at),
        1,
        [(VMEM, mixed_all), (VMEM, base)]
        + [(VMEM, vector) for vector in vectors]
        + [(VMEM, bq), (ANY, rest), (VMEM, shard)],
        [
            (VMEM, shape((rows, out_cols), BF16)),
            whole_f32,
            whole_low,
            (VMEM, shape((rows, units), F32)),
            (VMEM, shape((rows, units), BF16)),
            whole_f32,
            whole_low,
            (VMEM, shape((width, shard.shape[1]), BF16)),
            (ANY, shape((GROUP, rows, cols), BF16)),
            (ANY, shape((GROUP, rows, 2 * cols // 3), BF16)),
        ],
        [
            pltpu.VMEM((width, out_cols), BF16),
            pltpu.VMEM((width, units), BF16),
            pltpu.VMEM((width, units), BF16),
        ]
        + [pltpu.VMEM((rows, width), BF16)] * 4
        + [
            pltpu.VMEM((GROUP, rows, cols), BF16),
            copies,
            copies,
            pltpu.SemaphoreType.DMA((3,)),
            pltpu.SemaphoreType.DMA((chunks,)),
        ],
        flops=2 * rows * width * (total + out_cols + 2 * units),
        moved=rows * width * 20 + rows * units * 6 + width * (total + out_cols + 2 * units) * 2,
        late=tuple(range(8)),
    )


def pull_qkv_rows(first, back, links, full, back_got, w, target, sums):
    cols = full.shape[1] // GROUP
    rows = pl.ds(first, CHUNK[0])

    @pl.when(links.group < links.groups - 1)
    def _():
        for s in range(GROUP):
            at = pl.ds(
                pl.multiple_of((links.place ^ s) * cols + cols // 3, cols // 3), 2 * cols // 3
            )
            full[rows, at] = (full[rows, at].astype(F32) + back_got[s, rows].astype(F32)).astype(BF16)

    def tile(at):
        target[rows, at] = dot_last(full[rows, :], w[at, :]).astype(BF16)

    tiles(w.shape[0], 256, tile)

    def body(at):
        sums[...] += eight_rows(full[at, :].astype(F32))

    rows_within(first, body)


def trade_pulls(links, grad_q, grad_kv, grad_kv_back, full, back_got):
    part = grad_q.shape[2]
    copies = []
    for c in range(full.shape[0] // CHUNK[0]):
        rows = pl.ds(c * CHUNK[0], CHUNK[0])
        across, back = [], []
        for s in (2, 3, 1):
            for source, start, size in ((grad_kv, part, 2 * part), (grad_q, 0, part)):
                at = pl.ds(pl.multiple_of(links.place * 3 * part + start, part), size)
                across.append(
                    links.copy(source.at[links.place ^ s, rows], full.at[rows, at], links.peer(s))
                )
        for s in (2, 3, 1, 0):
            back.append(
                links.copy(
                    grad_kv_back.at[links.place ^ s, rows],
                    back_got.at[s, rows],
                    links.beyond(links.groups - 1, s),
                )
            )
        copies.append((across, back))

    def start():
        for across, back in copies:
            for one in across:
                one.start()

            @pl.when(links.group > 0)
            def _():
                for one in back:
                    one.start()

        first = pl.multiple_of(links.place * 3 * part, part)
        full[:, pl.ds(first, part)] = grad_q[links.place]
        full[:, pl.ds(pl.multiple_of(first + part, part), 2 * part)] = grad_kv[links.place]

    def wait(c):
        across, back = copies[c]
        for one in across:
            one.wait_recv()

        @pl.when(links.group < links.groups - 1)
        def _():
            for one in back:
                one.wait_recv()

    def finish():
        for across, back in copies:
            for one in across:
                one.wait_send()

            @pl.when(links.group > 0)
            def _():
                for one in back:
                    one.wait_send()

    return start, wait, finish


def pull_copies(rows):
    return rows // CHUNK[0] * (2 * (GROUP - 1) + GROUP)


def pull_norm_rows(first, grad, own, got, inputs, gain, grad_new, sums, low=None):
    def body(at):
        value = norm_pull_rows(at, grad, own, got, inputs, gain, grad_new, sums[0], sums[1])
        if low is not None:
            value = value.astype(BF16)
            low[at, :] = value
            sums[2][...] += eight_rows(value.astype(F32))

    rows_within(first, body)


def round_rows(first, grad, low, sums):
    def body(at):
        value = grad[at, :].astype(BF16)
        low[at, :] = value
        sums[...] += eight_rows(value.astype(F32))

    rows_within(first, body)


def pull_feed_rows(rows, low, proj, hidden, held, grad_hidden, sums, fc, target):
    def tile(at):
        value = dot(low[rows, :], proj[:, at]) * gelu_slope(hidden[held, at])
        value = value.astype(BF16)
        grad_hidden[rows, at] = value
        sums[:, at] += eight_rows(value.astype(F32))

    tiles(proj.shape[1], 512, tile)

    def tile_out(at):
        target[rows, at] = dot_last(grad_hidden[rows, :], fc[at, :]).astype(BF16)

    tiles(fc.shape[0], 256, tile_out)


def send_mixed_pull(links, low, w, ready, pieces, kept):
    cols = ready.shape[2]
    copies = []
    for c in range(low.shape[0] // CHUNK[0]):
        rows = pl.ds(c * CHUNK[0], CHUNK[0])
        across = {
            s: links.copy(ready.at[s, rows], pieces.at[links.place, rows], links.peer(s))
            for s in range(1, GROUP)
        }
        own = pltpu.make_async_copy(ready.at[0, rows], pieces.at[links.place, rows], kept.at[c])
        copies.append((across, own))

    def start(c):
        rows = pl.ds(c * CHUNK[0], CHUNK[0])
        across, own = copies[c]
        for s in (2, 3, 1, 0):
            at = columns(links.place ^ s, cols)
            ready[s, rows, :] = dot(low[rows, :], w[:, at]).astype(BF16)
            (across[s] if s else own).start()

    def finish():
        for across, own in copies:
            own.wait()
            for one in across.values():
                one.wait()

    return start, finish


def load_columns(plan, load):
    copies = []
    for i, (source, start, target) in enumerate(plan):
        if start is not None:
            source = source.at[:, pl.ds(start, target.shape[1])]
        copies.append(pltpu.make_async_copy(source, target, load.at[i]))
    for one in copies:
        one.start()
    return copies


def turn_body(
    at, mixed_all, base_in, grad_in, bout, gain_two, bias_two, bfc, rest, last,
    mixed, middle, low_two, act, part_two, low_proj, sum_proj, grad_hidden, sum_fc, grad_new, low_out,
    sum_gain, sum_bias, sum_out, pieces, stay0, go0, stay1, go1,
    w_out, w_fc, w_proj, base, grad, hidden, part, got, part_three, got_three, ready,
    plain, flipped, away0, away1, met0, met1, send, recv, load, kept, flush
):
    out_at, fc_at, proj_at = at
    links = Links(send, recv)
    loads = load_columns(
        (
            (rest, out_at, w_out),
            (base_in, None, base),
            (grad_in, None, grad),
            (rest, fc_at, w_fc),
            (rest, proj_at, w_proj.at[:, pl.ds(0, w_proj.shape[1] - TAIL)]),
            (last, last.shape[1] - TAIL, w_proj.at[:, pl.ds(w_proj.shape[1] - TAIL, TAIL)]),
        ),
        load,
    )
    links.greet([links.peer(s) for s in range(1, GROUP)] + [{"tp": links.other}])
    chunks = [pl.ds(c * CHUNK[0], CHUNK[0]) for c in range(base.shape[0] // CHUNK[0])]
    start_mixed, wait_mixed, finish_mixed = trade_mixed(links, mixed_all, mixed)
    swaps = [links.swap(part.at[rows], got.at[rows]) for rows in chunks]
    swaps_three = [links.swap(part_three.at[rows], got_three.at[rows]) for rows in chunks]
    start_pull, finish_pull = send_mixed_pull(links, low_out, w_out, ready, pieces, kept)
    core_sums = (
        CoreSum(links, stay0, go0, away0, met0),
        CoreSum(links, stay1, go1, away1, met1),
    )
    start_mixed()
    for total in (sum_proj, sum_fc, sum_gain, sum_bias, sum_out):
        total[...] = jnp.zeros_like(total)
    loads[0].wait()
    for c, rows in enumerate(chunks):
        wait_mixed(c)
        out_rows(rows, mixed, w_out, part)
        swaps[c].start()
    for one in loads[1:]:
        one.wait()
    for c in range(len(chunks)):
        round_rows(c * CHUNK[0], grad, low_proj, sum_proj)
    for c, rows in enumerate(chunks):
        swaps[c].wait()
        norm_rows(c * CHUNK[0], base, (part, got, bout), gain_two, bias_two, middle, low_two)

        def tile(at):
            value = dot(low_two[rows, :], w_fc[:, at]) + bfc[:, at]
            hidden[rows, at] = value
            act[rows, at] = gelu_rows(value).astype(BF16)

        tiles(w_fc.shape[1], 512, tile)
        pull_feed_rows(
            rows, low_proj, w_proj, hidden, rows, grad_hidden, sum_fc, w_fc, part_three
        )
        swaps_three[c].start()
    flush(0, 1, 2, 3, 5, 7)
    core_sums[0].multiply(low_two, grad_hidden, plain, flipped)
    core_sums[1].multiply(low_proj, act, plain, flipped)
    for rows in chunks:

        def tile_out(at):
            part_two[rows, at] = dot_last(act[rows, :], w_proj[at, :]).astype(BF16)

        tiles(w_proj.shape[0], 256, tile_out)
    flush(4)
    for c, rows in enumerate(chunks):
        swaps_three[c].wait()
        pull_norm_rows(
            c * CHUNK[0], grad, part_three, got_three, middle, gain_two, grad_new, (sum_gain, sum_bias, sum_out), low_out
        )
        start_pull(c)
    for one in core_sums:
        one.add()
    finish_mixed()
    finish_pull()


def turn_segment(mixed_all, base, grad, vectors, rest, last, at, units):
    CHUNK[0] = SIZES[2]
    rows, width = base.shape
    out_cols = at[1] - at[0]
    cols = out_cols // GROUP
    chunks = rows // CHUNK[0]
    copies = pltpu.SemaphoreType.DMA((2 * chunks * (GROUP - 1) + 2 * chunks + 2,))
    high = (VMEM, shape((rows, width), F32))
    low = (VMEM, shape((rows, width), BF16))
    sums = (VMEM, shape((8, width), F32))
    return run_links(
        functools.partial(turn_body, at),
        2,
        [(VMEM, mixed_all), (ANY, base), (ANY, grad)]
        + [(VMEM, vector) for vector in vectors]
        + [(ANY, rest), (ANY, last)],
        [
            (VMEM, shape((rows, out_cols), BF16)),
            high,
            low,
            (VMEM, shape((rows, units), BF16)),
            low,
            low,
            sums,
            (VMEM, shape((rows, units), BF16)),
            (VMEM, shape((8, units), F32)),
            high,
            low,
            sums,
            sums,
            sums,
            (ANY, shape((GROUP, rows, cols), BF16)),
        ]
        + [(VMEM, shape((width // 4, units), BF16))] * 4,
        [
            pltpu.VMEM((width, out_cols), BF16),
            pltpu.VMEM((width, units), BF16),
            pltpu.VMEM((width, units), BF16),
            pltpu.VMEM((rows, width), F32),
            pltpu.VMEM((rows, width), F32),
            pltpu.VMEM((rows, units), F32),
        ]
        + [pltpu.VMEM((rows, width), BF16)] * 4
        + [
            pltpu.VMEM((GROUP, rows, cols), BF16),
        ]
        + [pltpu.VMEM((width, rows), BF16)] * 2
        + [pltpu.VMEM((width // 2, units), BF16)] * 4
        + [
            copies,
            copies,
            pltpu.SemaphoreType.DMA((6,)),
            pltpu.SemaphoreType.DMA((chunks,)),
        ],
        flops=2 * rows * width * (2 * out_cols + 4 * units),
        moved=rows * width * 22 + rows * units * 4 + width * (out_cols + 2 * units) * 2,
        late=(0, 1, 2, 3, 4, 5, 7, 9, 10, 15, 16, 17, 18),
    )


def pull_both_body(
    at, grad_q, grad_kv, grad_kv_back, gain, gain_two, qkv, rest, grad_in, stream_in, hidden_in, middle_in,
    stay0_in, met0_in, stay1_in, go1, low_two_in, act_in,
    full, sum_qkv, sum_gain_one, sum_bias_one, low_proj, sum_proj, grad_hidden, sum_fc, grad_new, low_out,
    sum_gain, sum_bias, sum_out, pieces, total0, total1, near2, *refs, flush
):
    groups = lax.axis_size("fsdp") // GROUP
    far2, (stay3, go3), refs = refs[: groups - 1], refs[groups - 1 : groups + 1], refs[groups + 1 :]
    (w_qkv, w_out, w_fc, w_proj, grad, stream, hidden, back_got, part, got, part_two, got_two, ready,
    stay0, met0, far0, came0, stay1, met1, far1, came1,
    left, wide, plain, flipped, stay2, go2, met2, away, gone2, gone3, send, recv, load, kept) = refs
    out_at, fc_at, proj_at = at
    links = Links(send, recv)
    loads = load_columns(
        (
            (qkv, 0, w_qkv),
            (grad_in, None, grad),
            (stream_in, None, stream),
            (rest, proj_at, w_proj),
            (hidden_in.at[pl.ds(0, CHUNK[0])], None, hidden),
            (rest, fc_at, w_fc),
            (rest, out_at, w_out),
            (stay0_in, None, stay0),
            (met0_in, None, met0),
            (stay1_in, None, stay1),
            (low_two_in, None, left),
            (act_in, None, wide),
        ),
        load,
    )
    middle = stream
    load_middle = pltpu.make_async_copy(middle_in, middle, load.at[len(loads)])
    links.greet(
        [links.peer(s) for s in range(1, GROUP)]
        + [links.beyond(1, s) for s in range(GROUP)]
        + [links.beyond(links.groups - 1, s) for s in range(GROUP)]
        + [{"tp": links.other}]
        + group_greets(links)
    )
    chunks = [pl.ds(c * CHUNK[0], CHUNK[0]) for c in range(grad.shape[0] // CHUNK[0])]
    start_pulls, wait_pulls, finish_pulls = trade_pulls(
        links, grad_q, grad_kv, grad_kv_back, full, back_got
    )
    swaps = [links.swap(part.at[rows], got.at[rows]) for rows in chunks]
    swaps_two = [links.swap(part_two.at[rows], got_two.at[rows]) for rows in chunks]
    start_pull, finish_pull = send_mixed_pull(links, low_out, w_out, ready, pieces, kept)
    late_x = links.copy(go1, met1, links.peer(2))
    group_sums = (
        GroupSum(links, stay0, met0, far0, came0, total0),
        GroupSum(links, stay1, met1, far1, came1, total1),
    )
    core_sums = (
        CoreSum(links, stay2, go2, away, gone2),
        CoreSum(links, stay3, go3, away, gone3),
    )
    feed_x = links.copy(go2, met2, links.peer(2))
    start_pulls()
    for total in (sum_qkv, sum_gain_one, sum_bias_one, sum_proj, sum_fc, sum_gain, sum_bias, sum_out):
        total[...] = jnp.zeros_like(total)
    for one in loads:
        one.wait()
    for c, rows in enumerate(chunks):
        wait_pulls(c)
        if c == len(chunks) // 2:
            late_x.start()
            group_sums[0].send(0)
        pull_qkv_rows(c * CHUNK[0], None, links, full, back_got, w_qkv, part, sum_qkv)
        swaps[c].start()
    flush(0)
    for c, rows in enumerate(chunks):
        swaps[c].wait()
        pull_norm_rows(
            c * CHUNK[0], grad, part, got, stream, gain, grad_new, (sum_gain_one, sum_bias_one)
        )
        if c == len(chunks) - 1:
            load_middle.start()
        round_rows(c * CHUNK[0], grad_new, low_proj, sum_proj)
        if c:
            load_hidden.wait()
        pull_feed_rows(
            rows, low_proj, w_proj, hidden, pl.ds(0, CHUNK[0]), grad_hidden, sum_fc, w_fc, part_two
        )
        swaps_two[c].start()
        if c + 1 < len(chunks):
            load_hidden = pltpu.make_async_copy(
                hidden_in.at[pl.ds((c + 1) * CHUNK[0], CHUNK[0])], hidden, load.at[len(loads) + 1 + c]
            )
            load_hidden.start()
    flush(4, 6)
    core_sums[0].multiply(left, grad_hidden, plain, flipped)
    load_middle.wait()
    for c, rows in enumerate(chunks):
        swaps_two[c].wait()
        pull_norm_rows(
            c * CHUNK[0], grad_new, part_two, got_two, middle, gain_two, grad_new, (sum_gain, sum_bias, sum_out), low_out
        )
        start_pull(c)
        if c == 0:
            core_sums[0].add()
            feed_x.start()
            late_x.wait()
            group_sums[1].send(0)
            group_sums[0].pass_on(0)
            core_sums[1].multiply(low_proj, wide, plain, flipped)
    group_sums[1].pass_on(0)
    core_sums[1].add()
    feed_x.wait()
    add_slots(stay2, met2, (near2, *far2))
    finish_pulls()
    finish_pull()
    for one in group_sums:
        one.finish(2)


def pull_both_segment(pulls, gain, gain_two, qkv, rest, at, units, grad, stream, hidden, middle, sums_in, factors):
    CHUNK[0] = SIZES[3]
    rows, width = grad.shape
    out_cols = at[1] - at[0]
    cols = out_cols // GROUP
    total = 3 * out_cols
    chunks = rows // CHUNK[0]
    groups = lax.axis_size("fsdp") // GROUP
    stay = sums_in[0]
    copies = pltpu.SemaphoreType.DMA((pull_copies(rows) + chunks * (GROUP - 1) + 2 * chunks + 2 * groups + 2,))
    high = (VMEM, shape((rows, width), F32))
    low = (VMEM, shape((rows, width), BF16))
    sums = (VMEM, shape((8, width), F32))
    return run_links(
        functools.partial(pull_both_body, at),
        3,
        [(VMEM, pull) for pull in pulls]
        + [(VMEM, gain), (VMEM, gain_two)]
        + [(ANY, array) for array in (qkv, rest, grad, stream, hidden, middle)]
        + [(ANY, array) for array in (*sums_in, *factors)],
        [
            (VMEM, shape((rows, total), BF16)),
            (VMEM, shape((8, total), F32)),
            sums,
            sums,
            low,
            sums,
            (VMEM, shape((rows, units), BF16)),
            (VMEM, shape((8, units), F32)),
            high,
            low,
            sums,
            sums,
            sums,
            (ANY, shape((GROUP, rows, cols), BF16)),
        ]
        + [(VMEM, shape((stay.shape[0] // groups, stay.shape[1]), F32))] * 2
        + [(VMEM, shape((width // 4 // groups, units), F32))]
        + [(VMEM, shape((width // 4 // groups, units), BF16))] * (groups - 1)
        + [(VMEM, shape((width // 4, units), BF16))] * 2,
        [
            pltpu.VMEM((width, total), BF16),
            pltpu.VMEM((width, out_cols), BF16),
            pltpu.VMEM((width, units), BF16),
            pltpu.VMEM((width, units), BF16),
            pltpu.VMEM((rows, width), F32),
            pltpu.VMEM((rows, width), F32),
            pltpu.VMEM((CHUNK[0], units), F32),
            pltpu.VMEM((GROUP, rows, 2 * cols), BF16),
        ]
        + [pltpu.VMEM((rows, width), BF16)] * 4
        + [
            pltpu.VMEM((GROUP, rows, cols), BF16),
        ]
        + ([pltpu.VMEM(stay.shape, BF16)] + group_scratch(stay, groups, True)) * 2
        + [pltpu.VMEM((rows, width), BF16), pltpu.VMEM((rows, units), BF16)]
        + [pltpu.VMEM((width, rows), BF16)] * 2
        + [pltpu.VMEM((width // 4, units), BF16)] * 3
        + [pltpu.VMEM((width // 2, units), BF16)] * 3
        + [
            copies,
            copies,
            pltpu.SemaphoreType.DMA((12 + chunks,)),
            pltpu.SemaphoreType.DMA((chunks,)),
        ],
        flops=2 * rows * width * (total + out_cols + 2 * units),
        moved=rows * width * 22 + rows * units * 6 + width * (total + out_cols + 2 * units) * 2,
        late=(0, 4, 6, 8, 9),
    )


def add_slots(stay, met, slots):
    chunk = 16
    depth = slots[0].shape[0]
    for at, slot in enumerate(slots):

        def body(rows):
            from_row = pl.ds(pl.multiple_of(rows.start + at * depth, chunk), chunk)
            total = stay[from_row, :].astype(F32) + met[from_row, :].astype(F32)
            slot[rows, :] = total.astype(slot.dtype)

        each_rows(depth, chunk, body)


def pack_sums(sums, target, first):
    width = target.shape[1]
    at = first
    for one in sums:
        total = jnp.sum(one[...], 0, keepdims=True)
        for start in range(0, total.shape[1], width):
            size = min(width, total.shape[1] - start)
            target[at : at + 1, :size] = total[:, start : start + size]
            at += 1


def pack_body(wqkv, bqv, wout, wfc, wproj, rest, qkv0, qkv1, bq0, bq1):
    cols = bqv.shape[2] // GROUP
    at = 0
    for l in range(LAYERS):
        for part in (wout, wfc, wproj):
            size = part.shape[2]
            if part is wproj and l == LAYERS - 1:
                size -= TAIL
            rest[:, at : at + size] = part[l, :, :size]
            at += size
    qkv1[:, qkv1.shape[1] - TAIL :] = wproj[LAYERS - 1, :, wproj.shape[2] - TAIL :]
    for l, (qkv, bq) in enumerate(((qkv0, bq0), (qkv1, bq1))):
        bq[...] = jnp.zeros_like(bq)
        for place in range(GROUP):
            here = slice(place * cols, (place + 1) * cols)
            for c in range(3):
                where = (3 * place + c) * cols
                qkv[:, where : where + cols] = wqkv[l, c, :, here]
                if c != 1:
                    bq[:, where : where + cols] = bqv[l, c // 2 : c // 2 + 1, here]


def pack(w_qkv, b_qv, w_out, w_fc, w_proj):
    depth, out_cols, units = w_fc.shape[1], w_out.shape[1], w_fc.shape[2]
    rest = LAYERS * (out_cols + 2 * units) - TAIL
    outs = [shape((depth, rest), BF16), shape((depth, 3 * out_cols), BF16)]
    outs += [shape((depth, 3 * out_cols + TAIL), BF16)]
    outs += [shape((1, 3 * out_cols), F32)] * 2
    return pl.pallas_call(
        pack_body,
        in_specs=[VMEM] * 5,
        out_specs=[VMEM] * 5,
        out_shape=outs,
        compiler_params=pltpu.CompilerParams(vmem_limit_bytes=VMEM_BYTES),
    )(
        w_qkv.transpose(0, 2, 1, 3),
        b_qv,
        w_out.transpose(0, 2, 1),
        w_fc,
        w_proj.transpose(0, 2, 1),
    )


def finish_body(small, fc1, proj1, qkv1, out1, proj0, qkv0, out0, near, *refs):
    *came, grad_in, middle, own, other, bproj_in, outputs, grad, gain1, bias1, bqv, bout, gain2, bias2, bfc, bproj, wfc, wproj, wout, wqkv = refs
    def rows(at):
        grad[at, :] = grad_in[at, :]
        total = own[at, :].astype(F32) + other[at, :].astype(F32)
        outputs[at, :] = (middle[at, :] + total + bproj_in[...]).astype(BF16)

    each_rows(grad.shape[0], LN_ROWS, rows)
    fc0 = near[...]
    for one in came:
        fc0 = fc0 + one[...].astype(F32)
    width = small.shape[1]
    cols = bqv.shape[2] // GROUP
    wfc[0] = fc0
    wfc[1] = fc1[...]
    for l, proj, qkv, out in ((0, proj0, qkv0, out0), (1, proj1, qkv1, out1)):
        at = l * (small.shape[0] // 2)
        for target, where in ((gain1, 0), (bias1, 1), (bout, 4), (gain2, 5), (bias2, 6), (bproj, 9)):
            target[l : l + 1, :] = small[at + where : at + where + 1, :]
        for i in range(bfc.shape[1] // width):
            bfc[l : l + 1, i * width : (i + 1) * width] = small[at + 7 + i : at + 8 + i, :]
        for place in range(GROUP):
            for i in range(2):
                where = place * 3 * cols + 2 * i * cols
                line, lane = at + 2 + where // width, where % width
                bqv[l, i : i + 1, place * cols : (place + 1) * cols] = small[
                    line : line + 1, lane : lane + cols
                ]
        wproj[l] = proj[...]
        wout[l] = out[...]
        for place in range(GROUP):
            for c in range(3):
                at = (3 * place + c) * cols
                wqkv[l, c, :, place * cols : (place + 1) * cols] = qkv[:, at : at + cols]


def finish(small, totals, near, came, last, out_cols, units):
    depth, width = totals[0].shape[0], small.shape[1]
    vector = shape((LAYERS, width), F32)
    grad = last[0].shape
    outs = [shape(grad, BF16), shape(grad, F32)]
    outs += [vector, vector, shape((LAYERS, 2, out_cols), F32), vector, vector, vector]
    outs += [shape((LAYERS, units), F32), vector, shape((LAYERS, depth, units), F32)]
    outs += [shape((LAYERS, depth, units), F32), shape((LAYERS, depth, out_cols), F32)]
    outs += [shape((LAYERS, 3, depth, out_cols), F32)]
    return pl.pallas_call(
        finish_body,
        in_specs=[VMEM] * (2 + len(totals) + len(came) + len(last)),
        out_specs=[VMEM] * len(outs),
        out_shape=outs,
        compiler_params=pltpu.CompilerParams(vmem_limit_bytes=VMEM_BYTES),
    )(small, *totals, near, *came, *last)


def pull_last_body(
    grad_q, grad_kv, grad_kv_back, gain, qkv, grad_in, stream_in,
    low_one1_in, grad_qkv1_in, low_out1_in, mixed1_in, low_one_in, low_out_in, mixed_in, stay0_in, met0_in,
    gain1, bias1, bqkv1, bout1, gain2_1, bias2_1, bfc1, bproj1, bout0, gain2_0, bias2_0, bfc0, bproj0,
    grad_new, small, total0, total1, total2, total3, total4,
    full, sum_qkv, sum_gain, sum_bias, held, came, far, w_qkv, grad, stream, back_got, part, got,
    left1, wide1, right1, narrow1, left, right, narrow, plain, flipped,
    stay0, met0, far0, came0,
    away1, gone1, stay1, go1, met1, far1, came1,
    away2, gone2, stay2, go2, met2, far2, came2,
    away3, gone3, stay3, go3, met3, far3, came3,
    away4, gone4, stay4, go4, met4, far4, came4,
    send, recv, load, flush
):
    links = Links(send, recv)
    loads = load_columns(
        (
            (low_one1_in, None, left1),
            (grad_qkv1_in, None, wide1),
            (low_out1_in, None, right1),
            (mixed1_in, None, narrow1),
            (stay0_in, None, stay0),
            (met0_in, None, met0),
            (qkv, None, w_qkv),
            (grad_in, None, grad),
            (stream_in, None, stream),
            (low_one_in, None, left),
            (low_out_in, None, right),
            (mixed_in, None, narrow),
        ),
        load,
    )
    links.greet(
        [links.peer(s) for s in range(1, GROUP)]
        + [links.beyond(1, s) for s in range(GROUP)]
        + [links.beyond(links.groups - 1, s) for s in range(GROUP)]
        + [{"tp": links.other}]
        + group_greets(links)
    )
    chunks = [pl.ds(c * CHUNK[0], CHUNK[0]) for c in range(grad.shape[0] // CHUNK[0])]
    start_pulls, wait_pulls, finish_pulls = trade_pulls(
        links, grad_q, grad_kv, grad_kv_back, full, back_got
    )
    swaps = [links.swap(part.at[rows], got.at[rows]) for rows in chunks]
    parts = (
        (away1, gone1, stay1, go1, met1, far1, came1, total1),
        (away2, gone2, stay2, go2, met2, far2, came2, total2),
        (away3, gone3, stay3, go3, met3, far3, came3, total3),
        (away4, gone4, stay4, go4, met4, far4, came4, total4),
    )
    core_sums, over_x, group_sums, spans = [], [], [], []
    for at, (away, gone, stay, go, met, *rest) in enumerate(parts):
        core_sums.append(CoreSum(links, stay, go, away, gone))
        size = stay.shape[1]
        step = size if at % 2 else size // 2
        spans.append([])
        for start in range(0, size, step):
            place = pl.ds(start, step)
            spans[at].append(len(over_x))
            over_x.append(links.copy(go.at[:, place], met.at[:, place], links.peer(2)))
            group_sums.append(GroupSum(links, *[ref.at[:, place] for ref in (stay, met, *rest)]))
    early_sum = GroupSum(links, stay0, met0, far0, came0, total0)
    smalls = RowSum(links, held, came, far)
    sums_one = (gain1, bias1, bqkv1, bout1, gain2_1, bias2_1, bfc1, bproj1)
    sums_zero = (sum_gain, sum_bias, sum_qkv, bout0, gain2_0, bias2_0, bfc0, bproj0)
    start_pulls()
    for total in (sum_qkv, sum_gain, sum_bias):
        total[...] = jnp.zeros_like(total)
    for one in loads:
        one.wait()
    early_sum.send(0)
    core_sums[0].multiply(left1, wide1, plain, flipped)
    core_sums[1].multiply(right1, narrow1, plain, flipped)
    held[0] = jnp.zeros(held.shape[1:], F32)
    pack_sums(sums_one, held.at[0], held.shape[1] // 2)
    core_sums[0].add()
    core_sums[1].add()
    for at in spans[0] + spans[1]:
        over_x[at].start()
    for c, rows in enumerate(chunks):
        wait_pulls(c)
        pull_qkv_rows(c * CHUNK[0], None, links, full, back_got, w_qkv, part, sum_qkv)
        swaps[c].start()
    early_sum.pass_on(0)
    core_sums[2].multiply(left, full, plain, flipped)
    core_sums[3].multiply(right, narrow, plain, flipped)
    core_sums[2].add()
    for at in spans[2]:
        over_x[at].start()
    core_sums[3].add()
    for at in spans[3]:
        over_x[at].start()
    for c, rows in enumerate(chunks):
        swaps[c].wait()
        pull_norm_rows(c * CHUNK[0], grad, part, got, stream, gain, grad_new, (sum_gain, sum_bias))
    flush(0)
    pack_sums(sums_zero, held.at[0], 0)
    smalls.near[0].start()
    smalls.step(0)
    smalls.near[1].start()
    for at, one in enumerate(group_sums):
        over_x[at].wait()
        one.send(0)
        if at:
            group_sums[at - 1].pass_on(0)
        if at == 3:
            smalls.step(1)
            for far_one in smalls.along:
                far_one.start()
    group_sums[-1].pass_on(0)
    finish_pulls()
    small[...] = smalls.finish()
    early_sum.finish(2)
    for one in group_sums:
        one.finish(2)


def pull_last_segment(pulls, gain, qkv, grad, stream, factors, sums_in, smalls):
    CHUNK[0] = SIZES[4]
    rows, width = grad.shape
    cols = pulls[0].shape[2]
    out_cols = GROUP * cols
    total = 3 * out_cols
    units = sums_in[0].shape[1]
    chunks = rows // CHUNK[0]
    groups = lax.axis_size("fsdp") // GROUP
    copies = pltpu.SemaphoreType.DMA(
        (pull_copies(rows) + chunks + 10 + 7 * (groups - 1) + groups + 1,)
    )
    sizes = [total, out_cols, total, out_cols]
    quarter = width // 4
    scratch = []
    for size in sizes:
        stay = shape((quarter, size), BF16)
        scratch += [pltpu.VMEM((2 * quarter, size), BF16)] * 2
        scratch += [pltpu.VMEM(stay.shape, BF16)]
        scratch += [pltpu.VMEM(stay.shape, BF16)] + group_scratch(stay, groups, True)
    low = pltpu.VMEM((rows, width), BF16)
    high = pltpu.VMEM((rows, width), F32)
    mixed = pltpu.VMEM((rows, out_cols), BF16)
    flip = pltpu.VMEM((width, rows), BF16)
    eight = pltpu.VMEM((8, width), F32)
    return run_links(
        pull_last_body,
        4,
        [(VMEM, pull) for pull in pulls]
        + [(VMEM, gain)]
        + [(ANY, array) for array in (qkv, grad, stream, *factors, *sums_in)]
        + [(VMEM, array) for array in smalls],
        [(VMEM, shape((rows, width), F32)), (VMEM, shape((24, width), F32))]
        + [(VMEM, shape((quarter // groups, size), F32)) for size in [units] + sizes],
        [
            pltpu.VMEM((rows, total), BF16),
            pltpu.VMEM((8, total), F32),
            eight,
            eight,
            pltpu.VMEM((3, 24, width), F32),
            pltpu.VMEM((2, 24, width), F32),
            pltpu.VMEM((groups - 1, 24, width), F32),
            pltpu.VMEM((width, total), BF16),
            high,
            high,
            pltpu.VMEM((GROUP, rows, 2 * cols), BF16),
            low,
            low,
            low,
            pltpu.VMEM((rows, total), BF16),
            low,
            mixed,
            low,
            low,
            mixed,
            flip,
            flip,
            pltpu.VMEM((quarter, units), BF16),
        ]
        + group_scratch(shape((quarter, units), BF16), groups, True)
        + scratch
        + [copies, copies, pltpu.SemaphoreType.DMA((12,))],
        flops=2 * rows * width * (3 * total + 2 * out_cols),
        moved=rows * width * 24 + width * total * 2,
        late=(0,),
    )


def halving_order(count):
    order = [0]
    bit = count // 2
    while bit:
        order = order + [at + bit for at in order]
        bit //= 2
    return order


def flip_slots(links, source, plain, flipped):
    plain[...] = source[...].T
    depth = plain.shape[0] // (GROUP * links.groups)
    slot = 0
    for s in (0, 2, 1, 3):
        for other in halving_order(links.groups):
            owner = (links.group ^ other) * GROUP + (links.place ^ s)
            flipped[slot * depth : (slot + 1) * depth, :] = plain[
                pl.ds(pl.multiple_of(owner * depth, depth), depth), :
            ]
            slot += 1


class CoreSum:
    def __init__(self, links, stay, go, away, got):
        self.links, self.stay, self.go, self.away, self.got = links, stay, go, away, got
        self.copy = links.copy(away, got, links.peer(1))
        self.sent = False

    def release(self):
        self.copy.wait_send()
        self.sent = True

    def multiply(self, x, g, plain, flipped):
        flip_slots(self.links, x, plain, flipped)
        quarter = self.stay.shape[0]

        def far(at):
            self.away[:, at] = dot(flipped[2 * quarter :, :], g[:, at]).astype(BF16)

        def near(at):
            self.stay[:, at] = dot(flipped[:quarter, :], g[:, at]).astype(BF16)
            self.go[:, at] = dot(flipped[quarter : 2 * quarter, :], g[:, at]).astype(BF16)

        tiles(g.shape[1], 512, far)
        self.copy.start()
        tiles(g.shape[1], 512, near)

    def add(self):
        if not self.sent:
            self.release()
        self.copy.wait_recv()
        quarter = self.stay.shape[0]
        chunk = 16
        for target, first in ((self.go, quarter), (self.stay, 0)):

            def body(at):
                from_row = pl.ds(pl.multiple_of(at.start + first, chunk), chunk)
                total = target[at, :].astype(F32) + self.got[from_row, :].astype(F32)
                target[at, :] = total.astype(BF16)

            each_rows(quarter, chunk, body)


class GroupSum:
    def __init__(self, links, stay, met, far, came, result):
        self.stay, self.met, self.far, self.came, self.result = stay, met, far, came, result
        self.depth = result.shape[0]
        self.copies, self.counts = [], []
        first, count, bit = 0, links.groups // 2, 1
        while count:
            rows = pl.ds(first * self.depth, count * self.depth)
            device = {"fsdp": (links.group ^ bit) * GROUP + links.place}
            self.copies.append(links.copy(far.at[rows], came.at[rows], device))
            self.counts.append((first, count))
            first, count, bit = first + count, count // 2, bit * 2

    def add(self, step, target, target_first, first, count):
        chunk = 16

        def body(at):
            def rows(slot):
                return pl.ds(pl.multiple_of(at.start + slot * self.depth, chunk), chunk)

            total = self.stay[rows(first), :].astype(F32) + self.met[rows(first), :].astype(F32)
            for came_first, _ in self.counts[:step]:
                total = total + self.came[rows(came_first + first), :].astype(F32)
            target[rows(target_first), :] = total.astype(target.dtype)

        each_rows(count * self.depth, chunk, body)

    def send(self, step):
        first, count = self.counts[step]
        self.add(step, self.far, first, count, count)
        self.copies[step].start()

    def pass_on(self, step):
        self.copies[step].wait()
        self.send(step + 1)

    def finish(self, sent=1):
        for step in range(sent, len(self.copies)):
            self.pass_on(step - 1)
        self.copies[-1].wait()
        self.add(len(self.copies), self.result, 0, 0, 1)


def group_scratch(stay, groups, met):
    rows, size = stay.shape
    far = pltpu.VMEM((rows - rows // groups, size), BF16)
    return ([pltpu.VMEM((rows, size), BF16)] if met else []) + [far, far]


def group_greets(links):
    return [links.beyond(onward, 0) for onward in range(2, links.groups - 1)]


def doc_start_rows(sc, docs, positions):
    start = jnp.zeros_like(positions)
    for d in range(docs):
        first = sc[2 + d]
        start = jnp.where(first <= positions, jnp.maximum(start, first), start)
    return start


def doc_start_one(sc, docs, position):
    start = jnp.int32(0)
    for d in range(docs):
        first = sc[2 + d]
        start = jnp.where(first <= position, jnp.maximum(start, first), start)
    return start


def query_rows(sc, docs, block, size):
    first = sc[1] + block * size
    position = first + lax.broadcasted_iota(jnp.int32, (1, size), 1)
    start = doc_start_rows(sc, docs, position)
    return (
        jnp.concatenate([position, position], 1),
        jnp.concatenate([start, start], 1),
        doc_start_one(sc, docs, first),
    )


def head_stack(rows, scale):
    value = rows.astype(F32)
    if scale != 1.0:
        value = value * scale
    lane = lax.broadcasted_iota(jnp.int32, value.shape, 1)
    return jnp.concatenate(
        [jnp.where(lane < HEAD_DIM, value, 0.0), jnp.where(lane >= HEAD_DIM, value, 0.0)], 0
    ).astype(BF16)


def block_at(block, size):
    return pl.ds(pl.multiple_of(block * size, size), size)


def masked_scores(keys, queries, first_key, position, start):
    scores = dot_last(keys, queries)
    key_at = first_key + lax.broadcasted_iota(jnp.int32, (keys.shape[0], 1), 0)
    return jnp.where((key_at >= start) & (key_at <= position), scores, NEG)


def flash_step(keys, values_ref, queries, at, first_key, position, start, acc, carry):
    top, total = carry
    scores = masked_scores(keys, queries, first_key, position, start)
    top_new = jnp.maximum(top, jnp.max(scores, 0, keepdims=True))
    expo = jnp.exp(scores - top_new)
    shrink = jnp.exp(top - top_new)
    total = total * shrink + jnp.sum(expo, 0, keepdims=True)
    expo = expo.astype(BF16)
    for h in range(2):
        lanes = slice(h * QB, (h + 1) * QB)
        rows = slice(h * HEAD_DIM, (h + 1) * HEAD_DIM)
        acc[rows, :] = acc[rows, :] * shrink[:, lanes] + dot(values_ref[rows, at], expo[:, lanes])
    return top_new, total


def attend_body(docs, sc, qkv, kv, mixed, out, log_total, v_flip, v_back, acc):
    block = pl.program_id(0)
    span, cols = out.shape[0] * pl.num_programs(0), out.shape[1]
    rows = qkv.shape[0]

    @pl.when(block == 0)
    def _():
        for first in range(0, rows, QB):
            v_flip[:, first : first + QB] = qkv[first : first + QB, 2 * cols :].T
            v_back[:, first : first + QB] = kv[first : first + QB, cols:].T

    position, start, lowest = query_rows(sc, docs, block, QB)
    queries = head_stack(qkv[block_at(block, QB), :cols], HEAD_DIM**-0.5)
    acc[...] = jnp.zeros_like(acc)
    least = jnp.maximum(lowest - sc[1], 0) // KB
    last = ((block + 1) * QB - 1) // KB
    before = sc[1] - span

    def step(back, carry):
        at = block_at(last - back, KB)
        keys = qkv[at, cols : 2 * cols]
        first_key = sc[1] + (last - back) * KB
        return flash_step(keys, v_flip, queries, at, first_key, position, start, acc, carry)

    def step_back(where, carry):
        at = block_at(where, KB)
        return flash_step(
            kv[at, :cols], v_back, queries, at, before + where * KB, position, start, acc, carry
        )

    carry = (jnp.full((1, 2 * QB), NEG, F32), jnp.zeros((1, 2 * QB), F32))
    carry = lax.fori_loop(0, last - least + 1, step, carry)
    top, total = lax.fori_loop(
        jnp.minimum(jnp.maximum(lowest - before, 0), span) // KB, span // KB, step_back, carry
    )
    sums = top + jnp.log(total)
    share = 1.0 / total
    parts = []
    for h in range(2):
        lanes = slice(h * QB, (h + 1) * QB)
        log_total[h : h + 1, :] = sums[:, lanes]
        parts.append(acc[h * HEAD_DIM : (h + 1) * HEAD_DIM, :] * share[:, lanes])
    value = jnp.concatenate(parts, 0).T
    out[...] = value
    mixed[...] = value.astype(BF16)


def attend(sc, docs, pieces, kv):
    rows, cols = pieces.shape[1], pieces.shape[2] // 3
    span = GROUP * rows
    low_flip = pltpu.VMEM((cols, span), BF16)
    block = pl.BlockSpec((QB, cols), lambda j, sc: (j, 0))
    mixed, out, log_total = run_kernel(
        functools.partial(attend_body, docs),
        (span // QB,),
        sc,
        [
            (whole((span, 3 * cols)), pieces.reshape(span, 3 * cols)),
            (whole((span, 2 * cols)), kv.reshape(span, 2 * cols)),
        ],
        [
            (block, shape((span, cols), BF16)),
            (block, shape((span, cols), F32)),
            (pl.BlockSpec((8, QB), lambda j, sc: (0, j)), shape((8, span), F32)),
        ],
        scratch=[low_flip, low_flip, pltpu.VMEM((cols, QB), F32)],
        flops=span * span * cols * 4,
        moved=span * cols * 20,
    )
    return mixed.reshape(GROUP, rows, cols), out, log_total


def pull_step(keys, values, at, first_key, position, start, queries, grads, log_rows, delta, refs):
    k_flip, grad_k, grad_v, grad_q = refs
    scores = masked_scores(keys, queries, first_key, position, start)
    probs = jnp.exp(scores - log_rows)
    grad_probs = dot_last(values, grads)
    grad_scores = (probs * (grad_probs - delta)).astype(BF16)
    grad_v[at, :] += dot(probs.astype(BF16), grads)
    grad_k[at, :] += dot(grad_scores, queries)
    size = grad_q.shape[1]
    for h in range(2):
        rows = slice(h * HEAD_DIM, (h + 1) * HEAD_DIM)
        grad_q[rows, :] += dot(k_flip[rows, at], grad_scores[:, h * size : (h + 1) * size])


def pull_body(
    docs, sc, qkv, grad_mixed, kv, out, log_total, grad_q_out, grad_kv, grad_kv_back,
    k_flip, grad_k, grad_v, k_back_flip, grad_k_back, grad_v_back, grad_q
):
    block = pl.program_id(0)
    span, cols = qkv.shape[0], out.shape[1]
    size = out.shape[0]
    before = sc[1] - span

    @pl.when(block == 0)
    def _():
        for first in range(0, span, PULL_KB):
            k_flip[:, first : first + PULL_KB] = qkv[first : first + PULL_KB, cols : 2 * cols].T
            k_back_flip[:, first : first + PULL_KB] = kv[first : first + PULL_KB, :cols].T
        for total in (grad_k, grad_v, grad_k_back, grad_v_back):
            total[...] = jnp.zeros_like(total)

    grad_q[...] = jnp.zeros_like(grad_q)
    position, start, lowest = query_rows(sc, docs, block, size)
    queries = head_stack(qkv[block_at(block, size), :cols], HEAD_DIM**-0.5)
    grad_rows = grad_mixed[block_at(block, size), :]
    grads = head_stack(grad_rows, 1.0)
    flipped = (grad_rows.astype(F32) * out[...]).T
    heads = [slice(h * HEAD_DIM, (h + 1) * HEAD_DIM) for h in range(2)]
    delta = jnp.concatenate([jnp.sum(flipped[rows, :], 0, keepdims=True) for rows in heads], 1)
    log_rows = jnp.concatenate([log_total[h : h + 1, :] for h in range(2)], 1)

    def step(where, carry):
        at = block_at(where, PULL_KB)
        pull_step(
            qkv[at, cols : 2 * cols], qkv[at, 2 * cols :], at, sc[1] + where * PULL_KB,
            position, start, queries, grads, log_rows, delta, (k_flip, grad_k, grad_v, grad_q),
        )
        return carry

    def step_back(where, carry):
        at = block_at(where, PULL_KB)
        pull_step(
            kv[at, :cols], kv[at, cols:], at, before + where * PULL_KB,
            position, start, queries, grads, log_rows, delta, (k_back_flip, grad_k_back, grad_v_back, grad_q),
        )
        return carry

    last = ((block + 1) * size - 1) // PULL_KB
    lax.fori_loop(jnp.maximum(lowest - sc[1], 0) // PULL_KB, last + 1, step, 0)
    lax.fori_loop(
        jnp.minimum(jnp.maximum(lowest - before, 0), span) // PULL_KB, span // PULL_KB, step_back, 0
    )
    grad_q_out[...] = (grad_q[...] * HEAD_DIM**-0.5).T.astype(BF16)

    @pl.when(block == pl.num_programs(0) - 1)
    def _():
        grad_kv[:, :cols] = grad_k[...].astype(BF16)
        grad_kv[:, cols:] = grad_v[...].astype(BF16)
        grad_kv_back[:, :cols] = grad_k_back[...].astype(BF16)
        grad_kv_back[:, cols:] = grad_v_back[...].astype(BF16)


def attend_pull(sc, docs, pieces, grads, kv, out, log_total):
    rows, cols = pieces.shape[1], pieces.shape[2] // 3
    span = GROUP * rows
    block = pl.BlockSpec((PULL_QB, cols), lambda j, sc: (j, 0))
    both = (whole((span, 2 * cols)), shape((span, 2 * cols), BF16))
    low_flip = pltpu.VMEM((cols, span), BF16)
    high = pltpu.VMEM((span, cols), F32)
    parts = run_kernel(
        functools.partial(pull_body, docs),
        (span // PULL_QB,),
        sc,
        [
            (whole((span, 3 * cols)), pieces.reshape(span, 3 * cols)),
            (whole((span, cols)), grads.reshape(span, cols)),
            (whole((span, 2 * cols)), kv.reshape(span, 2 * cols)),
            (block, out),
            (pl.BlockSpec((8, PULL_QB), lambda j, sc: (0, j)), log_total),
        ],
        [(block, shape((span, cols), BF16)), both, both],
        scratch=[low_flip, high, high, low_flip, high, high, pltpu.VMEM((cols, PULL_QB), F32)],
        flops=span * span * cols * 9,
        moved=span * cols * 30,
    )
    return [part.reshape(GROUP, rows, part.shape[1]) for part in parts]


def swap_tp(value):
    return lax.ppermute(value, "tp", [(0, 1), (1, 0)])


def swap_fsdp(value, s):
    return lax.ppermute(value, "fsdp", [(i, i ^ s) for i in range(lax.axis_size("fsdp"))])


def shift_fsdp(value, by):
    size = lax.axis_size("fsdp")
    return lax.ppermute(value, "fsdp", [(i, i + by) for i in range(size) if 0 <= i + by < size])


def gather(shard):
    return lax.all_gather(shard, "fsdp", axis=0, tiled=True)


def tie(*values):
    return lax.optimization_barrier(values)


def shards(
    tokens,
    cotangent,
    segments,
    doc_batch,
    ln1_gain,
    ln1_bias,
    w_qkv,
    b_qv,
    w_out,
    b_out,
    ln2_gain,
    ln2_bias,
    w_fc,
    b_fc,
    w_proj,
    b_proj,
):
    rows, width = tokens.shape
    depth = w_qkv.shape[1]
    out_cols = w_out.shape[1]
    units = w_fc.shape[2]
    cols = out_cols // GROUP
    docs = doc_batch.shape[0]
    me = lax.axis_index("fsdp")
    total_rows = rows * lax.axis_size("fsdp")

    rest, *packed = pack(w_qkv, b_qv, w_out, w_fc, w_proj)
    rest = gather(rest)
    shards_qkv, bias_qkv = packed[:LAYERS], packed[LAYERS:]

    def rest_at(l):
        first = l * (out_cols + 2 * units)
        return (first, first + out_cols, first + out_cols + units)

    def row(vector):
        return vector.reshape(1, vector.shape[0])

    stored = []
    stream, low_one, full_qkv, doc_tokens, doc_first, pieces, kv_back = first_segment(
        tokens,
        row(ln1_gain[0]),
        row(ln1_bias[0]),
        shards_qkv[0],
        bias_qkv[0],
        segments.reshape(rows // 128, 128),
        docs,
    )
    qkv_of = [full_qkv]
    doc_tokens, doc_first = (value[:, 0].astype(jnp.int32) for value in (doc_tokens, doc_first))
    sc = jnp.concatenate(
        [jnp.stack([me % GROUP, (me // GROUP) * (GROUP * rows)]).astype(jnp.int32), doc_first]
    )
    doc_ids = jnp.arange(docs, dtype=jnp.int32)
    is_doc = segments[:, None] == doc_ids[None, :]
    in_batch = doc_batch[:, None] == jnp.arange(MB, dtype=jnp.int32)[None, :]
    counts = jnp.sum(jnp.where(in_batch, doc_tokens[:, None], 0), 0)
    doc_count = jnp.sum(jnp.where(in_batch, counts[None, :], 0), 1)
    row_count = jnp.sum(jnp.where(is_doc, doc_count[None, :], 0), 1).astype(F32)
    row_weight = total_rows / (MB * row_count)
    for l in range(LAYERS - 1):
        mixed, out, log_total = attend(sc, docs, pieces, kv_back)
        vectors = (b_out[l], ln2_gain[l], ln2_bias[l], b_fc[l], b_proj[l], ln1_gain[l + 1], ln1_bias[l + 1])
        mixed_full, middle, low_two, hidden, act, *later = between_segment(
            mixed,
            stream,
            [row(vector) for vector in vectors],
            bias_qkv[l + 1],
            rest,
            rest_at(l),
            units,
            shards_qkv[l + 1],
        )
        stored.append(
            (stream, low_one, pieces, kv_back, out, log_total, mixed_full, middle, low_two, hidden, act)
        )
        stream, low_one, full_qkv, pieces, kv_back = later
        qkv_of.append(full_qkv)

    l = LAYERS - 1
    mixed, out, log_total = attend(sc, docs, pieces, kv_back)
    grad = cotangent.astype(F32) * row_weight[:, None]
    (
        mixed_full,
        middle,
        low_two,
        act,
        part_two,
        low_proj,
        sum_bproj,
        grad_hidden,
        sum_bfc,
        grad,
        low_out,
        sum_gain_two,
        sum_bias_two,
        sum_bout,
        grad_mixed,
        *feed_parts,
    ) = turn_segment(
        mixed,
        stream,
        grad,
        [row(vector) for vector in (b_out[l], ln2_gain[l], ln2_bias[l], b_fc[l])],
        rest,
        qkv_of[l],
        rest_at(l),
        units,
    )
    last = [middle, part_two, swap_tp(part_two), row(b_proj[l])]

    stay0, go0, stay1, go1 = feed_parts
    met0 = swap_fsdp(go0, 2)
    grad_mixed, stay0 = tie(grad_mixed, stay0)
    pulls = attend_pull(sc, docs, pieces, grad_mixed, kv_back, out, log_total)
    *pulls, met0 = tie(*pulls, met0)
    sums_one = [sum_bout, sum_gain_two, sum_bias_two, sum_bfc, sum_bproj]
    low_one_kept, low_out_kept, mixed_kept = low_one, low_out, mixed_full
    (stream_below, low_one, pieces, kv_back, out, log_total, mixed_full, middle, low_two, hidden, act) = stored[0]
    (
        grad_qkv,
        sum_bqkv,
        sum_gain_one,
        sum_bias_one,
        low_proj,
        sum_bproj,
        grad_hidden,
        sum_bfc,
        grad,
        low_out,
        sum_gain_two,
        sum_bias_two,
        sum_bout,
        grad_mixed,
        *later,
    ) = pull_both_segment(
        pulls,
        row(ln1_gain[1]),
        row(ln2_gain[0]),
        qkv_of[1],
        rest,
        rest_at(0),
        units,
        grad,
        stream,
        hidden,
        middle,
        [stay0, met0, stay1, go1],
        [low_two, act],
    )
    feed_totals, near, far, (stay0, go0) = later[:2], later[2], later[3:-2], later[-2:]
    came = []
    others = halving_order(lax.axis_size("fsdp") // GROUP)[1:]
    for other, value in zip(others, far):
        came.append(swap_fsdp(value, GROUP * other))
    met0 = swap_fsdp(go0, 2)
    sums_one = [sum_gain_one, sum_bias_one, sum_bqkv] + sums_one
    pulls = attend_pull(sc, docs, pieces, grad_mixed, kv_back, out, log_total)
    *pulls, came, met0 = tie(*pulls, came, met0)
    sums_zero = [sum_bout, sum_gain_two, sum_bias_two, sum_bfc, sum_bproj]
    grad, small, proj0, qkv1, out1, qkv0, out0 = pull_last_segment(
        pulls,
        row(ln1_gain[0]),
        qkv_of[0],
        grad,
        stream_below,
        [low_one_kept, grad_qkv, low_out_kept, mixed_kept, low_one, low_out, mixed_full],
        [stay0, met0],
        sums_one + sums_zero,
    )
    (
        outputs,
        grad,
        gain1,
        bias1,
        bqv,
        bout,
        gain2,
        bias2,
        bfc,
        bproj,
        grad_wfc,
        grad_wproj,
        grad_wout,
        grad_wqkv,
    ) = finish(
        small, [*feed_totals, qkv1, out1, proj0, qkv0, out0], near, came, [grad, *last], out_cols, units
    )
    grad_wproj = grad_wproj.transpose(0, 2, 1)
    grad_wout = grad_wout.transpose(0, 2, 1)
    grad_wqkv = grad_wqkv.transpose(0, 2, 1, 3)

    return (
        outputs,
        grad,
        gain1,
        bias1,
        grad_wqkv,
        bqv,
        grad_wout,
        bout,
        gain2,
        bias2,
        grad_wfc,
        bfc,
        grad_wproj,
        bproj,
    )


def solution(mesh):
    placed = (
        P("fsdp", None),
        P("fsdp", None),
        P("fsdp"),
        P(),
        P(),
        P(),
        P(None, "fsdp", None, "tp"),
        P(None, None, "tp"),
        P(None, "tp", "fsdp"),
        P(),
        P(),
        P(),
        P(None, "fsdp", "tp"),
        P(None, "tp"),
        P(None, "tp", "fsdp"),
        P(),
    )
    return jax.shard_map(
        shards,
        mesh=mesh,
        in_specs=placed,
        out_specs=(
            P("fsdp", None),
            P("fsdp", None),
            P(),
            P(),
            P(None, "fsdp", None, "tp"),
            P(None, None, "tp"),
            P(None, "tp", "fsdp"),
            P(),
            P(),
            P(),
            P(None, "fsdp", "tp"),
            P(None, "tp"),
            P(None, "tp", "fsdp"),
            P(),
        ),
        check_vma=False,
    )
```
